32 devices in a mesh: dp: 8 (over z, x), tensor: 4 (over y, core).
Axes of the slice: x: 2, y: 2, z: 4, core: 2. Of those that a mesh axis runs over, the one named last changes fastest.
Arguments:
- inputs: bfloat16 [16384, 1024], P(('dp', 'tensor')), may hold values from -12 to 12
- cotangent: bfloat16 [16384, 1024], P(('dp', 'tensor')), may hold values from -12 to 12
- routes: int32 [16384, 1], P('dp'), may hold values from 0 to 3
- prefixes: int32 [16], P('dp'), may hold values from 102 to 512
- gain_one: float32 [1024], replicated, may hold values from 0.5 to 1.5
- shift_one: float32 [1024], replicated, may hold values from -1.25 to 1.25
- qkv_weight: bfloat16 [1024, 3, 1024], P(None, None, 'tensor'), may hold values from -0.1875 to 0.1875
- out_weight: bfloat16 [1024, 1024], P('tensor'), may hold values from -1.5 to 1.5
- gain_two: float32 [1024], replicated, may hold values from 0.5 to 1.5
- shift_two: float32 [1024], replicated, may hold values from -1.25 to 1.25
- up_weight: bfloat16 [1024, 4096], P(None, 'tensor'), may hold values from -0.1875 to 0.1875
- down_weight: bfloat16 [4096, 1024], P('tensor'), may hold values from -0.1875 to 0.1875
- expert_up: bfloat16 [4, 1024, 4096], P(None, None, 'tensor'), may hold values from -0.1875 to 0.1875
- expert_down: bfloat16 [4, 4096, 1024], P(None, 'tensor'), may hold values from -0.5 to 0.5
- router_weight: bfloat16 [1024, 4], replicated, may hold values from -0.125 to 0.125
- mix_weight: bfloat16 [1024, 2], replicated, may hold values from -0.125 to 0.125
Outputs:
- layer_output: bfloat16 [16384, 1024], P(('dp', 'tensor'))
- input_grad: float32 [16384, 1024], P(('dp', 'tensor'))
- gain_one_grad: float32 [1024], P(('dp', 'tensor'))
- shift_one_grad: float32 [1024], P(('dp', 'tensor'))
- qkv_weight_grad: float32 [1024, 3, 1024], P('dp', None, 'tensor')
- out_weight_grad: float32 [1024, 1024], P('tensor', 'dp')
- gain_two_grad: float32 [1024], P(('dp', 'tensor'))
- shift_two_grad: float32 [1024], P(('dp', 'tensor'))
- up_weight_grad: float32 [1024, 4096], P('dp', 'tensor')
- down_weight_grad: float32 [4096, 1024], P('tensor', 'dp')
- expert_up_grad: float32 [4, 1024, 4096], P(None, 'dp', 'tensor')
- expert_down_grad: float32 [4, 4096, 1024], P(None, 'tensor', 'dp')
- router_weight_grad: float32 [1024, 4], P(('dp', 'tensor'))
- mix_weight_grad: float32 [1024, 2], P(('dp', 'tensor'))
The draws below stay inside these ranges and needn't reach their ends.
All inputs are finite; a program needn't handle non-finite values.
Results may differ from the reference program's by a relative error of at most 0.03.
Values may be sent and summed in bfloat16 or wider, within the bound.
No kernel may reach another device: no remote copies, remote signals or barrier semaphores. Data moves between devices by JAX's collectives and lax.ppermute only.
A program may use at most 320 MiB of HBM per device.

```python
import jax
import jax.numpy as jnp
from jax import lax

D = 1024
H = 16
HD = 64
FF = 4096
EXPERTS = 4
SEQ_LEN = 1024
SEQ_DEV = 2
SEQS = 16
TOKENS = 16384
N_DP = 8


def plant(values, key, smallest, high):
    extent = values.shape
    spot = [jax.random.randint(jax.random.fold_in(key, axis), (), 0, extent[axis]) for axis in range(len(extent))]
    values = values.at[tuple(spot)].set(smallest)
    longest = extent.index(max(extent))
    spot[longest] = (spot[longest] + 1) % extent[longest]
    return values.at[tuple(spot)].set(high)


def strengthened(drawn, stream_key, source, target, blocks, factor):
    owner, partner = [(jnp.arange(drawn.shape[position]) // (drawn.shape[position] // blocks)).reshape([-1 if axis == position else 1 for axis in range(drawn.ndim)]) for position in (source, target)]
    chosen = jax.random.permutation(stream_key, blocks)[partner]
    strong = (owner == chosen) | (owner == (partner + blocks // 2) % blocks)
    return jnp.where(strong, factor * drawn, drawn)


def block_scale(key, shape, split, least, top_value):
    def one(dim, parts):
        draws = jax.random.uniform(jax.random.fold_in(jax.random.fold_in(key, 6), dim), (parts,), jnp.float32, least / len(split), top_value / len(split))
        return jnp.repeat(jnp.exp(draws), shape[dim] // parts).reshape((-1,) + (1,) * (len(shape) - dim - 1))

    level = one(*split[0])
    for cut in split[1:]:
        level = level * one(*cut)
    return level


def different_ones(stream_key, rows, amount, top, lift):
    sequence = jax.random.permutation(jax.random.fold_in(stream_key, 1), amount)
    pull = sequence
    for power in range(3):
        pull = pull * pull // amount
    pull = pull * lift // amount
    lots = jax.random.randint(jax.random.fold_in(stream_key, 2), (rows, amount), 0, 4096) + pull
    sure = jax.random.permutation(jax.random.fold_in(stream_key, 3), rows)[jnp.arange(amount) % rows]
    lots = jnp.where(jnp.arange(rows)[:, None] == sure[None, :], 1 << 14, lots)
    score = lots * amount + jnp.arange(amount)
    return lax.top_k(score.astype(jnp.int32), top)[1].astype(jnp.int32)


def scatter_about(rng, shape, width, bound, shards=(), dtype=jnp.bfloat16):
    factor_of = block_scale(rng, shape, shards, -0.22, 0.18) if shards else 1.0
    array = jax.random.normal(rng, shape, jnp.float32) * width * factor_of
    return jnp.minimum(jnp.maximum(array, -bound), bound).astype(dtype)


def heavy_noise(own_key, shape, width, bound, pieces, heavy, held_as=jnp.bfloat16):
    values = width * jax.random.normal(own_key, shape, jnp.float32)
    if pieces:
        values = values * block_scale(own_key, shape, pieces, -0.22, 0.18)
    return jnp.clip(strengthened(values, jax.random.fold_in(own_key, 3), *heavy), -bound, bound).astype(held_as)


def setup_inputs(seed: int = 0) -> dict:
    keys = jax.random.split(jax.random.key(seed), 17)
    return {
        "inputs": heavy_noise(keys[0], (TOKENS, D), 1.0, 12.0, ((0, 32),), (0, 1, 32, 2.75)),
        "cotangent": heavy_noise(keys[1], (TOKENS, D), 1.0, 12.0, ((0, 32),), (0, 1, 32, 2.75)),
        "routes": different_ones(keys[2], TOKENS, EXPERTS, 1, 2048),
        "prefixes": plant(jax.random.randint(keys[3], (SEQS,), SEQ_LEN // 10, SEQ_LEN // 2 + 1), jax.random.fold_in(keys[3], 1), SEQ_LEN // 10, (SEQ_LEN // 2 + 1) - 1).astype(jnp.int32),
        "gain_one": jnp.clip(1.0 + 0.1 * jax.random.normal(keys[4], (D,), jnp.float32), 0.5, 1.5),
        "shift_one": scatter_about(keys[5], (D,), 0.2, 1.25, (), jnp.float32),
        "qkv_weight": scatter_about(keys[6], (D, 3, H * HD), D ** -0.5, 0.1875, ((2, 4),)),
        "out_weight": scatter_about(keys[7], (H * HD, D), (H * HD // 64) ** -0.5, 1.5, ((0, 4),)),
        "gain_two": jnp.clip(1.0 + 0.1 * jax.random.normal(keys[8], (D,), jnp.float32), 0.5, 1.5),
        "shift_two": scatter_about(keys[9], (D,), 0.2, 1.25, (), jnp.float32),
        "up_weight": scatter_about(keys[10], (D, FF), D ** -0.5, 0.1875, ((1, 4),)),
        "down_weight": scatter_about(keys[11], (FF, D), (FF // 4) ** -0.5, 0.1875, ((0, 4),)),
        "expert_up": scatter_about(keys[12], (EXPERTS, D, FF), D ** -0.5, 0.1875, ((2, 4),)),
        "expert_down": scatter_about(keys[13], (EXPERTS, FF, D), (FF // 32) ** -0.5, 0.5, ((1, 4),)),
        "router_weight": scatter_about(keys[14], (D, EXPERTS), (2 * D) ** -0.5, 0.125),
        "mix_weight": scatter_about(keys[15], (D, 2), (2 * D) ** -0.5, 0.125),
    }


@jax.custom_vjp
def low(v):
    return lax.optimization_barrier(v.astype(jnp.bfloat16)).astype(jnp.float32)

@jax.custom_vjp
def low_back(v):
    return v

def low_keep(v):
    return (low(v), None)

def low_pass(kept, grad):
    return (grad,)

def back_keep(v):
    return (v, None)

def back_low(kept, grad):
    return (low(grad),)
low.defvjp(low_keep, low_pass)
low_back.defvjp(back_keep, back_low)
epsilon = 1e-05
exact_mode = lax.Precision.HIGHEST
masked_score = -1e+30

def matmul(left_side, right_side):
    return jnp.dot(left_side, right_side, precision=exact_mode, preferred_element_type=jnp.float32)

def layer_norm(values, norm_gain, norm_shift):
    average = lax.optimization_barrier(jnp.mean(values, axis=-1, keepdims=True))
    centered = values - average
    variance = lax.optimization_barrier(jnp.mean(centered * centered, axis=-1, keepdims=True))
    return centered * lax.rsqrt(variance + epsilon) * norm_gain + norm_shift

def gelu_exact(values):
    return jax.nn.gelu(values, approximate=False)

def visible_mask(first_row, row_count, length, prefix_len):
    query_pos = first_row + jnp.arange(row_count)[:, None]
    key_pos = jnp.arange(length)[None, :]
    return (key_pos <= query_pos) | (key_pos < prefix_len)

def attend(seq_pair):
    qkv_seq, prefix_len = seq_pair
    queries = qkv_seq[:, 0].reshape(SEQ_LEN, H, HD)
    key_rows = qkv_seq[:, 1].reshape(SEQ_LEN, H, HD)
    value_rows = qkv_seq[:, 2].reshape(SEQ_LEN, H, HD)
    scores = jnp.einsum('qhd,khd->hqk', queries, key_rows, precision=exact_mode) * HD ** (-0.5)
    scores = low_back(scores)
    visible = visible_mask(0, SEQ_LEN, SEQ_LEN, prefix_len)
    scores = jnp.where(visible[None], scores, masked_score)
    probability = low(jax.nn.softmax(scores, axis=-1))
    context = jnp.einsum('hqk,khd->qhd', probability, value_rows, precision=exact_mode)
    return context.reshape(SEQ_LEN, H * HD)

@jax.checkpoint
def expert_branch(normed, up_matrix, down_matrix):
    hidden = low(gelu_exact(low_back(matmul(normed, up_matrix))))
    return matmul(hidden, down_matrix)

def group_forward(rows_in, prefix_group, route_group, params):
    gain_one, shift_one, qkv_weight, out_weight, gain_two, shift_two, up_weight, down_weight, expert_up, expert_down, router_weight, mix_weight = params
    normed_one = low(layer_norm(rows_in, gain_one, shift_one))
    qkv_all = low_back(low(matmul(normed_one, qkv_weight.reshape(D, 3 * H * HD))))
    qkv_seq = qkv_all.reshape(SEQ_DEV, SEQ_LEN, 3, H * HD)
    context = lax.map(jax.checkpoint(attend), (qkv_seq, prefix_group))
    context = low_back(low(context.reshape(SEQ_DEV * SEQ_LEN, H * HD)))
    attention = low_back(matmul(context, out_weight))
    middle = rows_in + attention
    normed_two = low(layer_norm(middle, gain_two, shift_two))
    picked = (route_group[:, None] == jnp.arange(EXPERTS)[None, :]).astype(jnp.float32)
    route_prob = jax.nn.softmax(matmul(normed_two, router_weight), axis=-1)
    gate_prob = lax.optimization_barrier(jnp.sum(route_prob * picked, axis=-1))
    mixing = jax.nn.softmax(matmul(normed_two, mix_weight), axis=-1)
    dense_hidden = low(gelu_exact(low_back(matmul(normed_two, up_weight))))
    dense_out = low_back(matmul(dense_hidden, down_weight))
    expert_out = jnp.zeros_like(middle)
    for expert_index in range(EXPERTS):
        expert_out = expert_out + picked[:, expert_index:expert_index + 1] * expert_branch(normed_two, expert_up[expert_index], expert_down[expert_index])
    expert_out = low_back(expert_out)
    return middle + mixing[:, 0:1] * dense_out + (mixing[:, 1] * gate_prob)[:, None] * expert_out

def forward(inputs, weights, prefixes, routes):

    def one_group(running, group_item):
        rows_in, prefix_group, route_group = group_item
        return (running, group_forward(rows_in, prefix_group, route_group, weights))
    _, outputs = lax.scan(jax.checkpoint(one_group), jnp.zeros((), jnp.float32), (inputs.reshape(N_DP, SEQ_DEV * SEQ_LEN, D), prefixes.reshape(N_DP, SEQ_DEV), routes.reshape(N_DP, SEQ_DEV * SEQ_LEN)))
    return outputs.reshape(N_DP * SEQ_DEV * SEQ_LEN, D)

def reference(inputs, cotangent, routes, prefixes, gain_one, shift_one, qkv_weight, out_weight, gain_two, shift_two, up_weight, down_weight, expert_up, expert_down, router_weight, mix_weight):
    weights = (gain_one.astype(jnp.float32), shift_one.astype(jnp.float32), qkv_weight.astype(jnp.float32), out_weight.astype(jnp.float32), gain_two.astype(jnp.float32), shift_two.astype(jnp.float32), up_weight.astype(jnp.float32), down_weight.astype(jnp.float32), expert_up.astype(jnp.float32), expert_down.astype(jnp.float32), router_weight.astype(jnp.float32), mix_weight.astype(jnp.float32))

    def wrapped(inputs_wide, weight_tuple):
        return forward(inputs_wide, weight_tuple, prefixes, routes)
    output, pullback = jax.vjp(wrapped, inputs.astype(jnp.float32), weights)
    input_grad, grads = pullback(cotangent.astype(jnp.float32))
    return (output.astype(jnp.bfloat16), input_grad, grads[0], grads[1], grads[2], grads[3], grads[4], grads[5], grads[6], grads[7], grads[8], grads[9], grads[10], grads[11])
```

```python
from functools import partial
import jax, jax.numpy as jnp
from jax import lax
from jax.experimental import pallas as pl
from jax.experimental.pallas import tpu as pltpu
from jax.sharding import PartitionSpec as P

BF = jnp.bfloat16
F32 = jnp.float32
TILE_DENSE = 512
TILE_EXPERT = 256
PIECE = 16
VMEM = 60 * 1024 * 1024
ANY = pl.BlockSpec(memory_space=pl.ANY)
SMEM = pl.BlockSpec(memory_space=pltpu.SMEM)


def dot(a, b, ca, cb):
    return lax.dot_general(a, b, (((ca,), (cb,)), ((), ())), preferred_element_type=F32)


def bit_reverse(value, bits):
    out = jnp.int32(0)
    for k in range(bits):
        out = out | (((value >> k) & 1) << (bits - 1 - k))
    return out


def lane_softmax(logits, first, last):
    lane = lax.broadcasted_iota(jnp.int32, logits.shape, 1)
    inside = (lane >= first) & (lane < last)
    masked = jnp.where(inside, logits, -1e30)
    top = jnp.max(masked, axis=1, keepdims=True)
    e = jnp.where(inside, jnp.exp(masked - top), 0.0)
    return e / jnp.sum(e, axis=1, keepdims=True)


def pick_lane(v, index):
    lane = lax.broadcasted_iota(jnp.int32, v.shape, 1)
    return jnp.sum(jnp.where(lane == index, v, 0.0), axis=1, keepdims=True)


def gelu_parts(pre):
    phi = 0.5 * (1.0 + lax.erf(pre * 0.7071067811865476))
    pdf = jnp.exp(pre * pre * -0.5) * 0.3989422804014327
    return pre * phi, phi + pre * pdf


def ffn_kernel(cfg, *refs):
    (experts, chunks, rows, d, f, bits, TM) = cfg
    n = chunks * rows
    halves = 1 << (bits - 1)
    blk = d >> bits
    it = iter(refs)
    take = lambda k: [next(it) for _ in range(k)]
    me_ref, blk_ref, bnd_ref = take(3)
    x_hbm, dy_hbm = take(chunks), take(chunks)
    rm_ref, up_hbm, dn_hbm = take(3)
    if experts:
        out_in, rg_in, dots_in = take(3)
        groups = chunks // experts[1]
        out_refs, rg_refs = take(experts[1]), take(experts[1])
        dots_ref, = take(1)
        keep_refs, send_refs = take(experts[0]), take(experts[0])
    else:
        out_ref, rg_ref, dots_ref = take(3)
        keep_refs, send_refs = take(1), take(1)
    X, DY, UP, DN, UA, DA, ST, xsem, wsem, gsem = take(10)
    if experts:
        XG, DG, VAL, OA, RA, DOT, TR, TL, TH, osem = take(10)
    else:
        OB, RB, osem = take(3)
    me = me_ref[0]
    lanes = bnd_ref.shape[1] - 1
    copies = []
    for q in range(chunks):
        sl = pl.ds(q * rows, rows)
        copies.append(pltpu.make_async_copy(x_hbm[q], X.at[sl], xsem.at[q]))
        copies.append(pltpu.make_async_copy(dy_hbm[q], DY.at[sl], xsem.at[chunks + q]))

    def weights(e, slot):
        u = up_hbm.at[e] if experts else up_hbm
        w = dn_hbm.at[e] if experts else dn_hbm
        return (pltpu.make_async_copy(u, UP.at[slot], wsem.at[slot, 0]),
                pltpu.make_async_copy(w, DN.at[slot], wsem.at[slot, 1]))

    for c in weights(0, 0):
        c.start()
    for c in copies:
        c.start()

    def flush_copies(g):
        return (pltpu.make_async_copy(ST.at[:, pl.ds(0, halves)], keep_refs[g], gsem.at[0]),
                pltpu.make_async_copy(ST.at[:, pl.ds(halves, halves)], send_refs[g], gsem.at[1]))

    def stage():
        def body(c, _):
            slot = bit_reverse(c ^ me, bits)
            r = pl.ds(pl.multiple_of(c * blk, blk), blk)
            ST[0, slot] = UA[r, :].astype(BF)
            ST[1, slot] = DA[r, :].astype(BF)
            return 0
        lax.fori_loop(0, 1 << bits, body, 0)

    def tile(xt, dyt, coef_of, up_w, dn_w, first):
        logits = dot(xt, rm_ref[...], 1, 0)
        mixing = lane_softmax(logits, lanes, lanes + 2)
        coef = coef_of(logits, mixing)
        pre = dot(xt, up_w[...], 1, 0)
        g = dot(dyt, dn_w[...], 1, 1)
        hid, dg = gelu_parts(pre)
        hid = hid.astype(BF)
        dots = jnp.sum(hid.astype(F32) * g, axis=1, keepdims=True)
        pg = (g * dg * coef).astype(BF)
        cot = (dyt.astype(F32) * coef).astype(BF)
        ua = dot(xt, pg, 0, 0)
        da = dot(cot, hid, 0, 0)

        @pl.when(first)
        def _():
            UA[...] = ua
            DA[...] = da

        @pl.when(jnp.logical_not(first))
        def _():
            UA[...] += ua
            DA[...] += da
        out = dot(hid, dn_w[...], 1, 0) * coef
        rg = dot(pg, up_w[...], 1, 1)
        return dots, out, rg

    if not experts:
        for c in weights(0, 0):
            c.wait()

        def dense_tile(i, _):
            slot = i % 2
            sl = pl.ds(pl.multiple_of(i * TM, TM), TM)
            for q in range(chunks):
                @pl.when(i * TM == q * rows)
                def _(q=q):
                    copies[2 * q].wait()
                    copies[2 * q + 1].wait()
            outs = (pltpu.make_async_copy(OB.at[slot], out_ref.at[sl], osem.at[0, slot]),
                    pltpu.make_async_copy(RB.at[slot], rg_ref.at[sl], osem.at[1, slot]))
            dots, out, rg = tile(X[sl, :], DY[sl, :], lambda l, m: pick_lane(m, lanes), UP.at[0], DN.at[0], i == 0)
            dots_ref[:, sl] = jnp.broadcast_to(dots, (TM, 128)).T[0:8, :]

            @pl.when(i >= 2)
            def _():
                for c in outs:
                    c.wait()
            OB[slot] = out.astype(BF)
            RB[slot] = rg.astype(BF)
            for c in outs:
                c.start()
            return 0
        lax.fori_loop(0, n // TM, dense_tile, 0)
        stage()
        for c in flush_copies(0):
            c.start()
        for slot in range(min(2, n // TM)):
            sl = pl.ds(0, TM)
            pltpu.make_async_copy(OB.at[slot], out_ref.at[sl], osem.at[0, slot]).wait()
            pltpu.make_async_copy(RB.at[slot], rg_ref.at[sl], osem.at[1, slot]).wait()
        for c in flush_copies(0):
            c.wait()
        return

    count = experts[0]
    OA[...] = jnp.zeros_like(OA)
    RA[...] = jnp.zeros_like(RA)
    DOT[...] = jnp.zeros_like(DOT)
    dense = (pltpu.make_async_copy(out_in, X, xsem.at[0]), pltpu.make_async_copy(rg_in, DY, xsem.at[1]))
    for c in copies:
        c.wait()
    iota16 = lax.broadcasted_iota(jnp.int32, (PIECE, 128), 0)

    def one_expert(e, _):
        slot = e % 2
        for c in weights(e, slot):
            c.wait()

        @pl.when(e + 1 < count)
        def _():
            for c in weights(e + 1, 1 - slot):
                c.start()
        total = jnp.int32(0)
        for q in range(chunks):
            lo, hi = bnd_ref[blk_ref[q], e], bnd_ref[blk_ref[q], e + 1]
            p0 = lo // PIECE
            p1 = jnp.where(hi > lo, (hi + PIECE - 1) // PIECE, p0)

            def add(p, _, lo=lo, hi=hi, p0=p0, total=total, q=q):
                k = total + p - p0
                TR[k] = q * rows + p * PIECE
                TL[k] = lo - p * PIECE
                TH[k] = hi - p * PIECE
                return 0
            lax.fori_loop(p0, p1, add, 0)
            total = total + p1 - p0
        tiles = (total * PIECE + TM - 1) // TM

        def pad(k, _):
            TR[k] = 0
            TL[k] = 0
            TH[k] = 0
            return 0
        lax.fori_loop(total, tiles * (TM // PIECE), pad, 0)

        def expert_tile(i, _):
            base = i * (TM // PIECE)
            for p in range(TM // PIECE):
                r = pl.ds(pl.multiple_of(TR[base + p], PIECE), PIECE)
                XG[pl.ds(p * PIECE, PIECE), :] = X[r, :]
                DG[pl.ds(p * PIECE, PIECE), :] = DY[r, :]
                ok = (iota16 >= TL[base + p]) & (iota16 < TH[base + p])
                VAL[pl.ds(p * PIECE, PIECE), :] = jnp.where(ok, 1.0, 0.0)
            valid = VAL[:, 0:1]

            def coef_of(logits, mixing):
                return pick_lane(mixing, lanes + 1) * pick_lane(lane_softmax(logits, 0, lanes), e) * valid
            dots, out, rg = tile(XG[...], DG[...], coef_of, UP.at[slot], DN.at[slot], i == 0)
            dots = jnp.broadcast_to(dots * valid, (TM, 128))
            for p in range(TM // PIECE):
                r = pl.ds(pl.multiple_of(TR[base + p], PIECE), PIECE)
                s = slice(p * PIECE, (p + 1) * PIECE)
                OA[r, :] += out[s]
                RA[r, :] += rg[s]
                DOT[r, :] += dots[s]
            return 0

        @pl.when(tiles == 0)
        def _():
            UA[...] = jnp.zeros_like(UA)
            DA[...] = jnp.zeros_like(DA)
        lax.fori_loop(0, tiles, expert_tile, 0)

        @pl.when(e == count - 1)
        def _():
            for c in dense:
                c.start()

        @pl.when(e > 0)
        def _():
            for c in flush_copies(0):
                c.wait()
        stage()
        for g in range(count):
            @pl.when(e == g)
            def _(g=g):
                for c in flush_copies(g):
                    c.start()
        return 0
    lax.fori_loop(0, count, one_expert, 0)
    per = groups * rows
    for c in dense:
        c.wait()

    def finish(i, _):
        sl = pl.ds(pl.multiple_of(i * TM, TM), TM)
        X[sl, :] = (OA[sl, :] + X[sl, :].astype(F32)).astype(BF)
        DY[sl, :] = (RA[sl, :] + DY[sl, :].astype(F32)).astype(BF)
        return 0
    lax.fori_loop(0, n // TM, finish, 0)
    outs = []
    for k in range(experts[1]):
        sl = pl.ds(k * per, per)
        outs.append(pltpu.make_async_copy(X.at[sl], out_refs[k], osem.at[0, k]))
        outs.append(pltpu.make_async_copy(DY.at[sl], rg_refs[k], osem.at[1, k]))
    for c in outs:
        c.start()
    dots_t = jnp.concatenate([DOT[pl.ds(i * TM, TM), :].T[0:8, :] for i in range(n // TM)], axis=1)
    row = lax.broadcasted_iota(jnp.int32, (8, n), 0)
    dots_ref[...] = jnp.where(row == 0, dots_in[...], dots_t)
    for c in outs:
        c.wait()
    for c in flush_copies(0):
        c.wait()


def ffn_dense(me, blocks, bounds, xs, dys, rm, up, down, bits):
    chunks = len(xs)
    rows, d = xs[0].shape
    f = up.shape[1]
    n = chunks * rows
    halves = 1 << (bits - 1)
    blk = d >> bits
    tm = min(TILE_DENSE, rows)
    grad = jax.ShapeDtypeStruct((2, halves, blk, f), BF)
    flat = jax.ShapeDtypeStruct((n, d), BF)
    flops = 12 * n * d * f
    return pl.pallas_call(
        partial(ffn_kernel, (None, chunks, rows, d, f, bits, tm)),
        name="ffn_dense",
        out_shape=(flat, flat, jax.ShapeDtypeStruct((8, n), F32), grad, grad),
        in_specs=[SMEM, SMEM, SMEM] + [ANY] * (2 * chunks) + [pl.BlockSpec(memory_space=pltpu.VMEM)] + [ANY] * 2,
        out_specs=(ANY, ANY, pl.BlockSpec(memory_space=pltpu.VMEM), ANY, ANY),
        scratch_shapes=[
            pltpu.VMEM((n, d), BF), pltpu.VMEM((n, d), BF),
            pltpu.VMEM((1, d, f), BF), pltpu.VMEM((1, f, d), BF),
            pltpu.VMEM((d, f), F32), pltpu.VMEM((d, f), F32),
            pltpu.VMEM((2, 2 * halves, blk, f), BF),
            pltpu.SemaphoreType.DMA((2 * chunks,)), pltpu.SemaphoreType.DMA((1, 2)), pltpu.SemaphoreType.DMA((2,)),
            pltpu.VMEM((2, tm, d), BF), pltpu.VMEM((2, tm, d), BF), pltpu.SemaphoreType.DMA((2, 2)),
        ],
        cost_estimate=pl.CostEstimate(flops=flops, bytes_accessed=8 * n * d + 8 * d * f, transcendentals=n * f),
        compiler_params=pltpu.CompilerParams(vmem_limit_bytes=VMEM),
    )(me, blocks, bounds, *xs, *dys, rm, up, down)


def ffn_experts(me, blocks, bounds, xs, dys, rm, up, down, out_d, rg_d, dots_d, members, bits):
    chunks = len(xs)
    rows, d = xs[0].shape
    count, _, f = up.shape
    n = chunks * rows
    halves = 1 << (bits - 1)
    blk = d >> bits
    groups = chunks // members
    tm = TILE_EXPERT
    grad = jax.ShapeDtypeStruct((2, halves, blk, f), BF)
    part = jax.ShapeDtypeStruct((groups * rows, d), BF)
    table = n // PIECE + count * chunks + 2 * tm // PIECE
    vm = pl.BlockSpec(memory_space=pltpu.VMEM)
    return pl.pallas_call(
        partial(ffn_kernel, ((count, members), chunks, rows, d, f, bits, tm)),
        name="ffn_experts",
        out_shape=(part,) * (2 * members) + (jax.ShapeDtypeStruct((8, n), F32),) + (grad,) * (2 * count),
        in_specs=[SMEM, SMEM, SMEM] + [ANY] * (2 * chunks) + [vm] + [ANY] * 4 + [vm],
        out_specs=(ANY,) * (2 * members) + (vm,) + (ANY,) * (2 * count),
        scratch_shapes=[
            pltpu.VMEM((n, d), BF), pltpu.VMEM((n, d), BF),
            pltpu.VMEM((2, d, f), BF), pltpu.VMEM((2, f, d), BF),
            pltpu.VMEM((d, f), F32), pltpu.VMEM((d, f), F32),
            pltpu.VMEM((2, 2 * halves, blk, f), BF),
            pltpu.SemaphoreType.DMA((2 * chunks,)), pltpu.SemaphoreType.DMA((2, 2)), pltpu.SemaphoreType.DMA((2,)),
            pltpu.VMEM((tm, d), BF), pltpu.VMEM((tm, d), BF), pltpu.VMEM((tm, 128), F32),
            pltpu.VMEM((n, d), F32), pltpu.VMEM((n, d), F32), pltpu.VMEM((n, 128), F32),
            pltpu.SMEM((table,), jnp.int32), pltpu.SMEM((table,), jnp.int32), pltpu.SMEM((table,), jnp.int32),
            pltpu.SemaphoreType.DMA((2, members)),
        ],
        cost_estimate=pl.CostEstimate(flops=12 * n * d * f, bytes_accessed=16 * n * d + 8 * count * d * f, transcendentals=n * f),
        compiler_params=pltpu.CompilerParams(vmem_limit_bytes=VMEM),
    )(me, blocks, bounds, *xs, *dys, rm, up, down, out_d, rg_d, dots_d)


HD = 64
LANES = 128


def head_part(v, h):
    lane = lax.broadcasted_iota(jnp.int32, v.shape, 1)
    return jnp.where((lane // HD) == h, v, jnp.zeros((), v.dtype))


def masked_scores(st, key_first, query_first, prefix):
    key_pos = key_first + lax.broadcasted_iota(jnp.int32, st.shape, 0)
    query_pos = query_first + lax.broadcasted_iota(jnp.int32, st.shape, 1)
    seen = key_pos <= query_pos
    if prefix is not None:
        seen = seen | (key_pos < prefix)
    return jnp.where(seen, st, -1e30)


def score_block(k2, qm, half, length, prefix):
    mid = length // 2
    if half == 0:
        return masked_scores(dot(k2[0:mid], qm, 1, 1), 0, 0, prefix)
    low = dot(k2[0:mid], qm, 1, 1)
    high = masked_scores(dot(k2[mid:length], qm, 1, 1), mid, mid, None)
    return jnp.concatenate([low, high], 0)


def attn_forward_kernel(length, prefix_ref, n1_ref, w_ref, q_ref, k_ref, v_ref, ctx_ref, lse_ref):
    mid = length // 2
    prefix = prefix_ref[0]
    n1 = n1_ref[...]
    q_ref[...] = dot(n1, w_ref[0], 1, 0).astype(BF)
    k_ref[...] = dot(n1, w_ref[1], 1, 0).astype(BF)
    v_ref[...] = dot(n1, w_ref[2], 1, 0).astype(BF)
    vt = v_ref[...].T
    k2 = k_ref[...]
    for half in range(2):
        rows = pl.ds(half * mid, mid)
        q2 = q_ref[rows, :] * jnp.asarray(HD ** -0.5, BF)
        keys = mid * (half + 1)
        parts = []
        for h in range(2):
            st = score_block(k2, head_part(q2, h), half, length, prefix)
            top = jnp.max(st, axis=0, keepdims=True)
            p = jnp.exp(st - top)
            total = jnp.sum(p, axis=0, keepdims=True)
            c = dot(vt[h * HD:(h + 1) * HD, 0:keys], p.astype(BF), 1, 0)
            parts.append(c / total)
            lse_ref[0, h:h + 1, rows] = top + jnp.log(total)
        ctx_ref[rows, :] = jnp.concatenate(parts, 0).T.astype(BF)


def attn_forward(prefix, n1, w):
    length, d = n1.shape
    heads = w.shape[2]
    pairs = heads // LANES
    col = pl.BlockSpec((length, LANES), lambda p, *_: (0, p))
    out = jax.ShapeDtypeStruct((length, heads), BF)
    return pl.pallas_call(
        partial(attn_forward_kernel, length),
        name="attn_forward",
        grid_spec=pltpu.PrefetchScalarGridSpec(
            num_scalar_prefetch=1, grid=(pairs,),
            in_specs=[pl.BlockSpec((length, d), lambda p, *_: (0, 0)), pl.BlockSpec((3, d, LANES), lambda p, *_: (0, 0, p))],
            out_specs=[col] * 4 + [pl.BlockSpec((1, 8, length), lambda p, *_: (p, 0, 0))]),
        out_shape=[out] * 4 + [jax.ShapeDtypeStruct((pairs, 8, length), F32)],
        cost_estimate=pl.CostEstimate(flops=6 * length * d * heads + 12 * length * length * heads, bytes_accessed=4 * length * d + 10 * length * heads, transcendentals=length * length * heads // HD),
        compiler_params=pltpu.CompilerParams(vmem_limit_bytes=VMEM),
    )(prefix, n1, w)


def attn_backward_kernel(length, bits, members, based, prefix_ref, me_ref, j_ref, *refs):
    it = iter(refs)
    take = lambda k: [next(it) for _ in range(k)]
    mcs = take(members)
    n1_ref, wo_ref, w_ref, q_ref, k_ref, v_ref, ctx_ref, lse_ref = take(8)
    bases = take(members) if based else []
    ng_refs = take(members)
    grad_ref, NG, MC, DC, DK, DV, DQ, sem = it
    rows_each = length // members
    where = [pl.ds(pl.multiple_of(lax.rem(j_ref[0] + k, members) * rows_each, rows_each), rows_each) for k in range(members)]
    mid = length // 2
    prefix = prefix_ref[0]
    me = me_ref[0]
    pair = pl.program_id(0)
    copies = [pltpu.make_async_copy(mcs[k], MC.at[where[k]], sem.at[k]) for k in range(members)]

    @pl.when(pair == 0)
    def _():
        for c in copies:
            c.start()
        for c in copies:
            c.wait()
    mc = MC[...]
    DC[...] = dot(mc, wo_ref[...], 1, 1).astype(BF)
    k2, v2 = k_ref[...], v_ref[...]
    kt = k2.T
    scale = jnp.asarray(HD ** -0.5, BF)
    for half in range(2):
        rows = pl.ds(half * mid, mid)
        q2 = q_ref[rows, :] * scale
        dc2 = DC[rows, :]
        keys = mid * (half + 1)
        dv = jnp.zeros((keys, LANES), F32)
        dk = jnp.zeros((keys, LANES), F32)
        dq = []
        for h in range(2):
            qm, dcm = head_part(q2, h), head_part(dc2, h)
            st = score_block(k2, qm, half, length, prefix)
            p = jnp.exp(st - lse_ref[0, h:h + 1, rows])
            dv = dv + dot(p.astype(BF), dcm, 1, 0)
            dp = dot(v2[0:keys], dcm, 1, 1)
            ds = (p * (dp - jnp.sum(p * dp, axis=0, keepdims=True))).astype(BF)
            dk = dk + dot(ds, qm, 1, 0)
            dq.append(dot(kt[h * HD:(h + 1) * HD, 0:keys], ds, 1, 0))
        DQ[rows, :] = (jnp.concatenate(dq, 0) * HD ** -0.5).T.astype(BF)
        if half == 0:
            DK[0:mid, :] = dk
            DV[0:mid, :] = dv
        else:
            DK[0:mid, :] += dk[0:mid]
            DV[0:mid, :] += dv[0:mid]
            DK[mid:length, :] = dk[mid:length]
            DV[mid:length, :] = dv[mid:length]
    dq, dk, dv = DQ[...], DK[...].astype(BF), DV[...].astype(BF)
    ng = dot(dq, w_ref[0], 1, 1) + dot(dk, w_ref[1], 1, 1) + dot(dv, w_ref[2], 1, 1)

    @pl.when(pair == 0)
    def _():
        NG[...] = ng

    @pl.when(pair > 0)
    def _():
        NG[...] += ng
    n1 = n1_ref[...]
    grads = [dot(n1, x, 0, 0) for x in (dq, dk, dv)] + [dot(mc, ctx_ref[...], 0, 0)]
    blk = n1.shape[1] >> bits
    for c in range(1 << bits):
        slot = bit_reverse(jnp.int32(c) ^ me, bits)
        for i in range(4):
            grad_ref[slot, i] = grads[i][c * blk:(c + 1) * blk].astype(BF)

    @pl.when(pair == pl.num_programs(0) - 1)
    def _():
        for k in range(members):
            done = NG[where[k], :]
            if based:
                done = done + bases[k][...].astype(F32)
            ng_refs[k][...] = done.astype(BF)


def attn_backward(prefix, me, j, mcs, n1, wo, w, saved, base, bits):
    q, k, v, ctx, lse = saved
    length, d = n1.shape
    heads = w.shape[2]
    pairs = heads // LANES
    blk = d >> bits
    members = len(mcs)
    col = pl.BlockSpec((length, LANES), lambda p, *_: (0, p))
    full = pl.BlockSpec((length, d), lambda p, *_: (0, 0))
    part = pl.BlockSpec((length // members, d), lambda p, *_: (0, 0))
    extra = [] if base is None else list(base)
    res = pl.pallas_call(
        partial(attn_backward_kernel, length, bits, members, base is not None),
        name="attn_backward",
        grid_spec=pltpu.PrefetchScalarGridSpec(
            num_scalar_prefetch=3, grid=(pairs,),
            in_specs=[ANY] * members + [full, pl.BlockSpec((LANES, d), lambda p, *_: (p, 0)), pl.BlockSpec((3, d, LANES), lambda p, *_: (0, 0, p)),
                      col, col, col, col, pl.BlockSpec((1, 8, length), lambda p, *_: (p, 0, 0))] + [part] * len(extra),
            out_specs=[part] * members + [pl.BlockSpec((1 << bits, 4, blk, LANES), lambda p, *_: (0, 0, 0, p))],
            scratch_shapes=[pltpu.VMEM((length, d), F32), pltpu.VMEM((length, d), BF), pltpu.VMEM((length, LANES), BF),
                            pltpu.VMEM((length, LANES), F32), pltpu.VMEM((length, LANES), F32), pltpu.VMEM((length, LANES), BF),
                            pltpu.SemaphoreType.DMA((members,))]),
        out_shape=[jax.ShapeDtypeStruct((length // members, d), BF)] * members + [jax.ShapeDtypeStruct((1 << bits, 4, blk, heads), BF)],
        cost_estimate=pl.CostEstimate(flops=16 * length * d * heads + 30 * length * length * heads, bytes_accessed=8 * length * d + 20 * length * heads, transcendentals=length * length * heads // HD),
        compiler_params=pltpu.CompilerParams(vmem_limit_bytes=VMEM),
    )(prefix, me, j, *mcs, n1, wo, w, q, k, v, ctx, lse, *extra)
    return res[:members], res[members]


EPS = 1e-5


def normalise(v):
    centered = v - jnp.mean(v, axis=1, keepdims=True)
    r = lax.rsqrt(jnp.mean(centered * centered, axis=1, keepdims=True) + EPS)
    return centered * r, r


def norm_backward(xhat, r, grad, gain):
    scaled = grad * gain
    return r * (scaled - jnp.mean(scaled, axis=1, keepdims=True) - xhat * jnp.mean(scaled * xhat, axis=1, keepdims=True))


def order_rows(pos, rows_to_slots):
    n = pos.shape[1] if rows_to_slots else pos.shape[0]
    slot = lax.broadcasted_iota(jnp.int32, (n, n), 0 if rows_to_slots else 1)
    return jnp.where(slot == pos, 1.0, 0.0).astype(BF)


def first_norm_kernel(members, j_ref, *refs):
    xs, gain, shift, out = refs[:members], refs[members], refs[members + 1], refs[members + 2]
    for k in range(members):
        @pl.when(pl.program_id(0) == k)
        def _(k=k):
            xhat, _ = normalise(xs[k][...].astype(F32))
            out[...] = (xhat * gain[...] + shift[...]).astype(BF)


def first_norm(j, xs, gain, shift):
    members = len(xs)
    rows, d = xs[0].shape
    fixed = lambda shape: pl.BlockSpec(shape, lambda p, *_: (0, 0))
    return pl.pallas_call(
        partial(first_norm_kernel, members),
        name="first_norm",
        grid_spec=pltpu.PrefetchScalarGridSpec(
            num_scalar_prefetch=1, grid=(members,),
            in_specs=[fixed((rows, d))] * members + [fixed((1, d))] * 2,
            out_specs=pl.BlockSpec((rows, d), lambda p, j_ref: (lax.rem(j_ref[0] + p, members), 0))),
        out_shape=jax.ShapeDtypeStruct((members * rows, d), BF),
        cost_estimate=pl.CostEstimate(flops=10 * members * rows * d, bytes_accessed=4 * members * rows * d, transcendentals=0),
        compiler_params=pltpu.CompilerParams(vmem_limit_bytes=VMEM),
    )(j, *xs, gain, shift)


def project_others_kernel(parts, j_ref, *refs):
    out = refs[-1]
    total = dot(refs[0][...], refs[parts][...], 1, 0)
    for i in range(1, parts):
        total = total + dot(refs[i][...], refs[parts + i][...], 1, 0)
    out[0] = total.astype(BF)


def project_others(j, contexts, weights, members):
    parts = len(contexts)
    length, heads = contexts[0].shape
    d = weights[0].shape[1]
    rows = length // members
    return pl.pallas_call(
        partial(project_others_kernel, parts),
        name="project_others",
        grid_spec=pltpu.PrefetchScalarGridSpec(
            num_scalar_prefetch=1, grid=(members - 1,),
            in_specs=[pl.BlockSpec((rows, heads), lambda p, j_ref: (lax.rem(j_ref[0] + p + 1, members), 0))] * parts + [pl.BlockSpec((heads, d), lambda p, *_: (0, 0))] * parts,
            out_specs=pl.BlockSpec((1, rows, d), lambda p, *_: (p, 0, 0))),
        out_shape=jax.ShapeDtypeStruct((members - 1, rows, d), BF),
        cost_estimate=pl.CostEstimate(flops=2 * parts * length * heads * d, bytes_accessed=2 * length * d, transcendentals=0),
        compiler_params=pltpu.CompilerParams(vmem_limit_bytes=VMEM),
    )(j, *contexts, *weights)


def second_norm_kernel(parts, others, j_ref, *refs):
    it = iter(refs)
    ctx = [next(it) for _ in range(parts)]
    wo = [next(it) for _ in range(parts)]
    came = [next(it) for _ in range(others)]
    x, gain, shift, pos, middle, n2 = it
    total = dot(ctx[0][...], wo[0][...], 1, 0)
    for i in range(1, parts):
        total = total + dot(ctx[i][...], wo[i][...], 1, 0)
    for c in came:
        total = total + c[...].astype(F32)
    mid = x[...].astype(F32) + total
    middle[...] = mid
    xhat, _ = normalise(mid)
    normed = (xhat * gain[...] + shift[...]).astype(BF)
    n2[...] = dot(order_rows(pos[...], True), normed, 1, 0).astype(BF)


def second_norm(j, contexts, weights, came, x, gain, shift, pos, members):
    parts, others = len(contexts), len(came)
    rows, d = x.shape
    heads = contexts[0].shape[1]
    fixed = lambda shape: pl.BlockSpec(shape, lambda p, *_: (0, 0))
    return pl.pallas_call(
        partial(second_norm_kernel, parts, others),
        name="second_norm",
        grid_spec=pltpu.PrefetchScalarGridSpec(
            num_scalar_prefetch=1, grid=(1,),
            in_specs=[pl.BlockSpec((rows, heads), lambda p, j_ref: (j_ref[0], 0))] * parts + [fixed((heads, d))] * parts
            + [fixed((rows, d))] * (others + 1) + [fixed((1, d))] * 2 + [fixed((1, rows))],
            out_specs=[fixed((rows, d))] * 2),
        out_shape=[jax.ShapeDtypeStruct((rows, d), F32), jax.ShapeDtypeStruct((rows, d), BF)],
        cost_estimate=pl.CostEstimate(flops=2 * rows * d * (rows + parts * heads), bytes_accessed=12 * rows * d, transcendentals=0),
        compiler_params=pltpu.CompilerParams(vmem_limit_bytes=VMEM),
    )(j, *contexts, *weights, *came, x, gain, shift, pos)


def hi_lo(v):
    hi = v.astype(BF)
    return hi, (v - hi.astype(F32)).astype(BF)


def middle_backward_kernel(lead, single, bnd_ref, t_ref, *refs):
    it = iter(refs)
    stacked = [next(it) for _ in range(lead)]
    flat = [next(it) for _ in range(single)]
    dots, n2, rm, middle, dy, gain, pos, mg_ref, mc_ref, sums_ref = it
    t = t_ref[0]
    total = stacked[0][0].astype(F32)
    for s in stacked[1:]:
        total = total + s[0].astype(F32)
    for s in flat:
        total = total + s[...].astype(F32)
    n2v, rmv = n2[...], rm[...]
    rows = n2v.shape[0]
    experts = bnd_ref.shape[1] - 1
    logits = dot(n2v, rmv, 1, 0)
    route_prob = lane_softmax(logits, 0, experts)
    mixing = lane_softmax(logits, experts, experts + 2)
    row = lax.broadcasted_iota(jnp.int32, (rows, 1), 0)
    route = jnp.zeros((rows, 1), jnp.int32)
    for e in range(1, experts):
        route = route + (row >= bnd_ref[t, e]).astype(jnp.int32)
    gate = pick_lane(route_prob, route)
    m0, m1 = pick_lane(mixing, experts), pick_lane(mixing, experts + 1)
    dense_dot, expert_dot = dots[:, 0:1], dots[:, 1:2]
    d0, d1 = dense_dot, expert_dot * gate
    inner = m0 * d0 + m1 * d1
    lane = lax.broadcasted_iota(jnp.int32, logits.shape, 1)
    grad = expert_dot * (m1 * gate) * (jnp.where(lane == route, 1.0, 0.0) - route_prob)
    grad = jnp.where(lane < experts, grad, 0.0)
    grad = jnp.where(lane == experts, m0 * (d0 - inner), grad)
    grad = jnp.where(lane == experts + 1, m1 * (d1 - inner), grad)
    hi, lo = hi_lo(grad)
    total = total + dot(hi, rmv, 1, 1) + dot(lo, rmv, 1, 1)
    sums_ref[0:8, :] = (dot(hi.T, n2v, 1, 0) + dot(lo.T, n2v, 1, 0))[0:8]
    g = dot(order_rows(pos[...], False), total.astype(BF), 1, 0)
    xhat, r = normalise(middle[...])
    sums_ref[8:16, :] = jnp.zeros((8, g.shape[1]), F32)
    sums_ref[8:9, :] = jnp.sum(g * xhat, axis=0, keepdims=True)
    sums_ref[9:10, :] = jnp.sum(g, axis=0, keepdims=True)
    mg = dy[...].astype(F32) + norm_backward(xhat, r, g, gain[...])
    mg_ref[...] = mg
    mc_ref[...] = mg.astype(BF)


def middle_backward(bounds, t, stacked, flat, dots, n2, rm, middle, dy, gain, pos):
    rows, d = n2.shape
    fixed = lambda shape: pl.BlockSpec(shape, lambda p, *_: (0, 0))
    big = fixed((rows, d))
    return pl.pallas_call(
        partial(middle_backward_kernel, len(stacked), len(flat)),
        name="middle_backward",
        grid_spec=pltpu.PrefetchScalarGridSpec(
            num_scalar_prefetch=2, grid=(1,),
            in_specs=[pl.BlockSpec((1, rows, d), lambda p, *_: (0, 0, 0))] * len(stacked) + [big] * len(flat)
            + [fixed((rows, 8)), big, fixed((d, 128)), big, big, fixed((1, d)), fixed((rows, 1))],
            out_specs=[big, big, fixed((16, d))]),
        out_shape=[jax.ShapeDtypeStruct((rows, d), F32), jax.ShapeDtypeStruct((rows, d), BF), jax.ShapeDtypeStruct((16, d), F32)],
        cost_estimate=pl.CostEstimate(flops=2 * rows * d * rows, bytes_accessed=20 * rows * d, transcendentals=0),
        compiler_params=pltpu.CompilerParams(vmem_limit_bytes=VMEM),
    )(bounds, t, *stacked, *flat, dots, n2, rm, middle, dy, gain, pos)


def layer_out_kernel(lead, *refs):
    stacked, flat = refs[:lead], refs[lead:-3]
    middle, pos, out = refs[-3:]
    total = stacked[0][0].astype(F32)
    for s in stacked[1:]:
        total = total + s[0].astype(F32)
    for s in flat:
        total = total + s[...].astype(F32)
    hi, lo = hi_lo(total)
    move = order_rows(pos[...], False)
    out[...] = (middle[...] + dot(move, hi, 1, 0) + dot(move, lo, 1, 0)).astype(BF)


def layer_out(stacked, flat, middle, pos):
    rows, d = middle.shape
    fixed = lambda shape: pl.BlockSpec(shape, lambda p: (0, 0))
    big = fixed((rows, d))
    return pl.pallas_call(
        partial(layer_out_kernel, len(stacked)),
        name="layer_out",
        grid=(1,),
        in_specs=[pl.BlockSpec((1, rows, d), lambda p: (0, 0, 0))] * len(stacked) + [big] * len(flat) + [big, fixed((rows, 1))],
        out_specs=big,
        out_shape=jax.ShapeDtypeStruct((rows, d), BF),
        cost_estimate=pl.CostEstimate(flops=4 * rows * d * rows, bytes_accessed=14 * rows * d, transcendentals=0),
        compiler_params=pltpu.CompilerParams(vmem_limit_bytes=VMEM),
    )(*stacked, *flat, middle, pos)


def input_backward_kernel(count, *refs):
    parts = refs[:count]
    x, mg, gain, out, sums = refs[count:]
    g = parts[0][...].astype(F32)
    for p in parts[1:]:
        g = g + p[...].astype(F32)
    xhat, r = normalise(x[...].astype(F32))
    sums[...] = jnp.zeros_like(sums)
    sums[0:1, :] = jnp.sum(g * xhat, axis=0, keepdims=True)
    sums[1:2, :] = jnp.sum(g, axis=0, keepdims=True)
    out[...] = mg[...] + norm_backward(xhat, r, g, gain[...])


def input_backward(parts, x, mg, gain):
    rows, d = x.shape
    fixed = lambda shape: pl.BlockSpec(shape, lambda p: (0, 0))
    big = fixed((rows, d))
    return pl.pallas_call(
        partial(input_backward_kernel, len(parts)),
        name="input_backward",
        grid=(1,),
        in_specs=[big] * (len(parts) + 2) + [fixed((1, d))],
        out_specs=[big, fixed((8, d))],
        out_shape=[jax.ShapeDtypeStruct((rows, d), F32), jax.ShapeDtypeStruct((8, d), F32)],
        cost_estimate=pl.CostEstimate(flops=20 * rows * d, bytes_accessed=14 * rows * d, transcendentals=0),
        compiler_params=pltpu.CompilerParams(vmem_limit_bytes=VMEM),
    )(*parts, x, mg, gain)


def wide(v):
    return v.astype(F32)


def halve(keep, send, axis, slots):
    stage = 0
    while True:
        bit = slots[stage]
        n = lax.axis_size("dp")
        came = lax.ppermute(send, "dp", [(i, i ^ (1 << bit)) for i in range(n)])
        stage += 1
        if stage == len(slots):
            return lax.squeeze(wide(keep) + wide(came), (axis,))
        half = keep.shape[axis] // 2
        cut = lambda v, a: wide(lax.slice_in_dim(v, a * half, (a + 1) * half, axis=axis))
        keep, send = [(cut(keep, a) + cut(came, a)).astype(BF) for a in range(2)]


def sum_everywhere(v):
    for axis in ("tensor", "dp"):
        n = lax.axis_size(axis)
        bit = 1
        while bit < n:
            v = v + lax.ppermute(v, axis, [(i, i ^ bit) for i in range(n)])
            bit *= 2
    return v


def shards(inputs, cotangent, routes, prefixes, gain_one, shift_one, qkv_weight, out_weight, gain_two, shift_two,
           up_weight, down_weight, expert_up, expert_down, router_weight, mix_weight):
    rows, d = inputs.shape
    tensor = lax.axis_size("tensor")
    dp = lax.axis_size("dp")
    bits = dp.bit_length() - 1
    seqs = prefixes.shape[0]
    members = tensor // seqs
    experts = expert_up.shape[0]
    t = lax.axis_index("tensor")
    s, j = t // members, t % members
    me = lax.axis_index("dp").astype(jnp.int32).reshape(1)
    j1 = j.astype(jnp.int32).reshape(1)
    t1 = t.astype(jnp.int32).reshape(1)
    place = lambda a, b: (a % seqs) * members + b % members
    everyone = [(a, b) for a in range(seqs) for b in range(members)]

    def from_member(v, k):
        return lax.ppermute(v, "tensor", [(place(a, b), place(a, b - k)) for a, b in everyone])

    def to_member(v, k):
        return from_member(v, -k)

    def from_sequence(v, k):
        return lax.ppermute(v, "tensor", [(place(a, b), place(a - k, b)) for a, b in everyone])

    def to_sequence(v, k):
        return from_sequence(v, -k)

    route_blocks = routes.reshape(tensor, rows)
    counts = jnp.stack([jnp.sum((route_blocks == e).astype(jnp.int32), axis=1) for e in range(experts)], axis=1)
    bounds = jnp.concatenate([jnp.zeros((tensor, 1), jnp.int32)] + [jnp.sum(counts[:, :e + 1], axis=1, keepdims=True) for e in range(experts)], axis=1)
    own_route = lax.dynamic_slice_in_dim(routes, t * rows, rows, 0)
    key_col = own_route * rows + jnp.arange(rows, dtype=jnp.int32)[:, None]
    key_row = key_col.reshape(1, rows)
    pos_row = jnp.sum((key_col < key_row).astype(jnp.int32), axis=0, keepdims=True)
    pos_col = jnp.sum((key_row < key_col).astype(jnp.int32), axis=1, keepdims=True)
    blocks = jnp.stack([((s + ds) % seqs) * members + (j + dj) % members for dj in range(members) for ds in range(seqs)]).astype(jnp.int32)

    w_own = jnp.transpose(qkv_weight, (1, 0, 2))
    w_all = [w_own] + [from_sequence(w_own, ds) for ds in range(1, seqs)]
    wo_all = [out_weight] + [from_sequence(out_weight, ds) for ds in range(1, seqs)]
    xs = [inputs] + [from_member(inputs, k) for k in range(1, members)]
    gain_one, shift_one, gain_two, shift_two = [v.reshape(1, d) for v in (gain_one, shift_one, gain_two, shift_two)]
    prefix = lax.dynamic_slice_in_dim(prefixes, s, 1)
    n1 = first_norm(j1, xs, gain_one, shift_one)
    saved = [attn_forward(prefix, n1, w) for w in w_all]
    contexts = [v[3] for v in saved]
    sent = project_others(j1, contexts, wo_all, members)
    came = [to_member(sent[k - 1], k) for k in range(1, members)]
    middle, n2 = second_norm(j1, contexts, wo_all, came, inputs, gain_two, shift_two, pos_row, members)

    def gather(v):
        mine = [v] + [from_sequence(v, ds) for ds in range(1, seqs)]
        out = list(mine)
        for k in range(1, members):
            out += [from_member(m, k) for m in mine]
        return out

    dys = dot(order_rows(pos_row, True), cotangent, 1, 0).astype(BF)
    dy_all = gather(dys)
    n2_all = gather(n2)
    rm = jnp.concatenate([router_weight, mix_weight, jnp.zeros((d, 128 - experts - 2), BF)], axis=1)
    out_d, rg_d, dots_d, keep_d, send_d = ffn_dense(me, blocks, bounds, n2_all, dy_all, rm, up_weight, down_weight, bits)
    res = ffn_experts(me, blocks, bounds, n2_all, dy_all, rm, expert_up, expert_down, out_d, rg_d, dots_d, members, bits)
    outs, rgs, dots = res[:members], res[members:2 * members], res[2 * members]
    keep_e, send_e = res[2 * members + 1:2 * members + 1 + experts], res[2 * members + 1 + experts:]

    def scatter(parts):
        stacked = [parts[0]] + [to_member(parts[k], k) for k in range(1, members)]
        flat = []
        for ds in range(1, seqs):
            term = wide(stacked[0][ds])
            for v in stacked[1:]:
                term = term + wide(v[ds])
            flat.append(to_sequence(term.astype(BF), ds))
        return stacked, flat

    per = seqs * rows
    dot_parts = [dots[:, k * per:(k + 1) * per] for k in range(members)]
    for k in range(1, members):
        dot_parts[0] = dot_parts[0] + to_member(dot_parts[k], k)
    own_dots = dot_parts[0][:, 0:rows]
    for ds in range(1, seqs):
        own_dots = own_dots + to_sequence(dot_parts[0][:, ds * rows:(ds + 1) * rows], ds)
    stacked, flat = scatter([v.reshape(seqs, rows, d) for v in rgs])
    mg, mc, sums_two = middle_backward(bounds, t1, stacked, flat, own_dots.T, n2, rm, middle, cotangent, gain_two, pos_col)
    mcs = [mc] + [from_member(mc, k) for k in range(1, members)]
    ngs = None
    grads = [None] * seqs
    for ds in list(range(1, seqs)) + [0]:
        ngs, grads[ds] = attn_backward(prefix, me, j1, mcs, n1, wo_all[ds], w_all[ds], saved[ds], ngs, bits)
    ng_parts = [ngs[0]] + [to_member(ngs[k], k) for k in range(1, members)]
    input_grad, sums_one = input_backward(ng_parts, inputs, mg, gain_one)
    stacked_o, flat_o = scatter([v.reshape(seqs, rows, d) for v in outs])
    layer_output = layer_out(stacked_o, flat_o, middle, pos_col)

    slots = tuple(range(bits))
    totals = [halve(k, v, 1, slots) for k, v in zip([keep_d] + list(keep_e), [send_d] + list(send_e))]
    half = 1 << (bits - 1)
    attn_total = wide(grads[0])
    for ds in range(1, seqs):
        attn_total = attn_total + wide(to_sequence(grads[ds], ds))
    attn_total = attn_total.astype(BF)
    attn_grad = halve(attn_total[:half], attn_total[half:], 0, slots)
    up_out, down_out = totals[0][0], totals[0][1].T
    expert_up_out = jnp.stack([v[0] for v in totals[1:]])
    expert_down_out = jnp.stack([v[1].T for v in totals[1:]])
    qkv_out = jnp.transpose(attn_grad[0:3], (1, 0, 2))
    out_out = attn_grad[3].T
    lanes = d // (dp * tensor)
    first = (lax.axis_index("dp") * tensor + t) * lanes
    two = lax.dynamic_slice_in_dim(sum_everywhere(sums_two), first, lanes, 1)
    one = lax.dynamic_slice_in_dim(sum_everywhere(sums_one), first, lanes, 1)
    return (layer_output, input_grad, one[0], one[1], qkv_out, out_out, two[8], two[9], up_out, down_out,
            expert_up_out, expert_down_out, two[0:experts].T, two[experts:experts + 2].T)


def solution(mesh):
    both = ("dp", "tensor")
    in_specs = (P(both, None), P(both, None), P("dp", None), P("dp"), P(), P(), P(None, None, "tensor"), P("tensor", None), P(), P(),
                P(None, "tensor"), P("tensor", None), P(None, None, "tensor"), P(None, "tensor", None), P(), P())
    out_specs = (P(both, None), P(both, None), P(both), P(both), P("dp", None, "tensor"), P("tensor", "dp"), P(both), P(both),
                 P("dp", "tensor"), P("tensor", "dp"), P(None, "dp", "tensor"), P(None, "tensor", "dp"), P(both, None), P(both, None))
    return jax.shard_map(shards, mesh=mesh, in_specs=in_specs, out_specs=out_specs, check_vma=False)
```

```python
from functools import partial
import jax, jax.numpy as jnp
from jax import lax
from jax.experimental import pallas as pl
from jax.experimental.pallas import tpu as pltpu
from jax.sharding import PartitionSpec as P

BF = jnp.bfloat16
F32 = jnp.float32
TILE_DENSE = 512
TILE_EXPERT = 256
PIECE = 16
SMALL = pl.CostEstimate(flops=0, bytes_accessed=0, transcendentals=0)
VMEM = 60 * 1024 * 1024
ANY = pl.BlockSpec(memory_space=pl.ANY)
SMEM = pl.BlockSpec(memory_space=pltpu.SMEM)


def dot(a, b, ca, cb):
    return lax.dot_general(a, b, (((ca,), (cb,)), ((), ())), preferred_element_type=F32)


def slot_of(value, order):
    out = jnp.int32(0)
    for k, bit in enumerate(order):
        out = out | (((value >> bit) & 1) << (len(order) - 1 - k))
    return out


def skip(kernel, scalars, deps):
    return lambda *refs: kernel(*refs[:scalars], *refs[scalars + deps:])


def lane_softmax(logits, first, last):
    lane = lax.broadcasted_iota(jnp.int32, logits.shape, 1)
    inside = (lane >= first) & (lane < last)
    masked = jnp.where(inside, logits, -1e30)
    top = jnp.max(masked, axis=1, keepdims=True)
    e = jnp.where(inside, jnp.exp(masked - top), 0.0)
    return e / jnp.sum(e, axis=1, keepdims=True)


def pick_lane(v, index):
    lane = lax.broadcasted_iota(jnp.int32, v.shape, 1)
    return jnp.sum(jnp.where(lane == index, v, 0.0), axis=1, keepdims=True)


def gelu_parts(pre):
    phi = 0.5 * (1.0 + lax.erf(pre * 0.7071067811865476))
    pdf = jnp.exp(pre * pre * -0.5) * 0.3989422804014327
    return pre * phi, phi + pre * pdf


def ffn_tile(lanes, rm, xt, dyt, coef_of, up_w, dn_w, UA, DA, ready):
    logits = dot(xt, rm[...], 1, 0)
    mixing = lane_softmax(logits, lanes, lanes + 2)
    coef = coef_of(logits, mixing)
    pre = dot(xt, up_w[...], 1, 0)
    g = dot(dyt, dn_w[...], 1, 1)
    hid, dg = gelu_parts(pre)
    hid = hid.astype(BF)
    dots = jnp.sum(hid.astype(F32) * g, axis=1, keepdims=True)
    pg = (g * dg * coef).astype(BF)
    cot = (dyt.astype(F32) * coef).astype(BF)
    out = dot(hid, dn_w[...], 1, 0) * coef
    rg = dot(pg, up_w[...], 1, 1)
    ready()
    UA[...] += dot(xt, pg, 0, 0)
    DA[...] += dot(cot, hid, 0, 0)
    return dots, out, rg


def stage_grads(ST, UA, DA, me, up_order, dn_order):
    bits = len(up_order)
    blk = UA.shape[0] >> bits

    def body(c, _):
        r = pl.ds(pl.multiple_of(c * blk, blk), blk)
        ST[slot_of(c ^ me, up_order), 0] = UA[r, :].astype(BF)
        ST[slot_of(c ^ me, dn_order), 1] = DA[r, :].astype(BF)
        return 0
    lax.fori_loop(0, 1 << bits, body, 0)


def column(v, n):
    return jnp.broadcast_to(v, (v.shape[0], n))


def dense_kernel(cfg, me_ref, *refs):
    chunks, rows, tm, lanes, orders, first, deps = cfg
    it = iter(refs[deps:])
    take = lambda k: [next(it) for _ in range(k)]
    x_hbm, dy_hbm = take(chunks), take(chunks)
    rm, up_hbm, dn_hbm = take(3)
    base_o, base_r, sums_in = ([], [], []) if first else (take(chunks), take(chunks), take(2))
    out_refs, rg_refs = take(chunks), take(chunks)
    dots_ref, = take(1)
    ends = take(2) if first else take(4)
    X, DY, UP, DN, UA, DA, OB, RB, xsem, wsem, gsem, osem = take(12)
    ST, BO, BR, bsem = (None,) * 4 if first else take(4)
    per = rows // tm
    weights = [pltpu.make_async_copy(up_hbm, UP, wsem.at[0]), pltpu.make_async_copy(dn_hbm, DN, wsem.at[1])]
    loads, bases = [], []
    for q in range(chunks):
        sl = pl.ds(q * rows, rows)
        loads.append([pltpu.make_async_copy(x_hbm[q], X.at[sl], xsem.at[q]), pltpu.make_async_copy(dy_hbm[q], DY.at[sl], xsem.at[chunks + q])])
        if not first:
            bases.append([pltpu.make_async_copy(base_o[q], BO.at[sl], bsem.at[q]), pltpu.make_async_copy(base_r[q], BR.at[sl], bsem.at[chunks + q])])
    sums = [] if first else [pltpu.make_async_copy(sums_in[0], UA, gsem.at[0]), pltpu.make_async_copy(sums_in[1], DA, gsem.at[1])]
    for c in loads[0] + weights + sums + [c for q in loads[1:] for c in q] + [c for q in bases for c in q]:
        c.start()
    if first:
        UA[...] = jnp.zeros_like(UA)
        DA[...] = jnp.zeros_like(DA)
    for c in weights:
        c.wait()

    def outs(q, part, slot):
        sl = pl.ds(part * tm, tm)
        return [pltpu.make_async_copy(OB.at[slot], out_refs[q].at[sl], osem.at[0, slot]),
                pltpu.make_async_copy(RB.at[slot], rg_refs[q].at[sl], osem.at[1, slot])]

    def one(i, _):
        slot = i % 2
        sl = pl.ds(pl.multiple_of(i * tm, tm), tm)
        for q in range(chunks):
            @pl.when(i == q * per)
            def _(q=q):
                for c in loads[q]:
                    c.wait()

        def ready():
            if not first:
                @pl.when(i == 0)
                def _():
                    for c in sums:
                        c.wait()
        dots, out, rg = ffn_tile(lanes, rm, X[sl, :], DY[sl, :], lambda l, m: pick_lane(m, lanes), UP, DN, UA, DA, ready)
        dots_ref[:, sl] = column(dots, 128).T[0:8, :]
        if not first:
            for q in range(chunks):
                @pl.when(i == q * per)
                def _(q=q):
                    for c in bases[q]:
                        c.wait()
            out = out + BO[sl, :].astype(F32)
            rg = rg + BR[sl, :].astype(F32)

        @pl.when(i >= 2)
        def _():
            for c in outs(0, 0, slot):
                c.wait()
        OB[slot] = out.astype(BF)
        RB[slot] = rg.astype(BF)
        for q in range(chunks):
            for part in range(per):
                @pl.when(i == q * per + part)
                def _(q=q, part=part):
                    for c in outs(q, part, slot):
                        c.start()
        return 0
    lax.fori_loop(0, chunks * per, one, 0)
    row = lax.broadcasted_iota(jnp.int32, dots_ref.shape, 0)
    dots_ref[...] = jnp.where(row == 0, dots_ref[...], 0.0)
    if first:
        last = [pltpu.make_async_copy(UA, ends[0], gsem.at[0]), pltpu.make_async_copy(DA, ends[1], gsem.at[1])]
    else:
        stage_grads(ST, UA, DA, me_ref[0], *orders)
        half = ST.shape[0] // 2
        last = [pltpu.make_async_copy(ST.at[pl.ds(h * half, half), pl.ds(m, 1)], ends[2 * m + h], bsem.at[2 * m + h]) for m in range(2) for h in range(2)]
    for c in last:
        c.start()
    for slot in range(min(2, chunks * per)):
        for c in outs(0, 0, slot):
            c.wait()
    for c in last:
        c.wait()


def ffn_dense(me, xs, dys, rm, up, down, lanes, orders, base=None, sums=None, deps=()):
    chunks = len(xs)
    rows, d = xs[0].shape
    f = up.shape[1]
    n = chunks * rows
    tm = min(TILE_DENSE, rows)
    first = base is None
    bits = len(orders[0])
    half = 1 << (bits - 1)
    vm = pl.BlockSpec(memory_space=pltpu.VMEM)
    part = jax.ShapeDtypeStruct((rows, d), BF)
    total = jax.ShapeDtypeStruct((d, f), F32)
    grad = jax.ShapeDtypeStruct((half, 1, d >> bits, f), BF)
    ends = [total] * 2 if first else [grad] * 4
    more = [] if first else list(base[0]) + list(base[1]) + list(sums)
    scratch = [pltpu.VMEM((n, d), BF), pltpu.VMEM((n, d), BF), pltpu.VMEM((d, f), BF), pltpu.VMEM((f, d), BF), pltpu.VMEM((d, f), F32), pltpu.VMEM((d, f), F32),
               pltpu.VMEM((2, tm, d), BF), pltpu.VMEM((2, tm, d), BF),
               pltpu.SemaphoreType.DMA((2 * chunks,)), pltpu.SemaphoreType.DMA((2,)), pltpu.SemaphoreType.DMA((2,)), pltpu.SemaphoreType.DMA((2, 2))]
    if not first:
        scratch += [pltpu.VMEM((2 * half, 2, d >> bits, f), BF), pltpu.VMEM((n, d), BF), pltpu.VMEM((n, d), BF), pltpu.SemaphoreType.DMA((max(4, 2 * chunks),))]
    res = pl.pallas_call(
        partial(dense_kernel, (chunks, rows, tm, lanes, orders, first, len(deps))),
        name="ffn_dense",
        out_shape=[part] * (2 * chunks) + [jax.ShapeDtypeStruct((8, n), F32)] + ends,
        in_specs=[SMEM] + [ANY] * (len(deps) + 2 * chunks) + [vm] + [ANY] * (2 + len(more)),
        out_specs=[ANY] * (2 * chunks) + [vm] + [ANY] * len(ends),
        scratch_shapes=scratch,
        cost_estimate=SMALL,
        compiler_params=pltpu.CompilerParams(vmem_limit_bytes=VMEM),
    )(me, *deps, *xs, *dys, rm, up, down, *more)
    return res[:chunks], res[chunks:2 * chunks], res[2 * chunks], res[2 * chunks + 1:]


def expert_kernel(cfg, me_ref, blk_ref, bnd_ref, *refs):
    first, count, chunks, rows, d, tm, lanes, order, has, deps = cfg
    n = chunks * rows
    it = iter(refs[deps:])
    take = lambda k: [next(it) for _ in range(k)]
    x_hbm, dy_hbm = take(chunks), take(chunks)
    rm, up_hbm, dn_hbm = take(3)
    based = [q for q in range(chunks) if has[q]]
    base_o, base_r = take(len(based)), take(len(based))
    out_refs, rg_refs = take(chunks), take(chunks)
    dots_ref, = take(1)
    keep_refs, send_refs = take(count), take(count)
    X, DY, UP, DN, UA, DA, ST, XG, DG, VAL, OA, RA, DOT, TR, TL, TH, xsem, wsem, gsem, osem = it
    half = ST.shape[0] // 2
    pieces = tm // PIECE
    rows_of = [pl.ds(q * rows, rows) for q in range(chunks)]
    copies = []
    for q in range(chunks):
        copies.append(pltpu.make_async_copy(x_hbm[q], X.at[rows_of[q]], xsem.at[q]))
        copies.append(pltpu.make_async_copy(dy_hbm[q], DY.at[rows_of[q]], xsem.at[chunks + q]))
    earlier = []
    for k, q in enumerate(based):
        earlier.append(pltpu.make_async_copy(base_o[k], X.at[rows_of[q]], xsem.at[q]))
        earlier.append(pltpu.make_async_copy(base_r[k], DY.at[rows_of[q]], xsem.at[chunks + q]))

    def weights(e, slot):
        return [pltpu.make_async_copy(up_hbm.at[first + e], UP.at[slot], wsem.at[slot, 0]),
                pltpu.make_async_copy(dn_hbm.at[first + e], DN.at[slot], wsem.at[slot, 1])]

    def flush(g):
        return [pltpu.make_async_copy(ST.at[pl.ds(0, half)], keep_refs[g], gsem.at[0]),
                pltpu.make_async_copy(ST.at[pl.ds(half, half)], send_refs[g], gsem.at[1])]

    for c in copies + weights(0, 0):
        c.start()
    OA[...] = jnp.zeros_like(OA)
    RA[...] = jnp.zeros_like(RA)
    DOT[...] = jnp.zeros_like(DOT)
    iota16 = lax.broadcasted_iota(jnp.int32, (PIECE, 128), 0)

    def one_expert(e, _):
        slot = e % 2
        total = jnp.int32(0)
        for q in range(chunks):
            lo, hi = bnd_ref[blk_ref[q], first + e], bnd_ref[blk_ref[q], first + e + 1]
            p0 = lo // PIECE
            p1 = jnp.where(hi > lo, (hi + PIECE - 1) // PIECE, p0)

            def add(p, _, lo=lo, hi=hi, p0=p0, total=total, q=q):
                k = total + p - p0
                TR[k] = q * rows + p * PIECE
                TL[k] = lo - p * PIECE
                TH[k] = hi - p * PIECE
                return 0
            lax.fori_loop(p0, p1, add, 0)
            total = total + p1 - p0
        tiles = (total + pieces - 1) // pieces

        def pad(k, _):
            TR[k] = 0
            TL[k] = 0
            TH[k] = 0
            return 0
        lax.fori_loop(total, tiles * pieces, pad, 0)
        UA[...] = jnp.zeros_like(UA)
        DA[...] = jnp.zeros_like(DA)

        @pl.when(e == 0)
        def _():
            for c in copies:
                c.wait()
        for c in weights(e, slot):
            c.wait()

        @pl.when(e + 1 < count)
        def _():
            for c in weights(e + 1, 1 - slot):
                c.start()

        def one_tile(i, _):
            base = i * pieces
            for p in range(pieces):
                r = pl.ds(pl.multiple_of(TR[base + p], PIECE), PIECE)
                XG[pl.ds(p * PIECE, PIECE), :] = X[r, :]
                DG[pl.ds(p * PIECE, PIECE), :] = DY[r, :]
                ok = (iota16 >= TL[base + p]) & (iota16 < TH[base + p])
                VAL[pl.ds(p * PIECE, PIECE), :] = jnp.where(ok, 1.0, 0.0)
            valid = VAL[:, 0:1]

            def coef_of(logits, mixing):
                return pick_lane(mixing, lanes + 1) * pick_lane(lane_softmax(logits, 0, lanes), first + e) * valid
            dots, out, rg = ffn_tile(lanes, rm, XG[...], DG[...], coef_of, UP.at[slot], DN.at[slot], UA, DA, lambda: None)
            dots = column(dots * valid, 128)
            for p in range(pieces):
                r = pl.ds(pl.multiple_of(TR[base + p], PIECE), PIECE)
                s = slice(p * PIECE, (p + 1) * PIECE)
                OA[r, :] += out[s]
                RA[r, :] += rg[s]
                DOT[r, :] += dots[s]
            return 0
        lax.fori_loop(0, tiles, one_tile, 0)

        @pl.when(e == count - 1)
        def _():
            for c in earlier:
                c.start()

        @pl.when(e > 0)
        def _():
            for c in flush(0):
                c.wait()
        stage_grads(ST, UA, DA, me_ref[0], order, order)
        for g in range(count):
            @pl.when(e == g)
            def _(g=g):
                for c in flush(g):
                    c.start()
        return 0
    lax.fori_loop(0, count, one_expert, 0)
    for c in earlier:
        c.wait()
    last = []
    for q in range(chunks):
        r = rows_of[q]
        o, g = OA[r, :], RA[r, :]
        if has[q]:
            o, g = o + X[r, :].astype(F32), g + DY[r, :].astype(F32)
        X[r, :] = o.astype(BF)
        DY[r, :] = g.astype(BF)
        last += [pltpu.make_async_copy(X.at[r], out_refs[q], osem.at[0, q]), pltpu.make_async_copy(DY.at[r], rg_refs[q], osem.at[1, q])]
        for c in last[-2:]:
            c.start()
    step = min(256, rows)
    row = lax.broadcasted_iota(jnp.int32, (8, step), 0)
    for i in range(n // step):
        sl = pl.ds(i * step, step)
        dots_ref[:, sl] = jnp.where(row == 1, DOT[sl, :].T[0:8, :], 0.0)
    for c in last + flush(0):
        c.wait()


def ffn_experts(me, blocks, bounds, xs, dys, rm, up, down, first, count, base, order, deps=()):
    chunks = len(xs)
    rows, d = xs[0].shape
    lanes, _, f = up.shape
    n = chunks * rows
    tm = TILE_EXPERT
    bits = len(order)
    half = 1 << (bits - 1)
    grad = jax.ShapeDtypeStruct((half, 2, d >> bits, f), BF)
    part = jax.ShapeDtypeStruct((rows, d), BF)
    table = n // PIECE + chunks * lanes + 2 * tm // PIECE
    vm = pl.BlockSpec(memory_space=pltpu.VMEM)
    has = tuple(b is not None for b in base[0])
    more = [b for k in range(2) for b in base[k] if b is not None]
    res = pl.pallas_call(
        partial(expert_kernel, (first, count, chunks, rows, d, tm, lanes, order, has, len(deps))),
        name="ffn_experts",
        out_shape=[part] * (2 * chunks) + [jax.ShapeDtypeStruct((8, n), F32)] + [grad] * (2 * count),
        in_specs=[SMEM] * 3 + [ANY] * (len(deps) + 2 * chunks) + [vm] + [ANY] * (2 + len(more)),
        out_specs=[ANY] * (2 * chunks) + [vm] + [ANY] * (2 * count),
        scratch_shapes=[
            pltpu.VMEM((n, d), BF), pltpu.VMEM((n, d), BF), pltpu.VMEM((2, d, f), BF), pltpu.VMEM((2, f, d), BF),
            pltpu.VMEM((d, f), F32), pltpu.VMEM((d, f), F32), pltpu.VMEM((2 * half, 2, d >> bits, f), BF),
            pltpu.VMEM((tm, d), BF), pltpu.VMEM((tm, d), BF), pltpu.VMEM((tm, 128), F32),
            pltpu.VMEM((n, d), F32), pltpu.VMEM((n, d), F32), pltpu.VMEM((n, 128), F32),
            pltpu.SMEM((table,), jnp.int32), pltpu.SMEM((table,), jnp.int32), pltpu.SMEM((table,), jnp.int32),
            pltpu.SemaphoreType.DMA((2 * chunks,)), pltpu.SemaphoreType.DMA((2, 2)), pltpu.SemaphoreType.DMA((2,)), pltpu.SemaphoreType.DMA((2, chunks)),
        ],
        cost_estimate=SMALL,
        compiler_params=pltpu.CompilerParams(vmem_limit_bytes=VMEM),
    )(me, blocks, bounds, *deps, *xs, *dys, rm, up, down, *more)
    at = 2 * chunks + 1
    return res[:chunks], res[chunks:2 * chunks], res[2 * chunks], res[at:at + count], res[at + count:]


def split_add_kernel(deps, *refs):
    ka, kb, ca, cb, keep, send = refs[deps:]
    keep[...] = (ka[...].astype(F32) + ca[...].astype(F32)).astype(BF)
    send[...] = (kb[...].astype(F32) + cb[...].astype(F32)).astype(BF)


def split_add(kept, came, deps=()):
    h, m, blk, f = kept.shape
    near = pl.BlockSpec((1, 1, blk, f), lambda i, k: (i, k, 0, 0))
    far = pl.BlockSpec((1, 1, blk, f), lambda i, k: (i + h // 2, k, 0, 0))
    out = jax.ShapeDtypeStruct((h // 2, m, blk, f), BF)
    return pl.pallas_call(
        partial(split_add_kernel, len(deps)),
        name="split_add",
        grid=(h // 2, m),
        in_specs=[ANY] * len(deps) + [near, far, near, far],
        out_specs=[near, near],
        out_shape=[out, out],
        cost_estimate=SMALL,
        compiler_params=pltpu.CompilerParams(vmem_limit_bytes=VMEM),
    )(*deps, kept, kept, came, came)


def last_add_kernel(deps, turns, *refs):
    kept, came = refs[deps:deps + 2]
    outs = refs[-len(turns):]
    for k, turned in enumerate(turns):
        total = kept[0, k].astype(F32) + came[0, k].astype(F32)
        outs[k][...] = (total.T if turned else total).reshape(outs[k].shape)


def last_add(kept, came, turns, place=None, stacks=None, deps=()):
    _, m, blk, f = kept.shape
    shapes = [(f, blk) if turned else (blk, f) for turned in turns]
    aliases = {}
    if place is None:
        out_shape = [jax.ShapeDtypeStruct(s, F32) for s in shapes]
        out_specs = [pl.BlockSpec(s, lambda i: (0, 0)) for s in shapes]
    else:
        count, at = place
        out_shape = [jax.ShapeDtypeStruct((count,) + s, F32) for s in shapes]
        out_specs = [pl.BlockSpec((1,) + s, lambda i: (at, 0, 0)) for s in shapes]
        if stacks is not None:
            aliases = {k: k for k in range(m)}
            deps = tuple(stacks) + tuple(deps)
    full = pl.BlockSpec((1, m, blk, f), lambda i: (0, 0, 0, 0))
    return pl.pallas_call(
        partial(last_add_kernel, len(deps), turns),
        name="last_add",
        grid=(1,),
        in_specs=[ANY] * len(deps) + [full, full],
        out_specs=out_specs,
        out_shape=out_shape,
        input_output_aliases=aliases,
        cost_estimate=SMALL,
        compiler_params=pltpu.CompilerParams(vmem_limit_bytes=VMEM),
    )(*deps, kept, came)


def hold(v, deps):
    return pl.pallas_call(
        lambda *refs: None,
        name="hold",
        in_specs=[ANY] * (1 + len(deps)),
        out_specs=ANY,
        out_shape=jax.ShapeDtypeStruct(v.shape, v.dtype),
        input_output_aliases={0: 0},
        cost_estimate=SMALL,
    )(v, *deps)


HD = 64
LANES = 128


def head_part(v, h):
    lane = lax.broadcasted_iota(jnp.int32, v.shape, 1)
    return jnp.where((lane // HD) == h, v, jnp.zeros((), v.dtype))


def masked_scores(st, key_first, query_first, prefix):
    key_pos = key_first + lax.broadcasted_iota(jnp.int32, st.shape, 0)
    query_pos = query_first + lax.broadcasted_iota(jnp.int32, st.shape, 1)
    seen = key_pos <= query_pos
    if prefix is not None:
        seen = seen | (key_pos < prefix)
    return jnp.where(seen, st, -1e30)


def score_block(k2, qm, half, length, prefix):
    mid = length // 2
    if half == 0:
        return masked_scores(dot(k2[0:mid], qm, 1, 1), 0, 0, prefix)
    low = dot(k2[0:mid], qm, 1, 1)
    high = masked_scores(dot(k2[mid:length], qm, 1, 1), mid, mid, None)
    return jnp.concatenate([low, high], 0)


def attn_forward_kernel(length, pieces, aliased, prefix_ref, at_ref, *refs):
    n1_ref = refs[0]
    w_refs = [(r, i) for r, n in zip(refs[1:], pieces) for i in range(n)]
    q_ref, k_ref, v_ref, ctx_ref, lse_ref = refs[1 + len(pieces) + aliased:]
    mid = length // 2
    prefix = prefix_ref[0]
    n1 = n1_ref[...]
    for out, (w, i) in zip((q_ref, k_ref, v_ref), w_refs):
        out[...] = dot(n1, w[i], 1, 0).astype(BF)
    vt = v_ref[...].T
    k2 = k_ref[...]
    for half in range(2):
        rows = pl.ds(half * mid, mid)
        q2 = q_ref[rows, :] * jnp.asarray(HD ** -0.5, BF)
        keys = mid * (half + 1)
        parts = []
        for h in range(2):
            st = score_block(k2, head_part(q2, h), half, length, prefix)
            top = jnp.max(st, axis=0, keepdims=True)
            p = jnp.exp(st - top)
            total = jnp.sum(p, axis=0, keepdims=True)
            c = dot(vt[h * HD:(h + 1) * HD, 0:keys], p.astype(BF), 1, 0)
            parts.append(c / total)
            lse_ref[0, h:h + 1, rows] = top + jnp.log(total)
        ctx_ref[rows, :] = jnp.concatenate(parts, 0).T.astype(BF)


def attn_forward(prefix, at, n1, ws, heads, earlier=(), deps=()):
    length, d = n1.shape
    pairs = ws[0].shape[2] // LANES
    col = pl.BlockSpec((length, LANES), lambda p, _, at_ref: (0, at_ref[p]))
    out = jax.ShapeDtypeStruct((length, heads), BF)
    done = len(earlier)
    skipped = len(deps)
    return pl.pallas_call(
        skip(partial(attn_forward_kernel, length, tuple(w.shape[0] for w in ws), done), 2, skipped),
        name="attn_forward",
        grid_spec=pltpu.PrefetchScalarGridSpec(
            num_scalar_prefetch=2, grid=(pairs,),
            in_specs=[ANY] * skipped + [pl.BlockSpec((length, d), lambda p, *_: (0, 0))]
            + [pl.BlockSpec((w.shape[0], d, LANES), lambda p, *_: (0, 0, p)) for w in ws] + [ANY] * done,
            out_specs=[col] * 4 + [pl.BlockSpec((1, 8, length), lambda p, _, at_ref: (at_ref[p], 0, 0))]),
        out_shape=[out] * 4 + [jax.ShapeDtypeStruct((heads // LANES, 8, length), F32)],
        input_output_aliases={3 + skipped + len(ws) + k: k for k in range(done)},
        cost_estimate=SMALL,
        compiler_params=pltpu.CompilerParams(vmem_limit_bytes=VMEM),
    )(prefix, at, *deps, n1, *ws, *earlier)


def attn_backward_kernel(length, bits, members, based, prefix_ref, me_ref, j_ref, *refs):
    it = iter(refs)
    take = lambda k: [next(it) for _ in range(k)]
    mcs = take(members)
    n1_ref, wo_ref, w_ref, q_ref, k_ref, v_ref, ctx_ref, lse_ref = take(8)
    bases = take(members) if based else []
    ng_refs = take(members)
    grad_ref, NG, MC, DC, DK, DV, DQ, sem = it
    rows_each = length // members
    where = [pl.ds(pl.multiple_of(lax.rem(j_ref[0] + k, members) * rows_each, rows_each), rows_each) for k in range(members)]
    mid = length // 2
    prefix = prefix_ref[0]
    me = me_ref[0]
    pair = pl.program_id(0)
    copies = [pltpu.make_async_copy(mcs[k], MC.at[where[k]], sem.at[k]) for k in range(members)]

    @pl.when(pair == 0)
    def _():
        for c in copies:
            c.start()
        for c in copies:
            c.wait()
    mc = MC[...]
    DC[...] = dot(mc, wo_ref[...], 1, 1).astype(BF)
    k2, v2 = k_ref[...], v_ref[...]
    kt = k2.T
    scale = jnp.asarray(HD ** -0.5, BF)
    for half in range(2):
        rows = pl.ds(half * mid, mid)
        q2 = q_ref[rows, :] * scale
        dc2 = DC[rows, :]
        keys = mid * (half + 1)
        dv = jnp.zeros((keys, LANES), F32)
        dk = jnp.zeros((keys, LANES), F32)
        dq = []
        for h in range(2):
            qm, dcm = head_part(q2, h), head_part(dc2, h)
            st = score_block(k2, qm, half, length, prefix)
            p = jnp.exp(st - lse_ref[0, h:h + 1, rows])
            dv = dv + dot(p.astype(BF), dcm, 1, 0)
            dp = dot(v2[0:keys], dcm, 1, 1)
            ds = (p * (dp - jnp.sum(p * dp, axis=0, keepdims=True))).astype(BF)
            dk = dk + dot(ds, qm, 1, 0)
            dq.append(dot(kt[h * HD:(h + 1) * HD, 0:keys], ds, 1, 0))
        DQ[rows, :] = (jnp.concatenate(dq, 0) * HD ** -0.5).T.astype(BF)
        if half == 0:
            DK[0:mid, :] = dk
            DV[0:mid, :] = dv
        else:
            DK[0:mid, :] += dk[0:mid]
            DV[0:mid, :] += dv[0:mid]
            DK[mid:length, :] = dk[mid:length]
            DV[mid:length, :] = dv[mid:length]
    dq, dk, dv = DQ[...], DK[...].astype(BF), DV[...].astype(BF)
    ng = dot(dq, w_ref[0], 1, 1) + dot(dk, w_ref[1], 1, 1) + dot(dv, w_ref[2], 1, 1)

    @pl.when(pair == 0)
    def _():
        NG[...] = ng

    @pl.when(pair > 0)
    def _():
        NG[...] += ng
    n1 = n1_ref[...]
    grads = [dot(n1, x, 0, 0) for x in (dq, dk, dv)] + [dot(mc, ctx_ref[...], 0, 0)]
    blk = n1.shape[1] >> bits
    for c in range(1 << bits):
        slot = slot_of(jnp.int32(c) ^ me, range(bits))
        for i in range(4):
            grad_ref[slot, i] = grads[i][c * blk:(c + 1) * blk].astype(BF)

    @pl.when(pair == pl.num_programs(0) - 1)
    def _():
        for k in range(members):
            done = NG[where[k], :]
            if based:
                done = done + bases[k][...].astype(F32)
            ng_refs[k][...] = done.astype(BF)


def attn_backward(prefix, me, j, mcs, n1, wo, w, saved, base, bits, deps=()):
    q, k, v, ctx, lse = saved
    length, d = n1.shape
    heads = w.shape[2]
    pairs = heads // LANES
    blk = d >> bits
    members = len(mcs)
    col = pl.BlockSpec((length, LANES), lambda p, *_: (0, p))
    full = pl.BlockSpec((length, d), lambda p, *_: (0, 0))
    part = pl.BlockSpec((length // members, d), lambda p, *_: (0, 0))
    extra = [] if base is None else list(base)
    res = pl.pallas_call(
        skip(partial(attn_backward_kernel, length, bits, members, base is not None), 3, len(deps)),
        name="attn_backward",
        grid_spec=pltpu.PrefetchScalarGridSpec(
            num_scalar_prefetch=3, grid=(pairs,),
            in_specs=[ANY] * (len(deps) + members) + [full, pl.BlockSpec((LANES, d), lambda p, *_: (p, 0)), pl.BlockSpec((3, d, LANES), lambda p, *_: (0, 0, p)),
                      col, col, col, col, pl.BlockSpec((1, 8, length), lambda p, *_: (p, 0, 0))] + [part] * len(extra),
            out_specs=[part] * members + [pl.BlockSpec((1 << bits, 4, blk, LANES), lambda p, *_: (0, 0, 0, p))],
            scratch_shapes=[pltpu.VMEM((length, d), F32), pltpu.VMEM((length, d), BF), pltpu.VMEM((length, LANES), BF),
                            pltpu.VMEM((length, LANES), F32), pltpu.VMEM((length, LANES), F32), pltpu.VMEM((length, LANES), BF),
                            pltpu.SemaphoreType.DMA((members,))]),
        out_shape=[jax.ShapeDtypeStruct((length // members, d), BF)] * members + [jax.ShapeDtypeStruct((1 << bits, 4, blk, heads), BF)],
        cost_estimate=SMALL,
        compiler_params=pltpu.CompilerParams(vmem_limit_bytes=VMEM),
    )(prefix, me, j, *deps, *mcs, n1, wo, w, q, k, v, ctx, lse, *extra)
    return res[:members], res[members]


EPS = 1e-5


def normalise(v):
    centered = v - jnp.mean(v, axis=1, keepdims=True)
    r = lax.rsqrt(jnp.mean(centered * centered, axis=1, keepdims=True) + EPS)
    return centered * r, r


def norm_backward(xhat, r, grad, gain):
    scaled = grad * gain
    return r * (scaled - jnp.mean(scaled, axis=1, keepdims=True) - xhat * jnp.mean(scaled * xhat, axis=1, keepdims=True))


def order_rows(pos, rows_to_slots):
    n = pos.shape[1] if rows_to_slots else pos.shape[0]
    slot = lax.broadcasted_iota(jnp.int32, (n, n), 0 if rows_to_slots else 1)
    return jnp.where(slot == pos, 1.0, 0.0).astype(BF)


def first_norm_kernel(members, j_ref, *refs):
    xs, (gain, shift, dy, pos, out, sorted_dy) = refs[:members], refs[members:]
    for k in range(members):
        @pl.when(pl.program_id(0) == k)
        def _(k=k):
            xhat, _ = normalise(xs[k][...].astype(F32))
            out[...] = (xhat * gain[...] + shift[...]).astype(BF)
            if k == 0:
                sorted_dy[...] = dot(order_rows(pos[...], True), dy[...], 1, 0).astype(BF)


def first_norm(j, xs, gain, shift, dy, pos):
    members = len(xs)
    rows, d = xs[0].shape
    fixed = lambda shape: pl.BlockSpec(shape, lambda p, *_: (0, 0))
    return pl.pallas_call(
        partial(first_norm_kernel, members),
        name="first_norm",
        grid_spec=pltpu.PrefetchScalarGridSpec(
            num_scalar_prefetch=1, grid=(members,),
            in_specs=[fixed((rows, d))] * members + [fixed((1, d))] * 2 + [fixed((rows, d)), fixed((1, rows))],
            out_specs=[pl.BlockSpec((rows, d), lambda p, j_ref: (lax.rem(j_ref[0] + p, members), 0)), fixed((rows, d))]),
        out_shape=[jax.ShapeDtypeStruct((members * rows, d), BF), jax.ShapeDtypeStruct((rows, d), BF)],
        cost_estimate=SMALL,
        compiler_params=pltpu.CompilerParams(vmem_limit_bytes=VMEM),
    )(j, *xs, gain, shift, dy, pos)


def project_kernel(parts, *refs):
    total = dot(refs[0][...], refs[parts][...], 1, 0)
    for i in range(1, parts):
        total = total + dot(refs[i][...], refs[parts + i][...], 1, 0)
    refs[-1][0] = total.astype(BF)


def project(contexts, weights, members):
    parts = len(contexts)
    length, heads = contexts[0].shape
    d = weights[0].shape[1]
    rows = length // members
    return pl.pallas_call(
        partial(project_kernel, parts),
        name="project",
        grid=(members,),
        in_specs=[pl.BlockSpec((rows, heads), lambda p: (p, 0))] * parts + [pl.BlockSpec((heads, d), lambda p: (0, 0))] * parts,
        out_specs=pl.BlockSpec((1, rows, d), lambda p: (p, 0, 0)),
        out_shape=jax.ShapeDtypeStruct((members, rows, d), BF),
        cost_estimate=SMALL,
        compiler_params=pltpu.CompilerParams(vmem_limit_bytes=VMEM),
    )(*contexts, *weights)


def second_norm_kernel(came, x, gain, shift, pos, middle, n2):
    mid = x[...].astype(F32)
    for k in range(came.shape[0]):
        mid = mid + came[k].astype(F32)
    middle[...] = mid
    xhat, _ = normalise(mid)
    normed = (xhat * gain[...] + shift[...]).astype(BF)
    n2[...] = dot(order_rows(pos[...], True), normed, 1, 0).astype(BF)


def second_norm(came, x, gain, shift, pos):
    rows, d = x.shape
    fixed = lambda shape: pl.BlockSpec(shape, lambda p: (0,) * len(shape))
    return pl.pallas_call(
        second_norm_kernel,
        name="second_norm",
        grid=(1,),
        in_specs=[fixed(came.shape), fixed((rows, d)), fixed((1, d)), fixed((1, d)), fixed((1, rows))],
        out_specs=[fixed((rows, d))] * 2,
        out_shape=[jax.ShapeDtypeStruct((rows, d), F32), jax.ShapeDtypeStruct((rows, d), BF)],
        cost_estimate=SMALL,
        compiler_params=pltpu.CompilerParams(vmem_limit_bytes=VMEM),
    )(came, x, gain, shift, pos)


def add_small(a, b, deps):
    def kernel(*refs):
        refs[-1][...] = refs[-3][...] + refs[-2][...]
    full = pl.BlockSpec(memory_space=pltpu.VMEM)
    return pl.pallas_call(kernel, name="add_small", in_specs=[ANY] * len(deps) + [full, full], out_specs=full,
                          out_shape=jax.ShapeDtypeStruct(a.shape, a.dtype), cost_estimate=SMALL)(*deps, a, b)


def hi_lo(v):
    hi = v.astype(BF)
    return hi, (v - hi.astype(F32)).astype(BF)


def middle_backward_kernel(single, bnd_ref, t_ref, *refs):
    it = iter(refs)
    parts = [next(it) for _ in range(single)]
    dots, n2, rm, middle, dy, gain, pos, mg_ref, mc_ref, sums_ref = it
    t = t_ref[0]
    total = parts[0][...].astype(F32)
    for p in parts[1:]:
        total = total + p[...].astype(F32)
    n2v, rmv = n2[...], rm[...]
    rows = n2v.shape[0]
    experts = bnd_ref.shape[1] - 1
    logits = dot(n2v, rmv, 1, 0)
    route_prob = lane_softmax(logits, 0, experts)
    mixing = lane_softmax(logits, experts, experts + 2)
    row = lax.broadcasted_iota(jnp.int32, (rows, 1), 0)
    route = jnp.zeros((rows, 1), jnp.int32)
    for e in range(1, experts):
        route = route + (row >= bnd_ref[t, e]).astype(jnp.int32)
    gate = pick_lane(route_prob, route)
    m0, m1 = pick_lane(mixing, experts), pick_lane(mixing, experts + 1)
    dense_dot, expert_dot = dots[:, 0:1], dots[:, 1:2]
    d0, d1 = dense_dot, expert_dot * gate
    inner = m0 * d0 + m1 * d1
    lane = lax.broadcasted_iota(jnp.int32, logits.shape, 1)
    grad = expert_dot * (m1 * gate) * (jnp.where(lane == route, 1.0, 0.0) - route_prob)
    grad = jnp.where(lane < experts, grad, 0.0)
    grad = jnp.where(lane == experts, m0 * (d0 - inner), grad)
    grad = jnp.where(lane == experts + 1, m1 * (d1 - inner), grad)
    hi, lo = hi_lo(grad)
    total = total + dot(hi, rmv, 1, 1) + dot(lo, rmv, 1, 1)
    sums_ref[0:8, :] = (dot(hi.T, n2v, 1, 0) + dot(lo.T, n2v, 1, 0))[0:8]
    g = dot(order_rows(pos[...], False), total.astype(BF), 1, 0)
    xhat, r = normalise(middle[...])
    sums_ref[8:16, :] = jnp.zeros((8, g.shape[1]), F32)
    sums_ref[8:9, :] = jnp.sum(g * xhat, axis=0, keepdims=True)
    sums_ref[9:10, :] = jnp.sum(g, axis=0, keepdims=True)
    mg = dy[...].astype(F32) + norm_backward(xhat, r, g, gain[...])
    mg_ref[...] = mg
    mc_ref[...] = mg.astype(BF)


def middle_backward(bounds, t, parts, dots, n2, rm, middle, dy, gain, pos, deps=()):
    rows, d = n2.shape
    fixed = lambda shape: pl.BlockSpec(shape, lambda p, *_: (0, 0))
    big = fixed((rows, d))
    return pl.pallas_call(
        skip(partial(middle_backward_kernel, len(parts)), 2, len(deps)),
        name="middle_backward",
        grid_spec=pltpu.PrefetchScalarGridSpec(
            num_scalar_prefetch=2, grid=(1,),
            in_specs=[ANY] * len(deps) + [big] * len(parts)
            + [fixed((rows, 8)), big, fixed((d, 128)), big, big, fixed((1, d)), fixed((rows, 1))],
            out_specs=[big, big, fixed((16, d))]),
        out_shape=[jax.ShapeDtypeStruct((rows, d), F32), jax.ShapeDtypeStruct((rows, d), BF), jax.ShapeDtypeStruct((16, d), F32)],
        cost_estimate=SMALL,
        compiler_params=pltpu.CompilerParams(vmem_limit_bytes=VMEM),
    )(bounds, t, *deps, *parts, dots, n2, rm, middle, dy, gain, pos)


def layer_out_kernel(*refs):
    parts, (middle, pos, out) = refs[:-3], refs[-3:]
    total = parts[0][...].astype(F32)
    for p in parts[1:]:
        total = total + p[...].astype(F32)
    hi, lo = hi_lo(total)
    move = order_rows(pos[...], False)
    out[...] = (middle[...] + dot(move, hi, 1, 0) + dot(move, lo, 1, 0)).astype(BF)


def layer_out(parts, middle, pos, deps=()):
    rows, d = middle.shape
    big = pl.BlockSpec((rows, d), lambda p: (0, 0))
    return pl.pallas_call(
        skip(layer_out_kernel, 0, len(deps)),
        name="layer_out",
        grid=(1,),
        in_specs=[ANY] * len(deps) + [big] * (len(parts) + 1) + [pl.BlockSpec((rows, 1), lambda p: (0, 0))],
        out_specs=big,
        out_shape=jax.ShapeDtypeStruct((rows, d), BF),
        cost_estimate=SMALL,
        compiler_params=pltpu.CompilerParams(vmem_limit_bytes=VMEM),
    )(*deps, *parts, middle, pos)


def add_parts_kernel(*refs):
    total = refs[0][...].astype(F32)
    for p in refs[1:-1]:
        total = total + p[...].astype(F32)
    refs[-1][...] = total.astype(BF)


def add_parts(parts, deps=()):
    rows, d = parts[0].shape
    tile = pl.BlockSpec((rows // 2, d), lambda p: (p, 0))
    return pl.pallas_call(
        skip(add_parts_kernel, 0, len(deps)),
        name="add_parts",
        grid=(2,),
        in_specs=[ANY] * len(deps) + [tile] * len(parts),
        out_specs=tile,
        out_shape=jax.ShapeDtypeStruct((rows, d), BF),
        cost_estimate=SMALL,
        compiler_params=pltpu.CompilerParams(vmem_limit_bytes=VMEM),
    )(*deps, *parts)


def input_backward_kernel(count, *refs):
    parts = refs[:count]
    x, mg, gain, out, sums = refs[count:]
    g = parts[0][...].astype(F32)
    for p in parts[1:]:
        g = g + p[...].astype(F32)
    xhat, r = normalise(x[...].astype(F32))
    sums[...] = jnp.zeros_like(sums)
    sums[0:1, :] = jnp.sum(g * xhat, axis=0, keepdims=True)
    sums[1:2, :] = jnp.sum(g, axis=0, keepdims=True)
    out[...] = mg[...] + norm_backward(xhat, r, g, gain[...])


def input_backward(parts, x, mg, gain, deps=()):
    rows, d = x.shape
    fixed = lambda shape: pl.BlockSpec(shape, lambda p: (0, 0))
    big = fixed((rows, d))
    return pl.pallas_call(
        skip(partial(input_backward_kernel, len(parts)), 0, len(deps)),
        name="input_backward",
        grid=(1,),
        in_specs=[ANY] * len(deps) + [big] * (len(parts) + 2) + [fixed((1, d))],
        out_specs=[big, fixed((8, d))],
        out_shape=[jax.ShapeDtypeStruct((rows, d), F32), jax.ShapeDtypeStruct((8, d), F32)],
        cost_estimate=SMALL,
        compiler_params=pltpu.CompilerParams(vmem_limit_bytes=VMEM),
    )(*deps, *parts, x, mg, gain)


class Everywhere:
    def __init__(self, v):
        self.v = v
        self.hops = [(axis, 1 << b) for axis in ("tensor", "dp") for b in range(lax.axis_size(axis).bit_length() - 1)]
        self.launch()

    def launch(self):
        if self.hops:
            axis, bit = self.hops.pop(0)
            self.came = lax.ppermute(self.v, axis, [(i, i ^ bit) for i in range(lax.axis_size(axis))])
        else:
            self.came = None

    def add(self, mark):
        if self.came is None:
            return mark
        self.v = add_small(self.v, self.came, mark)
        self.launch()
        return (self.v,)


def over_dp(v, bit):
    return lax.ppermute(v, "dp", [(i, i ^ (1 << bit)) for i in range(lax.axis_size("dp"))])


def shards(inputs, cotangent, routes, prefixes, gain_one, shift_one, qkv_weight, out_weight, gain_two, shift_two,
           up_weight, down_weight, expert_up, expert_down, router_weight, mix_weight):
    rows, d = inputs.shape
    tensor = lax.axis_size("tensor")
    dp = lax.axis_size("dp")
    bits = dp.bit_length() - 1
    seqs = prefixes.shape[0]
    members = tensor // seqs
    experts = expert_up.shape[0]
    heads = qkv_weight.shape[2]
    pairs = heads // LANES
    t = lax.axis_index("tensor")
    s, j = t // members, t % members
    me = lax.axis_index("dp").astype(jnp.int32)
    me1, j1, t1 = me.reshape(1), j.astype(jnp.int32).reshape(1), t.astype(jnp.int32).reshape(1)
    place = lambda a, b: (a % seqs) * members + b % members
    everyone = [(a, b) for a in range(seqs) for b in range(members)]

    def from_member(v, k):
        return lax.ppermute(v, "tensor", [(place(a, b), place(a, b - k)) for a, b in everyone])

    def from_sequence(v, k):
        return lax.ppermute(v, "tensor", [(place(a, b), place(a - k, b)) for a, b in everyone])

    def to_member(v, k):
        return from_member(v, -k)

    def to_sequence(v, k):
        return from_sequence(v, -k)

    route_blocks = routes.reshape(tensor, rows)
    bounds = jnp.stack([jnp.sum((route_blocks < e).astype(jnp.int32), axis=1) for e in range(experts + 1)], axis=1)
    key_col = lax.dynamic_slice_in_dim(routes, t * rows, rows, 0) * rows + jnp.arange(rows, dtype=jnp.int32)[:, None]
    key_row = key_col.reshape(1, rows)
    pos_row = jnp.sum((key_col < key_row).astype(jnp.int32), axis=0, keepdims=True)
    pos_col = jnp.sum((key_row < key_col).astype(jnp.int32), axis=1, keepdims=True)
    chunk = [(dj, ds) for dj in range(members) for ds in range(seqs)]
    blocks = jnp.stack([((s + ds) % seqs) * members + (j + dj) % members for dj, ds in chunk]).astype(jnp.int32)
    near = [q for q, (dj, ds) in enumerate(chunk) if ds == 0]
    far = [q for q, (dj, ds) in enumerate(chunk) if ds > 0]

    xs = [inputs] + [from_member(inputs, k) for k in range(1, members)]
    flip = me & 1
    relay = pairs % 2 == 0 and dp > 1
    w_own = jnp.transpose(qkv_weight, (1, 0, 2))
    fetched = []
    for ds in range(1, seqs):
        if relay:
            half = lax.dynamic_slice_in_dim(qkv_weight, flip * (heads // 2), heads // 2, 2)
            fetched.append([from_sequence(jnp.transpose(half[:, a:b], (1, 0, 2)), ds) for a, b in ((0, 2), (2, 3))])
        else:
            fetched.append([from_sequence(w_own, ds)])
    wo_all = [out_weight] + [from_sequence(out_weight, ds) for ds in range(1, seqs)]
    gain_one, shift_one, gain_two, shift_two = [v.reshape(1, d) for v in (gain_one, shift_one, gain_two, shift_two)]
    prefix = lax.dynamic_slice_in_dim(prefixes, s, 1)
    n1, dys = first_norm(j1, xs, gain_one, shift_one, cotangent, pos_row)
    columns = jnp.arange(pairs, dtype=jnp.int32)
    pieces = [[] for _ in fetched]
    fence = (n1,)
    if relay:
        for k, got in enumerate(fetched):
            held = hold(got[0], (n1,))
            pieces[k] = [[held], [over_dp(held, 0)]]
            fence += (held,)
    saved = [attn_forward(prefix, columns, n1, [w_own], heads, deps=fence[1:])]
    if relay:
        for k, got in enumerate(fetched):
            held = hold(got[1], (saved[0][4],))
            pieces[k][0].append(held)
            pieces[k][1].append(over_dp(held, 0))
    else:
        pieces = [[got] for got in fetched]
    w_all = [w_own]
    for halves in pieces:
        part = ()
        for k, ws in enumerate(halves):
            at = (columns + (flip ^ k) * (pairs // 2))[:pairs // 2] if relay else columns
            part = attn_forward(prefix, at, n1, ws, heads, part, deps=() if part else (saved[-1][4],))
        saved.append(part)
        whole = [jnp.concatenate(ws, axis=0) for ws in halves]
        if relay:
            whole = [jnp.where(flip == 0, jnp.concatenate(whole, axis=2), jnp.concatenate(whole[::-1], axis=2))]
        w_all.append(whole[0])
    contexts = [v[3] for v in saved]

    def spread(mine):
        out = list(mine)
        for k in range(1, members):
            out += [from_member(m, k) for m in mine]
        return out

    dy_mine = [dys] + [from_sequence(dys, ds) for ds in range(1, seqs)]
    dy_near = [dys] + [from_member(dys, k) for k in range(1, members)]
    sent = project(contexts, wo_all, members)
    came = lax.all_to_all(sent, "tensor", 0, 0, axis_index_groups=[[place(a, b) for b in range(members)] for a in range(seqs)], tiled=True)
    middle, n2 = second_norm(came, inputs, gain_two, shift_two, pos_row)
    n2_mine = [n2] + [from_sequence(n2, ds) for ds in range(1, seqs)]
    n2_near = [n2] + [from_member(n2, k) for k in range(1, members)]

    rm = jnp.concatenate([router_weight, mix_weight, jnp.zeros((d, LANES - experts - 2), BF)], axis=1)
    straight = tuple(range(bits))
    turned = straight[1:] + straight[:1]
    orders = (straight, turned)
    pick = lambda v, which: [v[q] for q in which]
    out_a, rg_a, dots_a, sums = ffn_dense(me1, n2_near, dy_near, rm, up_weight, down_weight, experts, orders, deps=tuple(dy_mine[1:]))
    n2_all, dy_all = [], []
    n2_far, dy_far = [[hold(v, (out_a[0],)) for v in mine[1:]] for mine in (n2_mine, dy_mine)]
    for k in range(members):
        n2_all += [n2_near[k]] + [from_member(v, k) if k else v for v in n2_far]
        dy_all += [dy_near[k]] + [from_member(v, k) if k else v for v in dy_far]
    base = [[None] * tensor, [None] * tensor]
    for k, q in enumerate(near):
        base[0][q], base[1][q] = out_a[k], rg_a[k]
    cut = 1 if experts > 1 else experts
    out_e, rg_e, dots_e, keep_e, send_e = ffn_experts(me1, blocks, bounds, n2_all, dy_all, rm, expert_up, expert_down, 0, cut, base, straight)
    keep_e, send_e, dots = list(keep_e), list(send_e), dots_e
    if cut < experts:
        out_e, rg_e, dots_e, more_k, more_s = ffn_experts(me1, blocks, bounds, n2_all, dy_all, rm, expert_up, expert_down, cut, experts - cut, (out_e, rg_e), straight)
        keep_e, send_e, dots = keep_e + list(more_k), send_e + list(more_s), dots + dots_e
    out_e, rg_e = list(out_e), list(rg_e)
    out_b, rg_b, dots_b, ends = ffn_dense(me1, pick(n2_all, far), pick(dy_all, far), rm, up_weight, down_weight, experts, orders,
                                          (pick(out_e, far), pick(rg_e, far)), sums)
    for k, q in enumerate(far):
        out_e[q], rg_e[q] = out_b[k], rg_b[k]

    index = {c: q for q, c in enumerate(chunk)}
    cols = lambda v, k, n=1: v[:, k * rows:(k + n) * rows]
    dot_part = []
    for q, (dj, ds) in enumerate(chunk):
        dense_part = cols(dots_a, near.index(q)) if ds == 0 else cols(dots_b, far.index(q))
        dot_part.append(cols(dots, q) + dense_part)
    held = jnp.concatenate(dot_part[:seqs], axis=1)
    for k in range(1, members):
        held = held + to_member(jnp.concatenate(dot_part[k * seqs:(k + 1) * seqs], axis=1), k)
    own_dots = cols(held, 0)
    for ds in range(1, seqs):
        own_dots = own_dots + to_sequence(cols(held, ds), ds)

    def to_owner(parts):
        mine = [[parts[index[0, ds]]] + [to_member(parts[index[k, ds]], k) for k in range(1, members)] for ds in range(seqs)]
        return mine[0], mine[1:]

    def onward(terms, deps):
        sums = [add_parts(v, deps) for v in terms]
        return [to_sequence(v, ds + 1) for ds, v in enumerate(sums)], sums

    class Halving:
        def __init__(self, keep, send, order):
            self.keep, self.send, self.order, self.at = keep, send, order, 0

        def launch(self, deps=()):
            if deps:
                self.send = hold(self.send, deps)
            self.came = over_dp(self.send, self.order[self.at])
            self.at += 1

        def add(self, mark):
            self.keep, self.send = split_add(self.keep, self.came, mark)
            self.launch()
            return (self.send,)

        def rest(self, mark):
            while self.at < bits:
                mark = self.add(mark)
            return mark

    sums_e = [Halving(keep_e[e], send_e[e], straight) for e in range(experts)]
    down_sum, up_sum = Halving(ends[2], ends[3], turned), Halving(ends[0], ends[1], straight)
    rg_near, rg_far = to_owner(rg_e)
    for e in range(min(experts, 3)):
        sums_e[e].launch()
    down_sum.launch()
    came_far, terms = onward(rg_far, ())
    mark = tuple(terms[:1])
    for e in range(min(experts, 2)):
        mark = sums_e[e].add(mark)
    mg, mc, sums_two = middle_backward(bounds, t1, rg_near + came_far, own_dots.T, n2, rm, middle, cotangent, gain_two, pos_col, mark)
    mcs = [mc] + [from_member(mc, k) for k in range(1, members)]
    mark = down_sum.add((mc,))
    ngs = None
    grads = [None] * seqs
    for ds in list(range(1, seqs)) + [0]:
        ngs, grads[ds] = attn_backward(prefix, me1, j1, mcs, n1, wo_all[ds], w_all[ds], saved[ds], ngs, bits, mark)
        mark = (grads[ds],)
        if ds == 1 or seqs == 1:
            for e in range(3, experts):
                sums_e[e].launch(mark)
            mark = sums_e[0].add(mark)
            if experts > 2:
                mark = sums_e[2].add(mark)
    moved = [to_sequence(grads[ds], ds) for ds in range(1, seqs)]
    ng_parts = [ngs[0]] + [to_member(ngs[k], k) for k in range(1, members)]
    up_sum.launch(mark)
    if experts > 1:
        mark = sums_e[1].add(mark)
    input_grad, sums_one = input_backward(ng_parts, inputs, mg, gain_one, mark)
    mark = (sums_one,)
    sums = Everywhere(jnp.concatenate([sums_two, sums_one], axis=0))
    stacks = None

    def finish(e, mark):
        mark = sums_e[e].rest(mark)
        done = last_add(sums_e[e].keep, sums_e[e].came, (False, True), (experts, e), stacks, mark)
        return done, (done[1],)

    stacks, mark = finish(0, mark)
    if experts > 2:
        mark = sums_e[2].add(mark)
    mark = down_sum.add(mark)
    mark = sums.add(mark)
    for e in range(3, experts):
        mark = sums_e[e].add(mark)
    keep = grads[0]
    for v in moved[:-1]:
        keep = (keep.astype(F32) + v.astype(F32)).astype(BF)
    if moved:
        keep, send = split_add(keep, moved[-1], mark)
        mark = (send,)
    else:
        keep, send = keep[:dp // 2], keep[dp // 2:]
    attn_sum = Halving(keep, send, straight)
    attn_sum.launch()
    out_near, out_far = to_owner([hold(v, mark) for v in out_e])
    out_came, terms = onward(out_far, mark)
    mark = tuple(terms[:1]) or mark
    if experts > 1:
        stacks, mark = finish(1, mark)
    mark = sums.add(mark)
    mark = up_sum.add(mark)
    mark = down_sum.rest(mark)
    down_out, = last_add(down_sum.keep, down_sum.came, (True,), deps=mark)
    mark = (down_out,)
    for e in range(3, experts):
        mark = sums_e[e].add(mark)
    mark = sums.add(mark)
    if experts > 2:
        stacks, mark = finish(2, mark)
    layer_output = layer_out(out_near + out_came, middle, pos_col, mark)
    mark = (layer_output,)
    mark = attn_sum.add(mark)
    mark = sums.add(mark)
    mark = up_sum.add(mark)
    for e in range(3, experts):
        stacks, mark = finish(e, mark)
    expert_up_out, expert_down_out = stacks
    mark = attn_sum.add(mark)
    while sums.came is not None:
        mark = sums.add(mark)
    mark = up_sum.rest(mark)
    up_out, = last_add(up_sum.keep, up_sum.came, (False,), deps=mark)
    mark = attn_sum.rest((up_out,))
    *qkv_parts, out_out = last_add(attn_sum.keep, attn_sum.came, (False, False, False, True), deps=mark)
    lanes = d // (dp * tensor)
    begin = (me * tensor + t) * lanes
    small = lax.dynamic_slice_in_dim(sums.v, begin, lanes, 1)
    return (layer_output, input_grad, small[16], small[17], jnp.stack(qkv_parts, axis=1), out_out, small[8], small[9], up_out, down_out,
            expert_up_out, expert_down_out, small[0:experts].T, small[experts:experts + 2].T)


def solution(mesh):
    both = ("dp", "tensor")
    in_specs = (P(both, None), P(both, None), P("dp", None), P("dp"), P(), P(), P(None, None, "tensor"), P("tensor", None), P(), P(),
                P(None, "tensor"), P("tensor", None), P(None, None, "tensor"), P(None, "tensor", None), P(), P())
    out_specs = (P(both, None), P(both, None), P(both), P(both), P("dp", None, "tensor"), P("tensor", "dp"), P(both), P(both),
                 P("dp", "tensor"), P("tensor", "dp"), P(None, "dp", "tensor"), P(None, "tensor", "dp"), P(both, None), P(both, None))
    return jax.shard_map(shards, mesh=mesh, in_specs=in_specs, out_specs=out_specs, check_vma=False)
```

```python
from functools import partial
import jax, jax.numpy as jnp
from jax import lax
from jax.experimental import pallas as pl
from jax.experimental.pallas import tpu as pltpu
from jax.sharding import PartitionSpec as P

BF = jnp.bfloat16
F32 = jnp.float32
TILE_DENSE = 512
TILE_EXPERT = 256
PIECE = 16
SMALL = pl.CostEstimate(flops=0, bytes_accessed=0, transcendentals=0)
VMEM = 60 * 1024 * 1024
ANY = pl.BlockSpec(memory_space=pl.ANY)
SMEM = pl.BlockSpec(memory_space=pltpu.SMEM)


def dot(a, b, ca, cb):
    return lax.dot_general(a, b, (((ca,), (cb,)), ((), ())), preferred_element_type=F32)


def slot_of(value, order):
    out = jnp.int32(0)
    for k, bit in enumerate(order):
        out = out | (((value >> bit) & 1) << (len(order) - 1 - k))
    return out


def skip(kernel, scalars, deps):
    return lambda *refs: kernel(*refs[:scalars], *refs[scalars + deps:])


def lane_softmax(logits, first, last):
    lane = lax.broadcasted_iota(jnp.int32, logits.shape, 1)
    inside = (lane >= first) & (lane < last)
    masked = jnp.where(inside, logits, -1e30)
    top = jnp.max(masked, axis=1, keepdims=True)
    e = jnp.where(inside, jnp.exp(masked - top), 0.0)
    return e / jnp.sum(e, axis=1, keepdims=True)


def pick_lane(v, index):
    lane = lax.broadcasted_iota(jnp.int32, v.shape, 1)
    return jnp.sum(jnp.where(lane == index, v, 0.0), axis=1, keepdims=True)


def gelu_parts(pre):
    phi = 0.5 * (1.0 + lax.erf(pre * 0.7071067811865476))
    pdf = jnp.exp(pre * pre * -0.5) * 0.3989422804014327
    return pre * phi, phi + pre * pdf


def ffn_tile(lanes, rm, xt, dyt, coef_of, up_w, dn_w, UA, DA, ready):
    logits = dot(xt, rm[...], 1, 0)
    mixing = lane_softmax(logits, lanes, lanes + 2)
    coef = coef_of(logits, mixing)
    pre = dot(xt, up_w[...], 1, 0)
    g = dot(dyt, dn_w[...], 1, 1)
    hid, dg = gelu_parts(pre)
    hid = hid.astype(BF)
    dots = jnp.sum(hid.astype(F32) * g, axis=1, keepdims=True)
    pg = (g * dg * coef).astype(BF)
    cot = (dyt.astype(F32) * coef).astype(BF)
    out = dot(hid, dn_w[...], 1, 0) * coef
    rg = dot(pg, up_w[...], 1, 1)
    ready()
    UA[...] += dot(xt, pg, 0, 0)
    DA[...] += dot(cot, hid, 0, 0)
    return dots, out, rg


def stage_grads(ST, UA, DA, me, order, whole):
    bits = len(order)
    blk = UA.shape[0] >> bits

    def body(c, _):
        r = pl.ds(pl.multiple_of(c * blk, blk), blk)
        slot = jnp.where(whole, c, slot_of(c ^ me, order))
        ST[slot, 0] = UA[r, :].astype(BF)
        ST[slot, 1] = DA[r, :].astype(BF)
        return 0
    lax.fori_loop(0, 1 << bits, body, 0)


def dots_rows(dots):
    return jnp.broadcast_to(dots, (dots.shape[0], 128)).T[0:PIECE, :]


def dense_kernel(cfg, me_ref, *refs):
    chunks, rows, tm, lanes, order, first, deps = cfg
    it = iter(refs[deps:])
    take = lambda k: [next(it) for _ in range(k)]
    x_hbm, dy_hbm = take(chunks), take(chunks)
    rm, up_hbm, dn_hbm = take(3)
    base_o, base_r, sums_in = ([], [], []) if first else (take(chunks), take(chunks), take(2))
    out_refs, rg_refs = take(chunks), take(chunks)
    ends = take(2)
    X, DY, UP, DN, UA, DA, OB, RB, DT, OD, xsem, wsem, gsem, osem, dsem = take(15)
    ST, BO, BR, BD, bsem = (None,) * 5 if first else take(5)
    per = rows // tm
    weights = [pltpu.make_async_copy(up_hbm, UP, wsem.at[0]), pltpu.make_async_copy(dn_hbm, DN, wsem.at[1])]
    loads, bases = [], []
    for q in range(chunks):
        sl = pl.ds(q * rows, rows)
        loads.append([pltpu.make_async_copy(x_hbm[q], X.at[sl], xsem.at[q]), pltpu.make_async_copy(dy_hbm[q], DY.at[sl], xsem.at[chunks + q])])
        if not first:
            bases.append([pltpu.make_async_copy(base_o[q], BO.at[sl], bsem.at[q]), pltpu.make_async_copy(base_r[q].at[pl.ds(0, rows)], BR.at[sl], bsem.at[chunks + q]),
                          pltpu.make_async_copy(base_r[q].at[pl.ds(rows, PIECE)], BD.at[q], bsem.at[2 * chunks + q])])
    sums = [] if first else [pltpu.make_async_copy(sums_in[0], UA, gsem.at[0]), pltpu.make_async_copy(sums_in[1], DA, gsem.at[1])]
    for c in loads[0] + weights + sums + [c for q in loads[1:] for c in q] + [c for q in bases for c in q]:
        c.start()
    DT[...] = jnp.zeros_like(DT)
    if first:
        UA[...] = jnp.zeros_like(UA)
        DA[...] = jnp.zeros_like(DA)
    for c in weights:
        c.wait()

    def outs(q, part, slot):
        sl = pl.ds(part * tm, tm)
        return [pltpu.make_async_copy(OB.at[slot], out_refs[q].at[sl], osem.at[0, slot]),
                pltpu.make_async_copy(RB.at[slot], rg_refs[q].at[sl], osem.at[1, slot])]

    def one(i, _):
        slot = i % 2
        sl = pl.ds(pl.multiple_of(i * tm, tm), tm)
        for q in range(chunks):
            @pl.when(i == q * per)
            def _(q=q):
                for c in loads[q]:
                    c.wait()

        def ready():
            if not first:
                @pl.when(i == 0)
                def _():
                    for c in sums:
                        c.wait()
        dots, out, rg = ffn_tile(lanes, rm, X[sl, :], DY[sl, :], lambda l, m: pick_lane(m, lanes), UP, DN, UA, DA, ready)
        lines = dots_rows(dots)
        line = lax.broadcasted_iota(jnp.int32, lines.shape, 0)
        for q in range(chunks):
            for part in range(per):
                @pl.when(i == q * per + part)
                def _(q=q, part=part):
                    DT[q, :, part * tm:(part + 1) * tm] = jnp.where(line == 0, lines, 0.0)
        if not first:
            for q in range(chunks):
                @pl.when(i == q * per)
                def _(q=q):
                    for c in bases[q]:
                        c.wait()
            out = out + BO[sl, :].astype(F32)
            rg = rg + BR[sl, :].astype(F32)

        @pl.when(i >= 2)
        def _():
            for c in outs(0, 0, slot):
                c.wait()
        OB[slot] = out.astype(BF)
        RB[slot] = rg.astype(BF)
        for q in range(chunks):
            for part in range(per):
                @pl.when(i == q * per + part)
                def _(q=q, part=part):
                    for c in outs(q, part, slot):
                        c.start()
        return 0
    lax.fori_loop(0, chunks * per, one, 0)
    lines = []
    for q in range(chunks):
        total = DT[q] if first else DT[q] + BD[q].astype(F32)
        OD[q] = total.astype(BF)
        lines.append(pltpu.make_async_copy(OD.at[q], rg_refs[q].at[pl.ds(rows, PIECE)], dsem.at[q]))
    if first:
        last = lines + [pltpu.make_async_copy(UA, ends[0], gsem.at[0]), pltpu.make_async_copy(DA, ends[1], gsem.at[1])]
    else:
        stage_grads(ST, UA, DA, me_ref[0], order, False)
        half = ST.shape[0] // 2
        last = lines + [pltpu.make_async_copy(ST.at[pl.ds(h * half, half)], ends[h], gsem.at[h]) for h in range(2)]
    for c in last:
        c.start()
    for slot in range(min(2, chunks * per)):
        for c in outs(0, 0, slot):
            c.wait()
    for c in last:
        c.wait()


def ffn_dense(me, xs, dys, rm, up, down, lanes, order, base=None, sums=None, deps=()):
    chunks = len(xs)
    rows, d = xs[0].shape
    f = up.shape[1]
    n = chunks * rows
    tm = min(TILE_DENSE, rows)
    first = base is None
    bits = len(order)
    half = 1 << (bits - 1)
    vm = pl.BlockSpec(memory_space=pltpu.VMEM)
    part, lined = jax.ShapeDtypeStruct((rows, d), BF), jax.ShapeDtypeStruct((rows + PIECE, d), BF)
    total = jax.ShapeDtypeStruct((d, f), F32)
    grad = jax.ShapeDtypeStruct((half, 2, d >> bits, f), BF)
    ends = [total] * 2 if first else [grad] * 2
    more = [] if first else list(base[0]) + list(base[1]) + list(sums)
    scratch = [pltpu.VMEM((n, d), BF), pltpu.VMEM((n, d), BF), pltpu.VMEM((d, f), BF), pltpu.VMEM((f, d), BF), pltpu.VMEM((d, f), F32), pltpu.VMEM((d, f), F32),
               pltpu.VMEM((2, tm, d), BF), pltpu.VMEM((2, tm, d), BF), pltpu.VMEM((chunks, PIECE, d), F32), pltpu.VMEM((chunks, PIECE, d), BF),
               pltpu.SemaphoreType.DMA((2 * chunks,)), pltpu.SemaphoreType.DMA((2,)), pltpu.SemaphoreType.DMA((2,)), pltpu.SemaphoreType.DMA((2, 2)), pltpu.SemaphoreType.DMA((chunks,))]
    if not first:
        scratch += [pltpu.VMEM((2 * half, 2, d >> bits, f), BF), pltpu.VMEM((n, d), BF), pltpu.VMEM((n, d), BF), pltpu.VMEM((chunks, PIECE, d), BF), pltpu.SemaphoreType.DMA((3 * chunks,))]
    res = pl.pallas_call(
        partial(dense_kernel, (chunks, rows, tm, lanes, order, first, len(deps))),
        name="ffn_dense",
        out_shape=[part] * chunks + [lined] * chunks + ends,
        in_specs=[SMEM] + [ANY] * (len(deps) + 2 * chunks) + [vm] + [ANY] * (2 + len(more)),
        out_specs=[ANY] * (2 * chunks + len(ends)),
        scratch_shapes=scratch,
        cost_estimate=SMALL,
        compiler_params=pltpu.CompilerParams(vmem_limit_bytes=VMEM),
    )(me, *deps, *xs, *dys, rm, up, down, *more)
    return res[:chunks], res[chunks:2 * chunks], res[2 * chunks:]


def expert_kernel(cfg, me_ref, blk_ref, bnd_ref, *refs):
    first, count, whole, chunks, rows, d, tm, lanes, order, has, deps = cfg
    n = chunks * rows
    it = iter(refs[deps:])
    take = lambda k: [next(it) for _ in range(k)]
    x_hbm, dy_hbm = take(chunks), take(chunks)
    rm, up_hbm, dn_hbm = take(3)
    based = [q for q in range(chunks) if has[q]]
    base_o, base_r = take(len(based)), take(len(based))
    out_refs, rg_refs = take(chunks), take(chunks)
    whole_refs, keep_refs, send_refs = take(whole), take(count - whole), take(count - whole)
    X, DY, UP, DN, UA, DA, ST, XG, DG, VAL, OA, RA, DOT, BD, TR, TL, TH, xsem, wsem, gsem, osem, dsem = it
    half = ST.shape[0] // 2
    pieces = tm // PIECE
    rows_of = [pl.ds(q * rows, rows) for q in range(chunks)]
    copies = []
    for q in range(chunks):
        copies.append(pltpu.make_async_copy(x_hbm[q], X.at[rows_of[q]], xsem.at[q]))
        copies.append(pltpu.make_async_copy(dy_hbm[q], DY.at[rows_of[q]], xsem.at[chunks + q]))
    earlier = []
    for k, q in enumerate(based):
        earlier.append(pltpu.make_async_copy(base_o[k], X.at[rows_of[q]], xsem.at[q]))
        earlier.append(pltpu.make_async_copy(base_r[k].at[pl.ds(0, rows)], DY.at[rows_of[q]], xsem.at[chunks + q]))
        earlier.append(pltpu.make_async_copy(base_r[k].at[pl.ds(rows, PIECE)], BD.at[q], dsem.at[q]))

    def weights(e, slot):
        return [pltpu.make_async_copy(up_hbm.at[first + e], UP.at[slot], wsem.at[slot, 0]),
                pltpu.make_async_copy(dn_hbm.at[first + e], DN.at[slot], wsem.at[slot, 1])]

    def flush(g):
        if g < whole:
            return [pltpu.make_async_copy(ST, whole_refs[g], gsem.at[0])]
        g = g - whole
        return [pltpu.make_async_copy(ST.at[pl.ds(0, half)], keep_refs[g], gsem.at[0]),
                pltpu.make_async_copy(ST.at[pl.ds(half, half)], send_refs[g], gsem.at[1])]

    for c in copies + weights(0, 0):
        c.start()
    OA[...] = jnp.zeros_like(OA)
    RA[...] = jnp.zeros_like(RA)
    DOT[...] = jnp.zeros_like(DOT)
    iota16 = lax.broadcasted_iota(jnp.int32, (PIECE, 128), 0)

    def one_expert(e, _):
        slot = e % 2
        total = jnp.int32(0)
        for q in range(chunks):
            lo, hi = bnd_ref[blk_ref[q], first + e], bnd_ref[blk_ref[q], first + e + 1]
            p0 = lo // PIECE
            p1 = jnp.where(hi > lo, (hi + PIECE - 1) // PIECE, p0)

            def add(p, _, lo=lo, hi=hi, p0=p0, total=total, q=q):
                k = total + p - p0
                TR[k] = q * rows + p * PIECE
                TL[k] = lo - p * PIECE
                TH[k] = hi - p * PIECE
                return 0
            lax.fori_loop(p0, p1, add, 0)
            total = total + p1 - p0
        tiles = (total + pieces - 1) // pieces

        def pad(k, _):
            TR[k] = 0
            TL[k] = 0
            TH[k] = 0
            return 0
        lax.fori_loop(total, tiles * pieces, pad, 0)
        UA[...] = jnp.zeros_like(UA)
        DA[...] = jnp.zeros_like(DA)

        @pl.when(e == 0)
        def _():
            for c in copies:
                c.wait()
        for c in weights(e, slot):
            c.wait()

        @pl.when(e + 1 < count)
        def _():
            for c in weights(e + 1, 1 - slot):
                c.start()

        def one_tile(i, _):
            base = i * pieces
            for p in range(pieces):
                r = pl.ds(pl.multiple_of(TR[base + p], PIECE), PIECE)
                XG[pl.ds(p * PIECE, PIECE), :] = X[r, :]
                DG[pl.ds(p * PIECE, PIECE), :] = DY[r, :]
                ok = (iota16 >= TL[base + p]) & (iota16 < TH[base + p])
                VAL[pl.ds(p * PIECE, PIECE), :] = jnp.where(ok, 1.0, 0.0)
            valid = VAL[:, 0:1]

            def coef_of(logits, mixing):
                return pick_lane(mixing, lanes + 1) * pick_lane(lane_softmax(logits, 0, lanes), first + e) * valid
            dots, out, rg = ffn_tile(lanes, rm, XG[...], DG[...], coef_of, UP.at[slot], DN.at[slot], UA, DA, lambda: None)
            dots = jnp.broadcast_to(dots * valid, (tm, 128))
            for p in range(pieces):
                r = pl.ds(pl.multiple_of(TR[base + p], PIECE), PIECE)
                s = slice(p * PIECE, (p + 1) * PIECE)
                OA[r, :] += out[s]
                RA[r, :] += rg[s]
                DOT[r, :] += dots[s]
            return 0
        lax.fori_loop(0, tiles, one_tile, 0)

        @pl.when(e == count - 1)
        def _():
            for c in earlier:
                c.start()

        for g in range(count - 1):
            @pl.when(e == g + 1)
            def _(g=g):
                for c in flush(g):
                    c.wait()
        stage_grads(ST, UA, DA, me_ref[0], order, e < whole)
        for g in range(count):
            @pl.when(e == g)
            def _(g=g):
                for c in flush(g):
                    c.start()
        return 0
    lax.fori_loop(0, count, one_expert, 0)
    for c in earlier:
        c.wait()
    last = []
    step = min(256, rows)
    line = lax.broadcasted_iota(jnp.int32, (PIECE, step), 0)
    for q in range(chunks):
        r = rows_of[q]
        o, g = OA[r, :], RA[r, :]
        if has[q]:
            o, g = o + X[r, :].astype(F32), g + DY[r, :].astype(F32)
        X[r, :] = o.astype(BF)
        DY[r, :] = g.astype(BF)
        if not has[q]:
            BD[q] = jnp.zeros(BD.shape[1:], BF)
        for i in range(rows // step):
            sl = slice(i * step, (i + 1) * step)
            dots = jnp.where(line == 1, DOT[pl.ds(q * rows + i * step, step), :].T[0:PIECE, :], 0.0)
            BD[q, :, sl] = (BD[q, :, sl].astype(F32) + dots).astype(BF)
        last += [pltpu.make_async_copy(X.at[r], out_refs[q], osem.at[0, q]), pltpu.make_async_copy(DY.at[r], rg_refs[q].at[pl.ds(0, rows)], osem.at[1, q]),
                 pltpu.make_async_copy(BD.at[q], rg_refs[q].at[pl.ds(rows, PIECE)], dsem.at[q])]
        for c in last[-3:]:
            c.start()
    for c in last + flush(count - 1):
        c.wait()


def ffn_experts(me, blocks, bounds, xs, dys, rm, up, down, first, count, whole, base, order, deps=()):
    chunks = len(xs)
    rows, d = xs[0].shape
    lanes, _, f = up.shape
    n = chunks * rows
    tm = TILE_EXPERT
    bits = len(order)
    half = 1 << (bits - 1)
    grad, entire = [jax.ShapeDtypeStruct((k * half, 2, d >> bits, f), BF) for k in (1, 2)]
    part, lined = jax.ShapeDtypeStruct((rows, d), BF), jax.ShapeDtypeStruct((rows + PIECE, d), BF)
    table = n // PIECE + chunks * lanes + 2 * tm // PIECE
    vm = pl.BlockSpec(memory_space=pltpu.VMEM)
    has = tuple(b is not None for b in base[0])
    more = [b for k in range(2) for b in base[k] if b is not None]
    res = pl.pallas_call(
        partial(expert_kernel, (first, count, whole, chunks, rows, d, tm, lanes, order, has, len(deps))),
        name="ffn_experts",
        out_shape=[part] * chunks + [lined] * chunks + [entire] * whole + [grad] * (2 * (count - whole)),
        in_specs=[SMEM] * 3 + [ANY] * (len(deps) + 2 * chunks) + [vm] + [ANY] * (2 + len(more)),
        out_specs=[ANY] * (2 * chunks + 2 * count - whole),
        scratch_shapes=[
            pltpu.VMEM((n, d), BF), pltpu.VMEM((n, d), BF), pltpu.VMEM((2, d, f), BF), pltpu.VMEM((2, f, d), BF),
            pltpu.VMEM((d, f), F32), pltpu.VMEM((d, f), F32), pltpu.VMEM((2 * half, 2, d >> bits, f), BF),
            pltpu.VMEM((tm, d), BF), pltpu.VMEM((tm, d), BF), pltpu.VMEM((tm, 128), F32),
            pltpu.VMEM((n, d), F32), pltpu.VMEM((n, d), F32), pltpu.VMEM((n, 128), F32), pltpu.VMEM((chunks, PIECE, d), BF),
            pltpu.SMEM((table,), jnp.int32), pltpu.SMEM((table,), jnp.int32), pltpu.SMEM((table,), jnp.int32),
            pltpu.SemaphoreType.DMA((2 * chunks,)), pltpu.SemaphoreType.DMA((2, 2)), pltpu.SemaphoreType.DMA((2,)), pltpu.SemaphoreType.DMA((2, chunks)), pltpu.SemaphoreType.DMA((chunks,)),
        ],
        cost_estimate=SMALL,
        compiler_params=pltpu.CompilerParams(vmem_limit_bytes=VMEM),
    )(me, blocks, bounds, *deps, *xs, *dys, rm, up, down, *more)
    at = 2 * chunks + whole
    return res[:chunks], res[chunks:2 * chunks], res[2 * chunks:at], res[at:at + count - whole], res[at + count - whole:]


def split_add_kernel(deps, *refs):
    ka, kb, ca, cb, keep, send = refs[deps:]
    keep[...] = (ka[...].astype(F32) + ca[...].astype(F32)).astype(BF)
    send[...] = (kb[...].astype(F32) + cb[...].astype(F32)).astype(BF)


def split_add(kept, came, deps=()):
    h, m, blk, f = kept.shape
    near = pl.BlockSpec((1, 1, blk, f), lambda i, k: (i, k, 0, 0))
    far = pl.BlockSpec((1, 1, blk, f), lambda i, k: (i + h // 2, k, 0, 0))
    out = jax.ShapeDtypeStruct((h // 2, m, blk, f), BF)
    return pl.pallas_call(
        partial(split_add_kernel, len(deps)),
        name="split_add",
        grid=(h // 2, m),
        in_specs=[ANY] * len(deps) + [near, far, near, far],
        out_specs=[near, near],
        out_shape=[out, out],
        cost_estimate=SMALL,
        compiler_params=pltpu.CompilerParams(vmem_limit_bytes=VMEM),
    )(*deps, kept, kept, came, came)


def last_add_kernel(deps, turns, *refs):
    terms = refs[deps:-len(turns)]
    outs = refs[-len(turns):]
    for k, turned in enumerate(turns):
        total = terms[0][0, k].astype(F32)
        for v in terms[1:]:
            total = total + v[0, k].astype(F32)
        outs[k][...] = (total.T if turned else total).reshape(outs[k].shape)


def last_add(terms, turns, place=None, stacks=None, deps=()):
    _, m, blk, f = terms[0].shape
    shapes = [(f, blk) if turned else (blk, f) for turned in turns]
    aliases = {}
    if place is None:
        out_shape = [jax.ShapeDtypeStruct(s, F32) for s in shapes]
        out_specs = [pl.BlockSpec(s, lambda i: (0, 0)) for s in shapes]
    else:
        count, at = place
        out_shape = [jax.ShapeDtypeStruct((count,) + s, F32) for s in shapes]
        out_specs = [pl.BlockSpec((1,) + s, lambda i: (at, 0, 0)) for s in shapes]
        if stacks is not None:
            aliases = {k: k for k in range(m)}
            deps = tuple(stacks) + tuple(deps)
    full = pl.BlockSpec((1, m, blk, f), lambda i: (0, 0, 0, 0))
    return pl.pallas_call(
        partial(last_add_kernel, len(deps), turns),
        name="last_add",
        grid=(1,),
        in_specs=[ANY] * len(deps) + [full] * len(terms),
        out_specs=out_specs,
        out_shape=out_shape,
        input_output_aliases=aliases,
        cost_estimate=SMALL,
        compiler_params=pltpu.CompilerParams(vmem_limit_bytes=VMEM),
    )(*deps, *terms)


def hold(v, deps):
    return pl.pallas_call(
        lambda *refs: None,
        name="hold",
        in_specs=[ANY] * (1 + len(deps)),
        out_specs=ANY,
        out_shape=jax.ShapeDtypeStruct(v.shape, v.dtype),
        input_output_aliases={0: 0},
        cost_estimate=SMALL,
    )(v, *deps)


HD = 64
LANES = 128


def head_part(v, h):
    lane = lax.broadcasted_iota(jnp.int32, v.shape, 1)
    return jnp.where((lane // HD) == h, v, jnp.zeros((), v.dtype))


def masked_scores(st, key_first, query_first, prefix):
    key_pos = key_first + lax.broadcasted_iota(jnp.int32, st.shape, 0)
    query_pos = query_first + lax.broadcasted_iota(jnp.int32, st.shape, 1)
    seen = key_pos <= query_pos
    if prefix is not None:
        seen = seen | (key_pos < prefix)
    return jnp.where(seen, st, -1e30)


def score_block(k2, qm, half, length, prefix):
    mid = length // 2
    if half == 0:
        return masked_scores(dot(k2[0:mid], qm, 1, 1), 0, 0, prefix)
    low = dot(k2[0:mid], qm, 1, 1)
    high = masked_scores(dot(k2[mid:length], qm, 1, 1), mid, mid, None)
    return jnp.concatenate([low, high], 0)


def attn_forward_kernel(length, pieces, aliased, prefix_ref, at_ref, *refs):
    n1_ref = refs[0]
    w_refs = [(r, i) for r, n in zip(refs[1:], pieces) for i in range(n)]
    q_ref, k_ref, v_ref, ctx_ref, lse_ref = refs[1 + len(pieces) + aliased:]
    mid = length // 2
    prefix = prefix_ref[0]
    n1 = n1_ref[...]
    for out, (w, i) in zip((q_ref, k_ref, v_ref), w_refs):
        out[...] = dot(n1, w[i], 1, 0).astype(BF)
    vt = v_ref[...].T
    k2 = k_ref[...]
    for half in range(2):
        rows = pl.ds(half * mid, mid)
        q2 = q_ref[rows, :] * jnp.asarray(HD ** -0.5, BF)
        keys = mid * (half + 1)
        parts = []
        for h in range(2):
            st = score_block(k2, head_part(q2, h), half, length, prefix)
            top = jnp.max(st, axis=0, keepdims=True)
            p = jnp.exp(st - top)
            total = jnp.sum(p, axis=0, keepdims=True)
            c = dot(vt[h * HD:(h + 1) * HD, 0:keys], p.astype(BF), 1, 0)
            parts.append(c / total)
            lse_ref[0, h:h + 1, rows] = top + jnp.log(total)
        ctx_ref[rows, :] = jnp.concatenate(parts, 0).T.astype(BF)


def attn_forward(prefix, at, n1, ws, heads, earlier=(), deps=()):
    length, d = n1.shape
    pairs = ws[0].shape[2] // LANES
    col = pl.BlockSpec((length, LANES), lambda p, _, at_ref: (0, at_ref[p]))
    out = jax.ShapeDtypeStruct((length, heads), BF)
    done = len(earlier)
    skipped = len(deps)
    return pl.pallas_call(
        skip(partial(attn_forward_kernel, length, tuple(w.shape[0] for w in ws), done), 2, skipped),
        name="attn_forward",
        grid_spec=pltpu.PrefetchScalarGridSpec(
            num_scalar_prefetch=2, grid=(pairs,),
            in_specs=[ANY] * skipped + [pl.BlockSpec((length, d), lambda p, *_: (0, 0))]
            + [pl.BlockSpec((w.shape[0], d, LANES), lambda p, *_: (0, 0, p)) for w in ws] + [ANY] * done,
            out_specs=[col] * 4 + [pl.BlockSpec((1, 8, length), lambda p, _, at_ref: (at_ref[p], 0, 0))]),
        out_shape=[out] * 4 + [jax.ShapeDtypeStruct((heads // LANES, 8, length), F32)],
        input_output_aliases={3 + skipped + len(ws) + k: k for k in range(done)},
        cost_estimate=SMALL,
        compiler_params=pltpu.CompilerParams(vmem_limit_bytes=VMEM),
    )(prefix, at, *deps, n1, *ws, *earlier)


def attn_backward_kernel(length, bits, members, based, prefix_ref, me_ref, j_ref, *refs):
    it = iter(refs)
    take = lambda k: [next(it) for _ in range(k)]
    mcs = take(members)
    n1_ref, wo_ref, w_ref, q_ref, k_ref, v_ref, ctx_ref, lse_ref = take(8)
    bases = take(members) if based else []
    ng_refs = take(members)
    grad_ref, NG, MC, DC, DK, DV, DQ, sem = it
    rows_each = length // members
    where = [pl.ds(pl.multiple_of(lax.rem(j_ref[0] + k, members) * rows_each, rows_each), rows_each) for k in range(members)]
    mid = length // 2
    prefix = prefix_ref[0]
    me = me_ref[0]
    pair = pl.program_id(0)
    copies = [pltpu.make_async_copy(mcs[k], MC.at[where[k]], sem.at[k]) for k in range(members)]

    @pl.when(pair == 0)
    def _():
        for c in copies:
            c.start()
        for c in copies:
            c.wait()
    mc = MC[...]
    DC[...] = dot(mc, wo_ref[...], 1, 1).astype(BF)
    k2, v2 = k_ref[...], v_ref[...]
    kt = k2.T
    scale = jnp.asarray(HD ** -0.5, BF)
    for half in range(2):
        rows = pl.ds(half * mid, mid)
        q2 = q_ref[rows, :] * scale
        dc2 = DC[rows, :]
        keys = mid * (half + 1)
        dv = jnp.zeros((keys, LANES), F32)
        dk = jnp.zeros((keys, LANES), F32)
        dq = []
        for h in range(2):
            qm, dcm = head_part(q2, h), head_part(dc2, h)
            st = score_block(k2, qm, half, length, prefix)
            p = jnp.exp(st - lse_ref[0, h:h + 1, rows])
            dv = dv + dot(p.astype(BF), dcm, 1, 0)
            dp = dot(v2[0:keys], dcm, 1, 1)
            ds = (p * (dp - jnp.sum(p * dp, axis=0, keepdims=True))).astype(BF)
            dk = dk + dot(ds, qm, 1, 0)
            dq.append(dot(kt[h * HD:(h + 1) * HD, 0:keys], ds, 1, 0))
        DQ[rows, :] = (jnp.concatenate(dq, 0) * HD ** -0.5).T.astype(BF)
        if half == 0:
            DK[0:mid, :] = dk
            DV[0:mid, :] = dv
        else:
            DK[0:mid, :] += dk[0:mid]
            DV[0:mid, :] += dv[0:mid]
            DK[mid:length, :] = dk[mid:length]
            DV[mid:length, :] = dv[mid:length]
    dq, dk, dv = DQ[...], DK[...].astype(BF), DV[...].astype(BF)
    ng = dot(dq, w_ref[0], 1, 1) + dot(dk, w_ref[1], 1, 1) + dot(dv, w_ref[2], 1, 1)

    @pl.when(pair == 0)
    def _():
        NG[...] = ng

    @pl.when(pair > 0)
    def _():
        NG[...] += ng
    n1 = n1_ref[...]
    grads = [dot(n1, x, 0, 0) for x in (dq, dk, dv)] + [dot(mc, ctx_ref[...], 0, 0)]
    blk = n1.shape[1] >> bits
    for c in range(1 << bits):
        slot = slot_of(jnp.int32(c) ^ me, range(bits))
        for i in range(4):
            grad_ref[slot, i] = grads[i][c * blk:(c + 1) * blk].astype(BF)

    @pl.when(pair == pl.num_programs(0) - 1)
    def _():
        for k in range(members):
            done = NG[where[k], :]
            if based:
                done = done + bases[k][...].astype(F32)
            ng_refs[k][...] = done.astype(BF)


def attn_backward(prefix, me, j, mcs, n1, wo, w, saved, base, bits, deps=()):
    q, k, v, ctx, lse = saved
    length, d = n1.shape
    heads = w.shape[2]
    pairs = heads // LANES
    blk = d >> bits
    members = len(mcs)
    col = pl.BlockSpec((length, LANES), lambda p, *_: (0, p))
    full = pl.BlockSpec((length, d), lambda p, *_: (0, 0))
    part = pl.BlockSpec((length // members, d), lambda p, *_: (0, 0))
    extra = [] if base is None else list(base)
    res = pl.pallas_call(
        skip(partial(attn_backward_kernel, length, bits, members, base is not None), 3, len(deps)),
        name="attn_backward",
        grid_spec=pltpu.PrefetchScalarGridSpec(
            num_scalar_prefetch=3, grid=(pairs,),
            in_specs=[ANY] * (len(deps) + members) + [full, pl.BlockSpec((LANES, d), lambda p, *_: (p, 0)), pl.BlockSpec((3, d, LANES), lambda p, *_: (0, 0, p)),
                      col, col, col, col, pl.BlockSpec((1, 8, length), lambda p, *_: (p, 0, 0))] + [part] * len(extra),
            out_specs=[part] * members + [pl.BlockSpec((1 << bits, 4, blk, LANES), lambda p, *_: (0, 0, 0, p))],
            scratch_shapes=[pltpu.VMEM((length, d), F32), pltpu.VMEM((length, d), BF), pltpu.VMEM((length, LANES), BF),
                            pltpu.VMEM((length, LANES), F32), pltpu.VMEM((length, LANES), F32), pltpu.VMEM((length, LANES), BF),
                            pltpu.SemaphoreType.DMA((members,))]),
        out_shape=[jax.ShapeDtypeStruct((length // members, d), BF)] * members + [jax.ShapeDtypeStruct((1 << bits, 4, blk, heads), BF)],
        cost_estimate=SMALL,
        compiler_params=pltpu.CompilerParams(vmem_limit_bytes=VMEM),
    )(prefix, me, j, *deps, *mcs, n1, wo, w, q, k, v, ctx, lse, *extra)
    return res[:members], res[members]


EPS = 1e-5


def normalise(v):
    centered = v - jnp.mean(v, axis=1, keepdims=True)
    r = lax.rsqrt(jnp.mean(centered * centered, axis=1, keepdims=True) + EPS)
    return centered * r, r


def norm_backward(xhat, r, grad, gain):
    scaled = grad * gain
    return r * (scaled - jnp.mean(scaled, axis=1, keepdims=True) - xhat * jnp.mean(scaled * xhat, axis=1, keepdims=True))


def order_rows(pos, rows_to_slots):
    n = pos.shape[1] if rows_to_slots else pos.shape[0]
    slot = lax.broadcasted_iota(jnp.int32, (n, n), 0 if rows_to_slots else 1)
    return jnp.where(slot == pos, 1.0, 0.0).astype(BF)


def first_norm_kernel(members, j_ref, *refs):
    xs, (gain, shift, dy, pos, out, sorted_dy) = refs[:members], refs[members:]
    for k in range(members):
        @pl.when(pl.program_id(0) == k)
        def _(k=k):
            xhat, _ = normalise(xs[k][...].astype(F32))
            out[...] = (xhat * gain[...] + shift[...]).astype(BF)
            if k == 0:
                sorted_dy[...] = dot(order_rows(pos[...], True), dy[...], 1, 0).astype(BF)


def first_norm(j, xs, gain, shift, dy, pos):
    members = len(xs)
    rows, d = xs[0].shape
    fixed = lambda shape: pl.BlockSpec(shape, lambda p, *_: (0, 0))
    return pl.pallas_call(
        partial(first_norm_kernel, members),
        name="first_norm",
        grid_spec=pltpu.PrefetchScalarGridSpec(
            num_scalar_prefetch=1, grid=(members,),
            in_specs=[fixed((rows, d))] * members + [fixed((1, d))] * 2 + [fixed((rows, d)), fixed((1, rows))],
            out_specs=[pl.BlockSpec((rows, d), lambda p, j_ref: (lax.rem(j_ref[0] + p, members), 0)), fixed((rows, d))]),
        out_shape=[jax.ShapeDtypeStruct((members * rows, d), BF), jax.ShapeDtypeStruct((rows, d), BF)],
        cost_estimate=SMALL,
        compiler_params=pltpu.CompilerParams(vmem_limit_bytes=VMEM),
    )(j, *xs, gain, shift, dy, pos)


def project_kernel(parts, *refs):
    total = dot(refs[0][...], refs[parts][...], 1, 0)
    for i in range(1, parts):
        total = total + dot(refs[i][...], refs[parts + i][...], 1, 0)
    refs[-1][0] = total.astype(BF)


def project(contexts, weights, members):
    parts = len(contexts)
    length, heads = contexts[0].shape
    d = weights[0].shape[1]
    rows = length // members
    return pl.pallas_call(
        partial(project_kernel, parts),
        name="project",
        grid=(members,),
        in_specs=[pl.BlockSpec((rows, heads), lambda p: (p, 0))] * parts + [pl.BlockSpec((heads, d), lambda p: (0, 0))] * parts,
        out_specs=pl.BlockSpec((1, rows, d), lambda p: (p, 0, 0)),
        out_shape=jax.ShapeDtypeStruct((members, rows, d), BF),
        cost_estimate=SMALL,
        compiler_params=pltpu.CompilerParams(vmem_limit_bytes=VMEM),
    )(*contexts, *weights)


def second_norm_kernel(came, x, gain, shift, pos, middle, n2):
    mid = x[...].astype(F32)
    for k in range(came.shape[0]):
        mid = mid + came[k].astype(F32)
    middle[...] = mid
    xhat, _ = normalise(mid)
    normed = (xhat * gain[...] + shift[...]).astype(BF)
    n2[...] = dot(order_rows(pos[...], True), normed, 1, 0).astype(BF)


def second_norm(came, x, gain, shift, pos):
    rows, d = x.shape
    fixed = lambda shape: pl.BlockSpec(shape, lambda p: (0,) * len(shape))
    return pl.pallas_call(
        second_norm_kernel,
        name="second_norm",
        grid=(1,),
        in_specs=[fixed(came.shape), fixed((rows, d)), fixed((1, d)), fixed((1, d)), fixed((1, rows))],
        out_specs=[fixed((rows, d))] * 2,
        out_shape=[jax.ShapeDtypeStruct((rows, d), F32), jax.ShapeDtypeStruct((rows, d), BF)],
        cost_estimate=SMALL,
        compiler_params=pltpu.CompilerParams(vmem_limit_bytes=VMEM),
    )(came, x, gain, shift, pos)


def add_small(a, b, deps):
    def kernel(*refs):
        refs[-1][...] = refs[-3][...] + refs[-2][...]
    full = pl.BlockSpec(memory_space=pltpu.VMEM)
    return pl.pallas_call(kernel, name="add_small", in_specs=[ANY] * len(deps) + [full, full], out_specs=full,
                          out_shape=jax.ShapeDtypeStruct(a.shape, a.dtype), cost_estimate=SMALL)(*deps, a, b)


def hi_lo(v):
    hi = v.astype(BF)
    return hi, (v - hi.astype(F32)).astype(BF)


def middle_backward_kernel(single, bnd_ref, t_ref, *refs):
    it = iter(refs)
    parts = [next(it) for _ in range(single)]
    n2, rm, middle, dy, gain, pos, mg_ref, mc_ref, sums_ref = it
    t = t_ref[0]
    n2v, rmv = n2[...], rm[...]
    rows = n2v.shape[0]
    total = parts[0][0:rows, :].astype(F32)
    lines = parts[0][rows:rows + PIECE, 0:rows].astype(F32)
    for p in parts[1:]:
        total = total + p[0:rows, :].astype(F32)
        lines = lines + p[rows:rows + PIECE, 0:rows].astype(F32)
    dots = jnp.concatenate([lines, jnp.zeros((128 - PIECE, rows), F32)], axis=0).T
    experts = bnd_ref.shape[1] - 1
    logits = dot(n2v, rmv, 1, 0)
    route_prob = lane_softmax(logits, 0, experts)
    mixing = lane_softmax(logits, experts, experts + 2)
    row = lax.broadcasted_iota(jnp.int32, (rows, 1), 0)
    route = jnp.zeros((rows, 1), jnp.int32)
    for e in range(1, experts):
        route = route + (row >= bnd_ref[t, e]).astype(jnp.int32)
    gate = pick_lane(route_prob, route)
    m0, m1 = pick_lane(mixing, experts), pick_lane(mixing, experts + 1)
    dense_dot, expert_dot = dots[:, 0:1], dots[:, 1:2]
    d0, d1 = dense_dot, expert_dot * gate
    inner = m0 * d0 + m1 * d1
    lane = lax.broadcasted_iota(jnp.int32, logits.shape, 1)
    grad = expert_dot * (m1 * gate) * (jnp.where(lane == route, 1.0, 0.0) - route_prob)
    grad = jnp.where(lane < experts, grad, 0.0)
    grad = jnp.where(lane == experts, m0 * (d0 - inner), grad)
    grad = jnp.where(lane == experts + 1, m1 * (d1 - inner), grad)
    hi, lo = hi_lo(grad)
    total = total + dot(hi, rmv, 1, 1) + dot(lo, rmv, 1, 1)
    sums_ref[0:8, :] = (dot(hi.T, n2v, 1, 0) + dot(lo.T, n2v, 1, 0))[0:8]
    g = dot(order_rows(pos[...], False), total.astype(BF), 1, 0)
    xhat, r = normalise(middle[...])
    sums_ref[8:16, :] = jnp.zeros((8, g.shape[1]), F32)
    sums_ref[8:9, :] = jnp.sum(g * xhat, axis=0, keepdims=True)
    sums_ref[9:10, :] = jnp.sum(g, axis=0, keepdims=True)
    mg = dy[...].astype(F32) + norm_backward(xhat, r, g, gain[...])
    mg_ref[...] = mg
    mc_ref[...] = mg.astype(BF)


def middle_backward(bounds, t, parts, n2, rm, middle, dy, gain, pos, deps=()):
    rows, d = n2.shape
    fixed = lambda shape: pl.BlockSpec(shape, lambda p, *_: (0, 0))
    big = fixed((rows, d))
    return pl.pallas_call(
        skip(partial(middle_backward_kernel, len(parts)), 2, len(deps)),
        name="middle_backward",
        grid_spec=pltpu.PrefetchScalarGridSpec(
            num_scalar_prefetch=2, grid=(1,),
            in_specs=[ANY] * len(deps) + [fixed((rows + PIECE, d))] * len(parts)
            + [big, fixed((d, 128)), big, big, fixed((1, d)), fixed((rows, 1))],
            out_specs=[big, big, fixed((16, d))]),
        out_shape=[jax.ShapeDtypeStruct((rows, d), F32), jax.ShapeDtypeStruct((rows, d), BF), jax.ShapeDtypeStruct((16, d), F32)],
        cost_estimate=SMALL,
        compiler_params=pltpu.CompilerParams(vmem_limit_bytes=VMEM),
    )(bounds, t, *deps, *parts, n2, rm, middle, dy, gain, pos)


def layer_out_kernel(*refs):
    parts, (middle, pos, out) = refs[:-3], refs[-3:]
    total = parts[0][...].astype(F32)
    for p in parts[1:]:
        total = total + p[...].astype(F32)
    hi, lo = hi_lo(total)
    move = order_rows(pos[...], False)
    out[...] = (middle[...] + dot(move, hi, 1, 0) + dot(move, lo, 1, 0)).astype(BF)


def layer_out(parts, middle, pos, deps=()):
    rows, d = middle.shape
    big = pl.BlockSpec((rows, d), lambda p: (0, 0))
    return pl.pallas_call(
        skip(layer_out_kernel, 0, len(deps)),
        name="layer_out",
        grid=(1,),
        in_specs=[ANY] * len(deps) + [big] * (len(parts) + 1) + [pl.BlockSpec((rows, 1), lambda p: (0, 0))],
        out_specs=big,
        out_shape=jax.ShapeDtypeStruct((rows, d), BF),
        cost_estimate=SMALL,
        compiler_params=pltpu.CompilerParams(vmem_limit_bytes=VMEM),
    )(*deps, *parts, middle, pos)


def add_parts_kernel(*refs):
    total = refs[0][...].astype(F32)
    for p in refs[1:-1]:
        total = total + p[...].astype(F32)
    refs[-1][...] = total.astype(BF)


def add_parts(parts, deps=()):
    rows, d = parts[0].shape
    tile = pl.BlockSpec((rows, d), lambda p: (p, 0))
    return pl.pallas_call(
        skip(add_parts_kernel, 0, len(deps)),
        name="add_parts",
        grid=(1,),
        in_specs=[ANY] * len(deps) + [tile] * len(parts),
        out_specs=tile,
        out_shape=jax.ShapeDtypeStruct((rows, d), BF),
        cost_estimate=SMALL,
        compiler_params=pltpu.CompilerParams(vmem_limit_bytes=VMEM),
    )(*deps, *parts)


def input_backward_kernel(count, *refs):
    parts = refs[:count]
    x, mg, gain, out, sums = refs[count:]
    g = parts[0][...].astype(F32)
    for p in parts[1:]:
        g = g + p[...].astype(F32)
    xhat, r = normalise(x[...].astype(F32))
    sums[...] = jnp.zeros_like(sums)
    sums[0:1, :] = jnp.sum(g * xhat, axis=0, keepdims=True)
    sums[1:2, :] = jnp.sum(g, axis=0, keepdims=True)
    out[...] = mg[...] + norm_backward(xhat, r, g, gain[...])


def input_backward(parts, x, mg, gain, deps=()):
    rows, d = x.shape
    fixed = lambda shape: pl.BlockSpec(shape, lambda p: (0, 0))
    big = fixed((rows, d))
    return pl.pallas_call(
        skip(partial(input_backward_kernel, len(parts)), 0, len(deps)),
        name="input_backward",
        grid=(1,),
        in_specs=[ANY] * len(deps) + [big] * (len(parts) + 2) + [fixed((1, d))],
        out_specs=[big, fixed((8, d))],
        out_shape=[jax.ShapeDtypeStruct((rows, d), F32), jax.ShapeDtypeStruct((8, d), F32)],
        cost_estimate=SMALL,
        compiler_params=pltpu.CompilerParams(vmem_limit_bytes=VMEM),
    )(*deps, *parts, x, mg, gain)


class Everywhere:
    def __init__(self, v):
        self.v = v
        self.hops = [(axis, 1 << b) for axis in ("tensor", "dp") for b in range(lax.axis_size(axis).bit_length() - 1)]
        self.launch()

    def launch(self):
        if self.hops:
            axis, bit = self.hops.pop(0)
            self.came = lax.ppermute(self.v, axis, [(i, i ^ bit) for i in range(lax.axis_size(axis))])
        else:
            self.came = None

    def add(self, mark):
        if self.came is None:
            return mark
        self.v = add_small(self.v, self.came, mark)
        self.launch()
        return (self.v,)


def over_dp(v, bit):
    return lax.ppermute(v, "dp", [(i, i ^ (1 << bit)) for i in range(lax.axis_size("dp"))])


def shards(inputs, cotangent, routes, prefixes, gain_one, shift_one, qkv_weight, out_weight, gain_two, shift_two,
           up_weight, down_weight, expert_up, expert_down, router_weight, mix_weight):
    rows, d = inputs.shape
    tensor = lax.axis_size("tensor")
    dp = lax.axis_size("dp")
    bits = dp.bit_length() - 1
    seqs = prefixes.shape[0]
    members = tensor // seqs
    experts = expert_up.shape[0]
    heads = qkv_weight.shape[2]
    pairs = heads // LANES
    t = lax.axis_index("tensor")
    s, j = t // members, t % members
    me = lax.axis_index("dp").astype(jnp.int32)
    me1, j1, t1 = me.reshape(1), j.astype(jnp.int32).reshape(1), t.astype(jnp.int32).reshape(1)
    place = lambda a, b: (a % seqs) * members + b % members
    everyone = [(a, b) for a in range(seqs) for b in range(members)]

    def from_member(v, k):
        return lax.ppermute(v, "tensor", [(place(a, b), place(a, b - k)) for a, b in everyone])

    def from_sequence(v, k):
        return lax.ppermute(v, "tensor", [(place(a, b), place(a - k, b)) for a, b in everyone])

    def to_member(v, k):
        return from_member(v, -k)

    def to_sequence(v, k):
        return from_sequence(v, -k)

    route_blocks = routes.reshape(tensor, rows)
    bounds = jnp.stack([jnp.sum((route_blocks < e).astype(jnp.int32), axis=1) for e in range(experts + 1)], axis=1)
    key_col = lax.dynamic_slice_in_dim(routes, t * rows, rows, 0) * rows + jnp.arange(rows, dtype=jnp.int32)[:, None]
    key_row = key_col.reshape(1, rows)
    pos_row = jnp.sum((key_col < key_row).astype(jnp.int32), axis=0, keepdims=True)
    pos_col = jnp.sum((key_row < key_col).astype(jnp.int32), axis=1, keepdims=True)
    chunk = [(dj, ds) for dj in range(members) for ds in range(seqs)]
    blocks = jnp.stack([((s + ds) % seqs) * members + (j + dj) % members for dj, ds in chunk]).astype(jnp.int32)
    near = [q for q, (dj, ds) in enumerate(chunk) if ds == 0]
    far = [q for q, (dj, ds) in enumerate(chunk) if ds > 0]

    xs = [inputs] + [from_member(inputs, k) for k in range(1, members)]
    flip = me & 1
    relay = pairs % 2 == 0 and dp > 1
    w_own = jnp.transpose(qkv_weight, (1, 0, 2))
    fetched = []
    for ds in range(1, seqs):
        if relay:
            half = lax.dynamic_slice_in_dim(qkv_weight, flip * (heads // 2), heads // 2, 2)
            fetched.append([from_sequence(jnp.transpose(half[:, a:b], (1, 0, 2)), ds) for a, b in ((0, 2), (2, 3))])
        else:
            fetched.append([from_sequence(w_own, ds)])
    wo_all = [out_weight] + [from_sequence(out_weight, ds) for ds in range(1, seqs)]
    gain_one, shift_one, gain_two, shift_two = [v.reshape(1, d) for v in (gain_one, shift_one, gain_two, shift_two)]
    prefix = lax.dynamic_slice_in_dim(prefixes, s, 1)
    n1, dys = first_norm(j1, xs, gain_one, shift_one, cotangent, pos_row)
    columns = jnp.arange(pairs, dtype=jnp.int32)
    pieces = [[] for _ in fetched]
    fence = (n1,)
    if relay:
        for k, got in enumerate(fetched):
            held = hold(got[0], (n1,))
            pieces[k] = [[held], [over_dp(held, 0)]]
            fence += (held,)
    saved = [attn_forward(prefix, columns, n1, [w_own], heads, deps=fence[1:])]
    if relay:
        for k, got in enumerate(fetched):
            held = hold(got[1], (saved[0][4],))
            pieces[k][0].append(held)
            pieces[k][1].append(over_dp(held, 0))
    else:
        pieces = [[got] for got in fetched]
    w_all = [w_own]
    for halves in pieces:
        part = ()
        for k, ws in enumerate(halves):
            at = (columns + (flip ^ k) * (pairs // 2))[:pairs // 2] if relay else columns
            part = attn_forward(prefix, at, n1, ws, heads, part, deps=() if part else (saved[-1][4],))
        saved.append(part)
        whole = [jnp.concatenate(ws, axis=0) for ws in halves]
        if relay:
            whole = [jnp.where(flip == 0, jnp.concatenate(whole, axis=2), jnp.concatenate(whole[::-1], axis=2))]
        w_all.append(whole[0])
    contexts = [v[3] for v in saved]

    def spread(mine):
        out = list(mine)
        for k in range(1, members):
            out += [from_member(m, k) for m in mine]
        return out

    dy_mine = [dys] + [from_sequence(dys, ds) for ds in range(1, seqs)]
    dy_near = [dys] + [from_member(dys, k) for k in range(1, members)]
    sent = project(contexts, wo_all, members)
    came = lax.all_to_all(sent, "tensor", 0, 0, axis_index_groups=[[place(a, b) for b in range(members)] for a in range(seqs)], tiled=True)
    middle, n2 = second_norm(came, inputs, gain_two, shift_two, pos_row)
    n2_mine = [n2] + [from_sequence(n2, ds) for ds in range(1, seqs)]
    n2_near = [n2] + [from_member(n2, k) for k in range(1, members)]

    rm = jnp.concatenate([router_weight, mix_weight, jnp.zeros((d, LANES - experts - 2), BF)], axis=1)
    straight = tuple(range(bits))
    pick = lambda v, which: [v[q] for q in which]
    out_a, rg_a, sums = ffn_dense(me1, n2_near, dy_near, rm, up_weight, down_weight, experts, straight, deps=tuple(dy_mine[1:]))
    n2_all, dy_all = [], []
    n2_far, dy_far = [[hold(v, (out_a[0],)) for v in mine[1:]] for mine in (n2_mine, dy_mine)]
    for k in range(members):
        n2_all += [n2_near[k]] + [from_member(v, k) if k else v for v in n2_far]
        dy_all += [dy_near[k]] + [from_member(v, k) if k else v for v in dy_far]
    base = [[None] * tensor, [None] * tensor]
    for k, q in enumerate(near):
        base[0][q], base[1][q] = out_a[k], rg_a[k]
    apart = min(2, experts)
    whole = []
    for a, b in ((0, 1), (1, experts)):
        if a < b:
            out_e, rg_e, entire, keep_e, send_e = ffn_experts(me1, blocks, bounds, n2_all, dy_all, rm, expert_up, expert_down, a, b - a, 1, base, straight)
            base = (out_e, rg_e)
            whole += list(entire)
    out_e, rg_e = list(out_e), list(rg_e)
    out_b, rg_b, ends = ffn_dense(me1, pick(n2_all, far), pick(dy_all, far), rm, up_weight, down_weight, experts, straight,
                                  (pick(out_e, far), pick(rg_e, far)), sums)
    for k, q in enumerate(far):
        out_e[q], rg_e[q] = out_b[k], rg_b[k]

    index = {c: q for q, c in enumerate(chunk)}
    def to_owner(parts):
        mine = [[parts[index[0, ds]]] + [to_member(parts[index[k, ds]], k) for k in range(1, members)] for ds in range(seqs)]
        return mine[0], mine[1:]

    def onward(terms, deps):
        sums = [add_parts(v, deps) for v in terms]
        return [to_sequence(v, ds + 1) for ds, v in enumerate(sums)], sums

    class Halving:
        def __init__(self, keep, send, order):
            self.keep, self.send, self.order, self.at = keep, send, order, 0

        def launch(self, deps=()):
            if deps:
                self.send = hold(self.send, deps)
            self.came = over_dp(self.send, self.order[self.at])
            self.at += 1

        def add(self, mark):
            self.keep, self.send = split_add(self.keep, self.came, mark)
            self.launch()
            return (self.send,)

        def rest(self, mark):
            while self.at < bits:
                mark = self.add(mark)
            return mark

    scattered = []
    for v in whole:
        flat = v.reshape(-1, v.shape[-1])
        flat = lax.psum_scatter(flat, "dp", scatter_dimension=0, tiled=True)
        scattered.append(flat.reshape((1,) + v.shape[1:]))

    sums_e = [Halving(keep_e[e], send_e[e], straight) for e in range(len(keep_e))]
    dense_sum = Halving(ends[0], ends[1], straight)
    rg_near, rg_far = to_owner(rg_e)
    for v in sums_e + [dense_sum]:
        v.launch()
    came_far, terms = onward(rg_far, ())
    mark = tuple(terms[:1])
    mg, mc, sums_two = middle_backward(bounds, t1, rg_near + came_far, n2, rm, middle, cotangent, gain_two, pos_col, mark)
    mcs = [mc] + [from_member(mc, k) for k in range(1, members)]
    mark = (mc,)
    for v in sums_e[:1]:
        mark = v.add(mark)
    ngs = None
    grads = [None] * seqs
    for ds in list(range(1, seqs)) + [0]:
        ngs, grads[ds] = attn_backward(prefix, me1, j1, mcs, n1, wo_all[ds], w_all[ds], saved[ds], ngs, bits, mark)
        mark = (grads[ds],)
        if ds == 1 or seqs == 1:
            for v in sums_e[1:]:
                mark = v.add(mark)
            for v in sums_e[:1]:
                mark = v.add(mark)
    moved = [to_sequence(grads[ds], ds) for ds in range(1, seqs)]
    ng_parts = [ngs[0]] + [to_member(ngs[k], k) for k in range(1, members)]
    mark = dense_sum.add(mark)
    input_grad, sums_one = input_backward(ng_parts, inputs, mg, gain_one, mark)
    mark = (sums_one,)
    sums = Everywhere(jnp.concatenate([sums_two, sums_one], axis=0))
    stacks = None

    def finish(e, mark):
        if e < apart:
            terms = [scattered[e]]
        else:
            mark = sums_e[e - apart].rest(mark)
            terms = [sums_e[e - apart].keep, sums_e[e - apart].came]
        done = last_add(terms, (False, True), (experts, e), stacks, mark)
        return done, (done[1],)

    for v in sums_e[1:]:
        mark = v.add(mark)
    stacks, mark = finish(0, mark)
    if experts > apart:
        stacks, mark = finish(apart, mark)
    mark = sums.add(mark)
    keep = grads[0]
    for v in moved[:-1]:
        keep = (keep.astype(F32) + v.astype(F32)).astype(BF)
    if moved:
        keep, send = split_add(keep, moved[-1], mark)
        mark = (send,)
    else:
        keep, send = keep[:dp // 2], keep[dp // 2:]
    attn_sum = Halving(keep, send, straight)
    attn_sum.launch()
    mark = dense_sum.add(mark)
    out_near, out_far = to_owner([hold(v, mark) for v in out_e])
    out_came, terms = onward(out_far, mark)
    mark = tuple(terms[:1]) or mark
    mark = sums.add(mark)
    for e in range(apart + 1, experts):
        stacks, mark = finish(e, mark)
    mark = sums.add(mark)
    mark = attn_sum.add(mark)
    mark = sums.add(mark)
    mark = dense_sum.rest(mark)
    up_out, down_out = last_add([dense_sum.keep, dense_sum.came], (False, True), deps=mark)
    layer_output = layer_out(out_near + out_came, middle, pos_col, (up_out,))
    mark = attn_sum.add((layer_output,))
    for e in range(1, apart):
        stacks, mark = finish(e, mark)
    expert_up_out, expert_down_out = stacks
    while sums.came is not None:
        mark = sums.add(mark)
    mark = attn_sum.rest(mark)
    *qkv_parts, out_out = last_add([attn_sum.keep, attn_sum.came], (False, False, False, True), deps=mark)
    lanes = d // (dp * tensor)
    begin = (me * tensor + t) * lanes
    small = lax.dynamic_slice_in_dim(sums.v, begin, lanes, 1)
    return (layer_output, input_grad, small[16], small[17], jnp.stack(qkv_parts, axis=1), out_out, small[8], small[9], up_out, down_out,
            expert_up_out, expert_down_out, small[0:experts].T, small[experts:experts + 2].T)


def solution(mesh):
    both = ("dp", "tensor")
    in_specs = (P(both, None), P(both, None), P("dp", None), P("dp"), P(), P(), P(None, None, "tensor"), P("tensor", None), P(), P(),
                P(None, "tensor"), P("tensor", None), P(None, None, "tensor"), P(None, "tensor", None), P(), P())
    out_specs = (P(both, None), P(both, None), P(both), P(both), P("dp", None, "tensor"), P("tensor", "dp"), P(both), P(both),
                 P("dp", "tensor"), P("tensor", "dp"), P(None, "dp", "tensor"), P(None, "tensor", "dp"), P(both, None), P(both, None))
    return jax.shard_map(shards, mesh=mesh, in_specs=in_specs, out_specs=out_specs, check_vma=False)
```

```python
from functools import partial
import jax, jax.numpy as jnp
from jax import lax
from jax.experimental import pallas as pl
from jax.experimental.pallas import tpu as pltpu
from jax.sharding import PartitionSpec as P

BF = jnp.bfloat16
F32 = jnp.float32
TILE_DENSE = 512
TILE_EXPERT = 304
PIECE = 16
SMALL = pl.CostEstimate(flops=0, bytes_accessed=0, transcendentals=0)
VMEM = 60 * 1024 * 1024
ANY = pl.BlockSpec(memory_space=pltpu.HBM)
SMEM = pl.BlockSpec(memory_space=pltpu.SMEM)


def dot(a, b, ca, cb):
    return lax.dot_general(a, b, (((ca,), (cb,)), ((), ())), preferred_element_type=F32)


def slot_of(value, order):
    out = jnp.int32(0)
    for k, bit in enumerate(order):
        out = out | (((value >> bit) & 1) << (len(order) - 1 - k))
    return out


def skip(kernel, scalars, deps):
    return lambda *refs: kernel(*refs[:scalars], *refs[scalars + deps:])


def lane_softmax(logits, first, last):
    lane = lax.broadcasted_iota(jnp.int32, logits.shape, 1)
    inside = (lane >= first) & (lane < last)
    masked = jnp.where(inside, logits, -1e30)
    top = jnp.max(masked, axis=1, keepdims=True)
    e = jnp.where(inside, jnp.exp(masked - top), 0.0)
    return e / jnp.sum(e, axis=1, keepdims=True)


def pick_lane(v, index):
    lane = lax.broadcasted_iota(jnp.int32, v.shape, 1)
    return jnp.sum(jnp.where(lane == index, v, 0.0), axis=1, keepdims=True)


def gelu_parts(pre):
    phi = 0.5 * (1.0 + lax.erf(pre * 0.7071067811865476))
    pdf = jnp.exp(pre * pre * -0.5) * 0.3989422804014327
    return pre * phi, phi + pre * pdf


def ffn_tile(lanes, rm, xt, dyt, coef_of, up_w, dn_w, UA, DA, ready):
    logits = dot(xt, rm[...], 1, 0)
    mixing = lane_softmax(logits, lanes, lanes + 2)
    coef = coef_of(logits, mixing)
    pre = dot(xt, up_w[...], 1, 0)
    g = dot(dyt, dn_w[...], 1, 1)
    hid, dg = gelu_parts(pre)
    hid = hid.astype(BF)
    dots = jnp.sum(hid.astype(F32) * g, axis=1, keepdims=True)
    pg = (g * dg * coef).astype(BF)
    cot = (dyt.astype(F32) * coef).astype(BF)
    out = dot(hid, dn_w[...], 1, 0) * coef
    rg = dot(pg, up_w[...], 1, 1)
    ready()
    UA[...] += dot(xt, pg, 0, 0)
    DA[...] += dot(cot, hid, 0, 0)
    return dots, out, rg


def stage_grads(ST, UA, DA, me, order, whole):
    bits = len(order)
    blk = UA.shape[0] >> bits

    def body(c, _):
        r = pl.ds(pl.multiple_of(c * blk, blk), blk)
        slot = jnp.where(whole, c, slot_of(c ^ me, order))
        ST[slot, 0] = UA[r, :].astype(BF)
        ST[slot, 1] = DA[r, :].astype(BF)
        return 0
    lax.fori_loop(0, 1 << bits, body, 0)


def dots_rows(dots):
    return jnp.broadcast_to(dots, (dots.shape[0], 128)).T[0:PIECE, :]


def dense_kernel(cfg, me_ref, *refs):
    chunks, rows, tm, lanes, order, first, deps = cfg
    it = iter(refs[deps:])
    take = lambda k: [next(it) for _ in range(k)]
    x_hbm, dy_hbm = take(chunks), take(chunks)
    rm, up_hbm, dn_hbm = take(3)
    base_o, base_r, sums_in = ([], [], []) if first else (take(chunks), take(chunks), take(2))
    out_refs, rg_refs = take(chunks), take(chunks)
    ends = take(2)
    X, DY, UP, DN, UA, DA, OB, RB, DT, OD, xsem, wsem, gsem, osem, dsem = take(15)
    ST, BO, BR, BD, bsem = (None,) * 5 if first else take(5)
    per = rows // tm
    weights = [pltpu.make_async_copy(up_hbm, UP, wsem.at[0]), pltpu.make_async_copy(dn_hbm, DN, wsem.at[1])]
    loads, bases = [], []
    for q in range(chunks):
        sl = pl.ds(q * rows, rows)
        loads.append([pltpu.make_async_copy(x_hbm[q], X.at[sl], xsem.at[q]), pltpu.make_async_copy(dy_hbm[q], DY.at[sl], xsem.at[chunks + q])])
        if not first:
            bases.append([pltpu.make_async_copy(base_o[q], BO.at[sl], bsem.at[q]), pltpu.make_async_copy(base_r[q].at[pl.ds(0, rows)], BR.at[sl], bsem.at[chunks + q]),
                          pltpu.make_async_copy(base_r[q].at[pl.ds(rows, PIECE)], BD.at[q], bsem.at[2 * chunks + q])])
    sums = [] if first else [pltpu.make_async_copy(sums_in[0], UA, gsem.at[0]), pltpu.make_async_copy(sums_in[1], DA, gsem.at[1])]
    for c in loads[0] + weights + sums + [c for q in loads[1:] for c in q] + [c for q in bases for c in q]:
        c.start()
    DT[...] = jnp.zeros_like(DT)
    if first:
        UA[...] = jnp.zeros_like(UA)
        DA[...] = jnp.zeros_like(DA)
    for c in weights:
        c.wait()

    def outs(q, part, slot):
        sl = pl.ds(part * tm, tm)
        return [pltpu.make_async_copy(OB.at[slot], out_refs[q].at[sl], osem.at[0, slot]),
                pltpu.make_async_copy(RB.at[slot], rg_refs[q].at[sl], osem.at[1, slot])]

    def one(i, _):
        slot = i % 2
        sl = pl.ds(pl.multiple_of(i * tm, tm), tm)
        for q in range(chunks):
            @pl.when(i == q * per)
            def _(q=q):
                for c in loads[q]:
                    c.wait()

        def ready():
            if not first:
                @pl.when(i == 0)
                def _():
                    for c in sums:
                        c.wait()
        dots, out, rg = ffn_tile(lanes, rm, X[sl, :], DY[sl, :], lambda l, m: pick_lane(m, lanes), UP, DN, UA, DA, ready)
        lines = dots_rows(dots)
        line = lax.broadcasted_iota(jnp.int32, lines.shape, 0)
        for q in range(chunks):
            for part in range(per):
                @pl.when(i == q * per + part)
                def _(q=q, part=part):
                    DT[q, :, part * tm:(part + 1) * tm] = jnp.where(line == 0, lines, 0.0)
        if not first:
            for q in range(chunks):
                @pl.when(i == q * per)
                def _(q=q):
                    for c in bases[q]:
                        c.wait()
            out = out + BO[sl, :].astype(F32)
            rg = rg + BR[sl, :].astype(F32)

        @pl.when(i >= 2)
        def _():
            for c in outs(0, 0, slot):
                c.wait()
        OB[slot] = out.astype(BF)
        RB[slot] = rg.astype(BF)
        for q in range(chunks):
            for part in range(per):
                @pl.when(i == q * per + part)
                def _(q=q, part=part):
                    for c in outs(q, part, slot):
                        c.start()
        return 0
    lax.fori_loop(0, chunks * per, one, 0)
    lines = []
    for q in range(chunks):
        total = DT[q] if first else DT[q] + BD[q].astype(F32)
        OD[q] = total.astype(BF)
        lines.append(pltpu.make_async_copy(OD.at[q], rg_refs[q].at[pl.ds(rows, PIECE)], dsem.at[q]))
    if first:
        last = lines + [pltpu.make_async_copy(UA, ends[0], gsem.at[0]), pltpu.make_async_copy(DA, ends[1], gsem.at[1])]
    else:
        stage_grads(ST, UA, DA, me_ref[0], order, False)
        half = ST.shape[0] // 2
        last = lines + [pltpu.make_async_copy(ST.at[pl.ds(h * half, half)], ends[h], gsem.at[h]) for h in range(2)]
    for c in last:
        c.start()
    for slot in range(min(2, chunks * per)):
        for c in outs(0, 0, slot):
            c.wait()
    for c in last:
        c.wait()


def ffn_dense(me, xs, dys, rm, up, down, lanes, order, base=None, sums=None, deps=()):
    chunks = len(xs)
    rows, d = xs[0].shape
    f = up.shape[1]
    n = chunks * rows
    tm = min(TILE_DENSE, rows)
    first = base is None
    bits = len(order)
    half = 1 << (bits - 1)
    vm = pl.BlockSpec(memory_space=pltpu.VMEM)
    part, lined = jax.ShapeDtypeStruct((rows, d), BF), jax.ShapeDtypeStruct((rows + PIECE, d), BF)
    total = jax.ShapeDtypeStruct((d, f), F32)
    grad = jax.ShapeDtypeStruct((half, 2, d >> bits, f), BF)
    ends = [total] * 2 if first else [grad] * 2
    more = [] if first else list(base[0]) + list(base[1]) + list(sums)
    scratch = [pltpu.VMEM((n, d), BF), pltpu.VMEM((n, d), BF), pltpu.VMEM((d, f), BF), pltpu.VMEM((f, d), BF), pltpu.VMEM((d, f), F32), pltpu.VMEM((d, f), F32),
               pltpu.VMEM((2, tm, d), BF), pltpu.VMEM((2, tm, d), BF), pltpu.VMEM((chunks, PIECE, d), F32), pltpu.VMEM((chunks, PIECE, d), BF),
               pltpu.SemaphoreType.DMA((2 * chunks,)), pltpu.SemaphoreType.DMA((2,)), pltpu.SemaphoreType.DMA((2,)), pltpu.SemaphoreType.DMA((2, 2)), pltpu.SemaphoreType.DMA((chunks,))]
    if not first:
        scratch += [pltpu.VMEM((2 * half, 2, d >> bits, f), BF), pltpu.VMEM((n, d), BF), pltpu.VMEM((n, d), BF), pltpu.VMEM((chunks, PIECE, d), BF), pltpu.SemaphoreType.DMA((3 * chunks,))]
    res = pl.pallas_call(
        partial(dense_kernel, (chunks, rows, tm, lanes, order, first, len(deps))),
        name="ffn_dense",
        out_shape=[part] * chunks + [lined] * chunks + ends,
        in_specs=[SMEM] + [ANY] * (len(deps) + 2 * chunks) + [vm] + [ANY] * (2 + len(more)),
        out_specs=[ANY] * (2 * chunks + len(ends)),
        scratch_shapes=scratch,
        cost_estimate=SMALL,
        compiler_params=pltpu.CompilerParams(vmem_limit_bytes=VMEM),
    )(me, *deps, *xs, *dys, rm, up, down, *more)
    return res[:chunks], res[chunks:2 * chunks], res[2 * chunks:]


def expert_kernel(cfg, me_ref, blk_ref, bnd_ref, *refs):
    first, count, whole, chunks, rows, d, tm, lanes, order, has, deps = cfg
    n = chunks * rows
    it = iter(refs[deps:])
    take = lambda k: [next(it) for _ in range(k)]
    x_hbm, dy_hbm = take(chunks), take(chunks)
    rm, up_hbm, dn_hbm = take(3)
    based = [q for q in range(chunks) if has[q]]
    base_o, base_r = take(len(based)), take(len(based))
    out_refs, rg_refs = take(chunks), take(chunks)
    whole_refs, keep_refs, send_refs = take(whole), take(count - whole), take(count - whole)
    X, DY, UP, DN, UA, DA, ST, XG, DG, VAL, OA, RA, DOT, BD, TR, TL, TH, xsem, wsem, gsem, osem, dsem = it
    half = ST.shape[0] // 2
    pieces = tm // PIECE
    rows_of = [pl.ds(q * rows, rows) for q in range(chunks)]
    copies = []
    for q in range(chunks):
        copies.append(pltpu.make_async_copy(x_hbm[q], X.at[rows_of[q]], xsem.at[q]))
        copies.append(pltpu.make_async_copy(dy_hbm[q], DY.at[rows_of[q]], xsem.at[chunks + q]))
    earlier = []
    for k, q in enumerate(based):
        earlier.append(pltpu.make_async_copy(base_o[k], X.at[rows_of[q]], xsem.at[q]))
        earlier.append(pltpu.make_async_copy(base_r[k].at[pl.ds(0, rows)], DY.at[rows_of[q]], xsem.at[chunks + q]))
        earlier.append(pltpu.make_async_copy(base_r[k].at[pl.ds(rows, PIECE)], BD.at[q], dsem.at[q]))

    def weights(e, slot):
        return [pltpu.make_async_copy(up_hbm.at[first + e], UP.at[slot], wsem.at[slot, 0]),
                pltpu.make_async_copy(dn_hbm.at[first + e], DN.at[slot], wsem.at[slot, 1])]

    def flush(g):
        if g < whole:
            return [pltpu.make_async_copy(ST, whole_refs[g], gsem.at[0])]
        g = g - whole
        return [pltpu.make_async_copy(ST.at[pl.ds(0, half)], keep_refs[g], gsem.at[0]),
                pltpu.make_async_copy(ST.at[pl.ds(half, half)], send_refs[g], gsem.at[1])]

    for c in copies + weights(0, 0):
        c.start()
    OA[...] = jnp.zeros_like(OA)
    RA[...] = jnp.zeros_like(RA)
    DOT[...] = jnp.zeros_like(DOT)
    iota16 = lax.broadcasted_iota(jnp.int32, (PIECE, 128), 0)

    def one_expert(e, _):
        slot = e % 2
        total = jnp.int32(0)
        for q in range(chunks):
            lo, hi = bnd_ref[blk_ref[q], first + e], bnd_ref[blk_ref[q], first + e + 1]
            p0 = lo // PIECE
            p1 = jnp.where(hi > lo, (hi + PIECE - 1) // PIECE, p0)

            def add(p, _, lo=lo, hi=hi, p0=p0, total=total, q=q):
                k = total + p - p0
                TR[k] = q * rows + p * PIECE
                TL[k] = lo - p * PIECE
                TH[k] = hi - p * PIECE
                return 0
            lax.fori_loop(p0, p1, add, 0)
            total = total + p1 - p0
        tiles = (total + pieces - 1) // pieces

        def pad(k, _):
            TR[k] = 0
            TL[k] = 0
            TH[k] = 0
            return 0
        lax.fori_loop(total, tiles * pieces, pad, 0)
        UA[...] = jnp.zeros_like(UA)
        DA[...] = jnp.zeros_like(DA)

        @pl.when(e == 0)
        def _():
            for c in copies:
                c.wait()
        for c in weights(e, slot):
            c.wait()

        @pl.when(e + 1 < count)
        def _():
            for c in weights(e + 1, 1 - slot):
                c.start()

        def one_tile(i, _):
            base = i * pieces
            for p in range(pieces):
                r = pl.ds(pl.multiple_of(TR[base + p], PIECE), PIECE)
                XG[pl.ds(p * PIECE, PIECE), :] = X[r, :]
                DG[pl.ds(p * PIECE, PIECE), :] = DY[r, :]
                ok = (iota16 >= TL[base + p]) & (iota16 < TH[base + p])
                VAL[pl.ds(p * PIECE, PIECE), :] = jnp.where(ok, 1.0, 0.0)
            valid = VAL[:, 0:1]

            def coef_of(logits, mixing):
                return pick_lane(mixing, lanes + 1) * pick_lane(lane_softmax(logits, 0, lanes), first + e) * valid
            dots, out, rg = ffn_tile(lanes, rm, XG[...], DG[...], coef_of, UP.at[slot], DN.at[slot], UA, DA, lambda: None)
            dots = jnp.broadcast_to(dots * valid, (tm, 128))
            for p in range(pieces):
                r = pl.ds(pl.multiple_of(TR[base + p], PIECE), PIECE)
                s = slice(p * PIECE, (p + 1) * PIECE)
                OA[r, :] += out[s]
                RA[r, :] += rg[s]
                DOT[r, :] += dots[s]
            return 0
        lax.fori_loop(0, tiles, one_tile, 0)

        @pl.when(e == count - 1)
        def _():
            for c in earlier:
                c.start()

        for g in range(count - 1):
            @pl.when(e == g + 1)
            def _(g=g):
                for c in flush(g):
                    c.wait()
        stage_grads(ST, UA, DA, me_ref[0], order, e < whole)
        for g in range(count):
            @pl.when(e == g)
            def _(g=g):
                for c in flush(g):
                    c.start()
        return 0
    lax.fori_loop(0, count, one_expert, 0)
    for c in earlier:
        c.wait()
    last = []
    step = min(256, rows)
    line = lax.broadcasted_iota(jnp.int32, (PIECE, step), 0)
    for q in range(chunks):
        r = rows_of[q]
        o, g = OA[r, :], RA[r, :]
        if has[q]:
            o, g = o + X[r, :].astype(F32), g + DY[r, :].astype(F32)
        X[r, :] = o.astype(BF)
        DY[r, :] = g.astype(BF)
        if not has[q]:
            BD[q] = jnp.zeros(BD.shape[1:], BF)
        for i in range(rows // step):
            sl = slice(i * step, (i + 1) * step)
            dots = jnp.where(line == 1, DOT[pl.ds(q * rows + i * step, step), :].T[0:PIECE, :], 0.0)
            BD[q, :, sl] = (BD[q, :, sl].astype(F32) + dots).astype(BF)
        last += [pltpu.make_async_copy(X.at[r], out_refs[q], osem.at[0, q]), pltpu.make_async_copy(DY.at[r], rg_refs[q].at[pl.ds(0, rows)], osem.at[1, q]),
                 pltpu.make_async_copy(BD.at[q], rg_refs[q].at[pl.ds(rows, PIECE)], dsem.at[q])]
        for c in last[-3:]:
            c.start()
    for c in last + flush(count - 1):
        c.wait()


def ffn_experts(me, blocks, bounds, xs, dys, rm, up, down, first, count, whole, base, order, deps=()):
    chunks = len(xs)
    rows, d = xs[0].shape
    lanes, _, f = up.shape
    n = chunks * rows
    tm = TILE_EXPERT
    bits = len(order)
    half = 1 << (bits - 1)
    grad, entire = [jax.ShapeDtypeStruct((k * half, 2, d >> bits, f), BF) for k in (1, 2)]
    part, lined = jax.ShapeDtypeStruct((rows, d), BF), jax.ShapeDtypeStruct((rows + PIECE, d), BF)
    table = n // PIECE + chunks * lanes + 2 * tm // PIECE
    vm = pl.BlockSpec(memory_space=pltpu.VMEM)
    has = tuple(b is not None for b in base[0])
    more = [b for k in range(2) for b in base[k] if b is not None]
    res = pl.pallas_call(
        partial(expert_kernel, (first, count, whole, chunks, rows, d, tm, lanes, order, has, len(deps))),
        name="ffn_experts",
        out_shape=[part] * chunks + [lined] * chunks + [entire] * whole + [grad] * (2 * (count - whole)),
        in_specs=[SMEM] * 3 + [ANY] * (len(deps) + 2 * chunks) + [vm] + [ANY] * (2 + len(more)),
        out_specs=[ANY] * (2 * chunks + 2 * count - whole),
        scratch_shapes=[
            pltpu.VMEM((n, d), BF), pltpu.VMEM((n, d), BF), pltpu.VMEM((2, d, f), BF), pltpu.VMEM((2, f, d), BF),
            pltpu.VMEM((d, f), F32), pltpu.VMEM((d, f), F32), pltpu.VMEM((2 * half, 2, d >> bits, f), BF),
            pltpu.VMEM((tm, d), BF), pltpu.VMEM((tm, d), BF), pltpu.VMEM((tm, 128), F32),
            pltpu.VMEM((n, d), F32), pltpu.VMEM((n, d), F32), pltpu.VMEM((n, 128), F32), pltpu.VMEM((chunks, PIECE, d), BF),
            pltpu.SMEM((table,), jnp.int32), pltpu.SMEM((table,), jnp.int32), pltpu.SMEM((table,), jnp.int32),
            pltpu.SemaphoreType.DMA((2 * chunks,)), pltpu.SemaphoreType.DMA((2, 2)), pltpu.SemaphoreType.DMA((2,)), pltpu.SemaphoreType.DMA((2, chunks)), pltpu.SemaphoreType.DMA((chunks,)),
        ],
        cost_estimate=SMALL,
        compiler_params=pltpu.CompilerParams(vmem_limit_bytes=VMEM),
    )(me, blocks, bounds, *deps, *xs, *dys, rm, up, down, *more)
    at = 2 * chunks + whole
    return res[:chunks], res[chunks:2 * chunks], res[2 * chunks:at], res[at:at + count - whole], res[at + count - whole:]


def split_add_kernel(deps, *refs):
    ka, kb, ca, cb, keep, send = refs[deps:]
    keep[...] = (ka[...].astype(F32) + ca[...].astype(F32)).astype(BF)
    send[...] = (kb[...].astype(F32) + cb[...].astype(F32)).astype(BF)


def split_add(kept, came, deps=()):
    h, m, blk, f = kept.shape
    near = pl.BlockSpec((1, m, blk, f), lambda i: (i, 0, 0, 0))
    far = pl.BlockSpec((1, m, blk, f), lambda i: (i + h // 2, 0, 0, 0))
    out = jax.ShapeDtypeStruct((h // 2, m, blk, f), BF)
    return pl.pallas_call(
        partial(split_add_kernel, len(deps)),
        name="split_add",
        grid=(h // 2,),
        in_specs=[ANY] * len(deps) + [near, far, near, far],
        out_specs=[near, near],
        out_shape=[out, out],
        cost_estimate=SMALL,
        compiler_params=pltpu.CompilerParams(vmem_limit_bytes=VMEM),
    )(*deps, kept, kept, came, came)


def last_add_kernel(deps, turns, *refs):
    terms = refs[deps:-len(turns)]
    outs = refs[-len(turns):]
    for k, turned in enumerate(turns):
        total = terms[0][0, k].astype(F32)
        for v in terms[1:]:
            total = total + v[0, k].astype(F32)
        outs[k][...] = (total.T if turned else total).reshape(outs[k].shape)


def last_add(terms, turns, place=None, stacks=None, deps=()):
    _, m, blk, f = terms[0].shape
    shapes = [(f, blk) if turned else (blk, f) for turned in turns]
    aliases = {}
    if place is None:
        out_shape = [jax.ShapeDtypeStruct(s, F32) for s in shapes]
        out_specs = [pl.BlockSpec(s, lambda i: (0, 0)) for s in shapes]
    else:
        count, at = place
        out_shape = [jax.ShapeDtypeStruct((count,) + s, F32) for s in shapes]
        out_specs = [pl.BlockSpec((1,) + s, lambda i: (at, 0, 0)) for s in shapes]
        if stacks is not None:
            aliases = {k: k for k in range(m)}
            deps = tuple(stacks) + tuple(deps)
    full = pl.BlockSpec((1, m, blk, f), lambda i: (0, 0, 0, 0))
    return pl.pallas_call(
        partial(last_add_kernel, len(deps), turns),
        name="last_add",
        grid=(1,),
        in_specs=[ANY] * len(deps) + [full] * len(terms),
        out_specs=out_specs,
        out_shape=out_shape,
        input_output_aliases=aliases,
        cost_estimate=SMALL,
        compiler_params=pltpu.CompilerParams(vmem_limit_bytes=VMEM),
    )(*deps, *terms)


def hold(v, deps):
    return pl.pallas_call(
        lambda *refs: None,
        name="hold",
        in_specs=[ANY] * (1 + len(deps)),
        out_specs=ANY,
        out_shape=jax.ShapeDtypeStruct(v.shape, v.dtype),
        input_output_aliases={0: 0},
        cost_estimate=SMALL,
    )(v, *deps)


HD = 64
LANES = 128


def head_part(v, h):
    lane = lax.broadcasted_iota(jnp.int32, v.shape, 1)
    return jnp.where((lane // HD) == h, v, jnp.zeros((), v.dtype))


def masked_scores(st, key_first, query_first, prefix):
    key_pos = key_first + lax.broadcasted_iota(jnp.int32, st.shape, 0)
    query_pos = query_first + lax.broadcasted_iota(jnp.int32, st.shape, 1)
    seen = key_pos <= query_pos
    if prefix is not None:
        seen = seen | (key_pos < prefix)
    return jnp.where(seen, st, -1e30)


def score_block(k2, qm, half, length, prefix):
    mid = length // 2
    if half == 0:
        return masked_scores(dot(k2[0:mid], qm, 1, 1), 0, 0, prefix)
    low = dot(k2[0:mid], qm, 1, 1)
    high = masked_scores(dot(k2[mid:length], qm, 1, 1), mid, mid, None)
    return jnp.concatenate([low, high], 0)


def attn_forward_kernel(length, pieces, aliased, prefix_ref, at_ref, *refs):
    n1_ref = refs[0]
    w_refs = [(r, i) for r, n in zip(refs[1:], pieces) for i in range(n)]
    q_ref, k_ref, v_ref, ctx_ref, lse_ref = refs[1 + len(pieces) + aliased:]
    mid = length // 2
    prefix = prefix_ref[0]
    n1 = n1_ref[...]
    for out, (w, i) in zip((q_ref, k_ref, v_ref), w_refs):
        out[...] = dot(n1, w[i], 1, 0).astype(BF)
    vt = v_ref[...].T
    k2 = k_ref[...]
    for half in range(2):
        rows = pl.ds(half * mid, mid)
        q2 = q_ref[rows, :] * jnp.asarray(HD ** -0.5, BF)
        keys = mid * (half + 1)
        parts = []
        for h in range(2):
            st = score_block(k2, head_part(q2, h), half, length, prefix)
            top = jnp.max(st, axis=0, keepdims=True)
            p = jnp.exp(st - top)
            total = jnp.sum(p, axis=0, keepdims=True)
            c = dot(vt[h * HD:(h + 1) * HD, 0:keys], p.astype(BF), 1, 0)
            parts.append(c / total)
            lse_ref[0, h:h + 1, rows] = top + jnp.log(total)
        ctx_ref[rows, :] = jnp.concatenate(parts, 0).T.astype(BF)


def attn_forward(prefix, at, n1, ws, heads, earlier=(), deps=()):
    length, d = n1.shape
    pairs = ws[0].shape[2] // LANES
    col = pl.BlockSpec((length, LANES), lambda p, _, at_ref: (0, at_ref[p]))
    out = jax.ShapeDtypeStruct((length, heads), BF)
    done = len(earlier)
    skipped = len(deps)
    return pl.pallas_call(
        skip(partial(attn_forward_kernel, length, tuple(w.shape[0] for w in ws), done), 2, skipped),
        name="attn_forward",
        grid_spec=pltpu.PrefetchScalarGridSpec(
            num_scalar_prefetch=2, grid=(pairs,),
            in_specs=[ANY] * skipped + [pl.BlockSpec((length, d), lambda p, *_: (0, 0))]
            + [pl.BlockSpec((w.shape[0], d, LANES), lambda p, *_: (0, 0, p)) for w in ws] + [ANY] * done,
            out_specs=[col] * 4 + [pl.BlockSpec((1, 8, length), lambda p, _, at_ref: (at_ref[p], 0, 0))]),
        out_shape=[out] * 4 + [jax.ShapeDtypeStruct((heads // LANES, 8, length), F32)],
        input_output_aliases={3 + skipped + len(ws) + k: k for k in range(done)},
        cost_estimate=SMALL,
        compiler_params=pltpu.CompilerParams(vmem_limit_bytes=VMEM),
    )(prefix, at, *deps, n1, *ws, *earlier)


def attn_backward_kernel(length, bits, members, based, prefix_ref, me_ref, j_ref, *refs):
    it = iter(refs)
    take = lambda k: [next(it) for _ in range(k)]
    mcs = take(members)
    n1_ref, wo_ref, w_ref, q_ref, k_ref, v_ref, ctx_ref, lse_ref = take(8)
    bases = take(members) if based else []
    ng_refs = take(members)
    grad_ref, NG, MC, DC, DK, DV, DQ, sem = it
    rows_each = length // members
    where = [pl.ds(pl.multiple_of(lax.rem(j_ref[0] + k, members) * rows_each, rows_each), rows_each) for k in range(members)]
    mid = length // 2
    prefix = prefix_ref[0]
    me = me_ref[0]
    pair = pl.program_id(0)
    copies = [pltpu.make_async_copy(mcs[k], MC.at[where[k]], sem.at[k]) for k in range(members)]

    @pl.when(pair == 0)
    def _():
        for c in copies:
            c.start()
        for c in copies:
            c.wait()
    mc = MC[...]
    DC[...] = dot(mc, wo_ref[...], 1, 1).astype(BF)
    k2, v2 = k_ref[...], v_ref[...]
    kt = k2.T
    scale = jnp.asarray(HD ** -0.5, BF)
    for half in range(2):
        rows = pl.ds(half * mid, mid)
        q2 = q_ref[rows, :] * scale
        dc2 = DC[rows, :]
        keys = mid * (half + 1)
        dv = jnp.zeros((keys, LANES), F32)
        dk = jnp.zeros((keys, LANES), F32)
        dq = []
        for h in range(2):
            qm, dcm = head_part(q2, h), head_part(dc2, h)
            st = score_block(k2, qm, half, length, prefix)
            p = jnp.exp(st - lse_ref[0, h:h + 1, rows])
            dv = dv + dot(p.astype(BF), dcm, 1, 0)
            dp = dot(v2[0:keys], dcm, 1, 1)
            ds = (p * (dp - jnp.sum(p * dp, axis=0, keepdims=True))).astype(BF)
            dk = dk + dot(ds, qm, 1, 0)
            dq.append(dot(kt[h * HD:(h + 1) * HD, 0:keys], ds, 1, 0))
        DQ[rows, :] = (jnp.concatenate(dq, 0) * HD ** -0.5).T.astype(BF)
        if half == 0:
            DK[0:mid, :] = dk
            DV[0:mid, :] = dv
        else:
            DK[0:mid, :] += dk[0:mid]
            DV[0:mid, :] += dv[0:mid]
            DK[mid:length, :] = dk[mid:length]
            DV[mid:length, :] = dv[mid:length]
    dq, dk, dv = DQ[...], DK[...].astype(BF), DV[...].astype(BF)
    ng = dot(dq, w_ref[0], 1, 1) + dot(dk, w_ref[1], 1, 1) + dot(dv, w_ref[2], 1, 1)

    @pl.when(pair == 0)
    def _():
        NG[...] = ng

    @pl.when(pair > 0)
    def _():
        NG[...] += ng
    n1 = n1_ref[...]
    grads = [dot(n1, x, 0, 0) for x in (dq, dk, dv)] + [dot(mc, ctx_ref[...], 0, 0)]
    blk = n1.shape[1] >> bits
    for c in range(1 << bits):
        slot = slot_of(jnp.int32(c) ^ me, range(bits))
        for i in range(4):
            grad_ref[slot, i] = grads[i][c * blk:(c + 1) * blk].astype(BF)

    @pl.when(pair == pl.num_programs(0) - 1)
    def _():
        for k in range(members):
            done = NG[where[k], :]
            if based:
                done = done + bases[k][...].astype(F32)
            ng_refs[k][...] = done.astype(BF)


def attn_backward(prefix, me, j, mcs, n1, wo, w, saved, base, bits, deps=()):
    q, k, v, ctx, lse = saved
    length, d = n1.shape
    heads = w.shape[2]
    pairs = heads // LANES
    blk = d >> bits
    members = len(mcs)
    col = pl.BlockSpec((length, LANES), lambda p, *_: (0, p))
    full = pl.BlockSpec((length, d), lambda p, *_: (0, 0))
    part = pl.BlockSpec((length // members, d), lambda p, *_: (0, 0))
    extra = [] if base is None else list(base)
    res = pl.pallas_call(
        skip(partial(attn_backward_kernel, length, bits, members, base is not None), 3, len(deps)),
        name="attn_backward",
        grid_spec=pltpu.PrefetchScalarGridSpec(
            num_scalar_prefetch=3, grid=(pairs,),
            in_specs=[ANY] * (len(deps) + members) + [full, pl.BlockSpec((LANES, d), lambda p, *_: (p, 0)), pl.BlockSpec((3, d, LANES), lambda p, *_: (0, 0, p)),
                      col, col, col, col, pl.BlockSpec((1, 8, length), lambda p, *_: (p, 0, 0))] + [part] * len(extra),
            out_specs=[part] * members + [pl.BlockSpec((1 << bits, 4, blk, LANES), lambda p, *_: (0, 0, 0, p))],
            scratch_shapes=[pltpu.VMEM((length, d), F32), pltpu.VMEM((length, d), BF), pltpu.VMEM((length, LANES), BF),
                            pltpu.VMEM((length, LANES), F32), pltpu.VMEM((length, LANES), F32), pltpu.VMEM((length, LANES), BF),
                            pltpu.SemaphoreType.DMA((members,))]),
        out_shape=[jax.ShapeDtypeStruct((length // members, d), BF)] * members + [jax.ShapeDtypeStruct((1 << bits, 4, blk, heads), BF)],
        cost_estimate=SMALL,
        compiler_params=pltpu.CompilerParams(vmem_limit_bytes=VMEM),
    )(prefix, me, j, *deps, *mcs, n1, wo, w, q, k, v, ctx, lse, *extra)
    return res[:members], res[members]


EPS = 1e-5


def normalise(v):
    centered = v - jnp.mean(v, axis=1, keepdims=True)
    r = lax.rsqrt(jnp.mean(centered * centered, axis=1, keepdims=True) + EPS)
    return centered * r, r


def norm_backward(xhat, r, grad, gain):
    scaled = grad * gain
    return r * (scaled - jnp.mean(scaled, axis=1, keepdims=True) - xhat * jnp.mean(scaled * xhat, axis=1, keepdims=True))


def order_rows(pos, rows_to_slots):
    n = pos.shape[1] if rows_to_slots else pos.shape[0]
    slot = lax.broadcasted_iota(jnp.int32, (n, n), 0 if rows_to_slots else 1)
    return jnp.where(slot == pos, 1.0, 0.0).astype(BF)


def first_norm_kernel(members, j_ref, *refs):
    xs, (gain, shift, dy, pos, out, sorted_dy) = refs[:members], refs[members:]
    for k in range(members):
        @pl.when(pl.program_id(0) == k)
        def _(k=k):
            xhat, _ = normalise(xs[k][...].astype(F32))
            out[...] = (xhat * gain[...] + shift[...]).astype(BF)
            if k == 0:
                sorted_dy[...] = dot(order_rows(pos[...], True), dy[...], 1, 0).astype(BF)


def first_norm(j, xs, gain, shift, dy, pos):
    members = len(xs)
    rows, d = xs[0].shape
    fixed = lambda shape: pl.BlockSpec(shape, lambda p, *_: (0, 0))
    return pl.pallas_call(
        partial(first_norm_kernel, members),
        name="first_norm",
        grid_spec=pltpu.PrefetchScalarGridSpec(
            num_scalar_prefetch=1, grid=(members,),
            in_specs=[fixed((rows, d))] * members + [fixed((1, d))] * 2 + [fixed((rows, d)), fixed((1, rows))],
            out_specs=[pl.BlockSpec((rows, d), lambda p, j_ref: (lax.rem(j_ref[0] + p, members), 0)), fixed((rows, d))]),
        out_shape=[jax.ShapeDtypeStruct((members * rows, d), BF), jax.ShapeDtypeStruct((rows, d), BF)],
        cost_estimate=SMALL,
        compiler_params=pltpu.CompilerParams(vmem_limit_bytes=VMEM),
    )(j, *xs, gain, shift, dy, pos)


def project_kernel(parts, *refs):
    total = dot(refs[0][...], refs[parts][...], 1, 0)
    for i in range(1, parts):
        total = total + dot(refs[i][...], refs[parts + i][...], 1, 0)
    refs[-1][0] = total.astype(BF)


def project(contexts, weights, members):
    parts = len(contexts)
    length, heads = contexts[0].shape
    d = weights[0].shape[1]
    rows = length // members
    return pl.pallas_call(
        partial(project_kernel, parts),
        name="project",
        grid=(members,),
        in_specs=[pl.BlockSpec((rows, heads), lambda p: (p, 0))] * parts + [pl.BlockSpec((heads, d), lambda p: (0, 0))] * parts,
        out_specs=pl.BlockSpec((1, rows, d), lambda p: (p, 0, 0)),
        out_shape=jax.ShapeDtypeStruct((members, rows, d), BF),
        cost_estimate=SMALL,
        compiler_params=pltpu.CompilerParams(vmem_limit_bytes=VMEM),
    )(*contexts, *weights)


def second_norm_kernel(came, x, gain, shift, pos, middle, n2):
    mid = x[...].astype(F32)
    for k in range(came.shape[0]):
        mid = mid + came[k].astype(F32)
    middle[...] = mid
    xhat, _ = normalise(mid)
    normed = (xhat * gain[...] + shift[...]).astype(BF)
    n2[...] = dot(order_rows(pos[...], True), normed, 1, 0).astype(BF)


def second_norm(came, x, gain, shift, pos):
    rows, d = x.shape
    fixed = lambda shape: pl.BlockSpec(shape, lambda p: (0,) * len(shape))
    return pl.pallas_call(
        second_norm_kernel,
        name="second_norm",
        grid=(1,),
        in_specs=[fixed(came.shape), fixed((rows, d)), fixed((1, d)), fixed((1, d)), fixed((1, rows))],
        out_specs=[fixed((rows, d))] * 2,
        out_shape=[jax.ShapeDtypeStruct((rows, d), F32), jax.ShapeDtypeStruct((rows, d), BF)],
        cost_estimate=SMALL,
        compiler_params=pltpu.CompilerParams(vmem_limit_bytes=VMEM),
    )(came, x, gain, shift, pos)


def add_small(a, b, deps):
    def kernel(*refs):
        refs[-1][...] = refs[-3][...] + refs[-2][...]
    full = pl.BlockSpec(memory_space=pltpu.VMEM)
    return pl.pallas_call(kernel, name="add_small", in_specs=[ANY] * len(deps) + [full, full], out_specs=full,
                          out_shape=jax.ShapeDtypeStruct(a.shape, a.dtype), cost_estimate=SMALL)(*deps, a, b)


def hi_lo(v):
    hi = v.astype(BF)
    return hi, (v - hi.astype(F32)).astype(BF)


def middle_backward_kernel(single, bnd_ref, t_ref, *refs):
    it = iter(refs)
    parts = [next(it) for _ in range(single)]
    n2, rm, middle, dy, gain, pos, mg_ref, mc_ref, sums_ref = it
    t = t_ref[0]
    n2v, rmv = n2[...], rm[...]
    rows = n2v.shape[0]
    total = parts[0][0:rows, :].astype(F32)
    lines = parts[0][rows:rows + PIECE, 0:rows].astype(F32)
    for p in parts[1:]:
        total = total + p[0:rows, :].astype(F32)
        lines = lines + p[rows:rows + PIECE, 0:rows].astype(F32)
    dots = jnp.concatenate([lines, jnp.zeros((128 - PIECE, rows), F32)], axis=0).T
    experts = bnd_ref.shape[1] - 1
    logits = dot(n2v, rmv, 1, 0)
    route_prob = lane_softmax(logits, 0, experts)
    mixing = lane_softmax(logits, experts, experts + 2)
    row = lax.broadcasted_iota(jnp.int32, (rows, 1), 0)
    route = jnp.zeros((rows, 1), jnp.int32)
    for e in range(1, experts):
        route = route + (row >= bnd_ref[t, e]).astype(jnp.int32)
    gate = pick_lane(route_prob, route)
    m0, m1 = pick_lane(mixing, experts), pick_lane(mixing, experts + 1)
    dense_dot, expert_dot = dots[:, 0:1], dots[:, 1:2]
    d0, d1 = dense_dot, expert_dot * gate
    inner = m0 * d0 + m1 * d1
    lane = lax.broadcasted_iota(jnp.int32, logits.shape, 1)
    grad = expert_dot * (m1 * gate) * (jnp.where(lane == route, 1.0, 0.0) - route_prob)
    grad = jnp.where(lane < experts, grad, 0.0)
    grad = jnp.where(lane == experts, m0 * (d0 - inner), grad)
    grad = jnp.where(lane == experts + 1, m1 * (d1 - inner), grad)
    hi, lo = hi_lo(grad)
    total = total + dot(hi, rmv, 1, 1) + dot(lo, rmv, 1, 1)
    sums_ref[0:8, :] = (dot(hi.T, n2v, 1, 0) + dot(lo.T, n2v, 1, 0))[0:8]
    g = dot(order_rows(pos[...], False), total.astype(BF), 1, 0)
    xhat, r = normalise(middle[...])
    sums_ref[8:16, :] = jnp.zeros((8, g.shape[1]), F32)
    sums_ref[8:9, :] = jnp.sum(g * xhat, axis=0, keepdims=True)
    sums_ref[9:10, :] = jnp.sum(g, axis=0, keepdims=True)
    mg = dy[...].astype(F32) + norm_backward(xhat, r, g, gain[...])
    mg_ref[...] = mg
    mc_ref[...] = mg.astype(BF)


def middle_backward(bounds, t, parts, n2, rm, middle, dy, gain, pos, deps=()):
    rows, d = n2.shape
    fixed = lambda shape: pl.BlockSpec(shape, lambda p, *_: (0, 0))
    big = fixed((rows, d))
    return pl.pallas_call(
        skip(partial(middle_backward_kernel, len(parts)), 2, len(deps)),
        name="middle_backward",
        grid_spec=pltpu.PrefetchScalarGridSpec(
            num_scalar_prefetch=2, grid=(1,),
            in_specs=[ANY] * len(deps) + [fixed((rows + PIECE, d))] * len(parts)
            + [big, fixed((d, 128)), big, big, fixed((1, d)), fixed((rows, 1))],
            out_specs=[big, big, fixed((16, d))]),
        out_shape=[jax.ShapeDtypeStruct((rows, d), F32), jax.ShapeDtypeStruct((rows, d), BF), jax.ShapeDtypeStruct((16, d), F32)],
        cost_estimate=SMALL,
        compiler_params=pltpu.CompilerParams(vmem_limit_bytes=VMEM),
    )(bounds, t, *deps, *parts, n2, rm, middle, dy, gain, pos)


def layer_out_kernel(*refs):
    parts, (middle, pos, out) = refs[:-3], refs[-3:]
    total = parts[0][...].astype(F32)
    for p in parts[1:]:
        total = total + p[...].astype(F32)
    hi, lo = hi_lo(total)
    move = order_rows(pos[...], False)
    out[...] = (middle[...] + dot(move, hi, 1, 0) + dot(move, lo, 1, 0)).astype(BF)


def layer_out(parts, middle, pos, deps=()):
    rows, d = middle.shape
    big = pl.BlockSpec((rows, d), lambda p: (0, 0))
    return pl.pallas_call(
        skip(layer_out_kernel, 0, len(deps)),
        name="layer_out",
        grid=(1,),
        in_specs=[ANY] * len(deps) + [big] * (len(parts) + 1) + [pl.BlockSpec((rows, 1), lambda p: (0, 0))],
        out_specs=big,
        out_shape=jax.ShapeDtypeStruct((rows, d), BF),
        cost_estimate=SMALL,
        compiler_params=pltpu.CompilerParams(vmem_limit_bytes=VMEM),
    )(*deps, *parts, middle, pos)


def add_parts_kernel(*refs):
    total = refs[0][...].astype(F32)
    for p in refs[1:-1]:
        total = total + p[...].astype(F32)
    refs[-1][...] = total.astype(BF)


def add_parts(parts, deps=()):
    rows, d = parts[0].shape
    tile = pl.BlockSpec((rows, d), lambda p: (p, 0))
    return pl.pallas_call(
        skip(add_parts_kernel, 0, len(deps)),
        name="add_parts",
        grid=(1,),
        in_specs=[ANY] * len(deps) + [tile] * len(parts),
        out_specs=tile,
        out_shape=jax.ShapeDtypeStruct((rows, d), BF),
        cost_estimate=SMALL,
        compiler_params=pltpu.CompilerParams(vmem_limit_bytes=VMEM),
    )(*deps, *parts)


def input_backward_kernel(count, *refs):
    parts = refs[:count]
    x, mg, gain, out, sums = refs[count:]
    g = parts[0][...].astype(F32)
    for p in parts[1:]:
        g = g + p[...].astype(F32)
    xhat, r = normalise(x[...].astype(F32))
    sums[...] = jnp.zeros_like(sums)
    sums[0:1, :] = jnp.sum(g * xhat, axis=0, keepdims=True)
    sums[1:2, :] = jnp.sum(g, axis=0, keepdims=True)
    out[...] = mg[...] + norm_backward(xhat, r, g, gain[...])


def input_backward(parts, x, mg, gain, deps=()):
    rows, d = x.shape
    fixed = lambda shape: pl.BlockSpec(shape, lambda p: (0, 0))
    big = fixed((rows, d))
    return pl.pallas_call(
        skip(partial(input_backward_kernel, len(parts)), 0, len(deps)),
        name="input_backward",
        grid=(1,),
        in_specs=[ANY] * len(deps) + [big] * (len(parts) + 2) + [fixed((1, d))],
        out_specs=[big, fixed((8, d))],
        out_shape=[jax.ShapeDtypeStruct((rows, d), F32), jax.ShapeDtypeStruct((8, d), F32)],
        cost_estimate=SMALL,
        compiler_params=pltpu.CompilerParams(vmem_limit_bytes=VMEM),
    )(*deps, *parts, x, mg, gain)


class Everywhere:
    def __init__(self, v):
        self.v = v
        self.hops = [(axis, 1 << b) for axis in ("tensor", "dp") for b in range(lax.axis_size(axis).bit_length() - 1)]
        self.launch()

    def launch(self):
        if self.hops:
            axis, bit = self.hops.pop(0)
            self.came = lax.ppermute(self.v, axis, [(i, i ^ bit) for i in range(lax.axis_size(axis))])
        else:
            self.came = None

    def add(self, mark):
        if self.came is None:
            return mark
        self.v = add_small(self.v, self.came, mark)
        self.launch()
        return (self.v,)


def over_dp(v, bit):
    return lax.ppermute(v, "dp", [(i, i ^ (1 << bit)) for i in range(lax.axis_size("dp"))])


def shards(inputs, cotangent, routes, prefixes, gain_one, shift_one, qkv_weight, out_weight, gain_two, shift_two,
           up_weight, down_weight, expert_up, expert_down, router_weight, mix_weight):
    rows, d = inputs.shape
    tensor = lax.axis_size("tensor")
    dp = lax.axis_size("dp")
    bits = dp.bit_length() - 1
    seqs = prefixes.shape[0]
    members = tensor // seqs
    experts = expert_up.shape[0]
    heads = qkv_weight.shape[2]
    pairs = heads // LANES
    t = lax.axis_index("tensor")
    s, j = t // members, t % members
    me = lax.axis_index("dp").astype(jnp.int32)
    me1, j1, t1 = me.reshape(1), j.astype(jnp.int32).reshape(1), t.astype(jnp.int32).reshape(1)
    place = lambda a, b: (a % seqs) * members + b % members
    everyone = [(a, b) for a in range(seqs) for b in range(members)]

    def from_member(v, k):
        return lax.ppermute(v, "tensor", [(place(a, b), place(a, b - k)) for a, b in everyone])

    def from_sequence(v, k):
        return lax.ppermute(v, "tensor", [(place(a, b), place(a - k, b)) for a, b in everyone])

    def to_member(v, k):
        return from_member(v, -k)

    def to_sequence(v, k):
        return from_sequence(v, -k)

    route_blocks = routes.reshape(tensor, rows)
    bounds = jnp.stack([jnp.sum((route_blocks < e).astype(jnp.int32), axis=1) for e in range(experts + 1)], axis=1)
    key_col = lax.dynamic_slice_in_dim(routes, t * rows, rows, 0) * rows + jnp.arange(rows, dtype=jnp.int32)[:, None]
    key_row = key_col.reshape(1, rows)
    pos_row = jnp.sum((key_col < key_row).astype(jnp.int32), axis=0, keepdims=True)
    pos_col = jnp.sum((key_row < key_col).astype(jnp.int32), axis=1, keepdims=True)
    chunk = [(dj, ds) for dj in range(members) for ds in range(seqs)]
    blocks = jnp.stack([((s + ds) % seqs) * members + (j + dj) % members for dj, ds in chunk]).astype(jnp.int32)
    near = [q for q, (dj, ds) in enumerate(chunk) if ds == 0]
    far = [q for q, (dj, ds) in enumerate(chunk) if ds > 0]

    xs = [inputs] + [from_member(inputs, k) for k in range(1, members)]
    flip = me & 1
    relay = pairs % 2 == 0 and dp > 1
    w_own = jnp.transpose(qkv_weight, (1, 0, 2))
    fetched = []
    for ds in range(1, seqs):
        if relay:
            half = lax.dynamic_slice_in_dim(qkv_weight, flip * (heads // 2), heads // 2, 2)
            fetched.append([from_sequence(jnp.transpose(half[:, a:b], (1, 0, 2)), ds) for a, b in ((0, 2), (2, 3))])
        else:
            fetched.append([from_sequence(w_own, ds)])
    wo_all = [out_weight] + [from_sequence(out_weight, ds) for ds in range(1, seqs)]
    gain_one, shift_one, gain_two, shift_two = [v.reshape(1, d) for v in (gain_one, shift_one, gain_two, shift_two)]
    prefix = lax.dynamic_slice_in_dim(prefixes, s, 1)
    rm = jnp.concatenate([router_weight, mix_weight, jnp.zeros((d, LANES - experts - 2), BF)], axis=1)
    n1, dys = first_norm(j1, xs, gain_one, shift_one, cotangent, pos_row)
    columns = jnp.arange(pairs, dtype=jnp.int32)
    pieces = [[] for _ in fetched]
    fence = (n1,)
    if relay:
        for k, got in enumerate(fetched):
            held = hold(got[0], (n1,))
            pieces[k] = [[held], [over_dp(held, 0)]]
            fence += (held,)
    saved = [attn_forward(prefix, columns, n1, [w_own], heads, deps=fence[1:] + (rm,))]
    if relay:
        for k, got in enumerate(fetched):
            held = hold(got[1], (saved[0][4],))
            pieces[k][0].append(held)
            pieces[k][1].append(over_dp(held, 0))
    else:
        pieces = [[got] for got in fetched]
    w_all = [w_own]
    for halves in pieces:
        part = ()
        for k, ws in enumerate(halves):
            at = (columns + (flip ^ k) * (pairs // 2))[:pairs // 2] if relay else columns
            part = attn_forward(prefix, at, n1, ws, heads, part, deps=() if part else (saved[-1][4],))
        saved.append(part)
        whole = [jnp.concatenate(ws, axis=0) for ws in halves]
        if relay:
            whole = [jnp.where(flip == 0, jnp.concatenate(whole, axis=2), jnp.concatenate(whole[::-1], axis=2))]
        w_all.append(whole[0])
    contexts = [v[3] for v in saved]

    def spread(mine):
        out = list(mine)
        for k in range(1, members):
            out += [from_member(m, k) for m in mine]
        return out

    dy_mine = [dys] + [from_sequence(dys, ds) for ds in range(1, seqs)]
    dy_near = [dys] + [from_member(dys, k) for k in range(1, members)]
    sent = project(contexts, wo_all, members)
    came = lax.all_to_all(sent, "tensor", 0, 0, axis_index_groups=[[place(a, b) for b in range(members)] for a in range(seqs)], tiled=True)
    middle, n2 = second_norm(came, inputs, gain_two, shift_two, pos_row)
    n2_mine = [n2] + [from_sequence(n2, ds) for ds in range(1, seqs)]
    n2_near = [n2] + [from_member(n2, k) for k in range(1, members)]

    straight = tuple(range(bits))
    pick = lambda v, which: [v[q] for q in which]
    out_a, rg_a, sums = ffn_dense(me1, n2_near, dy_near, rm, up_weight, down_weight, experts, straight, deps=tuple(dy_mine[1:]))
    n2_all, dy_all = [], []
    n2_far, dy_far = [[hold(v, (out_a[0],)) for v in mine[1:]] for mine in (n2_mine, dy_mine)]
    for k in range(members):
        n2_all += [n2_near[k]] + [from_member(v, k) if k else v for v in n2_far]
        dy_all += [dy_near[k]] + [from_member(v, k) if k else v for v in dy_far]
    base = [[None] * tensor, [None] * tensor]
    for k, q in enumerate(near):
        base[0][q], base[1][q] = out_a[k], rg_a[k]
    apart = min(2, experts)
    whole = []
    for a, b in ((0, 1), (1, experts)):
        if a < b:
            out_e, rg_e, entire, keep_e, send_e = ffn_experts(me1, blocks, bounds, n2_all, dy_all, rm, expert_up, expert_down, a, b - a, 1, base, straight)
            base = (out_e, rg_e)
            whole += list(entire)
    out_e, rg_e = list(out_e), list(rg_e)
    out_b, rg_b, ends = ffn_dense(me1, pick(n2_all, far), pick(dy_all, far), rm, up_weight, down_weight, experts, straight,
                                  (pick(out_e, far), pick(rg_e, far)), sums)
    for k, q in enumerate(far):
        out_e[q], rg_e[q] = out_b[k], rg_b[k]

    index = {c: q for q, c in enumerate(chunk)}
    def to_owner(parts):
        mine = [[parts[index[0, ds]]] + [to_member(parts[index[k, ds]], k) for k in range(1, members)] for ds in range(seqs)]
        return mine[0], mine[1:]

    def onward(terms, deps):
        sums = [add_parts(v, deps) for v in terms]
        return [to_sequence(v, ds + 1) for ds, v in enumerate(sums)], sums

    class Halving:
        def __init__(self, keep, send, order):
            self.keep, self.send, self.order, self.at = keep, send, order, 0

        def launch(self, deps=()):
            if deps:
                self.send = hold(self.send, deps)
            self.came = over_dp(self.send, self.order[self.at])
            self.at += 1

        def add(self, mark):
            self.keep, self.send = split_add(self.keep, self.came, mark)
            self.launch()
            return (self.send,)

        def rest(self, mark):
            while self.at < bits:
                mark = self.add(mark)
            return mark

    scattered = []
    for v in whole:
        flat = v.reshape(-1, v.shape[-1])
        flat = lax.psum_scatter(flat, "dp", scatter_dimension=0, tiled=True)
        scattered.append(flat.reshape((1,) + v.shape[1:]))

    sums_e = [Halving(keep_e[e], send_e[e], straight) for e in range(len(keep_e))]
    dense_sum = Halving(ends[0], ends[1], straight)
    rg_near, rg_far = to_owner(rg_e)
    for v in sums_e + [dense_sum]:
        v.launch()
    came_far, terms = onward(rg_far, ())
    mark = tuple(terms[:1])
    for v in sums_e[:1]:
        mark = v.add(mark)
    mg, mc, sums_two = middle_backward(bounds, t1, rg_near + came_far, n2, rm, middle, cotangent, gain_two, pos_col, mark)
    mcs = [mc] + [from_member(mc, k) for k in range(1, members)]
    mark = (mc,)
    out_near, out_far = to_owner([hold(v, mark) for v in out_e])
    ngs = None
    grads = [None] * seqs
    for ds in list(range(1, seqs)) + [0]:
        ngs, grads[ds] = attn_backward(prefix, me1, j1, mcs, n1, wo_all[ds], w_all[ds], saved[ds], ngs, bits, mark)
        mark = (grads[ds],)
        if ds == 1 or seqs == 1:
            out_came, terms = onward(out_far, mark)
            mark = tuple(terms[:1]) or mark
    moved = [to_sequence(grads[ds], ds) for ds in range(1, seqs)]
    ng_parts = [ngs[0]] + [to_member(ngs[k], k) for k in range(1, members)]
    for v in sums_e[1:2]:
        mark = v.add(mark)
    input_grad, sums_one = input_backward(ng_parts, inputs, mg, gain_one, mark)
    mark = (sums_one,)
    sums = Everywhere(jnp.concatenate([sums_two, sums_one], axis=0))
    stacks = None

    def finish(e, mark):
        if e < apart:
            terms = [scattered[e]]
        else:
            mark = sums_e[e - apart].rest(mark)
            terms = [sums_e[e - apart].keep, sums_e[e - apart].came]
        done = last_add(terms, (False, True), (experts, e), stacks, mark)
        return done, (done[1],)

    for v in sums_e[:1]:
        mark = v.add(mark)
    mark = sums.add(mark)
    keep = grads[0]
    for v in moved[:-1]:
        keep = (keep.astype(F32) + v.astype(F32)).astype(BF)
    if moved:
        keep, send = split_add(keep, moved[-1], mark)
        mark = (send,)
    else:
        keep, send = keep[:dp // 2], keep[dp // 2:]
    attn_sum = Halving(keep, send, straight)
    attn_sum.launch()
    mark = sums.add(mark)
    mark = dense_sum.add(mark)
    stacks, mark = finish(0, mark)
    for v in sums_e[2:]:
        mark = v.add(mark)
    for v in sums_e[1:]:
        mark = v.add(mark)
    mark = sums.add(mark)
    layer_output = layer_out(out_near + out_came, middle, pos_col, mark)
    mark = (layer_output,)
    if experts > apart:
        stacks, mark = finish(apart, mark)
    mark = dense_sum.add(mark)
    mark = attn_sum.add(mark)
    mark = sums.add(mark)
    for e in range(apart + 1, experts):
        stacks, mark = finish(e, mark)
    mark = dense_sum.rest(mark)
    up_out, down_out = last_add([dense_sum.keep, dense_sum.came], (False, True), deps=mark)
    mark = attn_sum.add((up_out,))
    while sums.came is not None:
        mark = sums.add(mark)
    for e in range(1, apart):
        stacks, mark = finish(e, mark)
    expert_up_out, expert_down_out = stacks
    mark = attn_sum.rest(mark)
    *qkv_parts, out_out = last_add([attn_sum.keep, attn_sum.came], (False, False, False, True), deps=mark)
    lanes = d // (dp * tensor)
    begin = (me * tensor + t) * lanes
    small = lax.dynamic_slice_in_dim(sums.v, begin, lanes, 1)
    return (layer_output, input_grad, small[16], small[17], jnp.stack(qkv_parts, axis=1), out_out, small[8], small[9], up_out, down_out,
            expert_up_out, expert_down_out, small[0:experts].T, small[experts:experts + 2].T)


def solution(mesh):
    both = ("dp", "tensor")
    in_specs = (P(both, None), P(both, None), P("dp", None), P("dp"), P(), P(), P(None, None, "tensor"), P("tensor", None), P(), P(),
                P(None, "tensor"), P("tensor", None), P(None, None, "tensor"), P(None, "tensor", None), P(), P())
    out_specs = (P(both, None), P(both, None), P(both), P(both), P("dp", None, "tensor"), P("tensor", "dp"), P(both), P(both),
                 P("dp", "tensor"), P("tensor", "dp"), P(None, "dp", "tensor"), P(None, "tensor", "dp"), P(both, None), P(both, None))
    return jax.shard_map(shards, mesh=mesh, in_specs=in_specs, out_specs=out_specs, check_vma=False)
```

```python
from functools import partial
import jax, jax.numpy as jnp
from jax import lax
from jax.experimental import pallas as pl
from jax.experimental.pallas import tpu as pltpu
from jax.sharding import PartitionSpec as P

BF = jnp.bfloat16
F32 = jnp.float32
TILE_DENSE = 512
TILE_EXPERT = 304
PIECE = 16
SMALL = pl.CostEstimate(flops=0, bytes_accessed=0, transcendentals=0)
VMEM = 60 * 1024 * 1024
ANY = pl.BlockSpec(memory_space=pltpu.HBM)
SMEM = pl.BlockSpec(memory_space=pltpu.SMEM)


def dot(a, b, ca, cb):
    return lax.dot_general(a, b, (((ca,), (cb,)), ((), ())), preferred_element_type=F32)


def slot_of(value, order):
    out = jnp.int32(0)
    for k, bit in enumerate(order):
        out = out | (((value >> bit) & 1) << (len(order) - 1 - k))
    return out


def skip(kernel, scalars, deps):
    return lambda *refs: kernel(*refs[:scalars], *refs[scalars + deps:])


def lane_softmax(logits, first, last):
    lane = lax.broadcasted_iota(jnp.int32, logits.shape, 1)
    inside = (lane >= first) & (lane < last)
    masked = jnp.where(inside, logits, -1e30)
    top = jnp.max(masked, axis=1, keepdims=True)
    e = jnp.where(inside, jnp.exp(masked - top), 0.0)
    return e / jnp.sum(e, axis=1, keepdims=True)


def pick_lane(v, index):
    lane = lax.broadcasted_iota(jnp.int32, v.shape, 1)
    return jnp.sum(jnp.where(lane == index, v, 0.0), axis=1, keepdims=True)


def gelu_parts(pre):
    phi = 0.5 * (1.0 + lax.erf(pre * 0.7071067811865476))
    pdf = jnp.exp(pre * pre * -0.5) * 0.3989422804014327
    return pre * phi, phi + pre * pdf


def ffn_tile(lanes, rm, xt, dyt, coef_of, up_w, dn_w, UA, DA, ready):
    logits = dot(xt, rm[...], 1, 0)
    mixing = lane_softmax(logits, lanes, lanes + 2)
    coef = coef_of(logits, mixing)
    pre = dot(xt, up_w[...], 1, 0)
    g = dot(dyt, dn_w[...], 1, 1)
    hid, dg = gelu_parts(pre)
    hid = hid.astype(BF)
    dots = jnp.sum(hid.astype(F32) * g, axis=1, keepdims=True)
    pg = (g * dg * coef).astype(BF)
    cot = (dyt.astype(F32) * coef).astype(BF)
    out = dot(hid, dn_w[...], 1, 0) * coef
    rg = dot(pg, up_w[...], 1, 1)
    ready()
    UA[...] += dot(xt, pg, 0, 0)
    DA[...] += dot(cot, hid, 0, 0)
    return dots, out, rg


def stage_grads(ST, UA, DA, me, order, whole):
    bits = len(order)
    blk = UA.shape[0] >> bits

    def body(c, _):
        r = pl.ds(pl.multiple_of(c * blk, blk), blk)
        slot = jnp.where(whole, c, slot_of(c ^ me, order))
        ST[slot, 0] = UA[r, :].astype(BF)
        ST[slot, 1] = DA[r, :].astype(BF)
        return 0
    lax.fori_loop(0, 1 << bits, body, 0)


def dots_rows(dots):
    return jnp.broadcast_to(dots, (dots.shape[0], 128)).T[0:PIECE, :]


def dense_kernel(cfg, me_ref, *refs):
    chunks, rows, tm, lanes, order, first, deps = cfg
    it = iter(refs[deps:])
    take = lambda k: [next(it) for _ in range(k)]
    x_hbm, dy_hbm = take(chunks), take(chunks)
    rm, up_hbm, dn_hbm = take(3)
    base_o, base_r, sums_in = ([], [], []) if first else (take(chunks), take(chunks), take(2))
    out_refs, rg_refs = take(chunks), take(chunks)
    ends = take(2)
    X, DY, UP, DN, UA, DA, OB, RB, DT, OD, xsem, wsem, gsem, osem, dsem = take(15)
    ST, BO, BR, BD, bsem = (None,) * 5 if first else take(5)
    per = rows // tm
    weights = [pltpu.make_async_copy(up_hbm, UP, wsem.at[0]), pltpu.make_async_copy(dn_hbm, DN, wsem.at[1])]
    loads, bases = [], []
    for q in range(chunks):
        sl = pl.ds(q * rows, rows)
        loads.append([pltpu.make_async_copy(x_hbm[q], X.at[sl], xsem.at[q]), pltpu.make_async_copy(dy_hbm[q], DY.at[sl], xsem.at[chunks + q])])
        if not first:
            bases.append([pltpu.make_async_copy(base_o[q], BO.at[sl], bsem.at[q]), pltpu.make_async_copy(base_r[q].at[pl.ds(0, rows)], BR.at[sl], bsem.at[chunks + q]),
                          pltpu.make_async_copy(base_r[q].at[pl.ds(rows, PIECE)], BD.at[q], bsem.at[2 * chunks + q])])
    sums = [] if first else [pltpu.make_async_copy(sums_in[0], UA, gsem.at[0]), pltpu.make_async_copy(sums_in[1], DA, gsem.at[1])]
    for c in loads[0] + weights + sums + [c for q in loads[1:] for c in q] + [c for q in bases for c in q]:
        c.start()
    DT[...] = jnp.zeros_like(DT)
    if first:
        UA[...] = jnp.zeros_like(UA)
        DA[...] = jnp.zeros_like(DA)
    for c in weights:
        c.wait()

    def outs(q, part, slot):
        sl = pl.ds(part * tm, tm)
        return [pltpu.make_async_copy(OB.at[slot], out_refs[q].at[sl], osem.at[0, slot]),
                pltpu.make_async_copy(RB.at[slot], rg_refs[q].at[sl], osem.at[1, slot])]

    def one(i, _):
        slot = i % 2
        sl = pl.ds(pl.multiple_of(i * tm, tm), tm)
        for q in range(chunks):
            @pl.when(i == q * per)
            def _(q=q):
                for c in loads[q]:
                    c.wait()

        def ready():
            if not first:
                @pl.when(i == 0)
                def _():
                    for c in sums:
                        c.wait()
        dots, out, rg = ffn_tile(lanes, rm, X[sl, :], DY[sl, :], lambda l, m: pick_lane(m, lanes), UP, DN, UA, DA, ready)
        lines = dots_rows(dots)
        line = lax.broadcasted_iota(jnp.int32, lines.shape, 0)
        for q in range(chunks):
            for part in range(per):
                @pl.when(i == q * per + part)
                def _(q=q, part=part):
                    DT[q, :, part * tm:(part + 1) * tm] = jnp.where(line == 0, lines, 0.0)
        if not first:
            for q in range(chunks):
                @pl.when(i == q * per)
                def _(q=q):
                    for c in bases[q]:
                        c.wait()
            out = out + BO[sl, :].astype(F32)
            rg = rg + BR[sl, :].astype(F32)

        @pl.when(i >= 2)
        def _():
            for c in outs(0, 0, slot):
                c.wait()
        OB[slot] = out.astype(BF)
        RB[slot] = rg.astype(BF)
        for q in range(chunks):
            for part in range(per):
                @pl.when(i == q * per + part)
                def _(q=q, part=part):
                    for c in outs(q, part, slot):
                        c.start()
        return 0
    lax.fori_loop(0, chunks * per, one, 0)
    lines = []
    for q in range(chunks):
        total = DT[q] if first else DT[q] + BD[q].astype(F32)
        OD[q] = total.astype(BF)
        lines.append(pltpu.make_async_copy(OD.at[q], rg_refs[q].at[pl.ds(rows, PIECE)], dsem.at[q]))
    if first:
        last = lines + [pltpu.make_async_copy(UA, ends[0], gsem.at[0]), pltpu.make_async_copy(DA, ends[1], gsem.at[1])]
    else:
        stage_grads(ST, UA, DA, me_ref[0], order, False)
        half = ST.shape[0] // 2
        last = lines + [pltpu.make_async_copy(ST.at[pl.ds(h * half, half)], ends[h], gsem.at[h]) for h in range(2)]
    for c in last:
        c.start()
    for slot in range(min(2, chunks * per)):
        for c in outs(0, 0, slot):
            c.wait()
    for c in last:
        c.wait()


def ffn_dense(me, xs, dys, rm, up, down, lanes, order, base=None, sums=None, deps=()):
    chunks = len(xs)
    rows, d = xs[0].shape
    f = up.shape[1]
    n = chunks * rows
    tm = min(TILE_DENSE, rows)
    first = base is None
    bits = len(order)
    half = 1 << (bits - 1)
    vm = pl.BlockSpec(memory_space=pltpu.VMEM)
    part, lined = jax.ShapeDtypeStruct((rows, d), BF), jax.ShapeDtypeStruct((rows + PIECE, d), BF)
    total = jax.ShapeDtypeStruct((d, f), F32)
    grad = jax.ShapeDtypeStruct((half, 2, d >> bits, f), BF)
    ends = [total] * 2 if first else [grad] * 2
    more = [] if first else list(base[0]) + list(base[1]) + list(sums)
    scratch = [pltpu.VMEM((n, d), BF), pltpu.VMEM((n, d), BF), pltpu.VMEM((d, f), BF), pltpu.VMEM((f, d), BF), pltpu.VMEM((d, f), F32), pltpu.VMEM((d, f), F32),
               pltpu.VMEM((2, tm, d), BF), pltpu.VMEM((2, tm, d), BF), pltpu.VMEM((chunks, PIECE, d), F32), pltpu.VMEM((chunks, PIECE, d), BF),
               pltpu.SemaphoreType.DMA((2 * chunks,)), pltpu.SemaphoreType.DMA((2,)), pltpu.SemaphoreType.DMA((2,)), pltpu.SemaphoreType.DMA((2, 2)), pltpu.SemaphoreType.DMA((chunks,))]
    if not first:
        scratch += [pltpu.VMEM((2 * half, 2, d >> bits, f), BF), pltpu.VMEM((n, d), BF), pltpu.VMEM((n, d), BF), pltpu.VMEM((chunks, PIECE, d), BF), pltpu.SemaphoreType.DMA((3 * chunks,))]
    res = pl.pallas_call(
        partial(dense_kernel, (chunks, rows, tm, lanes, order, first, len(deps))),
        name="ffn_dense",
        out_shape=[part] * chunks + [lined] * chunks + ends,
        in_specs=[SMEM] + [ANY] * (len(deps) + 2 * chunks) + [vm] + [ANY] * (2 + len(more)),
        out_specs=[ANY] * (2 * chunks + len(ends)),
        scratch_shapes=scratch,
        cost_estimate=SMALL,
        compiler_params=pltpu.CompilerParams(vmem_limit_bytes=VMEM),
    )(me, *deps, *xs, *dys, rm, up, down, *more)
    return res[:chunks], res[chunks:2 * chunks], res[2 * chunks:]


def expert_kernel(cfg, me_ref, blk_ref, bnd_ref, *refs):
    first, count, whole, chunks, rows, d, tm, lanes, order, has, deps = cfg
    n = chunks * rows
    it = iter(refs[deps:])
    take = lambda k: [next(it) for _ in range(k)]
    x_hbm, dy_hbm = take(chunks), take(chunks)
    rm, up_hbm, dn_hbm = take(3)
    based = [q for q in range(chunks) if has[q]]
    base_o, base_r = take(len(based)), take(len(based))
    out_refs, rg_refs = take(chunks), take(chunks)
    entire = [g for g in range(count) if whole[g]]
    halved = [g for g in range(count) if not whole[g]]
    whole_refs, keep_refs, send_refs = take(len(entire)), take(len(halved)), take(len(halved))
    X, DY, UP, DN, UA, DA, ST, XG, DG, VAL, OA, RA, DOT, BD, TR, TL, TH, xsem, wsem, gsem, osem, dsem = it
    half = ST.shape[0] // 2
    pieces = tm // PIECE
    rows_of = [pl.ds(q * rows, rows) for q in range(chunks)]
    copies = []
    for q in range(chunks):
        copies.append(pltpu.make_async_copy(x_hbm[q], X.at[rows_of[q]], xsem.at[q]))
        copies.append(pltpu.make_async_copy(dy_hbm[q], DY.at[rows_of[q]], xsem.at[chunks + q]))
    earlier = []
    for k, q in enumerate(based):
        earlier.append(pltpu.make_async_copy(base_o[k], X.at[rows_of[q]], xsem.at[q]))
        earlier.append(pltpu.make_async_copy(base_r[k].at[pl.ds(0, rows)], DY.at[rows_of[q]], xsem.at[chunks + q]))
        earlier.append(pltpu.make_async_copy(base_r[k].at[pl.ds(rows, PIECE)], BD.at[q], dsem.at[q]))

    def weights(e, slot):
        return [pltpu.make_async_copy(up_hbm.at[first + e], UP.at[slot], wsem.at[slot, 0]),
                pltpu.make_async_copy(dn_hbm.at[first + e], DN.at[slot], wsem.at[slot, 1])]

    def flush(g):
        if whole[g]:
            return [pltpu.make_async_copy(ST, whole_refs[entire.index(g)], gsem.at[0])]
        g = halved.index(g)
        return [pltpu.make_async_copy(ST.at[pl.ds(0, half)], keep_refs[g], gsem.at[0]),
                pltpu.make_async_copy(ST.at[pl.ds(half, half)], send_refs[g], gsem.at[1])]

    for c in copies + weights(0, 0):
        c.start()
    OA[...] = jnp.zeros_like(OA)
    RA[...] = jnp.zeros_like(RA)
    DOT[...] = jnp.zeros_like(DOT)
    iota16 = lax.broadcasted_iota(jnp.int32, (PIECE, 128), 0)

    def one_expert(e, _):
        slot = e % 2
        total = jnp.int32(0)
        for q in range(chunks):
            lo, hi = bnd_ref[blk_ref[q], first + e], bnd_ref[blk_ref[q], first + e + 1]
            p0 = lo // PIECE
            p1 = jnp.where(hi > lo, (hi + PIECE - 1) // PIECE, p0)

            def add(p, _, lo=lo, hi=hi, p0=p0, total=total, q=q):
                k = total + p - p0
                TR[k] = q * rows + p * PIECE
                TL[k] = lo - p * PIECE
                TH[k] = hi - p * PIECE
                return 0
            lax.fori_loop(p0, p1, add, 0)
            total = total + p1 - p0
        tiles = (total + pieces - 1) // pieces

        def pad(k, _):
            TR[k] = 0
            TL[k] = 0
            TH[k] = 0
            return 0
        lax.fori_loop(total, tiles * pieces, pad, 0)
        UA[...] = jnp.zeros_like(UA)
        DA[...] = jnp.zeros_like(DA)

        @pl.when(e == 0)
        def _():
            for c in copies:
                c.wait()
        for c in weights(e, slot):
            c.wait()

        @pl.when(e + 1 < count)
        def _():
            for c in weights(e + 1, 1 - slot):
                c.start()

        def one_tile(i, _):
            base = i * pieces
            for p in range(pieces):
                r = pl.ds(pl.multiple_of(TR[base + p], PIECE), PIECE)
                XG[pl.ds(p * PIECE, PIECE), :] = X[r, :]
                DG[pl.ds(p * PIECE, PIECE), :] = DY[r, :]
                ok = (iota16 >= TL[base + p]) & (iota16 < TH[base + p])
                VAL[pl.ds(p * PIECE, PIECE), :] = jnp.where(ok, 1.0, 0.0)
            valid = VAL[:, 0:1]

            def coef_of(logits, mixing):
                return pick_lane(mixing, lanes + 1) * pick_lane(lane_softmax(logits, 0, lanes), first + e) * valid
            dots, out, rg = ffn_tile(lanes, rm, XG[...], DG[...], coef_of, UP.at[slot], DN.at[slot], UA, DA, lambda: None)
            dots = jnp.broadcast_to(dots * valid, (tm, 128))
            for p in range(pieces):
                r = pl.ds(pl.multiple_of(TR[base + p], PIECE), PIECE)
                s = slice(p * PIECE, (p + 1) * PIECE)
                OA[r, :] += out[s]
                RA[r, :] += rg[s]
                DOT[r, :] += dots[s]
            return 0
        lax.fori_loop(0, tiles, one_tile, 0)

        @pl.when(e == count - 1)
        def _():
            for c in earlier:
                c.start()

        for g in range(count - 1):
            @pl.when(e == g + 1)
            def _(g=g):
                for c in flush(g):
                    c.wait()
        kind = False
        for g in entire:
            kind = kind | (e == g)
        stage_grads(ST, UA, DA, me_ref[0], order, kind)
        for g in range(count):
            @pl.when(e == g)
            def _(g=g):
                for c in flush(g):
                    c.start()
        return 0
    lax.fori_loop(0, count, one_expert, 0)
    for c in earlier:
        c.wait()
    last = []
    step = min(256, rows)
    line = lax.broadcasted_iota(jnp.int32, (PIECE, step), 0)
    for q in range(chunks):
        r = rows_of[q]
        o, g = OA[r, :], RA[r, :]
        if has[q]:
            o, g = o + X[r, :].astype(F32), g + DY[r, :].astype(F32)
        X[r, :] = o.astype(BF)
        DY[r, :] = g.astype(BF)
        if not has[q]:
            BD[q] = jnp.zeros(BD.shape[1:], BF)
        for i in range(rows // step):
            sl = slice(i * step, (i + 1) * step)
            dots = jnp.where(line == 1, DOT[pl.ds(q * rows + i * step, step), :].T[0:PIECE, :], 0.0)
            BD[q, :, sl] = (BD[q, :, sl].astype(F32) + dots).astype(BF)
        last += [pltpu.make_async_copy(X.at[r], out_refs[q], osem.at[0, q]), pltpu.make_async_copy(DY.at[r], rg_refs[q].at[pl.ds(0, rows)], osem.at[1, q]),
                 pltpu.make_async_copy(BD.at[q], rg_refs[q].at[pl.ds(rows, PIECE)], dsem.at[q])]
        for c in last[-3:]:
            c.start()
    for c in last + flush(count - 1):
        c.wait()


def ffn_experts(me, blocks, bounds, xs, dys, rm, up, down, first, count, whole, base, order, deps=()):
    chunks = len(xs)
    rows, d = xs[0].shape
    lanes, _, f = up.shape
    n = chunks * rows
    tm = TILE_EXPERT
    bits = len(order)
    half = 1 << (bits - 1)
    grad, entire = [jax.ShapeDtypeStruct((k * half, 2, d >> bits, f), BF) for k in (1, 2)]
    part, lined = jax.ShapeDtypeStruct((rows, d), BF), jax.ShapeDtypeStruct((rows + PIECE, d), BF)
    table = n // PIECE + chunks * lanes + 2 * tm // PIECE
    vm = pl.BlockSpec(memory_space=pltpu.VMEM)
    has = tuple(b is not None for b in base[0])
    more = [b for k in range(2) for b in base[k] if b is not None]
    res = pl.pallas_call(
        partial(expert_kernel, (first, count, whole, chunks, rows, d, tm, lanes, order, has, len(deps))),
        name="ffn_experts",
        out_shape=[part] * chunks + [lined] * chunks + [entire] * sum(whole) + [grad] * (2 * (count - sum(whole))),
        in_specs=[SMEM] * 3 + [ANY] * (len(deps) + 2 * chunks) + [vm] + [ANY] * (2 + len(more)),
        out_specs=[ANY] * (2 * chunks + 2 * count - sum(whole)),
        scratch_shapes=[
            pltpu.VMEM((n, d), BF), pltpu.VMEM((n, d), BF), pltpu.VMEM((2, d, f), BF), pltpu.VMEM((2, f, d), BF),
            pltpu.VMEM((d, f), F32), pltpu.VMEM((d, f), F32), pltpu.VMEM((2 * half, 2, d >> bits, f), BF),
            pltpu.VMEM((tm, d), BF), pltpu.VMEM((tm, d), BF), pltpu.VMEM((tm, 128), F32),
            pltpu.VMEM((n, d), F32), pltpu.VMEM((n, d), F32), pltpu.VMEM((n, 128), F32), pltpu.VMEM((chunks, PIECE, d), BF),
            pltpu.SMEM((table,), jnp.int32), pltpu.SMEM((table,), jnp.int32), pltpu.SMEM((table,), jnp.int32),
            pltpu.SemaphoreType.DMA((2 * chunks,)), pltpu.SemaphoreType.DMA((2, 2)), pltpu.SemaphoreType.DMA((2,)), pltpu.SemaphoreType.DMA((2, chunks)), pltpu.SemaphoreType.DMA((chunks,)),
        ],
        cost_estimate=SMALL,
        compiler_params=pltpu.CompilerParams(vmem_limit_bytes=VMEM),
    )(me, blocks, bounds, *deps, *xs, *dys, rm, up, down, *more)
    at = 2 * chunks + sum(whole)
    rest = iter(res[at:])
    keep = [next(rest) for g in range(count) if not whole[g]]
    return res[:chunks], res[chunks:2 * chunks], res[2 * chunks:at], keep, list(rest)


def split_add_kernel(deps, *refs):
    ka, kb, ca, cb, keep, send = refs[deps:]
    keep[...] = (ka[...].astype(F32) + ca[...].astype(F32)).astype(BF)
    send[...] = (kb[...].astype(F32) + cb[...].astype(F32)).astype(BF)


def split_add(kept, came, deps=()):
    h, m, blk, f = kept.shape
    near = pl.BlockSpec((1, m, blk, f), lambda i: (i, 0, 0, 0))
    far = pl.BlockSpec((1, m, blk, f), lambda i: (i + h // 2, 0, 0, 0))
    out = jax.ShapeDtypeStruct((h // 2, m, blk, f), BF)
    return pl.pallas_call(
        partial(split_add_kernel, len(deps)),
        name="split_add",
        grid=(h // 2,),
        in_specs=[ANY] * len(deps) + [near, far, near, far],
        out_specs=[near, near],
        out_shape=[out, out],
        cost_estimate=SMALL,
        compiler_params=pltpu.CompilerParams(vmem_limit_bytes=VMEM),
    )(*deps, kept, kept, came, came)


def last_add_kernel(deps, turns, *refs):
    terms = refs[deps:-len(turns)]
    outs = refs[-len(turns):]
    for k, turned in enumerate(turns):
        total = terms[0][0, k].astype(F32)
        for v in terms[1:]:
            total = total + v[0, k].astype(F32)
        outs[k][...] = (total.T if turned else total).reshape(outs[k].shape)


def last_add(terms, turns, place=None, stacks=None, deps=()):
    _, m, blk, f = terms[0].shape
    shapes = [(f, blk) if turned else (blk, f) for turned in turns]
    aliases = {}
    if place is None:
        out_shape = [jax.ShapeDtypeStruct(s, F32) for s in shapes]
        out_specs = [pl.BlockSpec(s, lambda i: (0, 0)) for s in shapes]
    else:
        count, at = place
        out_shape = [jax.ShapeDtypeStruct((count,) + s, F32) for s in shapes]
        out_specs = [pl.BlockSpec((1,) + s, lambda i: (at, 0, 0)) for s in shapes]
        if stacks is not None:
            aliases = {k: k for k in range(m)}
            deps = tuple(stacks) + tuple(deps)
    full = pl.BlockSpec((1, m, blk, f), lambda i: (0, 0, 0, 0))
    return pl.pallas_call(
        partial(last_add_kernel, len(deps), turns),
        name="last_add",
        grid=(1,),
        in_specs=[ANY] * len(deps) + [full] * len(terms),
        out_specs=out_specs,
        out_shape=out_shape,
        input_output_aliases=aliases,
        cost_estimate=SMALL,
        compiler_params=pltpu.CompilerParams(vmem_limit_bytes=VMEM),
    )(*deps, *terms)


def hold(v, deps):
    return pl.pallas_call(
        lambda *refs: None,
        name="hold",
        in_specs=[ANY] * (1 + len(deps)),
        out_specs=ANY,
        out_shape=jax.ShapeDtypeStruct(v.shape, v.dtype),
        input_output_aliases={0: 0},
        cost_estimate=SMALL,
    )(v, *deps)


HD = 64
LANES = 128


def head_part(v, h):
    lane = lax.broadcasted_iota(jnp.int32, v.shape, 1)
    return jnp.where((lane // HD) == h, v, jnp.zeros((), v.dtype))


def masked_scores(st, key_first, query_first, prefix):
    key_pos = key_first + lax.broadcasted_iota(jnp.int32, st.shape, 0)
    query_pos = query_first + lax.broadcasted_iota(jnp.int32, st.shape, 1)
    seen = key_pos <= query_pos
    if prefix is not None:
        seen = seen | (key_pos < prefix)
    return jnp.where(seen, st, -1e30)


def score_block(k2, qm, half, length, prefix):
    mid = length // 2
    if half == 0:
        return masked_scores(dot(k2[0:mid], qm, 1, 1), 0, 0, prefix)
    low = dot(k2[0:mid], qm, 1, 1)
    high = masked_scores(dot(k2[mid:length], qm, 1, 1), mid, mid, None)
    return jnp.concatenate([low, high], 0)


def attn_forward_kernel(length, pieces, aliased, prefix_ref, at_ref, *refs):
    n1_ref = refs[0]
    w_refs = [(r, i) for r, n in zip(refs[1:], pieces) for i in range(n)]
    q_ref, k_ref, v_ref, ctx_ref, lse_ref = refs[1 + len(pieces) + aliased:]
    mid = length // 2
    prefix = prefix_ref[0]
    n1 = n1_ref[...]
    for out, (w, i) in zip((q_ref, k_ref, v_ref), w_refs):
        out[...] = dot(n1, w[i], 1, 0).astype(BF)
    vt = v_ref[...].T
    k2 = k_ref[...]
    for half in range(2):
        rows = pl.ds(half * mid, mid)
        q2 = q_ref[rows, :] * jnp.asarray(HD ** -0.5, BF)
        keys = mid * (half + 1)
        parts = []
        for h in range(2):
            st = score_block(k2, head_part(q2, h), half, length, prefix)
            top = jnp.max(st, axis=0, keepdims=True)
            p = jnp.exp(st - top)
            total = jnp.sum(p, axis=0, keepdims=True)
            c = dot(vt[h * HD:(h + 1) * HD, 0:keys], p.astype(BF), 1, 0)
            parts.append(c / total)
            lse_ref[0, h:h + 1, rows] = top + jnp.log(total)
        ctx_ref[rows, :] = jnp.concatenate(parts, 0).T.astype(BF)


def attn_forward(prefix, at, n1, ws, heads, earlier=(), deps=()):
    length, d = n1.shape
    pairs = ws[0].shape[2] // LANES
    col = pl.BlockSpec((length, LANES), lambda p, _, at_ref: (0, at_ref[p]))
    out = jax.ShapeDtypeStruct((length, heads), BF)
    done = len(earlier)
    skipped = len(deps)
    return pl.pallas_call(
        skip(partial(attn_forward_kernel, length, tuple(w.shape[0] for w in ws), done), 2, skipped),
        name="attn_forward",
        grid_spec=pltpu.PrefetchScalarGridSpec(
            num_scalar_prefetch=2, grid=(pairs,),
            in_specs=[ANY] * skipped + [pl.BlockSpec((length, d), lambda p, *_: (0, 0))]
            + [pl.BlockSpec((w.shape[0], d, LANES), lambda p, *_: (0, 0, p)) for w in ws] + [ANY] * done,
            out_specs=[col] * 4 + [pl.BlockSpec((1, 8, length), lambda p, _, at_ref: (at_ref[p], 0, 0))]),
        out_shape=[out] * 4 + [jax.ShapeDtypeStruct((heads // LANES, 8, length), F32)],
        input_output_aliases={3 + skipped + len(ws) + k: k for k in range(done)},
        cost_estimate=SMALL,
        compiler_params=pltpu.CompilerParams(vmem_limit_bytes=VMEM),
    )(prefix, at, *deps, n1, *ws, *earlier)


def attn_backward_kernel(length, bits, members, based, prefix_ref, me_ref, j_ref, *refs):
    it = iter(refs)
    take = lambda k: [next(it) for _ in range(k)]
    mcs = take(members)
    n1_ref, wo_ref, w_ref, q_ref, k_ref, v_ref, ctx_ref, lse_ref = take(8)
    bases = take(members) if based else []
    ng_refs = take(members)
    grad_ref, NG, MC, DC, DK, DV, DQ, sem = it
    rows_each = length // members
    where = [pl.ds(pl.multiple_of(lax.rem(j_ref[0] + k, members) * rows_each, rows_each), rows_each) for k in range(members)]
    mid = length // 2
    prefix = prefix_ref[0]
    me = me_ref[0]
    pair = pl.program_id(0)
    copies = [pltpu.make_async_copy(mcs[k], MC.at[where[k]], sem.at[k]) for k in range(members)]

    @pl.when(pair == 0)
    def _():
        for c in copies:
            c.start()
        for c in copies:
            c.wait()
    mc = MC[...]
    DC[...] = dot(mc, wo_ref[...], 1, 1).astype(BF)
    k2, v2 = k_ref[...], v_ref[...]
    kt = k2.T
    scale = jnp.asarray(HD ** -0.5, BF)
    for half in range(2):
        rows = pl.ds(half * mid, mid)
        q2 = q_ref[rows, :] * scale
        dc2 = DC[rows, :]
        keys = mid * (half + 1)
        dv = jnp.zeros((keys, LANES), F32)
        dk = jnp.zeros((keys, LANES), F32)
        dq = []
        for h in range(2):
            qm, dcm = head_part(q2, h), head_part(dc2, h)
            st = score_block(k2, qm, half, length, prefix)
            p = jnp.exp(st - lse_ref[0, h:h + 1, rows])
            dv = dv + dot(p.astype(BF), dcm, 1, 0)
            dp = dot(v2[0:keys], dcm, 1, 1)
            ds = (p * (dp - jnp.sum(p * dp, axis=0, keepdims=True))).astype(BF)
            dk = dk + dot(ds, qm, 1, 0)
            dq.append(dot(kt[h * HD:(h + 1) * HD, 0:keys], ds, 1, 0))
        DQ[rows, :] = (jnp.concatenate(dq, 0) * HD ** -0.5).T.astype(BF)
        if half == 0:
            DK[0:mid, :] = dk
            DV[0:mid, :] = dv
        else:
            DK[0:mid, :] += dk[0:mid]
            DV[0:mid, :] += dv[0:mid]
            DK[mid:length, :] = dk[mid:length]
            DV[mid:length, :] = dv[mid:length]
    dq, dk, dv = DQ[...], DK[...].astype(BF), DV[...].astype(BF)
    ng = dot(dq, w_ref[0], 1, 1) + dot(dk, w_ref[1], 1, 1) + dot(dv, w_ref[2], 1, 1)

    @pl.when(pair == 0)
    def _():
        NG[...] = ng

    @pl.when(pair > 0)
    def _():
        NG[...] += ng
    n1 = n1_ref[...]
    grads = [dot(n1, x, 0, 0) for x in (dq, dk, dv)] + [dot(mc, ctx_ref[...], 0, 0)]
    blk = n1.shape[1] >> bits
    for c in range(1 << bits):
        slot = slot_of(jnp.int32(c) ^ me, range(bits))
        for i in range(4):
            grad_ref[slot, i] = grads[i][c * blk:(c + 1) * blk].astype(BF)

    @pl.when(pair == pl.num_programs(0) - 1)
    def _():
        for k in range(members):
            done = NG[where[k], :]
            if based:
                done = done + bases[k][...].astype(F32)
            ng_refs[k][...] = done.astype(BF)


def attn_backward(prefix, me, j, mcs, n1, wo, w, saved, base, bits, deps=()):
    q, k, v, ctx, lse = saved
    length, d = n1.shape
    heads = w.shape[2]
    pairs = heads // LANES
    blk = d >> bits
    members = len(mcs)
    col = pl.BlockSpec((length, LANES), lambda p, *_: (0, p))
    full = pl.BlockSpec((length, d), lambda p, *_: (0, 0))
    part = pl.BlockSpec((length // members, d), lambda p, *_: (0, 0))
    extra = [] if base is None else list(base)
    res = pl.pallas_call(
        skip(partial(attn_backward_kernel, length, bits, members, base is not None), 3, len(deps)),
        name="attn_backward",
        grid_spec=pltpu.PrefetchScalarGridSpec(
            num_scalar_prefetch=3, grid=(pairs,),
            in_specs=[ANY] * (len(deps) + members) + [full, pl.BlockSpec((LANES, d), lambda p, *_: (p, 0)), pl.BlockSpec((3, d, LANES), lambda p, *_: (0, 0, p)),
                      col, col, col, col, pl.BlockSpec((1, 8, length), lambda p, *_: (p, 0, 0))] + [part] * len(extra),
            out_specs=[part] * members + [pl.BlockSpec((1 << bits, 4, blk, LANES), lambda p, *_: (0, 0, 0, p))],
            scratch_shapes=[pltpu.VMEM((length, d), F32), pltpu.VMEM((length, d), BF), pltpu.VMEM((length, LANES), BF),
                            pltpu.VMEM((length, LANES), F32), pltpu.VMEM((length, LANES), F32), pltpu.VMEM((length, LANES), BF),
                            pltpu.SemaphoreType.DMA((members,))]),
        out_shape=[jax.ShapeDtypeStruct((length // members, d), BF)] * members + [jax.ShapeDtypeStruct((1 << bits, 4, blk, heads), BF)],
        cost_estimate=SMALL,
        compiler_params=pltpu.CompilerParams(vmem_limit_bytes=VMEM),
    )(prefix, me, j, *deps, *mcs, n1, wo, w, q, k, v, ctx, lse, *extra)
    return res[:members], res[members]


EPS = 1e-5


def normalise(v):
    centered = v - jnp.mean(v, axis=1, keepdims=True)
    r = lax.rsqrt(jnp.mean(centered * centered, axis=1, keepdims=True) + EPS)
    return centered * r, r


def norm_backward(xhat, r, grad, gain):
    scaled = grad * gain
    return r * (scaled - jnp.mean(scaled, axis=1, keepdims=True) - xhat * jnp.mean(scaled * xhat, axis=1, keepdims=True))


def order_rows(pos, rows_to_slots):
    n = pos.shape[1] if rows_to_slots else pos.shape[0]
    slot = lax.broadcasted_iota(jnp.int32, (n, n), 0 if rows_to_slots else 1)
    return jnp.where(slot == pos, 1.0, 0.0).astype(BF)


def first_norm_kernel(members, j_ref, *refs):
    xs, (gain, shift, dy, pos, out, sorted_dy) = refs[:members], refs[members:]
    for k in range(members):
        @pl.when(pl.program_id(0) == k)
        def _(k=k):
            xhat, _ = normalise(xs[k][...].astype(F32))
            out[...] = (xhat * gain[...] + shift[...]).astype(BF)
            if k == 0:
                sorted_dy[...] = dot(order_rows(pos[...], True), dy[...], 1, 0).astype(BF)


def first_norm(j, xs, gain, shift, dy, pos):
    members = len(xs)
    rows, d = xs[0].shape
    fixed = lambda shape: pl.BlockSpec(shape, lambda p, *_: (0, 0))
    return pl.pallas_call(
        partial(first_norm_kernel, members),
        name="first_norm",
        grid_spec=pltpu.PrefetchScalarGridSpec(
            num_scalar_prefetch=1, grid=(members,),
            in_specs=[fixed((rows, d))] * members + [fixed((1, d))] * 2 + [fixed((rows, d)), fixed((1, rows))],
            out_specs=[pl.BlockSpec((rows, d), lambda p, j_ref: (lax.rem(j_ref[0] + p, members), 0)), fixed((rows, d))]),
        out_shape=[jax.ShapeDtypeStruct((members * rows, d), BF), jax.ShapeDtypeStruct((rows, d), BF)],
        cost_estimate=SMALL,
        compiler_params=pltpu.CompilerParams(vmem_limit_bytes=VMEM),
    )(j, *xs, gain, shift, dy, pos)


def project_kernel(parts, *refs):
    total = dot(refs[0][...], refs[parts][...], 1, 0)
    for i in range(1, parts):
        total = total + dot(refs[i][...], refs[parts + i][...], 1, 0)
    refs[-1][0] = total.astype(BF)


def project(contexts, weights, members):
    parts = len(contexts)
    length, heads = contexts[0].shape
    d = weights[0].shape[1]
    rows = length // members
    return pl.pallas_call(
        partial(project_kernel, parts),
        name="project",
        grid=(members,),
        in_specs=[pl.BlockSpec((rows, heads), lambda p: (p, 0))] * parts + [pl.BlockSpec((heads, d), lambda p: (0, 0))] * parts,
        out_specs=pl.BlockSpec((1, rows, d), lambda p: (p, 0, 0)),
        out_shape=jax.ShapeDtypeStruct((members, rows, d), BF),
        cost_estimate=SMALL,
        compiler_params=pltpu.CompilerParams(vmem_limit_bytes=VMEM),
    )(*contexts, *weights)


def second_norm_kernel(came, x, gain, shift, pos, middle, n2):
    mid = x[...].astype(F32)
    for k in range(came.shape[0]):
        mid = mid + came[k].astype(F32)
    middle[...] = mid
    xhat, _ = normalise(mid)
    normed = (xhat * gain[...] + shift[...]).astype(BF)
    n2[...] = dot(order_rows(pos[...], True), normed, 1, 0).astype(BF)


def second_norm(came, x, gain, shift, pos):
    rows, d = x.shape
    fixed = lambda shape: pl.BlockSpec(shape, lambda p: (0,) * len(shape))
    return pl.pallas_call(
        second_norm_kernel,
        name="second_norm",
        grid=(1,),
        in_specs=[fixed(came.shape), fixed((rows, d)), fixed((1, d)), fixed((1, d)), fixed((1, rows))],
        out_specs=[fixed((rows, d))] * 2,
        out_shape=[jax.ShapeDtypeStruct((rows, d), F32), jax.ShapeDtypeStruct((rows, d), BF)],
        cost_estimate=SMALL,
        compiler_params=pltpu.CompilerParams(vmem_limit_bytes=VMEM),
    )(came, x, gain, shift, pos)


def add_small(a, b, deps):
    def kernel(*refs):
        refs[-1][...] = refs[-3][...] + refs[-2][...]
    full = pl.BlockSpec(memory_space=pltpu.VMEM)
    return pl.pallas_call(kernel, name="add_small", in_specs=[ANY] * len(deps) + [full, full], out_specs=full,
                          out_shape=jax.ShapeDtypeStruct(a.shape, a.dtype), cost_estimate=SMALL)(*deps, a, b)


def hi_lo(v):
    hi = v.astype(BF)
    return hi, (v - hi.astype(F32)).astype(BF)


def middle_backward_kernel(single, bnd_ref, t_ref, *refs):
    it = iter(refs)
    parts = [next(it) for _ in range(single)]
    n2, rm, middle, dy, gain, pos, mg_ref, mc_ref, sums_ref = it
    t = t_ref[0]
    n2v, rmv = n2[...], rm[...]
    rows = n2v.shape[0]
    total = parts[0][0:rows, :].astype(F32)
    lines = parts[0][rows:rows + PIECE, 0:rows].astype(F32)
    for p in parts[1:]:
        total = total + p[0:rows, :].astype(F32)
        lines = lines + p[rows:rows + PIECE, 0:rows].astype(F32)
    dots = jnp.concatenate([lines, jnp.zeros((128 - PIECE, rows), F32)], axis=0).T
    experts = bnd_ref.shape[1] - 1
    logits = dot(n2v, rmv, 1, 0)
    route_prob = lane_softmax(logits, 0, experts)
    mixing = lane_softmax(logits, experts, experts + 2)
    row = lax.broadcasted_iota(jnp.int32, (rows, 1), 0)
    route = jnp.zeros((rows, 1), jnp.int32)
    for e in range(1, experts):
        route = route + (row >= bnd_ref[t, e]).astype(jnp.int32)
    gate = pick_lane(route_prob, route)
    m0, m1 = pick_lane(mixing, experts), pick_lane(mixing, experts + 1)
    dense_dot, expert_dot = dots[:, 0:1], dots[:, 1:2]
    d0, d1 = dense_dot, expert_dot * gate
    inner = m0 * d0 + m1 * d1
    lane = lax.broadcasted_iota(jnp.int32, logits.shape, 1)
    grad = expert_dot * (m1 * gate) * (jnp.where(lane == route, 1.0, 0.0) - route_prob)
    grad = jnp.where(lane < experts, grad, 0.0)
    grad = jnp.where(lane == experts, m0 * (d0 - inner), grad)
    grad = jnp.where(lane == experts + 1, m1 * (d1 - inner), grad)
    hi, lo = hi_lo(grad)
    total = total + dot(hi, rmv, 1, 1) + dot(lo, rmv, 1, 1)
    sums_ref[0:8, :] = (dot(hi.T, n2v, 1, 0) + dot(lo.T, n2v, 1, 0))[0:8]
    g = dot(order_rows(pos[...], False), total.astype(BF), 1, 0)
    xhat, r = normalise(middle[...])
    sums_ref[8:16, :] = jnp.zeros((8, g.shape[1]), F32)
    sums_ref[8:9, :] = jnp.sum(g * xhat, axis=0, keepdims=True)
    sums_ref[9:10, :] = jnp.sum(g, axis=0, keepdims=True)
    mg = dy[...].astype(F32) + norm_backward(xhat, r, g, gain[...])
    mg_ref[...] = mg
    mc_ref[...] = mg.astype(BF)


def middle_backward(bounds, t, parts, n2, rm, middle, dy, gain, pos, deps=()):
    rows, d = n2.shape
    fixed = lambda shape: pl.BlockSpec(shape, lambda p, *_: (0, 0))
    big = fixed((rows, d))
    return pl.pallas_call(
        skip(partial(middle_backward_kernel, len(parts)), 2, len(deps)),
        name="middle_backward",
        grid_spec=pltpu.PrefetchScalarGridSpec(
            num_scalar_prefetch=2, grid=(1,),
            in_specs=[ANY] * len(deps) + [fixed((rows + PIECE, d))] * len(parts)
            + [big, fixed((d, 128)), big, big, fixed((1, d)), fixed((rows, 1))],
            out_specs=[big, big, fixed((16, d))]),
        out_shape=[jax.ShapeDtypeStruct((rows, d), F32), jax.ShapeDtypeStruct((rows, d), BF), jax.ShapeDtypeStruct((16, d), F32)],
        cost_estimate=SMALL,
        compiler_params=pltpu.CompilerParams(vmem_limit_bytes=VMEM),
    )(bounds, t, *deps, *parts, n2, rm, middle, dy, gain, pos)


def layer_out_kernel(*refs):
    parts, (middle, pos, out) = refs[:-3], refs[-3:]
    total = parts[0][...].astype(F32)
    for p in parts[1:]:
        total = total + p[...].astype(F32)
    hi, lo = hi_lo(total)
    move = order_rows(pos[...], False)
    out[...] = (middle[...] + dot(move, hi, 1, 0) + dot(move, lo, 1, 0)).astype(BF)


def layer_out(parts, middle, pos, deps=()):
    rows, d = middle.shape
    big = pl.BlockSpec((rows, d), lambda p: (0, 0))
    return pl.pallas_call(
        skip(layer_out_kernel, 0, len(deps)),
        name="layer_out",
        grid=(1,),
        in_specs=[ANY] * len(deps) + [big] * (len(parts) + 1) + [pl.BlockSpec((rows, 1), lambda p: (0, 0))],
        out_specs=big,
        out_shape=jax.ShapeDtypeStruct((rows, d), BF),
        cost_estimate=SMALL,
        compiler_params=pltpu.CompilerParams(vmem_limit_bytes=VMEM),
    )(*deps, *parts, middle, pos)


def add_parts_kernel(*refs):
    total = refs[0][...].astype(F32)
    for p in refs[1:-1]:
        total = total + p[...].astype(F32)
    refs[-1][...] = total.astype(BF)


def add_parts(parts, deps=()):
    rows, d = parts[0].shape
    tile = pl.BlockSpec((rows, d), lambda p: (p, 0))
    return pl.pallas_call(
        skip(add_parts_kernel, 0, len(deps)),
        name="add_parts",
        grid=(1,),
        in_specs=[ANY] * len(deps) + [tile] * len(parts),
        out_specs=tile,
        out_shape=jax.ShapeDtypeStruct((rows, d), BF),
        cost_estimate=SMALL,
        compiler_params=pltpu.CompilerParams(vmem_limit_bytes=VMEM),
    )(*deps, *parts)


def input_backward_kernel(count, *refs):
    parts = refs[:count]
    x, mg, gain, out, sums = refs[count:]
    g = parts[0][...].astype(F32)
    for p in parts[1:]:
        g = g + p[...].astype(F32)
    xhat, r = normalise(x[...].astype(F32))
    sums[...] = jnp.zeros_like(sums)
    sums[0:1, :] = jnp.sum(g * xhat, axis=0, keepdims=True)
    sums[1:2, :] = jnp.sum(g, axis=0, keepdims=True)
    out[...] = mg[...] + norm_backward(xhat, r, g, gain[...])


def input_backward(parts, x, mg, gain, deps=()):
    rows, d = x.shape
    fixed = lambda shape: pl.BlockSpec(shape, lambda p: (0, 0))
    big = fixed((rows, d))
    return pl.pallas_call(
        skip(partial(input_backward_kernel, len(parts)), 0, len(deps)),
        name="input_backward",
        grid=(1,),
        in_specs=[ANY] * len(deps) + [big] * (len(parts) + 2) + [fixed((1, d))],
        out_specs=[big, fixed((8, d))],
        out_shape=[jax.ShapeDtypeStruct((rows, d), F32), jax.ShapeDtypeStruct((8, d), F32)],
        cost_estimate=SMALL,
        compiler_params=pltpu.CompilerParams(vmem_limit_bytes=VMEM),
    )(*deps, *parts, x, mg, gain)


class Everywhere:
    def __init__(self, v):
        self.v = v
        bits = {axis: lax.axis_size(axis).bit_length() - 1 for axis in ("tensor", "dp")}
        self.hops = [("tensor", 1 << b) for b in range(bits["tensor"])] + [("dp", 1 << b) for b in range(1, bits["dp"])] + [("dp", 1)]
        self.launch()

    def launch(self):
        if self.hops:
            axis, bit = self.hops.pop(0)
            self.came = lax.ppermute(self.v, axis, [(i, i ^ bit) for i in range(lax.axis_size(axis))])
        else:
            self.came = None

    def add(self, mark):
        if self.came is None:
            return mark
        self.v = add_small(self.v, self.came, mark)
        self.launch()
        return (self.v,)


def over_dp(v, bit):
    return lax.ppermute(v, "dp", [(i, i ^ (1 << bit)) for i in range(lax.axis_size("dp"))])


def shards(inputs, cotangent, routes, prefixes, gain_one, shift_one, qkv_weight, out_weight, gain_two, shift_two,
           up_weight, down_weight, expert_up, expert_down, router_weight, mix_weight):
    rows, d = inputs.shape
    tensor = lax.axis_size("tensor")
    dp = lax.axis_size("dp")
    bits = dp.bit_length() - 1
    seqs = prefixes.shape[0]
    members = tensor // seqs
    experts = expert_up.shape[0]
    heads = qkv_weight.shape[2]
    pairs = heads // LANES
    t = lax.axis_index("tensor")
    s, j = t // members, t % members
    me = lax.axis_index("dp").astype(jnp.int32)
    me1, j1, t1 = me.reshape(1), j.astype(jnp.int32).reshape(1), t.astype(jnp.int32).reshape(1)
    place = lambda a, b: (a % seqs) * members + b % members
    everyone = [(a, b) for a in range(seqs) for b in range(members)]

    def from_member(v, k):
        return lax.ppermute(v, "tensor", [(place(a, b), place(a, b - k)) for a, b in everyone])

    def from_sequence(v, k):
        return lax.ppermute(v, "tensor", [(place(a, b), place(a - k, b)) for a, b in everyone])

    def to_member(v, k):
        return from_member(v, -k)

    def to_sequence(v, k):
        return from_sequence(v, -k)

    route_blocks = routes.reshape(tensor, rows)
    bounds = jnp.stack([jnp.sum((route_blocks < e).astype(jnp.int32), axis=1) for e in range(experts + 1)], axis=1)
    key_col = lax.dynamic_slice_in_dim(routes, t * rows, rows, 0) * rows + jnp.arange(rows, dtype=jnp.int32)[:, None]
    key_row = key_col.reshape(1, rows)
    pos_row = jnp.sum((key_col < key_row).astype(jnp.int32), axis=0, keepdims=True)
    pos_col = jnp.sum((key_row < key_col).astype(jnp.int32), axis=1, keepdims=True)
    chunk = [(dj, ds) for dj in range(members) for ds in range(seqs)]
    blocks = jnp.stack([((s + ds) % seqs) * members + (j + dj) % members for dj, ds in chunk]).astype(jnp.int32)
    near = [q for q, (dj, ds) in enumerate(chunk) if ds == 0]
    far = [q for q, (dj, ds) in enumerate(chunk) if ds > 0]

    xs = [inputs] + [from_member(inputs, k) for k in range(1, members)]
    flip = me & 1
    relay = pairs % 2 == 0 and dp > 1
    w_own = jnp.transpose(qkv_weight, (1, 0, 2))
    fetched = []
    for ds in range(1, seqs):
        if relay:
            half = lax.dynamic_slice_in_dim(qkv_weight, flip * (heads // 2), heads // 2, 2)
            fetched.append([from_sequence(jnp.transpose(half[:, a:b], (1, 0, 2)), ds) for a, b in ((0, 2), (2, 3))])
        else:
            fetched.append([from_sequence(w_own, ds)])
    wo_all = [out_weight] + [from_sequence(out_weight, ds) for ds in range(1, seqs)]
    gain_one, shift_one, gain_two, shift_two = [v.reshape(1, d) for v in (gain_one, shift_one, gain_two, shift_two)]
    prefix = lax.dynamic_slice_in_dim(prefixes, s, 1)
    rm = jnp.concatenate([router_weight, mix_weight, jnp.zeros((d, LANES - experts - 2), BF)], axis=1)
    n1, dys = first_norm(j1, xs, gain_one, shift_one, cotangent, pos_row)
    columns = jnp.arange(pairs, dtype=jnp.int32)
    pieces = [[] for _ in fetched]
    fence = (n1,)
    if relay:
        for k, got in enumerate(fetched):
            held = hold(got[0], (n1,))
            pieces[k] = [[held], [over_dp(held, 0)]]
            fence += (held,)
    saved = [attn_forward(prefix, columns, n1, [w_own], heads, deps=fence[1:] + (rm,))]
    if relay:
        for k, got in enumerate(fetched):
            held = hold(got[1], (saved[0][4],))
            pieces[k][0].append(held)
            pieces[k][1].append(over_dp(held, 0))
    else:
        pieces = [[got] for got in fetched]
    w_all = [w_own]
    for halves in pieces:
        part = ()
        for k, ws in enumerate(halves):
            at = (columns + (flip ^ k) * (pairs // 2))[:pairs // 2] if relay else columns
            part = attn_forward(prefix, at, n1, ws, heads, part, deps=() if part else (saved[-1][4],))
        saved.append(part)
        whole = [jnp.concatenate(ws, axis=0) for ws in halves]
        if relay:
            whole = [jnp.where(flip == 0, jnp.concatenate(whole, axis=2), jnp.concatenate(whole[::-1], axis=2))]
        w_all.append(whole[0])
    contexts = [v[3] for v in saved]

    def spread(mine):
        out = list(mine)
        for k in range(1, members):
            out += [from_member(m, k) for m in mine]
        return out

    dy_mine = [dys] + [from_sequence(dys, ds) for ds in range(1, seqs)]
    dy_near = [dys] + [from_member(dys, k) for k in range(1, members)]
    sent = project(contexts, wo_all, members)
    came = lax.all_to_all(sent, "tensor", 0, 0, axis_index_groups=[[place(a, b) for b in range(members)] for a in range(seqs)], tiled=True)
    middle, n2 = second_norm(came, inputs, gain_two, shift_two, pos_row)
    n2_mine = [n2] + [from_sequence(n2, ds) for ds in range(1, seqs)]
    n2_near = [n2] + [from_member(n2, k) for k in range(1, members)]

    straight = tuple(range(bits))
    pick = lambda v, which: [v[q] for q in which]
    out_a, rg_a, sums = ffn_dense(me1, n2_near, dy_near, rm, up_weight, down_weight, experts, straight, deps=tuple(dy_mine[1:]))
    n2_all, dy_all = [], []
    n2_far, dy_far = [[hold(v, (out_a[0],)) for v in mine[1:]] for mine in (n2_mine, dy_mine)]
    for k in range(members):
        n2_all += [n2_near[k]] + [from_member(v, k) if k else v for v in n2_far]
        dy_all += [dy_near[k]] + [from_member(v, k) if k else v for v in dy_far]
    base = [[None] * tensor, [None] * tensor]
    for k, q in enumerate(near):
        base[0][q], base[1][q] = out_a[k], rg_a[k]
    by_scatter = [e == 0 for e in range(experts)]
    out_e, rg_e, whole, keep_e, send_e = ffn_experts(me1, blocks, bounds, n2_all, dy_all, rm, expert_up, expert_down, 0, 1, (True,), base, straight)
    out_e, rg_e, whole = list(out_e), list(rg_e), list(whole)
    out_b, rg_b, ends = ffn_dense(me1, pick(n2_all, far), pick(dy_all, far), rm, up_weight, down_weight, experts, straight,
                                  (pick(out_e, far), pick(rg_e, far)), sums)
    for k, q in enumerate(far):
        out_e[q], rg_e[q] = out_b[k], rg_b[k]
    if experts > 1:
        out_e, rg_e, entire, keep_e, send_e = ffn_experts(me1, blocks, bounds, n2_all, dy_all, rm, expert_up, expert_down, 1, experts - 1, tuple(by_scatter[1:]), (out_e, rg_e), straight)
        whole += list(entire)

    index = {c: q for q, c in enumerate(chunk)}
    def to_owner(parts):
        mine = [[parts[index[0, ds]]] + [to_member(parts[index[k, ds]], k) for k in range(1, members)] for ds in range(seqs)]
        return mine[0], mine[1:]

    def onward(terms, deps):
        sums = [add_parts(v, deps) for v in terms]
        return [to_sequence(v, ds + 1) for ds, v in enumerate(sums)], sums

    class Halving:
        def __init__(self, keep, send, order):
            self.keep, self.send, self.order, self.at = keep, send, order, 0

        def launch(self, deps=()):
            if deps:
                self.send = hold(self.send, deps)
            self.came = over_dp(self.send, self.order[self.at])
            self.at += 1

        def add(self, mark):
            self.keep, self.send = split_add(self.keep, self.came, mark)
            self.launch()
            return (self.send,)

        def rest(self, mark):
            while self.at < bits:
                mark = self.add(mark)
            return mark

    scattered = []
    for v in whole:
        flat = lax.psum_scatter(v.reshape(-1, v.shape[-1]), "dp", scatter_dimension=0, tiled=True)
        scattered.append(flat.reshape((1,) + v.shape[1:]))

    halvings = [Halving(keep, send, straight) for keep, send in zip(keep_e, send_e)]
    dense_sum = Halving(ends[0], ends[1], straight)
    sum_of = dict(enumerate(scattered + halvings))
    rg_near, rg_far = to_owner(rg_e)
    for v in [dense_sum] + halvings[:2]:
        v.launch()
    mark = dense_sum.add((out_e[0],))
    came_far, terms = onward(rg_far, mark)
    mark = tuple(terms[:1]) + tuple(w_all[1:])
    mg, mc, sums_two = middle_backward(bounds, t1, rg_near + came_far, n2, rm, middle, cotangent, gain_two, pos_col, mark)
    mcs = [mc] + [from_member(mc, k) for k in range(1, members)]
    mark = (mc,)
    out_near, out_far = to_owner([hold(v, mark) for v in out_e])
    ngs = None
    grads = [None] * seqs
    for ds in list(range(1, seqs)) + [0]:
        ngs, grads[ds] = attn_backward(prefix, me1, j1, mcs, n1, wo_all[ds], w_all[ds], saved[ds], ngs, bits, mark)
        mark = (grads[ds],)
        if ds == 1 or seqs == 1:
            out_came, terms = onward(out_far, mark)
            mark = tuple(terms[:1]) or mark
            mark = dense_sum.add(mark)
            for v in halvings[:1]:
                mark = v.add(mark)
            for v in halvings[2:]:
                v.launch(mark)
    moved = [to_sequence(grads[ds], ds) for ds in range(1, seqs)]
    ng_parts = [ngs[0]] + [to_member(ngs[k], k) for k in range(1, members)]
    for v in halvings[:1]:
        mark = v.add(mark)
    input_grad, sums_one = input_backward(ng_parts, inputs, mg, gain_one, mark)
    mark = (sums_one,)
    sums = Everywhere(jnp.concatenate([sums_two, sums_one], axis=0))
    stacks = None

    def finish(e, mark):
        if by_scatter[e]:
            terms = [sum_of[e]]
        else:
            mark = sum_of[e].rest(mark)
            terms = [sum_of[e].keep, sum_of[e].came]
        done = last_add(terms, (False, True), (experts, e), stacks, mark)
        return done, (done[1],)

    for v in halvings[1:2]:
        mark = v.add(mark)
    mark = sums.add(mark)
    keep = grads[0]
    for v in moved[:-1]:
        keep = (keep.astype(F32) + v.astype(F32)).astype(BF)
    if moved:
        keep, send = split_add(keep, moved[-1], mark)
        mark = (send,)
    else:
        keep, send = keep[:dp // 2], keep[dp // 2:]
    attn_sum = Halving(keep, send, straight)
    attn_sum.launch()
    mark = dense_sum.rest(mark)
    up_out, down_out = last_add([dense_sum.keep, dense_sum.came], (False, True), deps=mark)
    mark = (up_out,)
    stacks, mark = finish(0, mark)
    if experts > 1:
        stacks, mark = finish(1, mark)
    mark = sums.add(mark)
    for v in halvings[1:2]:
        mark = v.add(mark)
    layer_output = layer_out(out_near + out_came, middle, pos_col, mark)
    mark = (layer_output,)
    for v in halvings[2:]:
        mark = v.add(mark)
    mark = sums.add(mark)
    mark = sums.add(mark)
    if experts > 2:
        stacks, mark = finish(2, mark)
    mark = attn_sum.add(mark)
    for v in halvings[2:]:
        mark = v.add(mark)
    mark = attn_sum.add(mark)
    while sums.came is not None:
        mark = sums.add(mark)
    for e in range(3, experts):
        stacks, mark = finish(e, mark)
    expert_up_out, expert_down_out = stacks
    mark = attn_sum.rest(mark)
    *qkv_parts, out_out = last_add([attn_sum.keep, attn_sum.came], (False, False, False, True), deps=mark)
    lanes = d // (dp * tensor)
    begin = (me * tensor + t) * lanes
    small = lax.dynamic_slice_in_dim(sums.v, begin, lanes, 1)
    return (layer_output, input_grad, small[16], small[17], jnp.stack(qkv_parts, axis=1), out_out, small[8], small[9], up_out, down_out,
            expert_up_out, expert_down_out, small[0:experts].T, small[experts:experts + 2].T)


def solution(mesh):
    both = ("dp", "tensor")
    in_specs = (P(both, None), P(both, None), P("dp", None), P("dp"), P(), P(), P(None, None, "tensor"), P("tensor", None), P(), P(),
                P(None, "tensor"), P("tensor", None), P(None, None, "tensor"), P(None, "tensor", None), P(), P())
    out_specs = (P(both, None), P(both, None), P(both), P(both), P("dp", None, "tensor"), P("tensor", "dp"), P(both), P(both),
                 P("dp", "tensor"), P("tensor", "dp"), P(None, "dp", "tensor"), P(None, "tensor", "dp"), P(both, None), P(both, None))
    return jax.shard_map(shards, mesh=mesh, in_specs=in_specs, out_specs=out_specs, check_vma=False)
```

```python
from functools import partial
import jax, jax.numpy as jnp
from jax import lax
from jax.experimental import pallas as pl
from jax.experimental.pallas import tpu as pltpu
from jax.sharding import PartitionSpec as P

BF = jnp.bfloat16
F32 = jnp.float32
TILE_DENSE = 512
TILE_EXPERT = 304
PIECE = 16
SMALL = pl.CostEstimate(flops=0, bytes_accessed=0, transcendentals=0)
VMEM = 60 * 1024 * 1024
ANY = pl.BlockSpec(memory_space=pltpu.HBM)
SMEM = pl.BlockSpec(memory_space=pltpu.SMEM)


def dot(a, b, ca, cb):
    return lax.dot_general(a, b, (((ca,), (cb,)), ((), ())), preferred_element_type=F32)


def slot_of(value, order):
    out = jnp.int32(0)
    for k, bit in enumerate(order):
        out = out | (((value >> bit) & 1) << (len(order) - 1 - k))
    return out


def skip(kernel, scalars, deps):
    return lambda *refs: kernel(*refs[:scalars], *refs[scalars + deps:])


def lane_softmax(logits, first, last):
    lane = lax.broadcasted_iota(jnp.int32, logits.shape, 1)
    inside = (lane >= first) & (lane < last)
    masked = jnp.where(inside, logits, -1e30)
    top = jnp.max(masked, axis=1, keepdims=True)
    e = jnp.where(inside, jnp.exp(masked - top), 0.0)
    return e / jnp.sum(e, axis=1, keepdims=True)


def pick_lane(v, index):
    lane = lax.broadcasted_iota(jnp.int32, v.shape, 1)
    return jnp.sum(jnp.where(lane == index, v, 0.0), axis=1, keepdims=True)


def gelu_parts(pre):
    phi = 0.5 * (1.0 + lax.erf(pre * 0.7071067811865476))
    pdf = jnp.exp(pre * pre * -0.5) * 0.3989422804014327
    return pre * phi, phi + pre * pdf


def ffn_tile(lanes, rm, xt, dyt, coef_of, up_w, dn_w, UA, DA, ready):
    logits = dot(xt, rm[...], 1, 0)
    mixing = lane_softmax(logits, lanes, lanes + 2)
    coef = coef_of(logits, mixing)
    pre = dot(xt, up_w[...], 1, 0)
    g = dot(dyt, dn_w[...], 1, 1)
    hid, dg = gelu_parts(pre)
    hid = hid.astype(BF)
    dots = jnp.sum(hid.astype(F32) * g, axis=1, keepdims=True)
    pg = (g * dg * coef).astype(BF)
    cot = (dyt.astype(F32) * coef).astype(BF)
    out = dot(hid, dn_w[...], 1, 0) * coef
    rg = dot(pg, up_w[...], 1, 1)
    ready()
    UA[...] += dot(xt, pg, 0, 0)
    DA[...] += dot(cot, hid, 0, 0)
    return dots, out, rg


def stage_grads(ST, UA, DA, me, order, whole):
    bits = len(order)
    blk = UA.shape[0] >> bits

    def body(c, _):
        r = pl.ds(pl.multiple_of(c * blk, blk), blk)
        slot = jnp.where(whole, c, slot_of(c ^ me, order))
        ST[slot, 0] = UA[r, :].astype(BF)
        ST[slot, 1] = DA[r, :].astype(BF)
        return 0
    lax.fori_loop(0, 1 << bits, body, 0)


def dots_rows(dots):
    return jnp.broadcast_to(dots, (dots.shape[0], 128)).T[0:PIECE, :]


def dense_kernel(cfg, me_ref, *refs):
    chunks, rows, tm, lanes, order, first, deps = cfg
    it = iter(refs[deps:])
    take = lambda k: [next(it) for _ in range(k)]
    x_hbm, dy_hbm = take(chunks), take(chunks)
    rm, up_hbm, dn_hbm = take(3)
    base_o, base_r, sums_in = ([], [], []) if first else (take(chunks), take(chunks), take(2))
    out_refs, rg_refs = take(chunks), take(chunks)
    ends = take(2)
    X, DY, UP, DN, UA, DA, OB, RB, DT, OD, xsem, wsem, gsem, osem, dsem = take(15)
    ST, BO, BR, BD, bsem = (None,) * 5 if first else take(5)
    per = rows // tm
    weights = [pltpu.make_async_copy(up_hbm, UP, wsem.at[0]), pltpu.make_async_copy(dn_hbm, DN, wsem.at[1])]
    loads, bases = [], []
    for q in range(chunks):
        sl = pl.ds(q * rows, rows)
        loads.append([pltpu.make_async_copy(x_hbm[q], X.at[sl], xsem.at[q]), pltpu.make_async_copy(dy_hbm[q], DY.at[sl], xsem.at[chunks + q])])
        if not first:
            bases.append([pltpu.make_async_copy(base_o[q], BO.at[sl], bsem.at[q]), pltpu.make_async_copy(base_r[q].at[pl.ds(0, rows)], BR.at[sl], bsem.at[chunks + q]),
                          pltpu.make_async_copy(base_r[q].at[pl.ds(rows, PIECE)], BD.at[q], bsem.at[2 * chunks + q])])
    sums = [] if first else [pltpu.make_async_copy(sums_in[0], UA, gsem.at[0]), pltpu.make_async_copy(sums_in[1], DA, gsem.at[1])]
    for c in loads[0] + weights + sums + [c for q in loads[1:] for c in q] + [c for q in bases for c in q]:
        c.start()
    DT[...] = jnp.zeros_like(DT)
    if first:
        UA[...] = jnp.zeros_like(UA)
        DA[...] = jnp.zeros_like(DA)
    for c in weights:
        c.wait()

    def outs(q, part, slot):
        sl = pl.ds(part * tm, tm)
        return [pltpu.make_async_copy(OB.at[slot], out_refs[q].at[sl], osem.at[0, slot]),
                pltpu.make_async_copy(RB.at[slot], rg_refs[q].at[sl], osem.at[1, slot])]

    def one(i, _):
        slot = i % 2
        sl = pl.ds(pl.multiple_of(i * tm, tm), tm)
        for q in range(chunks):
            @pl.when(i == q * per)
            def _(q=q):
                for c in loads[q]:
                    c.wait()

        def ready():
            if not first:
                @pl.when(i == 0)
                def _():
                    for c in sums:
                        c.wait()
        dots, out, rg = ffn_tile(lanes, rm, X[sl, :], DY[sl, :], lambda l, m: pick_lane(m, lanes), UP, DN, UA, DA, ready)
        lines = dots_rows(dots)
        line = lax.broadcasted_iota(jnp.int32, lines.shape, 0)
        for q in range(chunks):
            for part in range(per):
                @pl.when(i == q * per + part)
                def _(q=q, part=part):
                    DT[q, :, part * tm:(part + 1) * tm] = jnp.where(line == 0, lines, 0.0)
        if not first:
            for q in range(chunks):
                @pl.when(i == q * per)
                def _(q=q):
                    for c in bases[q]:
                        c.wait()
            out = out + BO[sl, :].astype(F32)
            rg = rg + BR[sl, :].astype(F32)

        @pl.when(i >= 2)
        def _():
            for c in outs(0, 0, slot):
                c.wait()
        OB[slot] = out.astype(BF)
        RB[slot] = rg.astype(BF)
        for q in range(chunks):
            for part in range(per):
                @pl.when(i == q * per + part)
                def _(q=q, part=part):
                    for c in outs(q, part, slot):
                        c.start()
        return 0
    lax.fori_loop(0, chunks * per, one, 0)
    lines = []
    for q in range(chunks):
        total = DT[q] if first else DT[q] + BD[q].astype(F32)
        OD[q] = total.astype(BF)
        lines.append(pltpu.make_async_copy(OD.at[q], rg_refs[q].at[pl.ds(rows, PIECE)], dsem.at[q]))
    if first:
        last = lines + [pltpu.make_async_copy(UA, ends[0], gsem.at[0]), pltpu.make_async_copy(DA, ends[1], gsem.at[1])]
    else:
        stage_grads(ST, UA, DA, me_ref[0], order, False)
        half = ST.shape[0] // 2
        last = lines + [pltpu.make_async_copy(ST.at[pl.ds(h * half, half)], ends[h], gsem.at[h]) for h in range(2)]
    for c in last:
        c.start()
    for slot in range(min(2, chunks * per)):
        for c in outs(0, 0, slot):
            c.wait()
    for c in last:
        c.wait()


def ffn_dense(me, xs, dys, rm, up, down, lanes, order, base=None, sums=None, deps=()):
    chunks = len(xs)
    rows, d = xs[0].shape
    f = up.shape[1]
    n = chunks * rows
    tm = min(TILE_DENSE, rows)
    first = base is None
    bits = len(order)
    half = 1 << (bits - 1)
    vm = pl.BlockSpec(memory_space=pltpu.VMEM)
    part, lined = jax.ShapeDtypeStruct((rows, d), BF), jax.ShapeDtypeStruct((rows + PIECE, d), BF)
    total = jax.ShapeDtypeStruct((d, f), F32)
    grad = jax.ShapeDtypeStruct((half, 2, d >> bits, f), BF)
    ends = [total] * 2 if first else [grad] * 2
    more = [] if first else list(base[0]) + list(base[1]) + list(sums)
    scratch = [pltpu.VMEM((n, d), BF), pltpu.VMEM((n, d), BF), pltpu.VMEM((d, f), BF), pltpu.VMEM((f, d), BF), pltpu.VMEM((d, f), F32), pltpu.VMEM((d, f), F32),
               pltpu.VMEM((2, tm, d), BF), pltpu.VMEM((2, tm, d), BF), pltpu.VMEM((chunks, PIECE, d), F32), pltpu.VMEM((chunks, PIECE, d), BF),
               pltpu.SemaphoreType.DMA((2 * chunks,)), pltpu.SemaphoreType.DMA((2,)), pltpu.SemaphoreType.DMA((2,)), pltpu.SemaphoreType.DMA((2, 2)), pltpu.SemaphoreType.DMA((chunks,))]
    if not first:
        scratch += [pltpu.VMEM((2 * half, 2, d >> bits, f), BF), pltpu.VMEM((n, d), BF), pltpu.VMEM((n, d), BF), pltpu.VMEM((chunks, PIECE, d), BF), pltpu.SemaphoreType.DMA((3 * chunks,))]
    res = pl.pallas_call(
        partial(dense_kernel, (chunks, rows, tm, lanes, order, first, len(deps))),
        name="ffn_dense",
        out_shape=[part] * chunks + [lined] * chunks + ends,
        in_specs=[SMEM] + [ANY] * (len(deps) + 2 * chunks) + [vm] + [ANY] * (2 + len(more)),
        out_specs=[ANY] * (2 * chunks + len(ends)),
        scratch_shapes=scratch,
        cost_estimate=SMALL,
        compiler_params=pltpu.CompilerParams(vmem_limit_bytes=VMEM),
    )(me, *deps, *xs, *dys, rm, up, down, *more)
    return res[:chunks], res[chunks:2 * chunks], res[2 * chunks:]


def expert_kernel(cfg, me_ref, blk_ref, bnd_ref, *refs):
    first, count, whole, chunks, rows, d, tm, lanes, order, has, deps = cfg
    n = chunks * rows
    it = iter(refs[deps:])
    take = lambda k: [next(it) for _ in range(k)]
    x_hbm, dy_hbm = take(chunks), take(chunks)
    rm, up_hbm, dn_hbm = take(3)
    based = [q for q in range(chunks) if has[q]]
    base_o, base_r = take(len(based)), take(len(based))
    out_refs, rg_refs = take(chunks), take(chunks)
    entire = [g for g in range(count) if whole[g]]
    halved = [g for g in range(count) if not whole[g]]
    whole_refs, keep_refs, send_refs = take(len(entire)), take(len(halved)), take(len(halved))
    X, DY, UP, DN, UA, DA, ST, XG, DG, VAL, OA, RA, DOT, BD, TR, TL, TH, xsem, wsem, gsem, osem, dsem = it
    half = ST.shape[0] // 2
    pieces = tm // PIECE
    rows_of = [pl.ds(q * rows, rows) for q in range(chunks)]
    copies = []
    for q in range(chunks):
        copies.append(pltpu.make_async_copy(x_hbm[q], X.at[rows_of[q]], xsem.at[q]))
        copies.append(pltpu.make_async_copy(dy_hbm[q], DY.at[rows_of[q]], xsem.at[chunks + q]))
    earlier = []
    for k, q in enumerate(based):
        earlier.append(pltpu.make_async_copy(base_o[k], X.at[rows_of[q]], xsem.at[q]))
        earlier.append(pltpu.make_async_copy(base_r[k].at[pl.ds(0, rows)], DY.at[rows_of[q]], xsem.at[chunks + q]))
        earlier.append(pltpu.make_async_copy(base_r[k].at[pl.ds(rows, PIECE)], BD.at[q], dsem.at[q]))

    def weights(e, slot):
        return [pltpu.make_async_copy(up_hbm.at[first + e], UP.at[slot], wsem.at[slot, 0]),
                pltpu.make_async_copy(dn_hbm.at[first + e], DN.at[slot], wsem.at[slot, 1])]

    def flush(g):
        if whole[g]:
            return [pltpu.make_async_copy(ST, whole_refs[entire.index(g)], gsem.at[0])]
        g = halved.index(g)
        return [pltpu.make_async_copy(ST.at[pl.ds(0, half)], keep_refs[g], gsem.at[0]),
                pltpu.make_async_copy(ST.at[pl.ds(half, half)], send_refs[g], gsem.at[1])]

    for c in copies + weights(0, 0):
        c.start()
    OA[...] = jnp.zeros_like(OA)
    RA[...] = jnp.zeros_like(RA)
    DOT[...] = jnp.zeros_like(DOT)
    iota16 = lax.broadcasted_iota(jnp.int32, (PIECE, 128), 0)

    def one_expert(e, _):
        slot = e % 2
        total = jnp.int32(0)
        for q in range(chunks):
            lo, hi = bnd_ref[blk_ref[q], first + e], bnd_ref[blk_ref[q], first + e + 1]
            p0 = lo // PIECE
            p1 = jnp.where(hi > lo, (hi + PIECE - 1) // PIECE, p0)

            def add(p, _, lo=lo, hi=hi, p0=p0, total=total, q=q):
                k = total + p - p0
                TR[k] = q * rows + p * PIECE
                TL[k] = lo - p * PIECE
                TH[k] = hi - p * PIECE
                return 0
            lax.fori_loop(p0, p1, add, 0)
            total = total + p1 - p0
        tiles = (total + pieces - 1) // pieces

        def pad(k, _):
            TR[k] = 0
            TL[k] = 0
            TH[k] = 0
            return 0
        lax.fori_loop(total, tiles * pieces, pad, 0)
        UA[...] = jnp.zeros_like(UA)
        DA[...] = jnp.zeros_like(DA)

        @pl.when(e == 0)
        def _():
            for c in copies:
                c.wait()
        for c in weights(e, slot):
            c.wait()

        @pl.when(e + 1 < count)
        def _():
            for c in weights(e + 1, 1 - slot):
                c.start()

        def one_tile(i, _):
            base = i * pieces
            for p in range(pieces):
                r = pl.ds(pl.multiple_of(TR[base + p], PIECE), PIECE)
                XG[pl.ds(p * PIECE, PIECE), :] = X[r, :]
                DG[pl.ds(p * PIECE, PIECE), :] = DY[r, :]
                ok = (iota16 >= TL[base + p]) & (iota16 < TH[base + p])
                VAL[pl.ds(p * PIECE, PIECE), :] = jnp.where(ok, 1.0, 0.0)
            valid = VAL[:, 0:1]

            def coef_of(logits, mixing):
                return pick_lane(mixing, lanes + 1) * pick_lane(lane_softmax(logits, 0, lanes), first + e) * valid
            dots, out, rg = ffn_tile(lanes, rm, XG[...], DG[...], coef_of, UP.at[slot], DN.at[slot], UA, DA, lambda: None)
            dots = jnp.broadcast_to(dots * valid, (tm, 128))
            for p in range(pieces):
                r = pl.ds(pl.multiple_of(TR[base + p], PIECE), PIECE)
                s = slice(p * PIECE, (p + 1) * PIECE)
                OA[r, :] += out[s]
                RA[r, :] += rg[s]
                DOT[r, :] += dots[s]
            return 0
        lax.fori_loop(0, tiles, one_tile, 0)

        @pl.when(e == count - 1)
        def _():
            for c in earlier:
                c.start()

        for g in range(count - 1):
            @pl.when(e == g + 1)
            def _(g=g):
                for c in flush(g):
                    c.wait()
        kind = False
        for g in entire:
            kind = kind | (e == g)
        stage_grads(ST, UA, DA, me_ref[0], order, kind)
        for g in range(count):
            @pl.when(e == g)
            def _(g=g):
                for c in flush(g):
                    c.start()
        return 0
    lax.fori_loop(0, count, one_expert, 0)
    for c in earlier:
        c.wait()
    last = []
    step = min(256, rows)
    line = lax.broadcasted_iota(jnp.int32, (PIECE, step), 0)
    for q in range(chunks):
        r = rows_of[q]
        o, g = OA[r, :], RA[r, :]
        if has[q]:
            o, g = o + X[r, :].astype(F32), g + DY[r, :].astype(F32)
        X[r, :] = o.astype(BF)
        DY[r, :] = g.astype(BF)
        if not has[q]:
            BD[q] = jnp.zeros(BD.shape[1:], BF)
        for i in range(rows // step):
            sl = slice(i * step, (i + 1) * step)
            dots = jnp.where(line == 1, DOT[pl.ds(q * rows + i * step, step), :].T[0:PIECE, :], 0.0)
            BD[q, :, sl] = (BD[q, :, sl].astype(F32) + dots).astype(BF)
        last += [pltpu.make_async_copy(X.at[r], out_refs[q], osem.at[0, q]), pltpu.make_async_copy(DY.at[r], rg_refs[q].at[pl.ds(0, rows)], osem.at[1, q]),
                 pltpu.make_async_copy(BD.at[q], rg_refs[q].at[pl.ds(rows, PIECE)], dsem.at[q])]
        for c in last[-3:]:
            c.start()
    for c in last + flush(count - 1):
        c.wait()


def ffn_experts(me, blocks, bounds, xs, dys, rm, up, down, first, count, whole, base, order, deps=()):
    chunks = len(xs)
    rows, d = xs[0].shape
    lanes, _, f = up.shape
    n = chunks * rows
    tm = TILE_EXPERT
    bits = len(order)
    half = 1 << (bits - 1)
    grad, entire = [jax.ShapeDtypeStruct((k * half, 2, d >> bits, f), BF) for k in (1, 2)]
    part, lined = jax.ShapeDtypeStruct((rows, d), BF), jax.ShapeDtypeStruct((rows + PIECE, d), BF)
    table = n // PIECE + chunks * lanes + 2 * tm // PIECE
    vm = pl.BlockSpec(memory_space=pltpu.VMEM)
    has = tuple(b is not None for b in base[0])
    more = [b for k in range(2) for b in base[k] if b is not None]
    res = pl.pallas_call(
        partial(expert_kernel, (first, count, whole, chunks, rows, d, tm, lanes, order, has, len(deps))),
        name="ffn_experts",
        out_shape=[part] * chunks + [lined] * chunks + [entire] * sum(whole) + [grad] * (2 * (count - sum(whole))),
        in_specs=[SMEM] * 3 + [ANY] * (len(deps) + 2 * chunks) + [vm] + [ANY] * (2 + len(more)),
        out_specs=[ANY] * (2 * chunks + 2 * count - sum(whole)),
        scratch_shapes=[
            pltpu.VMEM((n, d), BF), pltpu.VMEM((n, d), BF), pltpu.VMEM((2, d, f), BF), pltpu.VMEM((2, f, d), BF),
            pltpu.VMEM((d, f), F32), pltpu.VMEM((d, f), F32), pltpu.VMEM((2 * half, 2, d >> bits, f), BF),
            pltpu.VMEM((tm, d), BF), pltpu.VMEM((tm, d), BF), pltpu.VMEM((tm, 128), F32),
            pltpu.VMEM((n, d), F32), pltpu.VMEM((n, d), F32), pltpu.VMEM((n, 128), F32), pltpu.VMEM((chunks, PIECE, d), BF),
            pltpu.SMEM((table,), jnp.int32), pltpu.SMEM((table,), jnp.int32), pltpu.SMEM((table,), jnp.int32),
            pltpu.SemaphoreType.DMA((2 * chunks,)), pltpu.SemaphoreType.DMA((2, 2)), pltpu.SemaphoreType.DMA((2,)), pltpu.SemaphoreType.DMA((2, chunks)), pltpu.SemaphoreType.DMA((chunks,)),
        ],
        cost_estimate=SMALL,
        compiler_params=pltpu.CompilerParams(vmem_limit_bytes=VMEM),
    )(me, blocks, bounds, *deps, *xs, *dys, rm, up, down, *more)
    at = 2 * chunks + sum(whole)
    rest = iter(res[at:])
    keep = [next(rest) for g in range(count) if not whole[g]]
    return res[:chunks], res[chunks:2 * chunks], res[2 * chunks:at], keep, list(rest)


def split_add_kernel(deps, *refs):
    ka, kb, ca, cb, keep, send = refs[deps:]
    keep[...] = (ka[...].astype(F32) + ca[...].astype(F32)).astype(BF)
    send[...] = (kb[...].astype(F32) + cb[...].astype(F32)).astype(BF)


def split_add(kept, came, deps=()):
    h, m, blk, f = kept.shape
    near = pl.BlockSpec((1, m, blk, f), lambda i: (i, 0, 0, 0))
    far = pl.BlockSpec((1, m, blk, f), lambda i: (i + h // 2, 0, 0, 0))
    out = jax.ShapeDtypeStruct((h // 2, m, blk, f), BF)
    return pl.pallas_call(
        partial(split_add_kernel, len(deps)),
        name="split_add",
        grid=(h // 2,),
        in_specs=[ANY] * len(deps) + [near, far, near, far],
        out_specs=[near, near],
        out_shape=[out, out],
        cost_estimate=SMALL,
        compiler_params=pltpu.CompilerParams(vmem_limit_bytes=VMEM),
    )(*deps, kept, kept, came, came)


def last_add_kernel(deps, turns, *refs):
    terms = refs[deps:-len(turns)]
    outs = refs[-len(turns):]
    for k, turned in enumerate(turns):
        total = terms[0][0, k].astype(F32)
        for v in terms[1:]:
            total = total + v[0, k].astype(F32)
        outs[k][...] = (total.T if turned else total).reshape(outs[k].shape)


def last_add(terms, turns, place=None, stacks=None, deps=()):
    _, m, blk, f = terms[0].shape
    shapes = [(f, blk) if turned else (blk, f) for turned in turns]
    aliases = {}
    if place is None:
        out_shape = [jax.ShapeDtypeStruct(s, F32) for s in shapes]
        out_specs = [pl.BlockSpec(s, lambda i: (0, 0)) for s in shapes]
    else:
        count, at = place
        out_shape = [jax.ShapeDtypeStruct((count,) + s, F32) for s in shapes]
        out_specs = [pl.BlockSpec((1,) + s, lambda i: (at, 0, 0)) for s in shapes]
        if stacks is not None:
            aliases = {k: k for k in range(m)}
            deps = tuple(stacks) + tuple(deps)
    full = pl.BlockSpec((1, m, blk, f), lambda i: (0, 0, 0, 0))
    return pl.pallas_call(
        partial(last_add_kernel, len(deps), turns),
        name="last_add",
        grid=(1,),
        in_specs=[ANY] * len(deps) + [full] * len(terms),
        out_specs=out_specs,
        out_shape=out_shape,
        input_output_aliases=aliases,
        cost_estimate=SMALL,
        compiler_params=pltpu.CompilerParams(vmem_limit_bytes=VMEM),
    )(*deps, *terms)


def hold(v, deps):
    return pl.pallas_call(
        lambda *refs: None,
        name="hold",
        in_specs=[ANY] * (1 + len(deps)),
        out_specs=ANY,
        out_shape=jax.ShapeDtypeStruct(v.shape, v.dtype),
        input_output_aliases={0: 0},
        cost_estimate=SMALL,
    )(v, *deps)


HD = 64
LANES = 128


def head_part(v, h):
    lane = lax.broadcasted_iota(jnp.int32, v.shape, 1)
    return jnp.where((lane // HD) == h, v, jnp.zeros((), v.dtype))


def masked_scores(st, key_first, query_first, prefix):
    key_pos = key_first + lax.broadcasted_iota(jnp.int32, st.shape, 0)
    query_pos = query_first + lax.broadcasted_iota(jnp.int32, st.shape, 1)
    seen = key_pos <= query_pos
    if prefix is not None:
        seen = seen | (key_pos < prefix)
    return jnp.where(seen, st, -1e30)


def score_block(k2, qm, half, length, prefix):
    mid = length // 2
    if half == 0:
        return masked_scores(dot(k2[0:mid], qm, 1, 1), 0, 0, prefix)
    low = dot(k2[0:mid], qm, 1, 1)
    high = masked_scores(dot(k2[mid:length], qm, 1, 1), mid, mid, None)
    return jnp.concatenate([low, high], 0)


def attn_forward_kernel(length, pieces, aliased, prefix_ref, at_ref, *refs):
    n1_ref = refs[0]
    w_refs = [(r, i) for r, n in zip(refs[1:], pieces) for i in range(n)]
    q_ref, k_ref, v_ref, ctx_ref, lse_ref = refs[1 + len(pieces) + aliased:]
    mid = length // 2
    prefix = prefix_ref[0]
    n1 = n1_ref[...]
    for out, (w, i) in zip((q_ref, k_ref, v_ref), w_refs):
        out[...] = dot(n1, w[i], 1, 0).astype(BF)
    vt = v_ref[...].T
    k2 = k_ref[...]
    for half in range(2):
        rows = pl.ds(half * mid, mid)
        q2 = q_ref[rows, :] * jnp.asarray(HD ** -0.5, BF)
        keys = mid * (half + 1)
        parts = []
        for h in range(2):
            st = score_block(k2, head_part(q2, h), half, length, prefix)
            top = jnp.max(st, axis=0, keepdims=True)
            p = jnp.exp(st - top)
            total = jnp.sum(p, axis=0, keepdims=True)
            c = dot(vt[h * HD:(h + 1) * HD, 0:keys], p.astype(BF), 1, 0)
            parts.append(c / total)
            lse_ref[0, h:h + 1, rows] = top + jnp.log(total)
        ctx_ref[rows, :] = jnp.concatenate(parts, 0).T.astype(BF)


def attn_forward(prefix, at, n1, ws, heads, earlier=(), deps=()):
    length, d = n1.shape
    pairs = ws[0].shape[2] // LANES
    col = pl.BlockSpec((length, LANES), lambda p, _, at_ref: (0, at_ref[p]))
    out = jax.ShapeDtypeStruct((length, heads), BF)
    done = len(earlier)
    skipped = len(deps)
    return pl.pallas_call(
        skip(partial(attn_forward_kernel, length, tuple(w.shape[0] for w in ws), done), 2, skipped),
        name="attn_forward",
        grid_spec=pltpu.PrefetchScalarGridSpec(
            num_scalar_prefetch=2, grid=(pairs,),
            in_specs=[ANY] * skipped + [pl.BlockSpec((length, d), lambda p, *_: (0, 0))]
            + [pl.BlockSpec((w.shape[0], d, LANES), lambda p, *_: (0, 0, p)) for w in ws] + [ANY] * done,
            out_specs=[col] * 4 + [pl.BlockSpec((1, 8, length), lambda p, _, at_ref: (at_ref[p], 0, 0))]),
        out_shape=[out] * 4 + [jax.ShapeDtypeStruct((heads // LANES, 8, length), F32)],
        input_output_aliases={3 + skipped + len(ws) + k: k for k in range(done)},
        cost_estimate=SMALL,
        compiler_params=pltpu.CompilerParams(vmem_limit_bytes=VMEM),
    )(prefix, at, *deps, n1, *ws, *earlier)


def attn_backward_kernel(length, bits, members, based, prefix_ref, me_ref, j_ref, *refs):
    it = iter(refs)
    take = lambda k: [next(it) for _ in range(k)]
    mcs = take(members)
    n1_ref, wo_ref, w_ref, q_ref, k_ref, v_ref, ctx_ref, lse_ref = take(8)
    bases = take(members) if based else []
    ng_refs = take(members)
    grad_ref, NG, MC, DC, DK, DV, DQ, sem = it
    rows_each = length // members
    where = [pl.ds(pl.multiple_of(lax.rem(j_ref[0] + k, members) * rows_each, rows_each), rows_each) for k in range(members)]
    mid = length // 2
    prefix = prefix_ref[0]
    me = me_ref[0]
    pair = pl.program_id(0)
    copies = [pltpu.make_async_copy(mcs[k], MC.at[where[k]], sem.at[k]) for k in range(members)]

    @pl.when(pair == 0)
    def _():
        for c in copies:
            c.start()
        for c in copies:
            c.wait()
    mc = MC[...]
    DC[...] = dot(mc, wo_ref[...], 1, 1).astype(BF)
    k2, v2 = k_ref[...], v_ref[...]
    kt = k2.T
    scale = jnp.asarray(HD ** -0.5, BF)
    for half in range(2):
        rows = pl.ds(half * mid, mid)
        q2 = q_ref[rows, :] * scale
        dc2 = DC[rows, :]
        keys = mid * (half + 1)
        dv = jnp.zeros((keys, LANES), F32)
        dk = jnp.zeros((keys, LANES), F32)
        dq = []
        for h in range(2):
            qm, dcm = head_part(q2, h), head_part(dc2, h)
            st = score_block(k2, qm, half, length, prefix)
            p = jnp.exp(st - lse_ref[0, h:h + 1, rows])
            dv = dv + dot(p.astype(BF), dcm, 1, 0)
            dp = dot(v2[0:keys], dcm, 1, 1)
            ds = (p * (dp - jnp.sum(p * dp, axis=0, keepdims=True))).astype(BF)
            dk = dk + dot(ds, qm, 1, 0)
            dq.append(dot(kt[h * HD:(h + 1) * HD, 0:keys], ds, 1, 0))
        DQ[rows, :] = (jnp.concatenate(dq, 0) * HD ** -0.5).T.astype(BF)
        if half == 0:
            DK[0:mid, :] = dk
            DV[0:mid, :] = dv
        else:
            DK[0:mid, :] += dk[0:mid]
            DV[0:mid, :] += dv[0:mid]
            DK[mid:length, :] = dk[mid:length]
            DV[mid:length, :] = dv[mid:length]
    dq, dk, dv = DQ[...], DK[...].astype(BF), DV[...].astype(BF)
    ng = dot(dq, w_ref[0], 1, 1) + dot(dk, w_ref[1], 1, 1) + dot(dv, w_ref[2], 1, 1)

    @pl.when(pair == 0)
    def _():
        NG[...] = ng

    @pl.when(pair > 0)
    def _():
        NG[...] += ng
    n1 = n1_ref[...]
    grads = [dot(n1, x, 0, 0) for x in (dq, dk, dv)] + [dot(mc, ctx_ref[...], 0, 0)]
    blk = n1.shape[1] >> bits
    for c in range(1 << bits):
        slot = slot_of(jnp.int32(c) ^ me, range(bits))
        for i in range(4):
            grad_ref[slot, i] = grads[i][c * blk:(c + 1) * blk].astype(BF)

    @pl.when(pair == pl.num_programs(0) - 1)
    def _():
        for k in range(members):
            done = NG[where[k], :]
            if based:
                done = done + bases[k][...].astype(F32)
            ng_refs[k][...] = done.astype(BF)


def attn_backward(prefix, me, j, mcs, n1, wo, w, saved, base, bits, deps=()):
    q, k, v, ctx, lse = saved
    length, d = n1.shape
    heads = w.shape[2]
    pairs = heads // LANES
    blk = d >> bits
    members = len(mcs)
    col = pl.BlockSpec((length, LANES), lambda p, *_: (0, p))
    full = pl.BlockSpec((length, d), lambda p, *_: (0, 0))
    part = pl.BlockSpec((length // members, d), lambda p, *_: (0, 0))
    extra = [] if base is None else list(base)
    res = pl.pallas_call(
        skip(partial(attn_backward_kernel, length, bits, members, base is not None), 3, len(deps)),
        name="attn_backward",
        grid_spec=pltpu.PrefetchScalarGridSpec(
            num_scalar_prefetch=3, grid=(pairs,),
            in_specs=[ANY] * (len(deps) + members) + [full, pl.BlockSpec((LANES, d), lambda p, *_: (p, 0)), pl.BlockSpec((3, d, LANES), lambda p, *_: (0, 0, p)),
                      col, col, col, col, pl.BlockSpec((1, 8, length), lambda p, *_: (p, 0, 0))] + [part] * len(extra),
            out_specs=[part] * members + [pl.BlockSpec((1 << bits, 4, blk, LANES), lambda p, *_: (0, 0, 0, p))],
            scratch_shapes=[pltpu.VMEM((length, d), F32), pltpu.VMEM((length, d), BF), pltpu.VMEM((length, LANES), BF),
                            pltpu.VMEM((length, LANES), F32), pltpu.VMEM((length, LANES), F32), pltpu.VMEM((length, LANES), BF),
                            pltpu.SemaphoreType.DMA((members,))]),
        out_shape=[jax.ShapeDtypeStruct((length // members, d), BF)] * members + [jax.ShapeDtypeStruct((1 << bits, 4, blk, heads), BF)],
        cost_estimate=SMALL,
        compiler_params=pltpu.CompilerParams(vmem_limit_bytes=VMEM),
    )(prefix, me, j, *deps, *mcs, n1, wo, w, q, k, v, ctx, lse, *extra)
    return res[:members], res[members]


EPS = 1e-5


def normalise(v):
    centered = v - jnp.mean(v, axis=1, keepdims=True)
    r = lax.rsqrt(jnp.mean(centered * centered, axis=1, keepdims=True) + EPS)
    return centered * r, r


def norm_backward(xhat, r, grad, gain):
    scaled = grad * gain
    return r * (scaled - jnp.mean(scaled, axis=1, keepdims=True) - xhat * jnp.mean(scaled * xhat, axis=1, keepdims=True))


def order_rows(pos, rows_to_slots):
    n = pos.shape[1] if rows_to_slots else pos.shape[0]
    slot = lax.broadcasted_iota(jnp.int32, (n, n), 0 if rows_to_slots else 1)
    return jnp.where(slot == pos, 1.0, 0.0).astype(BF)


def first_norm_kernel(members, j_ref, *refs):
    xs, (gain, shift, dy, pos, out, sorted_dy) = refs[:members], refs[members:]
    for k in range(members):
        @pl.when(pl.program_id(0) == k)
        def _(k=k):
            xhat, _ = normalise(xs[k][...].astype(F32))
            out[...] = (xhat * gain[...] + shift[...]).astype(BF)
            if k == 0:
                sorted_dy[...] = dot(order_rows(pos[...], True), dy[...], 1, 0).astype(BF)


def first_norm(j, xs, gain, shift, dy, pos):
    members = len(xs)
    rows, d = xs[0].shape
    fixed = lambda shape: pl.BlockSpec(shape, lambda p, *_: (0, 0))
    return pl.pallas_call(
        partial(first_norm_kernel, members),
        name="first_norm",
        grid_spec=pltpu.PrefetchScalarGridSpec(
            num_scalar_prefetch=1, grid=(members,),
            in_specs=[fixed((rows, d))] * members + [fixed((1, d))] * 2 + [fixed((rows, d)), fixed((1, rows))],
            out_specs=[pl.BlockSpec((rows, d), lambda p, j_ref: (lax.rem(j_ref[0] + p, members), 0)), fixed((rows, d))]),
        out_shape=[jax.ShapeDtypeStruct((members * rows, d), BF), jax.ShapeDtypeStruct((rows, d), BF)],
        cost_estimate=SMALL,
        compiler_params=pltpu.CompilerParams(vmem_limit_bytes=VMEM),
    )(j, *xs, gain, shift, dy, pos)


def project_kernel(parts, *refs):
    total = dot(refs[0][...], refs[parts][...], 1, 0)
    for i in range(1, parts):
        total = total + dot(refs[i][...], refs[parts + i][...], 1, 0)
    refs[-1][0] = total.astype(BF)


def project(contexts, weights, members):
    parts = len(contexts)
    length, heads = contexts[0].shape
    d = weights[0].shape[1]
    rows = length // members
    return pl.pallas_call(
        partial(project_kernel, parts),
        name="project",
        grid=(members,),
        in_specs=[pl.BlockSpec((rows, heads), lambda p: (p, 0))] * parts + [pl.BlockSpec((heads, d), lambda p: (0, 0))] * parts,
        out_specs=pl.BlockSpec((1, rows, d), lambda p: (p, 0, 0)),
        out_shape=jax.ShapeDtypeStruct((members, rows, d), BF),
        cost_estimate=SMALL,
        compiler_params=pltpu.CompilerParams(vmem_limit_bytes=VMEM),
    )(*contexts, *weights)


def second_norm_kernel(came, x, gain, shift, pos, middle, n2):
    mid = x[...].astype(F32)
    for k in range(came.shape[0]):
        mid = mid + came[k].astype(F32)
    middle[...] = mid
    xhat, _ = normalise(mid)
    normed = (xhat * gain[...] + shift[...]).astype(BF)
    n2[...] = dot(order_rows(pos[...], True), normed, 1, 0).astype(BF)


def second_norm(came, x, gain, shift, pos):
    rows, d = x.shape
    fixed = lambda shape: pl.BlockSpec(shape, lambda p: (0,) * len(shape))
    return pl.pallas_call(
        second_norm_kernel,
        name="second_norm",
        grid=(1,),
        in_specs=[fixed(came.shape), fixed((rows, d)), fixed((1, d)), fixed((1, d)), fixed((1, rows))],
        out_specs=[fixed((rows, d))] * 2,
        out_shape=[jax.ShapeDtypeStruct((rows, d), F32), jax.ShapeDtypeStruct((rows, d), BF)],
        cost_estimate=SMALL,
        compiler_params=pltpu.CompilerParams(vmem_limit_bytes=VMEM),
    )(came, x, gain, shift, pos)


def add_small(a, b, deps):
    def kernel(*refs):
        refs[-1][...] = refs[-3][...] + refs[-2][...]
    full = pl.BlockSpec(memory_space=pltpu.VMEM)
    return pl.pallas_call(kernel, name="add_small", in_specs=[ANY] * len(deps) + [full, full], out_specs=full,
                          out_shape=jax.ShapeDtypeStruct(a.shape, a.dtype), cost_estimate=SMALL)(*deps, a, b)


def hi_lo(v):
    hi = v.astype(BF)
    return hi, (v - hi.astype(F32)).astype(BF)


def middle_backward_kernel(single, bnd_ref, t_ref, *refs):
    it = iter(refs)
    parts = [next(it) for _ in range(single)]
    n2, rm, middle, dy, gain, pos, mg_ref, mc_ref, sums_ref = it
    t = t_ref[0]
    n2v, rmv = n2[...], rm[...]
    rows = n2v.shape[0]
    total = parts[0][0:rows, :].astype(F32)
    lines = parts[0][rows:rows + PIECE, 0:rows].astype(F32)
    for p in parts[1:]:
        total = total + p[0:rows, :].astype(F32)
        lines = lines + p[rows:rows + PIECE, 0:rows].astype(F32)
    dots = jnp.concatenate([lines, jnp.zeros((128 - PIECE, rows), F32)], axis=0).T
    experts = bnd_ref.shape[1] - 1
    logits = dot(n2v, rmv, 1, 0)
    route_prob = lane_softmax(logits, 0, experts)
    mixing = lane_softmax(logits, experts, experts + 2)
    row = lax.broadcasted_iota(jnp.int32, (rows, 1), 0)
    route = jnp.zeros((rows, 1), jnp.int32)
    for e in range(1, experts):
        route = route + (row >= bnd_ref[t, e]).astype(jnp.int32)
    gate = pick_lane(route_prob, route)
    m0, m1 = pick_lane(mixing, experts), pick_lane(mixing, experts + 1)
    dense_dot, expert_dot = dots[:, 0:1], dots[:, 1:2]
    d0, d1 = dense_dot, expert_dot * gate
    inner = m0 * d0 + m1 * d1
    lane = lax.broadcasted_iota(jnp.int32, logits.shape, 1)
    grad = expert_dot * (m1 * gate) * (jnp.where(lane == route, 1.0, 0.0) - route_prob)
    grad = jnp.where(lane < experts, grad, 0.0)
    grad = jnp.where(lane == experts, m0 * (d0 - inner), grad)
    grad = jnp.where(lane == experts + 1, m1 * (d1 - inner), grad)
    hi, lo = hi_lo(grad)
    total = total + dot(hi, rmv, 1, 1) + dot(lo, rmv, 1, 1)
    sums_ref[0:8, :] = (dot(hi.T, n2v, 1, 0) + dot(lo.T, n2v, 1, 0))[0:8]
    g = dot(order_rows(pos[...], False), total.astype(BF), 1, 0)
    xhat, r = normalise(middle[...])
    sums_ref[8:16, :] = jnp.zeros((8, g.shape[1]), F32)
    sums_ref[8:9, :] = jnp.sum(g * xhat, axis=0, keepdims=True)
    sums_ref[9:10, :] = jnp.sum(g, axis=0, keepdims=True)
    mg = dy[...].astype(F32) + norm_backward(xhat, r, g, gain[...])
    mg_ref[...] = mg
    mc_ref[...] = mg.astype(BF)


def middle_backward(bounds, t, parts, n2, rm, middle, dy, gain, pos, deps=()):
    rows, d = n2.shape
    fixed = lambda shape: pl.BlockSpec(shape, lambda p, *_: (0, 0))
    big = fixed((rows, d))
    return pl.pallas_call(
        skip(partial(middle_backward_kernel, len(parts)), 2, len(deps)),
        name="middle_backward",
        grid_spec=pltpu.PrefetchScalarGridSpec(
            num_scalar_prefetch=2, grid=(1,),
            in_specs=[ANY] * len(deps) + [fixed((rows + PIECE, d))] * len(parts)
            + [big, fixed((d, 128)), big, big, fixed((1, d)), fixed((rows, 1))],
            out_specs=[big, big, fixed((16, d))]),
        out_shape=[jax.ShapeDtypeStruct((rows, d), F32), jax.ShapeDtypeStruct((rows, d), BF), jax.ShapeDtypeStruct((16, d), F32)],
        cost_estimate=SMALL,
        compiler_params=pltpu.CompilerParams(vmem_limit_bytes=VMEM),
    )(bounds, t, *deps, *parts, n2, rm, middle, dy, gain, pos)


def layer_out_kernel(*refs):
    parts, (middle, pos, out) = refs[:-3], refs[-3:]
    total = parts[0][...].astype(F32)
    for p in parts[1:]:
        total = total + p[...].astype(F32)
    hi, lo = hi_lo(total)
    move = order_rows(pos[...], False)
    out[...] = (middle[...] + dot(move, hi, 1, 0) + dot(move, lo, 1, 0)).astype(BF)


def layer_out(parts, middle, pos, deps=()):
    rows, d = middle.shape
    big = pl.BlockSpec((rows, d), lambda p: (0, 0))
    return pl.pallas_call(
        skip(layer_out_kernel, 0, len(deps)),
        name="layer_out",
        grid=(1,),
        in_specs=[ANY] * len(deps) + [big] * (len(parts) + 1) + [pl.BlockSpec((rows, 1), lambda p: (0, 0))],
        out_specs=big,
        out_shape=jax.ShapeDtypeStruct((rows, d), BF),
        cost_estimate=SMALL,
        compiler_params=pltpu.CompilerParams(vmem_limit_bytes=VMEM),
    )(*deps, *parts, middle, pos)


def add_parts_kernel(*refs):
    total = refs[0][...].astype(F32)
    for p in refs[1:-1]:
        total = total + p[...].astype(F32)
    refs[-1][...] = total.astype(BF)


def add_parts(parts, deps=()):
    rows, d = parts[0].shape
    tile = pl.BlockSpec((rows, d), lambda p: (p, 0))
    return pl.pallas_call(
        skip(add_parts_kernel, 0, len(deps)),
        name="add_parts",
        grid=(1,),
        in_specs=[ANY] * len(deps) + [tile] * len(parts),
        out_specs=tile,
        out_shape=jax.ShapeDtypeStruct((rows, d), BF),
        cost_estimate=SMALL,
        compiler_params=pltpu.CompilerParams(vmem_limit_bytes=VMEM),
    )(*deps, *parts)


def input_backward_kernel(count, *refs):
    parts = refs[:count]
    x, mg, gain, out, sums = refs[count:]
    g = parts[0][...].astype(F32)
    for p in parts[1:]:
        g = g + p[...].astype(F32)
    xhat, r = normalise(x[...].astype(F32))
    sums[...] = jnp.zeros_like(sums)
    sums[0:1, :] = jnp.sum(g * xhat, axis=0, keepdims=True)
    sums[1:2, :] = jnp.sum(g, axis=0, keepdims=True)
    out[...] = mg[...] + norm_backward(xhat, r, g, gain[...])


def input_backward(parts, x, mg, gain, deps=()):
    rows, d = x.shape
    fixed = lambda shape: pl.BlockSpec(shape, lambda p: (0, 0))
    big = fixed((rows, d))
    return pl.pallas_call(
        skip(partial(input_backward_kernel, len(parts)), 0, len(deps)),
        name="input_backward",
        grid=(1,),
        in_specs=[ANY] * len(deps) + [big] * (len(parts) + 2) + [fixed((1, d))],
        out_specs=[big, fixed((8, d))],
        out_shape=[jax.ShapeDtypeStruct((rows, d), F32), jax.ShapeDtypeStruct((8, d), F32)],
        cost_estimate=SMALL,
        compiler_params=pltpu.CompilerParams(vmem_limit_bytes=VMEM),
    )(*deps, *parts, x, mg, gain)


class Everywhere:
    def __init__(self, v):
        self.v = v
        bits = {axis: lax.axis_size(axis).bit_length() - 1 for axis in ("tensor", "dp")}
        self.hops = [("tensor", 1 << b) for b in range(bits["tensor"])] + [("dp", 1 << b) for b in range(bits["dp"])]
        self.launch()

    def launch(self):
        if self.hops:
            axis, bit = self.hops.pop(0)
            self.came = lax.ppermute(self.v, axis, [(i, i ^ bit) for i in range(lax.axis_size(axis))])
        else:
            self.came = None

    def add(self, mark):
        if self.came is None:
            return mark
        self.v = add_small(self.v, self.came, mark)
        self.launch()
        return (self.v,)


def over_dp(v, bit):
    return lax.ppermute(v, "dp", [(i, i ^ (1 << bit)) for i in range(lax.axis_size("dp"))])


def shards(inputs, cotangent, routes, prefixes, gain_one, shift_one, qkv_weight, out_weight, gain_two, shift_two,
           up_weight, down_weight, expert_up, expert_down, router_weight, mix_weight):
    rows, d = inputs.shape
    tensor = lax.axis_size("tensor")
    dp = lax.axis_size("dp")
    bits = dp.bit_length() - 1
    seqs = prefixes.shape[0]
    members = tensor // seqs
    experts = expert_up.shape[0]
    heads = qkv_weight.shape[2]
    pairs = heads // LANES
    t = lax.axis_index("tensor")
    s, j = t // members, t % members
    me = lax.axis_index("dp").astype(jnp.int32)
    me1, j1, t1 = me.reshape(1), j.astype(jnp.int32).reshape(1), t.astype(jnp.int32).reshape(1)
    place = lambda a, b: (a % seqs) * members + b % members
    everyone = [(a, b) for a in range(seqs) for b in range(members)]

    def from_member(v, k):
        return lax.ppermute(v, "tensor", [(place(a, b), place(a, b - k)) for a, b in everyone])

    def from_sequence(v, k):
        return lax.ppermute(v, "tensor", [(place(a, b), place(a - k, b)) for a, b in everyone])

    def to_member(v, k):
        return from_member(v, -k)

    def to_sequence(v, k):
        return from_sequence(v, -k)

    route_blocks = routes.reshape(tensor, rows)
    bounds = jnp.stack([jnp.sum((route_blocks < e).astype(jnp.int32), axis=1) for e in range(experts + 1)], axis=1)
    key_col = lax.dynamic_slice_in_dim(routes, t * rows, rows, 0) * rows + jnp.arange(rows, dtype=jnp.int32)[:, None]
    key_row = key_col.reshape(1, rows)
    pos_row = jnp.sum((key_col < key_row).astype(jnp.int32), axis=0, keepdims=True)
    pos_col = jnp.sum((key_row < key_col).astype(jnp.int32), axis=1, keepdims=True)
    chunk = [(dj, ds) for dj in range(members) for ds in range(seqs)]
    blocks = jnp.stack([((s + ds) % seqs) * members + (j + dj) % members for dj, ds in chunk]).astype(jnp.int32)
    near = [q for q, (dj, ds) in enumerate(chunk) if ds == 0]
    far = [q for q, (dj, ds) in enumerate(chunk) if ds > 0]

    xs = [inputs] + [from_member(inputs, k) for k in range(1, members)]
    flip = me & 1
    relay = pairs % 2 == 0 and dp > 1
    w_own = jnp.transpose(qkv_weight, (1, 0, 2))
    fetched = []
    for ds in range(1, seqs):
        if relay:
            half = lax.dynamic_slice_in_dim(qkv_weight, flip * (heads // 2), heads // 2, 2)
            fetched.append([from_sequence(jnp.transpose(half[:, a:b], (1, 0, 2)), ds) for a, b in ((0, 2), (2, 3))])
        else:
            fetched.append([from_sequence(w_own, ds)])
    wo_all = [out_weight] + [from_sequence(out_weight, ds) for ds in range(1, seqs)]
    gain_one, shift_one, gain_two, shift_two = [v.reshape(1, d) for v in (gain_one, shift_one, gain_two, shift_two)]
    prefix = lax.dynamic_slice_in_dim(prefixes, s, 1)
    rm = jnp.concatenate([router_weight, mix_weight, jnp.zeros((d, LANES - experts - 2), BF)], axis=1)
    n1, dys = first_norm(j1, xs, gain_one, shift_one, cotangent, pos_row)
    columns = jnp.arange(pairs, dtype=jnp.int32)
    pieces = [[] for _ in fetched]
    fence = (n1,)
    if relay:
        for k, got in enumerate(fetched):
            held = hold(got[0], (n1,))
            pieces[k] = [[held], [over_dp(held, 0)]]
            fence += (held,)
    saved = [attn_forward(prefix, columns, n1, [w_own], heads, deps=fence[1:] + (rm,))]
    if relay:
        for k, got in enumerate(fetched):
            held = hold(got[1], (saved[0][4],))
            pieces[k][0].append(held)
            pieces[k][1].append(over_dp(held, 0))
    else:
        pieces = [[got] for got in fetched]
    w_all = [w_own]
    for halves in pieces:
        part = ()
        for k, ws in enumerate(halves):
            at = (columns + (flip ^ k) * (pairs // 2))[:pairs // 2] if relay else columns
            part = attn_forward(prefix, at, n1, ws, heads, part, deps=() if part else (saved[-1][4],))
        saved.append(part)
        whole = [jnp.concatenate(ws, axis=0) for ws in halves]
        if relay:
            whole = [jnp.where(flip == 0, jnp.concatenate(whole, axis=2), jnp.concatenate(whole[::-1], axis=2))]
        w_all.append(whole[0])
    contexts = [v[3] for v in saved]

    def spread(mine):
        out = list(mine)
        for k in range(1, members):
            out += [from_member(m, k) for m in mine]
        return out

    dy_mine = [dys] + [from_sequence(dys, ds) for ds in range(1, seqs)]
    dy_near = [dys] + [from_member(dys, k) for k in range(1, members)]
    sent = project(contexts, wo_all, members)
    came = lax.all_to_all(sent, "tensor", 0, 0, axis_index_groups=[[place(a, b) for b in range(members)] for a in range(seqs)], tiled=True)
    middle, n2 = second_norm(came, inputs, gain_two, shift_two, pos_row)
    n2_mine = [n2] + [from_sequence(n2, ds) for ds in range(1, seqs)]
    n2_near = [n2] + [from_member(n2, k) for k in range(1, members)]

    straight = tuple(range(bits))
    pick = lambda v, which: [v[q] for q in which]
    out_a, rg_a, sums = ffn_dense(me1, n2_near, dy_near, rm, up_weight, down_weight, experts, straight, deps=tuple(dy_mine[1:]))
    n2_all, dy_all = [], []
    n2_far, dy_far = [[hold(v, (out_a[0],)) for v in mine[1:]] for mine in (n2_mine, dy_mine)]
    for k in range(members):
        n2_all += [n2_near[k]] + [from_member(v, k) if k else v for v in n2_far]
        dy_all += [dy_near[k]] + [from_member(v, k) if k else v for v in dy_far]
    base = [[None] * tensor, [None] * tensor]
    for k, q in enumerate(near):
        base[0][q], base[1][q] = out_a[k], rg_a[k]
    by_scatter = [e == 0 for e in range(experts)]
    out_e, rg_e, whole, keep_e, send_e = ffn_experts(me1, blocks, bounds, n2_all, dy_all, rm, expert_up, expert_down, 0, 1, (True,), base, straight)
    out_e, rg_e, whole = list(out_e), list(rg_e), list(whole)
    out_b, rg_b, ends = ffn_dense(me1, pick(n2_all, far), pick(dy_all, far), rm, up_weight, down_weight, experts, straight,
                                  (pick(out_e, far), pick(rg_e, far)), sums)
    for k, q in enumerate(far):
        out_e[q], rg_e[q] = out_b[k], rg_b[k]
    if experts > 1:
        out_e, rg_e, entire, keep_e, send_e = ffn_experts(me1, blocks, bounds, n2_all, dy_all, rm, expert_up, expert_down, 1, experts - 1, tuple(by_scatter[1:]), (out_e, rg_e), straight)
        whole += list(entire)

    index = {c: q for q, c in enumerate(chunk)}
    def to_owner(parts):
        mine = [[parts[index[0, ds]]] + [to_member(parts[index[k, ds]], k) for k in range(1, members)] for ds in range(seqs)]
        return mine[0], mine[1:]

    def onward(terms, deps):
        sums = [add_parts(v, deps) for v in terms]
        return [to_sequence(v, ds + 1) for ds, v in enumerate(sums)], sums

    class Halving:
        def __init__(self, keep, send, order):
            self.keep, self.send, self.order, self.at = keep, send, order, 0

        def launch(self, deps=()):
            if deps:
                self.send = hold(self.send, deps)
            self.came = over_dp(self.send, self.order[self.at])
            self.at += 1

        def add(self, mark):
            self.keep, self.send = split_add(self.keep, self.came, mark)
            self.launch()
            return (self.send,)

        def rest(self, mark):
            while self.at < bits:
                mark = self.add(mark)
            return mark

    scattered = []
    for v in whole:
        flat = lax.psum_scatter(v.reshape(-1, v.shape[-1]), "dp", scatter_dimension=0, tiled=True)
        scattered.append(flat.reshape((1,) + v.shape[1:]))

    halvings = [Halving(keep, send, straight) for keep, send in zip(keep_e, send_e)]
    dense_sum = Halving(ends[0], ends[1], straight)
    sum_of = dict(enumerate(scattered + halvings))
    rg_near, rg_far = to_owner(rg_e)
    for v in [dense_sum] + halvings[:2]:
        v.launch()
    mark = dense_sum.add((out_e[0],))
    came_far, terms = onward(rg_far, mark)
    mark = tuple(terms[:1]) + tuple(w_all[1:])
    mg, mc, sums_two = middle_backward(bounds, t1, rg_near + came_far, n2, rm, middle, cotangent, gain_two, pos_col, mark)
    mcs = [mc] + [from_member(mc, k) for k in range(1, members)]
    mark = (mc,)
    ngs = None
    grads = [None] * seqs
    for ds in list(range(1, seqs)) + [0]:
        ngs, grads[ds] = attn_backward(prefix, me1, j1, mcs, n1, wo_all[ds], w_all[ds], saved[ds], ngs, bits, mark)
        mark = (grads[ds],)
        if ds == 1 or seqs == 1:
            for v in halvings[2:]:
                v.launch(mark)
            mark = dense_sum.add(mark)
            for v in halvings[:1]:
                mark = v.add(mark)
    moved = [to_sequence(grads[ds], ds) for ds in range(1, seqs)]
    ng_parts = [ngs[0]] + [to_member(ngs[k], k) for k in range(1, members)]
    mark = dense_sum.rest(mark)
    up_out, down_out = last_add([dense_sum.keep, dense_sum.came], (False, True), deps=mark)
    mark = (up_out,)
    for v in halvings[1:2]:
        mark = v.add(mark)
    input_grad, sums_one = input_backward(ng_parts, inputs, mg, gain_one, mark)
    mark = (sums_one,)
    sums = Everywhere(jnp.concatenate([sums_two, sums_one], axis=0))
    stacks = None

    def finish(e, mark):
        if by_scatter[e]:
            terms = [sum_of[e]]
        else:
            mark = sum_of[e].rest(mark)
            terms = [sum_of[e].keep, sum_of[e].came]
        done = last_add(terms, (False, True), (experts, e), stacks, mark)
        return done, (done[1],)

    keep = grads[0]
    for v in moved[:-1]:
        keep = (keep.astype(F32) + v.astype(F32)).astype(BF)
    if moved:
        keep, send = split_add(keep, moved[-1], mark)
        mark = (send,)
    else:
        keep, send = keep[:dp // 2], keep[dp // 2:]
    attn_sum = Halving(keep, send, straight)
    attn_sum.launch()
    for v in halvings[:1]:
        mark = v.add(mark)
    mark = sums.add(mark)
    stacks, mark = finish(0, mark)
    for v in halvings[1:2]:
        mark = v.add(mark)
    out_near, out_far = to_owner([hold(v, mark) for v in out_e])
    out_came, terms = onward(out_far, mark)
    mark = tuple(terms[:1]) or mark
    if experts > 1:
        stacks, mark = finish(1, mark)
    for v in halvings[2:]:
        mark = v.add(mark)
    layer_output = layer_out(out_near + out_came, middle, pos_col, mark)
    mark = sums.add((layer_output,))
    mark = attn_sum.add(mark)
    if experts > 2:
        stacks, mark = finish(2, mark)
    for v in halvings[2:]:
        mark = v.add(mark)
    mark = attn_sum.add(mark)
    mark = sums.add(mark)
    mark = sums.add(mark)
    for e in range(3, experts):
        stacks, mark = finish(e, mark)
    expert_up_out, expert_down_out = stacks
    while sums.came is not None:
        mark = sums.add(mark)
    mark = attn_sum.rest(mark)
    *qkv_parts, out_out = last_add([attn_sum.keep, attn_sum.came], (False, False, False, True), deps=mark)
    lanes = d // (dp * tensor)
    begin = (me * tensor + t) * lanes
    small = lax.dynamic_slice_in_dim(sums.v, begin, lanes, 1)
    return (layer_output, input_grad, small[16], small[17], jnp.stack(qkv_parts, axis=1), out_out, small[8], small[9], up_out, down_out,
            expert_up_out, expert_down_out, small[0:experts].T, small[experts:experts + 2].T)


def solution(mesh):
    both = ("dp", "tensor")
    in_specs = (P(both, None), P(both, None), P("dp", None), P("dp"), P(), P(), P(None, None, "tensor"), P("tensor", None), P(), P(),
                P(None, "tensor"), P("tensor", None), P(None, None, "tensor"), P(None, "tensor", None), P(), P())
    out_specs = (P(both, None), P(both, None), P(both), P(both), P("dp", None, "tensor"), P("tensor", "dp"), P(both), P(both),
                 P("dp", "tensor"), P("tensor", "dp"), P(None, "dp", "tensor"), P(None, "tensor", "dp"), P(both, None), P(both, None))
    return jax.shard_map(shards, mesh=mesh, in_specs=in_specs, out_specs=out_specs, check_vma=False)
```

```python
from functools import partial
import jax, jax.numpy as jnp
from jax import lax
from jax.experimental import pallas as pl
from jax.experimental.pallas import tpu as pltpu
from jax.sharding import PartitionSpec as P

BF = jnp.bfloat16
F32 = jnp.float32
TILE_DENSE = 512
TILE_EXPERT = 304
PIECE = 16
SMALL = pl.CostEstimate(flops=0, bytes_accessed=0, transcendentals=0)
VMEM = 60 * 1024 * 1024
ANY = pl.BlockSpec(memory_space=pltpu.HBM)
SMEM = pl.BlockSpec(memory_space=pltpu.SMEM)


def dot(a, b, ca, cb):
    return lax.dot_general(a, b, (((ca,), (cb,)), ((), ())), preferred_element_type=F32)


def slot_of(value, order):
    out = jnp.int32(0)
    for k, bit in enumerate(order):
        out = out | (((value >> bit) & 1) << (len(order) - 1 - k))
    return out


def skip(kernel, scalars, deps):
    return lambda *refs: kernel(*refs[:scalars], *refs[scalars + deps:])


def lane_softmax(logits, first, last):
    lane = lax.broadcasted_iota(jnp.int32, logits.shape, 1)
    inside = (lane >= first) & (lane < last)
    masked = jnp.where(inside, logits, -1e30)
    top = jnp.max(masked, axis=1, keepdims=True)
    e = jnp.where(inside, jnp.exp(masked - top), 0.0)
    return e / jnp.sum(e, axis=1, keepdims=True)


def pick_lane(v, index):
    lane = lax.broadcasted_iota(jnp.int32, v.shape, 1)
    return jnp.sum(jnp.where(lane == index, v, 0.0), axis=1, keepdims=True)


def gelu_parts(pre):
    phi = 0.5 * (1.0 + lax.erf(pre * 0.7071067811865476))
    pdf = jnp.exp(pre * pre * -0.5) * 0.3989422804014327
    return pre * phi, phi + pre * pdf


def ffn_tile(lanes, rm, xt, dyt, coef_of, up_w, dn_w, UA, DA, ready):
    logits = dot(xt, rm[...], 1, 0)
    mixing = lane_softmax(logits, lanes, lanes + 2)
    coef = coef_of(logits, mixing)
    pre = dot(xt, up_w[...], 1, 0)
    g = dot(dyt, dn_w[...], 1, 1)
    hid, dg = gelu_parts(pre)
    hid = hid.astype(BF)
    dots = jnp.sum(hid.astype(F32) * g, axis=1, keepdims=True)
    pg = (g * dg * coef).astype(BF)
    cot = (dyt.astype(F32) * coef).astype(BF)
    out = dot(hid, dn_w[...], 1, 0) * coef
    rg = dot(pg, up_w[...], 1, 1)
    ready()
    UA[...] += dot(xt, pg, 0, 0)
    DA[...] += dot(cot, hid, 0, 0)
    return dots, out, rg


def stage_grads(ST, UA, DA, me, order, whole):
    bits = len(order)
    blk = UA.shape[0] >> bits

    def body(c, _):
        r = pl.ds(pl.multiple_of(c * blk, blk), blk)
        slot = jnp.where(whole, c, slot_of(c ^ me, order))
        ST[slot, 0] = UA[r, :].astype(BF)
        ST[slot, 1] = DA[r, :].astype(BF)
        return 0
    lax.fori_loop(0, 1 << bits, body, 0)


def dots_rows(dots):
    return jnp.broadcast_to(dots, (dots.shape[0], 128)).T[0:PIECE, :]


def dense_kernel(cfg, me_ref, *refs):
    chunks, rows, tm, lanes, order, first, deps = cfg
    it = iter(refs[deps:])
    take = lambda k: [next(it) for _ in range(k)]
    x_hbm, dy_hbm = take(chunks), take(chunks)
    rm, up_hbm, dn_hbm = take(3)
    base_o, base_r, sums_in = ([], [], []) if first else (take(chunks), take(chunks), take(2))
    out_refs, rg_refs = take(chunks), take(chunks)
    ends = take(2)
    X, DY, UP, DN, UA, DA, OB, RB, DT, OD, xsem, wsem, gsem, osem, dsem = take(15)
    ST, BO, BR, BD, bsem = (None,) * 5 if first else take(5)
    per = rows // tm
    weights = [pltpu.make_async_copy(up_hbm, UP, wsem.at[0]), pltpu.make_async_copy(dn_hbm, DN, wsem.at[1])]
    loads, bases = [], []
    for q in range(chunks):
        sl = pl.ds(q * rows, rows)
        loads.append([pltpu.make_async_copy(x_hbm[q], X.at[sl], xsem.at[q]), pltpu.make_async_copy(dy_hbm[q], DY.at[sl], xsem.at[chunks + q])])
        if not first:
            bases.append([pltpu.make_async_copy(base_o[q], BO.at[sl], bsem.at[q]), pltpu.make_async_copy(base_r[q].at[pl.ds(0, rows)], BR.at[sl], bsem.at[chunks + q]),
                          pltpu.make_async_copy(base_r[q].at[pl.ds(rows, PIECE)], BD.at[q], bsem.at[2 * chunks + q])])
    sums = [] if first else [pltpu.make_async_copy(sums_in[0], UA, gsem.at[0]), pltpu.make_async_copy(sums_in[1], DA, gsem.at[1])]
    for c in loads[0] + weights + sums + [c for q in loads[1:] for c in q] + [c for q in bases for c in q]:
        c.start()
    DT[...] = jnp.zeros_like(DT)
    if first:
        UA[...] = jnp.zeros_like(UA)
        DA[...] = jnp.zeros_like(DA)
    for c in weights:
        c.wait()

    def outs(q, part, slot):
        sl = pl.ds(part * tm, tm)
        return [pltpu.make_async_copy(OB.at[slot], out_refs[q].at[sl], osem.at[0, slot]),
                pltpu.make_async_copy(RB.at[slot], rg_refs[q].at[sl], osem.at[1, slot])]

    def one(i, _):
        slot = i % 2
        sl = pl.ds(pl.multiple_of(i * tm, tm), tm)
        for q in range(chunks):
            @pl.when(i == q * per)
            def _(q=q):
                for c in loads[q]:
                    c.wait()

        def ready():
            if not first:
                @pl.when(i == 0)
                def _():
                    for c in sums:
                        c.wait()
        dots, out, rg = ffn_tile(lanes, rm, X[sl, :], DY[sl, :], lambda l, m: pick_lane(m, lanes), UP, DN, UA, DA, ready)
        lines = dots_rows(dots)
        line = lax.broadcasted_iota(jnp.int32, lines.shape, 0)
        for q in range(chunks):
            for part in range(per):
                @pl.when(i == q * per + part)
                def _(q=q, part=part):
                    DT[q, :, part * tm:(part + 1) * tm] = jnp.where(line == 0, lines, 0.0)
        if not first:
            for q in range(chunks):
                @pl.when(i == q * per)
                def _(q=q):
                    for c in bases[q]:
                        c.wait()
            out = out + BO[sl, :].astype(F32)
            rg = rg + BR[sl, :].astype(F32)

        @pl.when(i >= 2)
        def _():
            for c in outs(0, 0, slot):
                c.wait()
        OB[slot] = out.astype(BF)
        RB[slot] = rg.astype(BF)
        for q in range(chunks):
            for part in range(per):
                @pl.when(i == q * per + part)
                def _(q=q, part=part):
                    for c in outs(q, part, slot):
                        c.start()
        return 0
    lax.fori_loop(0, chunks * per, one, 0)
    lines = []
    for q in range(chunks):
        total = DT[q] if first else DT[q] + BD[q].astype(F32)
        OD[q] = total.astype(BF)
        lines.append(pltpu.make_async_copy(OD.at[q], rg_refs[q].at[pl.ds(rows, PIECE)], dsem.at[q]))
    if first:
        last = lines + [pltpu.make_async_copy(UA, ends[0], gsem.at[0]), pltpu.make_async_copy(DA, ends[1], gsem.at[1])]
    else:
        stage_grads(ST, UA, DA, me_ref[0], order, False)
        half = ST.shape[0] // 2
        last = lines + [pltpu.make_async_copy(ST.at[pl.ds(h * half, half)], ends[h], gsem.at[h]) for h in range(2)]
    for c in last:
        c.start()
    for slot in range(min(2, chunks * per)):
        for c in outs(0, 0, slot):
            c.wait()
    for c in last:
        c.wait()


def ffn_dense(me, xs, dys, rm, up, down, lanes, order, base=None, sums=None, deps=()):
    chunks = len(xs)
    rows, d = xs[0].shape
    f = up.shape[1]
    n = chunks * rows
    tm = min(TILE_DENSE, rows)
    first = base is None
    bits = len(order)
    half = 1 << (bits - 1)
    vm = pl.BlockSpec(memory_space=pltpu.VMEM)
    part, lined = jax.ShapeDtypeStruct((rows, d), BF), jax.ShapeDtypeStruct((rows + PIECE, d), BF)
    total = jax.ShapeDtypeStruct((d, f), F32)
    grad = jax.ShapeDtypeStruct((half, 2, d >> bits, f), BF)
    ends = [total] * 2 if first else [grad] * 2
    more = [] if first else list(base[0]) + list(base[1]) + list(sums)
    scratch = [pltpu.VMEM((n, d), BF), pltpu.VMEM((n, d), BF), pltpu.VMEM((d, f), BF), pltpu.VMEM((f, d), BF), pltpu.VMEM((d, f), F32), pltpu.VMEM((d, f), F32),
               pltpu.VMEM((2, tm, d), BF), pltpu.VMEM((2, tm, d), BF), pltpu.VMEM((chunks, PIECE, d), F32), pltpu.VMEM((chunks, PIECE, d), BF),
               pltpu.SemaphoreType.DMA((2 * chunks,)), pltpu.SemaphoreType.DMA((2,)), pltpu.SemaphoreType.DMA((2,)), pltpu.SemaphoreType.DMA((2, 2)), pltpu.SemaphoreType.DMA((chunks,))]
    if not first:
        scratch += [pltpu.VMEM((2 * half, 2, d >> bits, f), BF), pltpu.VMEM((n, d), BF), pltpu.VMEM((n, d), BF), pltpu.VMEM((chunks, PIECE, d), BF), pltpu.SemaphoreType.DMA((3 * chunks,))]
    res = pl.pallas_call(
        partial(dense_kernel, (chunks, rows, tm, lanes, order, first, len(deps))),
        name="ffn_dense",
        out_shape=[part] * chunks + [lined] * chunks + ends,
        in_specs=[SMEM] + [ANY] * (len(deps) + 2 * chunks) + [vm] + [ANY] * (2 + len(more)),
        out_specs=[ANY] * (2 * chunks + len(ends)),
        scratch_shapes=scratch,
        cost_estimate=SMALL,
        compiler_params=pltpu.CompilerParams(vmem_limit_bytes=VMEM),
    )(me, *deps, *xs, *dys, rm, up, down, *more)
    return res[:chunks], res[chunks:2 * chunks], res[2 * chunks:]


def expert_kernel(cfg, me_ref, blk_ref, bnd_ref, *refs):
    first, count, whole, chunks, rows, d, tm, lanes, order, has, deps = cfg
    n = chunks * rows
    it = iter(refs[deps:])
    take = lambda k: [next(it) for _ in range(k)]
    x_hbm, dy_hbm = take(chunks), take(chunks)
    rm, up_hbm, dn_hbm = take(3)
    based = [q for q in range(chunks) if has[q]]
    base_o, base_r = take(len(based)), take(len(based))
    out_refs, rg_refs = take(chunks), take(chunks)
    entire = [g for g in range(count) if whole[g]]
    halved = [g for g in range(count) if not whole[g]]
    whole_refs, keep_refs, send_refs = take(len(entire)), take(len(halved)), take(len(halved))
    X, DY, UP, DN, UA, DA, ST, XG, DG, VAL, OA, RA, DOT, BD, TR, TL, TH, xsem, wsem, gsem, osem, dsem = it
    half = ST.shape[0] // 2
    pieces = tm // PIECE
    rows_of = [pl.ds(q * rows, rows) for q in range(chunks)]
    copies = []
    for q in range(chunks):
        copies.append(pltpu.make_async_copy(x_hbm[q], X.at[rows_of[q]], xsem.at[q]))
        copies.append(pltpu.make_async_copy(dy_hbm[q], DY.at[rows_of[q]], xsem.at[chunks + q]))
    earlier = []
    for k, q in enumerate(based):
        earlier.append(pltpu.make_async_copy(base_o[k], X.at[rows_of[q]], xsem.at[q]))
        earlier.append(pltpu.make_async_copy(base_r[k].at[pl.ds(0, rows)], DY.at[rows_of[q]], xsem.at[chunks + q]))
        earlier.append(pltpu.make_async_copy(base_r[k].at[pl.ds(rows, PIECE)], BD.at[q], dsem.at[q]))

    def weights(e, slot):
        return [pltpu.make_async_copy(up_hbm.at[first + e], UP.at[slot], wsem.at[slot, 0]),
                pltpu.make_async_copy(dn_hbm.at[first + e], DN.at[slot], wsem.at[slot, 1])]

    def flush(g):
        if whole[g]:
            return [pltpu.make_async_copy(ST, whole_refs[entire.index(g)], gsem.at[0])]
        g = halved.index(g)
        return [pltpu.make_async_copy(ST.at[pl.ds(0, half)], keep_refs[g], gsem.at[0]),
                pltpu.make_async_copy(ST.at[pl.ds(half, half)], send_refs[g], gsem.at[1])]

    for c in copies + weights(0, 0):
        c.start()
    OA[...] = jnp.zeros_like(OA)
    RA[...] = jnp.zeros_like(RA)
    DOT[...] = jnp.zeros_like(DOT)
    iota16 = lax.broadcasted_iota(jnp.int32, (PIECE, 128), 0)

    def one_expert(e, _):
        slot = e % 2
        total = jnp.int32(0)
        for q in range(chunks):
            lo, hi = bnd_ref[blk_ref[q], first + e], bnd_ref[blk_ref[q], first + e + 1]
            p0 = lo // PIECE
            p1 = jnp.where(hi > lo, (hi + PIECE - 1) // PIECE, p0)

            def add(p, _, lo=lo, hi=hi, p0=p0, total=total, q=q):
                k = total + p - p0
                TR[k] = q * rows + p * PIECE
                TL[k] = lo - p * PIECE
                TH[k] = hi - p * PIECE
                return 0
            lax.fori_loop(p0, p1, add, 0)
            total = total + p1 - p0
        tiles = (total + pieces - 1) // pieces

        def pad(k, _):
            TR[k] = 0
            TL[k] = 0
            TH[k] = 0
            return 0
        lax.fori_loop(total, tiles * pieces, pad, 0)
        UA[...] = jnp.zeros_like(UA)
        DA[...] = jnp.zeros_like(DA)

        @pl.when(e == 0)
        def _():
            for c in copies:
                c.wait()
        for c in weights(e, slot):
            c.wait()

        @pl.when(e + 1 < count)
        def _():
            for c in weights(e + 1, 1 - slot):
                c.start()

        def one_tile(i, _):
            base = i * pieces
            for p in range(pieces):
                r = pl.ds(pl.multiple_of(TR[base + p], PIECE), PIECE)
                XG[pl.ds(p * PIECE, PIECE), :] = X[r, :]
                DG[pl.ds(p * PIECE, PIECE), :] = DY[r, :]
                ok = (iota16 >= TL[base + p]) & (iota16 < TH[base + p])
                VAL[pl.ds(p * PIECE, PIECE), :] = jnp.where(ok, 1.0, 0.0)
            valid = VAL[:, 0:1]

            def coef_of(logits, mixing):
                return pick_lane(mixing, lanes + 1) * pick_lane(lane_softmax(logits, 0, lanes), first + e) * valid
            dots, out, rg = ffn_tile(lanes, rm, XG[...], DG[...], coef_of, UP.at[slot], DN.at[slot], UA, DA, lambda: None)
            dots = jnp.broadcast_to(dots * valid, (tm, 128))
            for p in range(pieces):
                r = pl.ds(pl.multiple_of(TR[base + p], PIECE), PIECE)
                s = slice(p * PIECE, (p + 1) * PIECE)
                OA[r, :] += out[s]
                RA[r, :] += rg[s]
                DOT[r, :] += dots[s]
            return 0
        lax.fori_loop(0, tiles, one_tile, 0)

        @pl.when(e == count - 1)
        def _():
            for c in earlier:
                c.start()

        for g in range(count - 1):
            @pl.when(e == g + 1)
            def _(g=g):
                for c in flush(g):
                    c.wait()
        kind = False
        for g in entire:
            kind = kind | (e == g)
        stage_grads(ST, UA, DA, me_ref[0], order, kind)
        for g in range(count):
            @pl.when(e == g)
            def _(g=g):
                for c in flush(g):
                    c.start()
        return 0
    lax.fori_loop(0, count, one_expert, 0)
    for c in earlier:
        c.wait()
    last = []
    step = min(256, rows)
    line = lax.broadcasted_iota(jnp.int32, (PIECE, step), 0)
    for q in range(chunks):
        r = rows_of[q]
        o, g = OA[r, :], RA[r, :]
        if has[q]:
            o, g = o + X[r, :].astype(F32), g + DY[r, :].astype(F32)
        X[r, :] = o.astype(BF)
        DY[r, :] = g.astype(BF)
        if not has[q]:
            BD[q] = jnp.zeros(BD.shape[1:], BF)
        for i in range(rows // step):
            sl = slice(i * step, (i + 1) * step)
            dots = jnp.where(line == 1, DOT[pl.ds(q * rows + i * step, step), :].T[0:PIECE, :], 0.0)
            BD[q, :, sl] = (BD[q, :, sl].astype(F32) + dots).astype(BF)
        last += [pltpu.make_async_copy(X.at[r], out_refs[q], osem.at[0, q]), pltpu.make_async_copy(DY.at[r], rg_refs[q].at[pl.ds(0, rows)], osem.at[1, q]),
                 pltpu.make_async_copy(BD.at[q], rg_refs[q].at[pl.ds(rows, PIECE)], dsem.at[q])]
        for c in last[-3:]:
            c.start()
    for c in last + flush(count - 1):
        c.wait()


def ffn_experts(me, blocks, bounds, xs, dys, rm, up, down, first, count, whole, base, order, deps=()):
    chunks = len(xs)
    rows, d = xs[0].shape
    lanes, _, f = up.shape
    n = chunks * rows
    tm = TILE_EXPERT
    bits = len(order)
    half = 1 << (bits - 1)
    grad, entire = [jax.ShapeDtypeStruct((k * half, 2, d >> bits, f), BF) for k in (1, 2)]
    part, lined = jax.ShapeDtypeStruct((rows, d), BF), jax.ShapeDtypeStruct((rows + PIECE, d), BF)
    table = n // PIECE + chunks * lanes + 2 * tm // PIECE
    vm = pl.BlockSpec(memory_space=pltpu.VMEM)
    has = tuple(b is not None for b in base[0])
    more = [b for k in range(2) for b in base[k] if b is not None]
    res = pl.pallas_call(
        partial(expert_kernel, (first, count, whole, chunks, rows, d, tm, lanes, order, has, len(deps))),
        name="ffn_experts",
        out_shape=[part] * chunks + [lined] * chunks + [entire] * sum(whole) + [grad] * (2 * (count - sum(whole))),
        in_specs=[SMEM] * 3 + [ANY] * (len(deps) + 2 * chunks) + [vm] + [ANY] * (2 + len(more)),
        out_specs=[ANY] * (2 * chunks + 2 * count - sum(whole)),
        scratch_shapes=[
            pltpu.VMEM((n, d), BF), pltpu.VMEM((n, d), BF), pltpu.VMEM((2, d, f), BF), pltpu.VMEM((2, f, d), BF),
            pltpu.VMEM((d, f), F32), pltpu.VMEM((d, f), F32), pltpu.VMEM((2 * half, 2, d >> bits, f), BF),
            pltpu.VMEM((tm, d), BF), pltpu.VMEM((tm, d), BF), pltpu.VMEM((tm, 128), F32),
            pltpu.VMEM((n, d), F32), pltpu.VMEM((n, d), F32), pltpu.VMEM((n, 128), F32), pltpu.VMEM((chunks, PIECE, d), BF),
            pltpu.SMEM((table,), jnp.int32), pltpu.SMEM((table,), jnp.int32), pltpu.SMEM((table,), jnp.int32),
            pltpu.SemaphoreType.DMA((2 * chunks,)), pltpu.SemaphoreType.DMA((2, 2)), pltpu.SemaphoreType.DMA((2,)), pltpu.SemaphoreType.DMA((2, chunks)), pltpu.SemaphoreType.DMA((chunks,)),
        ],
        cost_estimate=SMALL,
        compiler_params=pltpu.CompilerParams(vmem_limit_bytes=VMEM),
    )(me, blocks, bounds, *deps, *xs, *dys, rm, up, down, *more)
    at = 2 * chunks + sum(whole)
    rest = iter(res[at:])
    keep = [next(rest) for g in range(count) if not whole[g]]
    return res[:chunks], res[chunks:2 * chunks], res[2 * chunks:at], keep, list(rest)


def split_add_kernel(deps, *refs):
    ka, kb, ca, cb, keep, send = refs[deps:]
    keep[...] = (ka[...].astype(F32) + ca[...].astype(F32)).astype(BF)
    send[...] = (kb[...].astype(F32) + cb[...].astype(F32)).astype(BF)


def split_add(kept, came, deps=()):
    h, m, blk, f = kept.shape
    near = pl.BlockSpec((1, m, blk, f), lambda i: (i, 0, 0, 0))
    far = pl.BlockSpec((1, m, blk, f), lambda i: (i + h // 2, 0, 0, 0))
    out = jax.ShapeDtypeStruct((h // 2, m, blk, f), BF)
    return pl.pallas_call(
        partial(split_add_kernel, len(deps)),
        name="split_add",
        grid=(h // 2,),
        in_specs=[ANY] * len(deps) + [near, far, near, far],
        out_specs=[near, near],
        out_shape=[out, out],
        cost_estimate=SMALL,
        compiler_params=pltpu.CompilerParams(vmem_limit_bytes=VMEM),
    )(*deps, kept, kept, came, came)


def last_add_kernel(deps, turns, *refs):
    terms = refs[deps:-len(turns)]
    outs = refs[-len(turns):]
    for k, turned in enumerate(turns):
        total = terms[0][0, k].astype(F32)
        for v in terms[1:]:
            total = total + v[0, k].astype(F32)
        outs[k][...] = (total.T if turned else total).reshape(outs[k].shape)


def last_add(terms, turns, place=None, stacks=None, deps=()):
    _, m, blk, f = terms[0].shape
    shapes = [(f, blk) if turned else (blk, f) for turned in turns]
    aliases = {}
    if place is None:
        out_shape = [jax.ShapeDtypeStruct(s, F32) for s in shapes]
        out_specs = [pl.BlockSpec(s, lambda i: (0, 0)) for s in shapes]
    else:
        count, at = place
        out_shape = [jax.ShapeDtypeStruct((count,) + s, F32) for s in shapes]
        out_specs = [pl.BlockSpec((1,) + s, lambda i: (at, 0, 0)) for s in shapes]
        if stacks is not None:
            aliases = {k: k for k in range(m)}
            deps = tuple(stacks) + tuple(deps)
    full = pl.BlockSpec((1, m, blk, f), lambda i: (0, 0, 0, 0))
    return pl.pallas_call(
        partial(last_add_kernel, len(deps), turns),
        name="last_add",
        grid=(1,),
        in_specs=[ANY] * len(deps) + [full] * len(terms),
        out_specs=out_specs,
        out_shape=out_shape,
        input_output_aliases=aliases,
        cost_estimate=SMALL,
        compiler_params=pltpu.CompilerParams(vmem_limit_bytes=VMEM),
    )(*deps, *terms)


def hold(v, deps):
    return pl.pallas_call(
        lambda *refs: None,
        name="hold",
        in_specs=[ANY] * (1 + len(deps)),
        out_specs=ANY,
        out_shape=jax.ShapeDtypeStruct(v.shape, v.dtype),
        input_output_aliases={0: 0},
        cost_estimate=SMALL,
    )(v, *deps)


HD = 64
LANES = 128


def head_part(v, h):
    lane = lax.broadcasted_iota(jnp.int32, v.shape, 1)
    return jnp.where((lane // HD) == h, v, jnp.zeros((), v.dtype))


def masked_scores(st, key_first, query_first, prefix):
    key_pos = key_first + lax.broadcasted_iota(jnp.int32, st.shape, 0)
    query_pos = query_first + lax.broadcasted_iota(jnp.int32, st.shape, 1)
    seen = key_pos <= query_pos
    if prefix is not None:
        seen = seen | (key_pos < prefix)
    return jnp.where(seen, st, -1e30)


def score_block(k2, qm, half, length, prefix):
    mid = length // 2
    if half == 0:
        return masked_scores(dot(k2[0:mid], qm, 1, 1), 0, 0, prefix)
    low = dot(k2[0:mid], qm, 1, 1)
    high = masked_scores(dot(k2[mid:length], qm, 1, 1), mid, mid, None)
    return jnp.concatenate([low, high], 0)


def attn_forward_kernel(length, pieces, aliased, prefix_ref, at_ref, *refs):
    n1_ref = refs[0]
    w_refs = [(r, i) for r, n in zip(refs[1:], pieces) for i in range(n)]
    q_ref, k_ref, v_ref, ctx_ref, lse_ref = refs[1 + len(pieces) + aliased:]
    mid = length // 2
    prefix = prefix_ref[0]
    n1 = n1_ref[...]
    for out, (w, i) in zip((q_ref, k_ref, v_ref), w_refs):
        out[...] = dot(n1, w[i], 1, 0).astype(BF)
    vt = v_ref[...].T
    k2 = k_ref[...]
    for half in range(2):
        rows = pl.ds(half * mid, mid)
        q2 = q_ref[rows, :] * jnp.asarray(HD ** -0.5, BF)
        keys = mid * (half + 1)
        parts = []
        for h in range(2):
            st = score_block(k2, head_part(q2, h), half, length, prefix)
            top = jnp.max(st, axis=0, keepdims=True)
            p = jnp.exp(st - top)
            total = jnp.sum(p, axis=0, keepdims=True)
            c = dot(vt[h * HD:(h + 1) * HD, 0:keys], p.astype(BF), 1, 0)
            parts.append(c / total)
            lse_ref[0, h:h + 1, rows] = top + jnp.log(total)
        ctx_ref[rows, :] = jnp.concatenate(parts, 0).T.astype(BF)


def attn_forward(prefix, at, n1, ws, heads, earlier=(), deps=()):
    length, d = n1.shape
    pairs = ws[0].shape[2] // LANES
    col = pl.BlockSpec((length, LANES), lambda p, _, at_ref: (0, at_ref[p]))
    out = jax.ShapeDtypeStruct((length, heads), BF)
    done = len(earlier)
    skipped = len(deps)
    return pl.pallas_call(
        skip(partial(attn_forward_kernel, length, tuple(w.shape[0] for w in ws), done), 2, skipped),
        name="attn_forward",
        grid_spec=pltpu.PrefetchScalarGridSpec(
            num_scalar_prefetch=2, grid=(pairs,),
            in_specs=[ANY] * skipped + [pl.BlockSpec((length, d), lambda p, *_: (0, 0))]
            + [pl.BlockSpec((w.shape[0], d, LANES), lambda p, *_: (0, 0, p)) for w in ws] + [ANY] * done,
            out_specs=[col] * 4 + [pl.BlockSpec((1, 8, length), lambda p, _, at_ref: (at_ref[p], 0, 0))]),
        out_shape=[out] * 4 + [jax.ShapeDtypeStruct((heads // LANES, 8, length), F32)],
        input_output_aliases={3 + skipped + len(ws) + k: k for k in range(done)},
        cost_estimate=SMALL,
        compiler_params=pltpu.CompilerParams(vmem_limit_bytes=VMEM),
    )(prefix, at, *deps, n1, *ws, *earlier)


def attn_backward_kernel(length, bits, based, prefix_ref, me_ref, mc_ref, n1_ref, wo_ref, w_ref, q_ref, k_ref, v_ref, ctx_ref, lse_ref, *refs):
    base_ref = refs[0] if based else None
    ng_ref, grad_ref, NG, DC, DK, DV, DQ = refs[based:]
    mid = length // 2
    prefix = prefix_ref[0]
    me = me_ref[0]
    pair = pl.program_id(0)
    mc = mc_ref[...]
    DC[...] = dot(mc, wo_ref[...], 1, 1).astype(BF)
    k2, v2 = k_ref[...], v_ref[...]
    kt = k2.T
    scale = jnp.asarray(HD ** -0.5, BF)
    for half in range(2):
        rows = pl.ds(half * mid, mid)
        q2 = q_ref[rows, :] * scale
        dc2 = DC[rows, :]
        keys = mid * (half + 1)
        dv = jnp.zeros((keys, LANES), F32)
        dk = jnp.zeros((keys, LANES), F32)
        dq = []
        for h in range(2):
            qm, dcm = head_part(q2, h), head_part(dc2, h)
            st = score_block(k2, qm, half, length, prefix)
            p = jnp.exp(st - lse_ref[0, h:h + 1, rows])
            dv = dv + dot(p.astype(BF), dcm, 1, 0)
            dp = dot(v2[0:keys], dcm, 1, 1)
            ds = (p * (dp - jnp.sum(p * dp, axis=0, keepdims=True))).astype(BF)
            dk = dk + dot(ds, qm, 1, 0)
            dq.append(dot(kt[h * HD:(h + 1) * HD, 0:keys], ds, 1, 0))
        DQ[rows, :] = (jnp.concatenate(dq, 0) * HD ** -0.5).T.astype(BF)
        if half == 0:
            DK[0:mid, :] = dk
            DV[0:mid, :] = dv
        else:
            DK[0:mid, :] += dk[0:mid]
            DV[0:mid, :] += dv[0:mid]
            DK[mid:length, :] = dk[mid:length]
            DV[mid:length, :] = dv[mid:length]
    dq, dk, dv = DQ[...], DK[...].astype(BF), DV[...].astype(BF)
    ng = dot(dq, w_ref[0], 1, 1) + dot(dk, w_ref[1], 1, 1) + dot(dv, w_ref[2], 1, 1)

    @pl.when(pair == 0)
    def _():
        NG[...] = ng

    @pl.when(pair > 0)
    def _():
        NG[...] += ng
    n1 = n1_ref[...]
    grads = [dot(n1, x, 0, 0) for x in (dq, dk, dv)] + [dot(mc, ctx_ref[...], 0, 0)]
    blk = n1.shape[1] >> bits
    for c in range(1 << bits):
        slot = slot_of(jnp.int32(c) ^ me, range(bits))
        for i in range(4):
            grad_ref[slot, i] = grads[i][c * blk:(c + 1) * blk].astype(BF)

    @pl.when(pair == pl.num_programs(0) - 1)
    def _():
        done = NG[...]
        if based:
            done = done + base_ref[...].astype(F32)
        ng_ref[...] = done.astype(BF)


def attn_backward(prefix, me, mc, n1, wo, w, saved, base, bits, deps=()):
    q, k, v, ctx, lse = saved
    length, d = n1.shape
    heads = w.shape[2]
    pairs = heads // LANES
    blk = d >> bits
    col = pl.BlockSpec((length, LANES), lambda p, *_: (0, p))
    full = pl.BlockSpec((length, d), lambda p, *_: (0, 0))
    extra = [] if base is None else [base]
    return pl.pallas_call(
        skip(partial(attn_backward_kernel, length, bits, len(extra)), 2, len(deps)),
        name="attn_backward",
        grid_spec=pltpu.PrefetchScalarGridSpec(
            num_scalar_prefetch=2, grid=(pairs,),
            in_specs=[ANY] * len(deps) + [full, full, pl.BlockSpec((LANES, d), lambda p, *_: (p, 0)), pl.BlockSpec((3, d, LANES), lambda p, *_: (0, 0, p)),
                      col, col, col, col, pl.BlockSpec((1, 8, length), lambda p, *_: (p, 0, 0))] + [full] * len(extra),
            out_specs=[full, pl.BlockSpec((1 << bits, 4, blk, LANES), lambda p, *_: (0, 0, 0, p))],
            scratch_shapes=[pltpu.VMEM((length, d), F32), pltpu.VMEM((length, LANES), BF),
                            pltpu.VMEM((length, LANES), F32), pltpu.VMEM((length, LANES), F32), pltpu.VMEM((length, LANES), BF)]),
        out_shape=[jax.ShapeDtypeStruct((length, d), BF), jax.ShapeDtypeStruct((1 << bits, 4, blk, heads), BF)],
        cost_estimate=SMALL,
        compiler_params=pltpu.CompilerParams(vmem_limit_bytes=VMEM),
    )(prefix, me, *deps, mc, n1, wo, w, q, k, v, ctx, lse, *extra)


EPS = 1e-5


def normalise(v):
    centered = v - jnp.mean(v, axis=1, keepdims=True)
    r = lax.rsqrt(jnp.mean(centered * centered, axis=1, keepdims=True) + EPS)
    return centered * r, r


def norm_backward(xhat, r, grad, gain):
    scaled = grad * gain
    return r * (scaled - jnp.mean(scaled, axis=1, keepdims=True) - xhat * jnp.mean(scaled * xhat, axis=1, keepdims=True))


def order_rows(pos, rows_to_slots):
    n = pos.shape[1] if rows_to_slots else pos.shape[0]
    slot = lax.broadcasted_iota(jnp.int32, (n, n), 0 if rows_to_slots else 1)
    return jnp.where(slot == pos, 1.0, 0.0).astype(BF)


def first_norm_kernel(members, j_ref, *refs):
    xs, (gain, shift, dy, pos, out, sorted_dy) = refs[:members], refs[members:]
    for k in range(members):
        @pl.when(pl.program_id(0) == k)
        def _(k=k):
            xhat, _ = normalise(xs[k][...].astype(F32))
            out[...] = (xhat * gain[...] + shift[...]).astype(BF)
            if k == 0:
                sorted_dy[...] = dot(order_rows(pos[...], True), dy[...], 1, 0).astype(BF)


def first_norm(j, xs, gain, shift, dy, pos):
    members = len(xs)
    rows, d = xs[0].shape
    fixed = lambda shape: pl.BlockSpec(shape, lambda p, *_: (0, 0))
    return pl.pallas_call(
        partial(first_norm_kernel, members),
        name="first_norm",
        grid_spec=pltpu.PrefetchScalarGridSpec(
            num_scalar_prefetch=1, grid=(members,),
            in_specs=[fixed((rows, d))] * members + [fixed((1, d))] * 2 + [fixed((rows, d)), fixed((1, rows))],
            out_specs=[pl.BlockSpec((rows, d), lambda p, j_ref: (lax.rem(j_ref[0] + p, members), 0)), fixed((rows, d))]),
        out_shape=[jax.ShapeDtypeStruct((members * rows, d), BF), jax.ShapeDtypeStruct((rows, d), BF)],
        cost_estimate=SMALL,
        compiler_params=pltpu.CompilerParams(vmem_limit_bytes=VMEM),
    )(j, *xs, gain, shift, dy, pos)


def project_kernel(parts, *refs):
    total = dot(refs[0][...], refs[parts][...], 1, 0)
    for i in range(1, parts):
        total = total + dot(refs[i][...], refs[parts + i][...], 1, 0)
    refs[-1][0] = total.astype(BF)


def project(contexts, weights, members):
    parts = len(contexts)
    length, heads = contexts[0].shape
    d = weights[0].shape[1]
    rows = length // members
    return pl.pallas_call(
        partial(project_kernel, parts),
        name="project",
        grid=(members,),
        in_specs=[pl.BlockSpec((rows, heads), lambda p: (p, 0))] * parts + [pl.BlockSpec((heads, d), lambda p: (0, 0))] * parts,
        out_specs=pl.BlockSpec((1, rows, d), lambda p: (p, 0, 0)),
        out_shape=jax.ShapeDtypeStruct((members, rows, d), BF),
        cost_estimate=SMALL,
        compiler_params=pltpu.CompilerParams(vmem_limit_bytes=VMEM),
    )(*contexts, *weights)


def second_norm_kernel(came, x, gain, shift, pos, middle, n2):
    mid = x[...].astype(F32)
    for k in range(came.shape[0]):
        mid = mid + came[k].astype(F32)
    middle[...] = mid
    xhat, _ = normalise(mid)
    normed = (xhat * gain[...] + shift[...]).astype(BF)
    n2[...] = dot(order_rows(pos[...], True), normed, 1, 0).astype(BF)


def second_norm(came, x, gain, shift, pos):
    rows, d = x.shape
    fixed = lambda shape: pl.BlockSpec(shape, lambda p: (0,) * len(shape))
    return pl.pallas_call(
        second_norm_kernel,
        name="second_norm",
        grid=(1,),
        in_specs=[fixed(came.shape), fixed((rows, d)), fixed((1, d)), fixed((1, d)), fixed((1, rows))],
        out_specs=[fixed((rows, d))] * 2,
        out_shape=[jax.ShapeDtypeStruct((rows, d), F32), jax.ShapeDtypeStruct((rows, d), BF)],
        cost_estimate=SMALL,
        compiler_params=pltpu.CompilerParams(vmem_limit_bytes=VMEM),
    )(came, x, gain, shift, pos)


def add_small(a, b, deps):
    def kernel(*refs):
        refs[-1][...] = refs[-3][...] + refs[-2][...]
    full = pl.BlockSpec(memory_space=pltpu.VMEM)
    return pl.pallas_call(kernel, name="add_small", in_specs=[ANY] * len(deps) + [full, full], out_specs=full,
                          out_shape=jax.ShapeDtypeStruct(a.shape, a.dtype), cost_estimate=SMALL)(*deps, a, b)


def hi_lo(v):
    hi = v.astype(BF)
    return hi, (v - hi.astype(F32)).astype(BF)


def middle_backward_kernel(single, bnd_ref, t_ref, *refs):
    it = iter(refs)
    parts = [next(it) for _ in range(single)]
    n2, rm, middle, dy, gain, pos, mg_ref, mc_ref, sums_ref = it
    t = t_ref[0]
    n2v, rmv = n2[...], rm[...]
    rows = n2v.shape[0]
    total = parts[0][0:rows, :].astype(F32)
    lines = parts[0][rows:rows + PIECE, 0:rows].astype(F32)
    for p in parts[1:]:
        total = total + p[0:rows, :].astype(F32)
        lines = lines + p[rows:rows + PIECE, 0:rows].astype(F32)
    dots = jnp.concatenate([lines, jnp.zeros((128 - PIECE, rows), F32)], axis=0).T
    experts = bnd_ref.shape[1] - 1
    logits = dot(n2v, rmv, 1, 0)
    route_prob = lane_softmax(logits, 0, experts)
    mixing = lane_softmax(logits, experts, experts + 2)
    row = lax.broadcasted_iota(jnp.int32, (rows, 1), 0)
    route = jnp.zeros((rows, 1), jnp.int32)
    for e in range(1, experts):
        route = route + (row >= bnd_ref[t, e]).astype(jnp.int32)
    gate = pick_lane(route_prob, route)
    m0, m1 = pick_lane(mixing, experts), pick_lane(mixing, experts + 1)
    dense_dot, expert_dot = dots[:, 0:1], dots[:, 1:2]
    d0, d1 = dense_dot, expert_dot * gate
    inner = m0 * d0 + m1 * d1
    lane = lax.broadcasted_iota(jnp.int32, logits.shape, 1)
    grad = expert_dot * (m1 * gate) * (jnp.where(lane == route, 1.0, 0.0) - route_prob)
    grad = jnp.where(lane < experts, grad, 0.0)
    grad = jnp.where(lane == experts, m0 * (d0 - inner), grad)
    grad = jnp.where(lane == experts + 1, m1 * (d1 - inner), grad)
    hi, lo = hi_lo(grad)
    total = total + dot(hi, rmv, 1, 1) + dot(lo, rmv, 1, 1)
    sums_ref[0:8, :] = (dot(hi.T, n2v, 1, 0) + dot(lo.T, n2v, 1, 0))[0:8]
    g = dot(order_rows(pos[...], False), total.astype(BF), 1, 0)
    xhat, r = normalise(middle[...])
    sums_ref[8:16, :] = jnp.zeros((8, g.shape[1]), F32)
    sums_ref[8:9, :] = jnp.sum(g * xhat, axis=0, keepdims=True)
    sums_ref[9:10, :] = jnp.sum(g, axis=0, keepdims=True)
    mg = dy[...].astype(F32) + norm_backward(xhat, r, g, gain[...])
    mg_ref[...] = mg
    for k in range(mc_ref.shape[0]):
        mc_ref[k] = mg.astype(BF)


def middle_backward(bounds, t, parts, n2, rm, middle, dy, gain, pos, members, deps=()):
    rows, d = n2.shape
    fixed = lambda shape: pl.BlockSpec(shape, lambda p, *_: (0, 0))
    big = fixed((rows, d))
    return pl.pallas_call(
        skip(partial(middle_backward_kernel, len(parts)), 2, len(deps)),
        name="middle_backward",
        grid_spec=pltpu.PrefetchScalarGridSpec(
            num_scalar_prefetch=2, grid=(1,),
            in_specs=[ANY] * len(deps) + [fixed((rows + PIECE, d))] * len(parts)
            + [big, fixed((d, 128)), big, big, fixed((1, d)), fixed((rows, 1))],
            out_specs=[big, pl.BlockSpec((members, rows, d), lambda p, *_: (0, 0, 0)), fixed((16, d))]),
        out_shape=[jax.ShapeDtypeStruct((rows, d), F32), jax.ShapeDtypeStruct((members, rows, d), BF), jax.ShapeDtypeStruct((16, d), F32)],
        cost_estimate=SMALL,
        compiler_params=pltpu.CompilerParams(vmem_limit_bytes=VMEM),
    )(bounds, t, *deps, *parts, n2, rm, middle, dy, gain, pos)


def layer_out_kernel(*refs):
    parts, (middle, pos, out) = refs[:-3], refs[-3:]
    total = parts[0][...].astype(F32)
    for p in parts[1:]:
        total = total + p[...].astype(F32)
    hi, lo = hi_lo(total)
    move = order_rows(pos[...], False)
    out[...] = (middle[...] + dot(move, hi, 1, 0) + dot(move, lo, 1, 0)).astype(BF)


def layer_out(parts, middle, pos, deps=()):
    rows, d = middle.shape
    big = pl.BlockSpec((rows, d), lambda p: (0, 0))
    return pl.pallas_call(
        skip(layer_out_kernel, 0, len(deps)),
        name="layer_out",
        grid=(1,),
        in_specs=[ANY] * len(deps) + [big] * (len(parts) + 1) + [pl.BlockSpec((rows, 1), lambda p: (0, 0))],
        out_specs=big,
        out_shape=jax.ShapeDtypeStruct((rows, d), BF),
        cost_estimate=SMALL,
        compiler_params=pltpu.CompilerParams(vmem_limit_bytes=VMEM),
    )(*deps, *parts, middle, pos)


def add_parts_kernel(*refs):
    total = refs[0][...].astype(F32)
    for p in refs[1:-1]:
        total = total + p[...].astype(F32)
    refs[-1][...] = total.astype(BF)


def add_parts(parts, deps=()):
    rows, d = parts[0].shape
    tile = pl.BlockSpec((rows, d), lambda p: (p, 0))
    return pl.pallas_call(
        skip(add_parts_kernel, 0, len(deps)),
        name="add_parts",
        grid=(1,),
        in_specs=[ANY] * len(deps) + [tile] * len(parts),
        out_specs=tile,
        out_shape=jax.ShapeDtypeStruct((rows, d), BF),
        cost_estimate=SMALL,
        compiler_params=pltpu.CompilerParams(vmem_limit_bytes=VMEM),
    )(*deps, *parts)


def input_backward_kernel(parts, x, mg, gain, out, sums):
    g = parts[0].astype(F32)
    for k in range(1, parts.shape[0]):
        g = g + parts[k].astype(F32)
    xhat, r = normalise(x[...].astype(F32))
    sums[...] = jnp.zeros_like(sums)
    sums[0:1, :] = jnp.sum(g * xhat, axis=0, keepdims=True)
    sums[1:2, :] = jnp.sum(g, axis=0, keepdims=True)
    out[...] = mg[...] + norm_backward(xhat, r, g, gain[...])


def input_backward(parts, x, mg, gain, deps=()):
    rows, d = x.shape
    fixed = lambda shape: pl.BlockSpec(shape, lambda p: (0, 0))
    big = fixed((rows, d))
    return pl.pallas_call(
        skip(input_backward_kernel, 0, len(deps)),
        name="input_backward",
        grid=(1,),
        in_specs=[ANY] * len(deps) + [pl.BlockSpec(parts.shape, lambda p: (0, 0, 0))] + [big] * 2 + [fixed((1, d))],
        out_specs=[big, fixed((8, d))],
        out_shape=[jax.ShapeDtypeStruct((rows, d), F32), jax.ShapeDtypeStruct((8, d), F32)],
        cost_estimate=SMALL,
        compiler_params=pltpu.CompilerParams(vmem_limit_bytes=VMEM),
    )(*deps, parts, x, mg, gain)


class Everywhere:
    def __init__(self, v):
        self.v = v
        bits = {axis: lax.axis_size(axis).bit_length() - 1 for axis in ("tensor", "dp")}
        self.hops = [("tensor", 1 << b) for b in range(bits["tensor"])] + [("dp", 1 << b) for b in range(bits["dp"])]
        self.launch()

    def launch(self):
        if self.hops:
            axis, bit = self.hops.pop(0)
            self.came = lax.ppermute(self.v, axis, [(i, i ^ bit) for i in range(lax.axis_size(axis))])
        else:
            self.came = None

    def add(self, mark):
        if self.came is None:
            return mark
        self.v = add_small(self.v, self.came, mark)
        self.launch()
        return (self.v,)


def over_dp(v, bit):
    return lax.ppermute(v, "dp", [(i, i ^ (1 << bit)) for i in range(lax.axis_size("dp"))])


def shards(inputs, cotangent, routes, prefixes, gain_one, shift_one, qkv_weight, out_weight, gain_two, shift_two,
           up_weight, down_weight, expert_up, expert_down, router_weight, mix_weight):
    rows, d = inputs.shape
    tensor = lax.axis_size("tensor")
    dp = lax.axis_size("dp")
    bits = dp.bit_length() - 1
    seqs = prefixes.shape[0]
    members = tensor // seqs
    experts = expert_up.shape[0]
    heads = qkv_weight.shape[2]
    pairs = heads // LANES
    t = lax.axis_index("tensor")
    s, j = t // members, t % members
    me = lax.axis_index("dp").astype(jnp.int32)
    me1, j1, t1 = me.reshape(1), j.astype(jnp.int32).reshape(1), t.astype(jnp.int32).reshape(1)
    place = lambda a, b: (a % seqs) * members + b % members
    everyone = [(a, b) for a in range(seqs) for b in range(members)]

    def from_member(v, k):
        return lax.ppermute(v, "tensor", [(place(a, b), place(a, b - k)) for a, b in everyone])

    def from_sequence(v, k):
        return lax.ppermute(v, "tensor", [(place(a, b), place(a - k, b)) for a, b in everyone])

    def to_member(v, k):
        return from_member(v, -k)

    def to_sequence(v, k):
        return from_sequence(v, -k)

    route_blocks = routes.reshape(tensor, rows)
    bounds = jnp.stack([jnp.sum((route_blocks < e).astype(jnp.int32), axis=1) for e in range(experts + 1)], axis=1)
    key_col = lax.dynamic_slice_in_dim(routes, t * rows, rows, 0) * rows + jnp.arange(rows, dtype=jnp.int32)[:, None]
    key_row = key_col.reshape(1, rows)
    pos_row = jnp.sum((key_col < key_row).astype(jnp.int32), axis=0, keepdims=True)
    pos_col = jnp.sum((key_row < key_col).astype(jnp.int32), axis=1, keepdims=True)
    chunk = [(dj, ds) for dj in range(members) for ds in range(seqs)]
    blocks = jnp.stack([((s + ds) % seqs) * members + (j + dj) % members for dj, ds in chunk]).astype(jnp.int32)
    near = [q for q, (dj, ds) in enumerate(chunk) if ds == 0]
    far = [q for q, (dj, ds) in enumerate(chunk) if ds > 0]

    xs = [inputs] + [from_member(inputs, k) for k in range(1, members)]
    flip = me & 1
    relay = pairs % 2 == 0 and dp > 1
    w_own = jnp.transpose(qkv_weight, (1, 0, 2))
    fetched = []
    for ds in range(1, seqs):
        if relay:
            half = lax.dynamic_slice_in_dim(qkv_weight, flip * (heads // 2), heads // 2, 2)
            fetched.append([from_sequence(jnp.transpose(half[:, a:b], (1, 0, 2)), ds) for a, b in ((0, 2), (2, 3))])
        else:
            fetched.append([from_sequence(w_own, ds)])
    wo_all = [out_weight] + [from_sequence(out_weight, ds) for ds in range(1, seqs)]
    gain_one, shift_one, gain_two, shift_two = [v.reshape(1, d) for v in (gain_one, shift_one, gain_two, shift_two)]
    prefix = lax.dynamic_slice_in_dim(prefixes, s, 1)
    rm = jnp.concatenate([router_weight, mix_weight, jnp.zeros((d, LANES - experts - 2), BF)], axis=1)
    n1, dys = first_norm(j1, xs, gain_one, shift_one, cotangent, pos_row)
    columns = jnp.arange(pairs, dtype=jnp.int32)
    pieces = [[] for _ in fetched]
    fence = (n1,)
    if relay:
        for k, got in enumerate(fetched):
            held = hold(got[0], (n1,))
            pieces[k] = [[held], [over_dp(held, 0)]]
            fence += (held,)
    saved = [attn_forward(prefix, columns, n1, [w_own], heads, deps=fence[1:] + (rm,))]
    if relay:
        for k, got in enumerate(fetched):
            held = hold(got[1], (saved[0][4],))
            pieces[k][0].append(held)
            pieces[k][1].append(over_dp(held, 0))
    else:
        pieces = [[got] for got in fetched]
    w_all = [w_own]
    for halves in pieces:
        part = ()
        for k, ws in enumerate(halves):
            at = (columns + (flip ^ k) * (pairs // 2))[:pairs // 2] if relay else columns
            part = attn_forward(prefix, at, n1, ws, heads, part, deps=() if part else (saved[-1][4],))
        saved.append(part)
        whole = [jnp.concatenate(ws, axis=0) for ws in halves]
        if relay:
            whole = [jnp.where(flip == 0, jnp.concatenate(whole, axis=2), jnp.concatenate(whole[::-1], axis=2))]
        w_all.append(whole[0])
    contexts = [v[3] for v in saved]

    def spread(mine):
        out = list(mine)
        for k in range(1, members):
            out += [from_member(m, k) for m in mine]
        return out

    dy_mine = [dys] + [from_sequence(dys, ds) for ds in range(1, seqs)]
    dy_near = [dys] + [from_member(dys, k) for k in range(1, members)]
    sent = project(contexts, wo_all, members)

    def exchange(v):
        return lax.all_to_all(v, "tensor", 0, 0, axis_index_groups=[[place(a, b) for b in range(members)] for a in range(seqs)], tiled=True)

    came = exchange(sent)
    middle, n2 = second_norm(came, inputs, gain_two, shift_two, pos_row)
    n2_mine = [n2] + [from_sequence(n2, ds) for ds in range(1, seqs)]
    n2_near = [n2] + [from_member(n2, k) for k in range(1, members)]

    straight = tuple(range(bits))
    pick = lambda v, which: [v[q] for q in which]
    out_a, rg_a, sums = ffn_dense(me1, n2_near, dy_near, rm, up_weight, down_weight, experts, straight, deps=tuple(dy_mine[1:]))
    n2_all, dy_all = [], []
    n2_far, dy_far = [[hold(v, (out_a[0],)) for v in mine[1:]] for mine in (n2_mine, dy_mine)]
    for k in range(members):
        n2_all += [n2_near[k]] + [from_member(v, k) if k else v for v in n2_far]
        dy_all += [dy_near[k]] + [from_member(v, k) if k else v for v in dy_far]
    base = [[None] * tensor, [None] * tensor]
    for k, q in enumerate(near):
        base[0][q], base[1][q] = out_a[k], rg_a[k]
    by_scatter = [e == 0 for e in range(experts)]
    out_e, rg_e, whole, keep_e, send_e = ffn_experts(me1, blocks, bounds, n2_all, dy_all, rm, expert_up, expert_down, 0, 1, (True,), base, straight)
    out_e, rg_e, whole = list(out_e), list(rg_e), list(whole)
    out_b, rg_b, ends = ffn_dense(me1, pick(n2_all, far), pick(dy_all, far), rm, up_weight, down_weight, experts, straight,
                                  (pick(out_e, far), pick(rg_e, far)), sums)
    for k, q in enumerate(far):
        out_e[q], rg_e[q] = out_b[k], rg_b[k]
    if experts > 1:
        out_e, rg_e, entire, keep_e, send_e = ffn_experts(me1, blocks, bounds, n2_all, dy_all, rm, expert_up, expert_down, 1, experts - 1, tuple(by_scatter[1:]), (out_e, rg_e), straight)
        whole += list(entire)

    index = {c: q for q, c in enumerate(chunk)}
    def to_owner(parts):
        mine = [[parts[index[0, ds]]] + [to_member(parts[index[k, ds]], k) for k in range(1, members)] for ds in range(seqs)]
        return mine[0], mine[1:]

    def onward(terms, deps):
        sums = [add_parts(v, deps) for v in terms]
        return [to_sequence(v, ds + 1) for ds, v in enumerate(sums)], sums

    class Halving:
        def __init__(self, keep, send, order):
            self.keep, self.send, self.order, self.at = keep, send, order, 0

        def launch(self, deps=()):
            if deps:
                self.send = hold(self.send, deps)
            self.came = over_dp(self.send, self.order[self.at])
            self.at += 1

        def add(self, mark):
            self.keep, self.send = split_add(self.keep, self.came, mark)
            self.launch()
            return (self.send,)

        def rest(self, mark):
            while self.at < bits:
                mark = self.add(mark)
            return mark

    scattered = []
    for v in whole:
        flat = lax.psum_scatter(v.reshape(-1, v.shape[-1]), "dp", scatter_dimension=0, tiled=True)
        scattered.append(flat.reshape((1,) + v.shape[1:]))

    halvings = [Halving(keep, send, straight) for keep, send in zip(keep_e, send_e)]
    dense_sum = Halving(ends[0], ends[1], straight)
    sum_of = dict(enumerate(scattered + halvings))
    rg_near, rg_far = to_owner(rg_e)
    for v in [dense_sum] + halvings[:2]:
        v.launch()
    mark = dense_sum.add((out_e[0],))
    came_far, terms = onward(rg_far, mark)
    mark = tuple(terms[:1]) + tuple(w_all[1:])
    mg, mc, sums_two = middle_backward(bounds, t1, rg_near + came_far, n2, rm, middle, cotangent, gain_two, pos_col, members, mark)
    mcs = exchange(mc).reshape(members * rows, d)
    mark = dense_sum.add((mc,))
    ngs = None
    grads = [None] * seqs
    for ds in list(range(1, seqs)) + [0]:
        ngs, grads[ds] = attn_backward(prefix, me1, mcs, n1, wo_all[ds], w_all[ds], saved[ds], ngs, bits, mark)
        mark = (grads[ds],)
        if ds == 1 or seqs == 1:
            for v in halvings[2:]:
                v.launch()
            mark = dense_sum.rest(mark)
            for v in halvings[:1]:
                mark = v.add(mark)
    moved = [to_sequence(grads[ds], ds) for ds in range(1, seqs)]
    ng_parts = exchange(ngs.reshape(members, rows, d))
    up_out, down_out = last_add([dense_sum.keep, dense_sum.came], (False, True), deps=mark)
    mark = (up_out,)
    for v in halvings[1:2]:
        mark = v.add(mark)
    input_grad, sums_one = input_backward(ng_parts, inputs, mg, gain_one, mark)
    mark = (sums_one,)
    sums = Everywhere(jnp.concatenate([sums_two, sums_one], axis=0))
    stacks = None

    def finish(e, mark):
        if by_scatter[e]:
            terms = [sum_of[e]]
        else:
            mark = sum_of[e].rest(mark)
            terms = [sum_of[e].keep, sum_of[e].came]
        done = last_add(terms, (False, True), (experts, e), stacks, mark)
        return done, (done[1],)

    keep = grads[0]
    for v in moved[:-1]:
        keep = (keep.astype(F32) + v.astype(F32)).astype(BF)
    if moved:
        keep, send = split_add(keep, moved[-1], mark)
        mark = (send,)
    else:
        keep, send = keep[:dp // 2], keep[dp // 2:]
    attn_sum = Halving(keep, send, straight)
    attn_sum.launch()
    for v in halvings[:1]:
        mark = v.add(mark)
    mark = sums.add(mark)
    stacks, mark = finish(0, mark)
    for v in halvings[1:2]:
        mark = v.add(mark)
    out_near, out_far = to_owner([hold(v, mark) for v in out_e])
    out_came, terms = onward(out_far, mark)
    mark = tuple(terms[:1]) or mark
    if experts > 1:
        stacks, mark = finish(1, mark)
    for v in halvings[2:]:
        mark = v.add(mark)
    layer_output = layer_out(out_near + out_came, middle, pos_col, mark)
    mark = sums.add((layer_output,))
    mark = attn_sum.add(mark)
    if experts > 2:
        stacks, mark = finish(2, mark)
    for v in halvings[2:]:
        mark = v.add(mark)
    mark = attn_sum.add(mark)
    mark = sums.add(mark)
    mark = sums.add(mark)
    for e in range(3, experts):
        stacks, mark = finish(e, mark)
    expert_up_out, expert_down_out = stacks
    while sums.came is not None:
        mark = sums.add(mark)
    mark = attn_sum.rest(mark)
    *qkv_parts, out_out = last_add([attn_sum.keep, attn_sum.came], (False, False, False, True), deps=mark)
    lanes = d // (dp * tensor)
    begin = (me * tensor + t) * lanes
    small = lax.dynamic_slice_in_dim(sums.v, begin, lanes, 1)
    return (layer_output, input_grad, small[16], small[17], jnp.stack(qkv_parts, axis=1), out_out, small[8], small[9], up_out, down_out,
            expert_up_out, expert_down_out, small[0:experts].T, small[experts:experts + 2].T)


def solution(mesh):
    both = ("dp", "tensor")
    in_specs = (P(both, None), P(both, None), P("dp", None), P("dp"), P(), P(), P(None, None, "tensor"), P("tensor", None), P(), P(),
                P(None, "tensor"), P("tensor", None), P(None, None, "tensor"), P(None, "tensor", None), P(), P())
    out_specs = (P(both, None), P(both, None), P(both), P(both), P("dp", None, "tensor"), P("tensor", "dp"), P(both), P(both),
                 P("dp", "tensor"), P("tensor", "dp"), P(None, "dp", "tensor"), P(None, "tensor", "dp"), P(both, None), P(both, None))
    return jax.shard_map(shards, mesh=mesh, in_specs=in_specs, out_specs=out_specs, check_vma=False)
```

```python
from functools import partial
import jax, jax.numpy as jnp
from jax import lax
from jax.experimental import pallas as pl
from jax.experimental.pallas import tpu as pltpu
from jax.sharding import PartitionSpec as P

BF = jnp.bfloat16
F32 = jnp.float32
TILE_DENSE = 512
TILE_EXPERT = 304
PIECE = 16
SMALL = pl.CostEstimate(flops=0, bytes_accessed=0, transcendentals=0)
VMEM = 60 * 1024 * 1024
ANY = pl.BlockSpec(memory_space=pltpu.HBM)
SMEM = pl.BlockSpec(memory_space=pltpu.SMEM)


def dot(a, b, ca, cb):
    return lax.dot_general(a, b, (((ca,), (cb,)), ((), ())), preferred_element_type=F32)


def slot_of(value, order):
    out = jnp.int32(0)
    for k, bit in enumerate(order):
        out = out | (((value >> bit) & 1) << (len(order) - 1 - k))
    return out


def skip(kernel, scalars, deps):
    return lambda *refs: kernel(*refs[:scalars], *refs[scalars + deps:])


def lane_softmax(logits, first, last):
    lane = lax.broadcasted_iota(jnp.int32, logits.shape, 1)
    inside = (lane >= first) & (lane < last)
    masked = jnp.where(inside, logits, -1e30)
    top = jnp.max(masked, axis=1, keepdims=True)
    e = jnp.where(inside, jnp.exp(masked - top), 0.0)
    return e / jnp.sum(e, axis=1, keepdims=True)


def pick_lane(v, index):
    lane = lax.broadcasted_iota(jnp.int32, v.shape, 1)
    return jnp.sum(jnp.where(lane == index, v, 0.0), axis=1, keepdims=True)


def gelu_parts(pre):
    phi = 0.5 * (1.0 + lax.erf(pre * 0.7071067811865476))
    pdf = jnp.exp(pre * pre * -0.5) * 0.3989422804014327
    return pre * phi, phi + pre * pdf


def ffn_tile(lanes, rm, xt, dyt, coef_of, up_w, dn_w, UA, DA, ready):
    logits = dot(xt, rm[...], 1, 0)
    mixing = lane_softmax(logits, lanes, lanes + 2)
    coef = coef_of(logits, mixing)
    pre = dot(xt, up_w[...], 1, 0)
    g = dot(dyt, dn_w[...], 1, 1)
    hid, dg = gelu_parts(pre)
    hid = hid.astype(BF)
    dots = jnp.sum(hid.astype(F32) * g, axis=1, keepdims=True)
    pg = (g * dg * coef).astype(BF)
    cot = (dyt.astype(F32) * coef).astype(BF)
    out = dot(hid, dn_w[...], 1, 0) * coef
    rg = dot(pg, up_w[...], 1, 1)
    ready()
    UA[...] += dot(xt, pg, 0, 0)
    DA[...] += dot(cot, hid, 0, 0)
    return dots, out, rg


def stage_grads(ST, UA, DA, me, order, whole):
    bits = len(order)
    blk = UA.shape[0] >> bits

    def body(c, _):
        r = pl.ds(pl.multiple_of(c * blk, blk), blk)
        slot = jnp.where(whole, c, slot_of(c ^ me, order))
        ST[slot, 0] = UA[r, :].astype(BF)
        ST[slot, 1] = DA[r, :].astype(BF)
        return 0
    lax.fori_loop(0, 1 << bits, body, 0)


def dots_rows(dots):
    return jnp.broadcast_to(dots, (dots.shape[0], 128)).T[0:PIECE, :]


def dense_kernel(cfg, me_ref, *refs):
    chunks, rows, tm, lanes, order, first, deps = cfg
    it = iter(refs[deps:])
    take = lambda k: [next(it) for _ in range(k)]
    x_hbm, dy_hbm = take(chunks), take(chunks)
    rm, up_hbm, dn_hbm = take(3)
    base_o, base_r, sums_in = ([], [], []) if first else (take(chunks), take(chunks), take(2))
    out_refs, rg_refs = take(chunks), take(chunks)
    ends = take(2)
    X, DY, UP, DN, UA, DA, OB, RB, DT, OD, xsem, wsem, gsem, osem, dsem = take(15)
    ST, BO, BR, BD, bsem = (None,) * 5 if first else take(5)
    per = rows // tm
    weights = [pltpu.make_async_copy(up_hbm, UP, wsem.at[0]), pltpu.make_async_copy(dn_hbm, DN, wsem.at[1])]
    loads, bases = [], []
    for q in range(chunks):
        sl = pl.ds(q * rows, rows)
        loads.append([pltpu.make_async_copy(x_hbm[q], X.at[sl], xsem.at[q]), pltpu.make_async_copy(dy_hbm[q], DY.at[sl], xsem.at[chunks + q])])
        if not first:
            bases.append([pltpu.make_async_copy(base_o[q], BO.at[sl], bsem.at[q]), pltpu.make_async_copy(base_r[q].at[pl.ds(0, rows)], BR.at[sl], bsem.at[chunks + q]),
                          pltpu.make_async_copy(base_r[q].at[pl.ds(rows, PIECE)], BD.at[q], bsem.at[2 * chunks + q])])
    sums = [] if first else [pltpu.make_async_copy(sums_in[0], UA, gsem.at[0]), pltpu.make_async_copy(sums_in[1], DA, gsem.at[1])]
    for c in loads[0] + weights + sums + [c for q in loads[1:] for c in q] + [c for q in bases for c in q]:
        c.start()
    DT[...] = jnp.zeros_like(DT)
    if first:
        UA[...] = jnp.zeros_like(UA)
        DA[...] = jnp.zeros_like(DA)
    for c in weights:
        c.wait()

    def outs(q, part, slot):
        sl = pl.ds(part * tm, tm)
        return [pltpu.make_async_copy(OB.at[slot], out_refs[q].at[sl], osem.at[0, slot]),
                pltpu.make_async_copy(RB.at[slot], rg_refs[q].at[sl], osem.at[1, slot])]

    def one(i, _):
        slot = i % 2
        sl = pl.ds(pl.multiple_of(i * tm, tm), tm)
        for q in range(chunks):
            @pl.when(i == q * per)
            def _(q=q):
                for c in loads[q]:
                    c.wait()

        def ready():
            if not first:
                @pl.when(i == 0)
                def _():
                    for c in sums:
                        c.wait()
        dots, out, rg = ffn_tile(lanes, rm, X[sl, :], DY[sl, :], lambda l, m: pick_lane(m, lanes), UP, DN, UA, DA, ready)
        lines = dots_rows(dots)
        line = lax.broadcasted_iota(jnp.int32, lines.shape, 0)
        for q in range(chunks):
            for part in range(per):
                @pl.when(i == q * per + part)
                def _(q=q, part=part):
                    DT[q, :, part * tm:(part + 1) * tm] = jnp.where(line == 0, lines, 0.0)
        if not first:
            for q in range(chunks):
                @pl.when(i == q * per)
                def _(q=q):
                    for c in bases[q]:
                        c.wait()
            out = out + BO[sl, :].astype(F32)
            rg = rg + BR[sl, :].astype(F32)

        @pl.when(i >= 2)
        def _():
            for c in outs(0, 0, slot):
                c.wait()
        OB[slot] = out.astype(BF)
        RB[slot] = rg.astype(BF)
        for q in range(chunks):
            for part in range(per):
                @pl.when(i == q * per + part)
                def _(q=q, part=part):
                    for c in outs(q, part, slot):
                        c.start()
        return 0
    lax.fori_loop(0, chunks * per, one, 0)
    lines = []
    for q in range(chunks):
        total = DT[q] if first else DT[q] + BD[q].astype(F32)
        OD[q] = total.astype(BF)
        lines.append(pltpu.make_async_copy(OD.at[q], rg_refs[q].at[pl.ds(rows, PIECE)], dsem.at[q]))
    if first:
        last = lines + [pltpu.make_async_copy(UA, ends[0], gsem.at[0]), pltpu.make_async_copy(DA, ends[1], gsem.at[1])]
    else:
        stage_grads(ST, UA, DA, me_ref[0], order, False)
        half = ST.shape[0] // 2
        last = lines + [pltpu.make_async_copy(ST.at[pl.ds(h * half, half)], ends[h], gsem.at[h]) for h in range(2)]
    for c in last:
        c.start()
    for slot in range(min(2, chunks * per)):
        for c in outs(0, 0, slot):
            c.wait()
    for c in last:
        c.wait()


def ffn_dense(me, xs, dys, rm, up, down, lanes, order, base=None, sums=None, deps=()):
    chunks = len(xs)
    rows, d = xs[0].shape
    f = up.shape[1]
    n = chunks * rows
    tm = min(TILE_DENSE, rows)
    first = base is None
    bits = len(order)
    half = 1 << (bits - 1)
    vm = pl.BlockSpec(memory_space=pltpu.VMEM)
    part, lined = jax.ShapeDtypeStruct((rows, d), BF), jax.ShapeDtypeStruct((rows + PIECE, d), BF)
    total = jax.ShapeDtypeStruct((d, f), F32)
    grad = jax.ShapeDtypeStruct((half, 2, d >> bits, f), BF)
    ends = [total] * 2 if first else [grad] * 2
    more = [] if first else list(base[0]) + list(base[1]) + list(sums)
    scratch = [pltpu.VMEM((n, d), BF), pltpu.VMEM((n, d), BF), pltpu.VMEM((d, f), BF), pltpu.VMEM((f, d), BF), pltpu.VMEM((d, f), F32), pltpu.VMEM((d, f), F32),
               pltpu.VMEM((2, tm, d), BF), pltpu.VMEM((2, tm, d), BF), pltpu.VMEM((chunks, PIECE, d), F32), pltpu.VMEM((chunks, PIECE, d), BF),
               pltpu.SemaphoreType.DMA((2 * chunks,)), pltpu.SemaphoreType.DMA((2,)), pltpu.SemaphoreType.DMA((2,)), pltpu.SemaphoreType.DMA((2, 2)), pltpu.SemaphoreType.DMA((chunks,))]
    if not first:
        scratch += [pltpu.VMEM((2 * half, 2, d >> bits, f), BF), pltpu.VMEM((n, d), BF), pltpu.VMEM((n, d), BF), pltpu.VMEM((chunks, PIECE, d), BF), pltpu.SemaphoreType.DMA((3 * chunks,))]
    res = pl.pallas_call(
        partial(dense_kernel, (chunks, rows, tm, lanes, order, first, len(deps))),
        name="ffn_dense",
        out_shape=[part] * chunks + [lined] * chunks + ends,
        in_specs=[SMEM] + [ANY] * (len(deps) + 2 * chunks) + [vm] + [ANY] * (2 + len(more)),
        out_specs=[ANY] * (2 * chunks + len(ends)),
        scratch_shapes=scratch,
        cost_estimate=SMALL,
        compiler_params=pltpu.CompilerParams(vmem_limit_bytes=VMEM),
    )(me, *deps, *xs, *dys, rm, up, down, *more)
    return res[:chunks], res[chunks:2 * chunks], res[2 * chunks:]


def expert_kernel(cfg, me_ref, blk_ref, bnd_ref, *refs):
    first, count, whole, chunks, rows, d, tm, lanes, order, has, deps = cfg
    n = chunks * rows
    it = iter(refs[deps:])
    take = lambda k: [next(it) for _ in range(k)]
    x_hbm, dy_hbm = take(chunks), take(chunks)
    rm, up_hbm, dn_hbm = take(3)
    based = [q for q in range(chunks) if has[q]]
    base_o, base_r = take(len(based)), take(len(based))
    out_refs, rg_refs = take(chunks), take(chunks)
    entire = [g for g in range(count) if whole[g]]
    halved = [g for g in range(count) if not whole[g]]
    whole_refs, keep_refs, send_refs = take(len(entire)), take(len(halved)), take(len(halved))
    X, DY, UP, DN, UA, DA, ST, XG, DG, VAL, OA, RA, DOT, BD, TR, TL, TH, xsem, wsem, gsem, osem, dsem = it
    half = ST.shape[0] // 2
    pieces = tm // PIECE
    rows_of = [pl.ds(q * rows, rows) for q in range(chunks)]
    copies = []
    for q in range(chunks):
        copies.append(pltpu.make_async_copy(x_hbm[q], X.at[rows_of[q]], xsem.at[q]))
        copies.append(pltpu.make_async_copy(dy_hbm[q], DY.at[rows_of[q]], xsem.at[chunks + q]))
    earlier = []
    for k, q in enumerate(based):
        earlier.append(pltpu.make_async_copy(base_o[k], X.at[rows_of[q]], xsem.at[q]))
        earlier.append(pltpu.make_async_copy(base_r[k].at[pl.ds(0, rows)], DY.at[rows_of[q]], xsem.at[chunks + q]))
        earlier.append(pltpu.make_async_copy(base_r[k].at[pl.ds(rows, PIECE)], BD.at[q], dsem.at[q]))

    def weights(e, slot):
        return [pltpu.make_async_copy(up_hbm.at[first + e], UP.at[slot], wsem.at[slot, 0]),
                pltpu.make_async_copy(dn_hbm.at[first + e], DN.at[slot], wsem.at[slot, 1])]

    def flush(g):
        if whole[g]:
            return [pltpu.make_async_copy(ST, whole_refs[entire.index(g)], gsem.at[0])]
        g = halved.index(g)
        return [pltpu.make_async_copy(ST.at[pl.ds(0, half)], keep_refs[g], gsem.at[0]),
                pltpu.make_async_copy(ST.at[pl.ds(half, half)], send_refs[g], gsem.at[1])]

    for c in copies + weights(0, 0):
        c.start()
    OA[...] = jnp.zeros_like(OA)
    RA[...] = jnp.zeros_like(RA)
    DOT[...] = jnp.zeros_like(DOT)
    iota16 = lax.broadcasted_iota(jnp.int32, (PIECE, 128), 0)

    def one_expert(e, _):
        slot = e % 2
        total = jnp.int32(0)
        for q in range(chunks):
            lo, hi = bnd_ref[blk_ref[q], first + e], bnd_ref[blk_ref[q], first + e + 1]
            p0 = lo // PIECE
            p1 = jnp.where(hi > lo, (hi + PIECE - 1) // PIECE, p0)

            def add(p, _, lo=lo, hi=hi, p0=p0, total=total, q=q):
                k = total + p - p0
                TR[k] = q * rows + p * PIECE
                TL[k] = lo - p * PIECE
                TH[k] = hi - p * PIECE
                return 0
            lax.fori_loop(p0, p1, add, 0)
            total = total + p1 - p0
        tiles = (total + pieces - 1) // pieces

        def pad(k, _):
            TR[k] = 0
            TL[k] = 0
            TH[k] = 0
            return 0
        lax.fori_loop(total, tiles * pieces, pad, 0)
        UA[...] = jnp.zeros_like(UA)
        DA[...] = jnp.zeros_like(DA)

        @pl.when(e == 0)
        def _():
            for c in copies:
                c.wait()
        for c in weights(e, slot):
            c.wait()

        @pl.when(e + 1 < count)
        def _():
            for c in weights(e + 1, 1 - slot):
                c.start()

        def one_tile(i, _):
            base = i * pieces
            for p in range(pieces):
                r = pl.ds(pl.multiple_of(TR[base + p], PIECE), PIECE)
                XG[pl.ds(p * PIECE, PIECE), :] = X[r, :]
                DG[pl.ds(p * PIECE, PIECE), :] = DY[r, :]
                ok = (iota16 >= TL[base + p]) & (iota16 < TH[base + p])
                VAL[pl.ds(p * PIECE, PIECE), :] = jnp.where(ok, 1.0, 0.0)
            valid = VAL[:, 0:1]

            def coef_of(logits, mixing):
                return pick_lane(mixing, lanes + 1) * pick_lane(lane_softmax(logits, 0, lanes), first + e) * valid
            dots, out, rg = ffn_tile(lanes, rm, XG[...], DG[...], coef_of, UP.at[slot], DN.at[slot], UA, DA, lambda: None)
            dots = jnp.broadcast_to(dots * valid, (tm, 128))
            for p in range(pieces):
                r = pl.ds(pl.multiple_of(TR[base + p], PIECE), PIECE)
                s = slice(p * PIECE, (p + 1) * PIECE)
                OA[r, :] += out[s]
                RA[r, :] += rg[s]
                DOT[r, :] += dots[s]
            return 0
        lax.fori_loop(0, tiles, one_tile, 0)

        @pl.when(e == count - 1)
        def _():
            for c in earlier:
                c.start()

        for g in range(count - 1):
            @pl.when(e == g + 1)
            def _(g=g):
                for c in flush(g):
                    c.wait()
        kind = False
        for g in entire:
            kind = kind | (e == g)
        stage_grads(ST, UA, DA, me_ref[0], order, kind)
        for g in range(count):
            @pl.when(e == g)
            def _(g=g):
                for c in flush(g):
                    c.start()
        return 0
    lax.fori_loop(0, count, one_expert, 0)
    for c in earlier:
        c.wait()
    last = []
    step = min(256, rows)
    line = lax.broadcasted_iota(jnp.int32, (PIECE, step), 0)
    for q in range(chunks):
        r = rows_of[q]
        o, g = OA[r, :], RA[r, :]
        if has[q]:
            o, g = o + X[r, :].astype(F32), g + DY[r, :].astype(F32)
        X[r, :] = o.astype(BF)
        DY[r, :] = g.astype(BF)
        if not has[q]:
            BD[q] = jnp.zeros(BD.shape[1:], BF)
        for i in range(rows // step):
            sl = slice(i * step, (i + 1) * step)
            dots = jnp.where(line == 1, DOT[pl.ds(q * rows + i * step, step), :].T[0:PIECE, :], 0.0)
            BD[q, :, sl] = (BD[q, :, sl].astype(F32) + dots).astype(BF)
        last += [pltpu.make_async_copy(X.at[r], out_refs[q], osem.at[0, q]), pltpu.make_async_copy(DY.at[r], rg_refs[q].at[pl.ds(0, rows)], osem.at[1, q]),
                 pltpu.make_async_copy(BD.at[q], rg_refs[q].at[pl.ds(rows, PIECE)], dsem.at[q])]
        for c in last[-3:]:
            c.start()
    for c in last + flush(count - 1):
        c.wait()


def ffn_experts(me, blocks, bounds, xs, dys, rm, up, down, first, count, whole, base, order, deps=()):
    chunks = len(xs)
    rows, d = xs[0].shape
    lanes, _, f = up.shape
    n = chunks * rows
    tm = TILE_EXPERT
    bits = len(order)
    half = 1 << (bits - 1)
    grad, entire = [jax.ShapeDtypeStruct((k * half, 2, d >> bits, f), BF) for k in (1, 2)]
    part, lined = jax.ShapeDtypeStruct((rows, d), BF), jax.ShapeDtypeStruct((rows + PIECE, d), BF)
    table = n // PIECE + chunks * lanes + 2 * tm // PIECE
    vm = pl.BlockSpec(memory_space=pltpu.VMEM)
    has = tuple(b is not None for b in base[0])
    more = [b for k in range(2) for b in base[k] if b is not None]
    res = pl.pallas_call(
        partial(expert_kernel, (first, count, whole, chunks, rows, d, tm, lanes, order, has, len(deps))),
        name="ffn_experts",
        out_shape=[part] * chunks + [lined] * chunks + [entire] * sum(whole) + [grad] * (2 * (count - sum(whole))),
        in_specs=[SMEM] * 3 + [ANY] * (len(deps) + 2 * chunks) + [vm] + [ANY] * (2 + len(more)),
        out_specs=[ANY] * (2 * chunks + 2 * count - sum(whole)),
        scratch_shapes=[
            pltpu.VMEM((n, d), BF), pltpu.VMEM((n, d), BF), pltpu.VMEM((2, d, f), BF), pltpu.VMEM((2, f, d), BF),
            pltpu.VMEM((d, f), F32), pltpu.VMEM((d, f), F32), pltpu.VMEM((2 * half, 2, d >> bits, f), BF),
            pltpu.VMEM((tm, d), BF), pltpu.VMEM((tm, d), BF), pltpu.VMEM((tm, 128), F32),
            pltpu.VMEM((n, d), F32), pltpu.VMEM((n, d), F32), pltpu.VMEM((n, 128), F32), pltpu.VMEM((chunks, PIECE, d), BF),
            pltpu.SMEM((table,), jnp.int32), pltpu.SMEM((table,), jnp.int32), pltpu.SMEM((table,), jnp.int32),
            pltpu.SemaphoreType.DMA((2 * chunks,)), pltpu.SemaphoreType.DMA((2, 2)), pltpu.SemaphoreType.DMA((2,)), pltpu.SemaphoreType.DMA((2, chunks)), pltpu.SemaphoreType.DMA((chunks,)),
        ],
        cost_estimate=SMALL,
        compiler_params=pltpu.CompilerParams(vmem_limit_bytes=VMEM),
    )(me, blocks, bounds, *deps, *xs, *dys, rm, up, down, *more)
    at = 2 * chunks + sum(whole)
    rest = iter(res[at:])
    keep = [next(rest) for g in range(count) if not whole[g]]
    return res[:chunks], res[chunks:2 * chunks], res[2 * chunks:at], keep, list(rest)


def split_add_kernel(deps, *refs):
    ka, kb, ca, cb, keep, send = refs[deps:]
    keep[...] = (ka[...].astype(F32) + ca[...].astype(F32)).astype(BF)
    send[...] = (kb[...].astype(F32) + cb[...].astype(F32)).astype(BF)


def split_add(kept, came, deps=()):
    h, m, blk, f = kept.shape
    near = pl.BlockSpec((1, m, blk, f), lambda i: (i, 0, 0, 0))
    far = pl.BlockSpec((1, m, blk, f), lambda i: (i + h // 2, 0, 0, 0))
    out = jax.ShapeDtypeStruct((h // 2, m, blk, f), BF)
    return pl.pallas_call(
        partial(split_add_kernel, len(deps)),
        name="split_add",
        grid=(h // 2,),
        in_specs=[ANY] * len(deps) + [near, far, near, far],
        out_specs=[near, near],
        out_shape=[out, out],
        cost_estimate=SMALL,
        compiler_params=pltpu.CompilerParams(vmem_limit_bytes=VMEM),
    )(*deps, kept, kept, came, came)


def last_add_kernel(deps, turns, *refs):
    terms = refs[deps:-len(turns)]
    outs = refs[-len(turns):]
    for k, turned in enumerate(turns):
        total = terms[0][0, k].astype(F32)
        for v in terms[1:]:
            total = total + v[0, k].astype(F32)
        outs[k][...] = (total.T if turned else total).reshape(outs[k].shape)


def last_add(terms, turns, place=None, stacks=None, deps=()):
    _, m, blk, f = terms[0].shape
    shapes = [(f, blk) if turned else (blk, f) for turned in turns]
    aliases = {}
    if place is None:
        out_shape = [jax.ShapeDtypeStruct(s, F32) for s in shapes]
        out_specs = [pl.BlockSpec(s, lambda i: (0, 0)) for s in shapes]
    else:
        count, at = place
        out_shape = [jax.ShapeDtypeStruct((count,) + s, F32) for s in shapes]
        out_specs = [pl.BlockSpec((1,) + s, lambda i: (at, 0, 0)) for s in shapes]
        if stacks is not None:
            aliases = {k: k for k in range(m)}
            deps = tuple(stacks) + tuple(deps)
    full = pl.BlockSpec((1, m, blk, f), lambda i: (0, 0, 0, 0))
    return pl.pallas_call(
        partial(last_add_kernel, len(deps), turns),
        name="last_add",
        grid=(1,),
        in_specs=[ANY] * len(deps) + [full] * len(terms),
        out_specs=out_specs,
        out_shape=out_shape,
        input_output_aliases=aliases,
        cost_estimate=SMALL,
        compiler_params=pltpu.CompilerParams(vmem_limit_bytes=VMEM),
    )(*deps, *terms)


def hold(v, deps):
    return pl.pallas_call(
        lambda *refs: None,
        name="hold",
        in_specs=[ANY] * (1 + len(deps)),
        out_specs=ANY,
        out_shape=jax.ShapeDtypeStruct(v.shape, v.dtype),
        input_output_aliases={0: 0},
        cost_estimate=SMALL,
    )(v, *deps)


HD = 64
LANES = 128


def head_part(v, h):
    lane = lax.broadcasted_iota(jnp.int32, v.shape, 1)
    return jnp.where((lane // HD) == h, v, jnp.zeros((), v.dtype))


def masked_scores(st, key_first, query_first, prefix):
    key_pos = key_first + lax.broadcasted_iota(jnp.int32, st.shape, 0)
    query_pos = query_first + lax.broadcasted_iota(jnp.int32, st.shape, 1)
    seen = key_pos <= query_pos
    if prefix is not None:
        seen = seen | (key_pos < prefix)
    return jnp.where(seen, st, -1e30)


def score_block(k2, qm, half, length, prefix):
    mid = length // 2
    if half == 0:
        return masked_scores(dot(k2[0:mid], qm, 1, 1), 0, 0, prefix)
    low = dot(k2[0:mid], qm, 1, 1)
    high = masked_scores(dot(k2[mid:length], qm, 1, 1), mid, mid, None)
    return jnp.concatenate([low, high], 0)


def attn_forward_kernel(length, pieces, aliased, prefix_ref, at_ref, *refs):
    n1_ref = refs[0]
    w_refs = [(r, i) for r, n in zip(refs[1:], pieces) for i in range(n)]
    q_ref, k_ref, v_ref, ctx_ref, lse_ref = refs[1 + len(pieces) + aliased:]
    mid = length // 2
    prefix = prefix_ref[0]
    n1 = n1_ref[...]
    for out, (w, i) in zip((q_ref, k_ref, v_ref), w_refs):
        out[...] = dot(n1, w[i], 1, 0).astype(BF)
    vt = v_ref[...].T
    k2 = k_ref[...]
    for half in range(2):
        rows = pl.ds(half * mid, mid)
        q2 = q_ref[rows, :] * jnp.asarray(HD ** -0.5, BF)
        keys = mid * (half + 1)
        parts = []
        for h in range(2):
            st = score_block(k2, head_part(q2, h), half, length, prefix)
            top = jnp.max(st, axis=0, keepdims=True)
            p = jnp.exp(st - top)
            total = jnp.sum(p, axis=0, keepdims=True)
            c = dot(vt[h * HD:(h + 1) * HD, 0:keys], p.astype(BF), 1, 0)
            parts.append(c / total)
            lse_ref[0, h:h + 1, rows] = top + jnp.log(total)
        ctx_ref[rows, :] = jnp.concatenate(parts, 0).T.astype(BF)


def attn_forward(prefix, at, n1, ws, heads, earlier=(), deps=()):
    length, d = n1.shape
    pairs = ws[0].shape[2] // LANES
    col = pl.BlockSpec((length, LANES), lambda p, _, at_ref: (0, at_ref[p]))
    out = jax.ShapeDtypeStruct((length, heads), BF)
    done = len(earlier)
    skipped = len(deps)
    return pl.pallas_call(
        skip(partial(attn_forward_kernel, length, tuple(w.shape[0] for w in ws), done), 2, skipped),
        name="attn_forward",
        grid_spec=pltpu.PrefetchScalarGridSpec(
            num_scalar_prefetch=2, grid=(pairs,),
            in_specs=[ANY] * skipped + [pl.BlockSpec((length, d), lambda p, *_: (0, 0))]
            + [pl.BlockSpec((w.shape[0], d, LANES), lambda p, *_: (0, 0, p)) for w in ws] + [ANY] * done,
            out_specs=[col] * 4 + [pl.BlockSpec((1, 8, length), lambda p, _, at_ref: (at_ref[p], 0, 0))]),
        out_shape=[out] * 4 + [jax.ShapeDtypeStruct((heads // LANES, 8, length), F32)],
        input_output_aliases={3 + skipped + len(ws) + k: k for k in range(done)},
        cost_estimate=SMALL,
        compiler_params=pltpu.CompilerParams(vmem_limit_bytes=VMEM),
    )(prefix, at, *deps, n1, *ws, *earlier)


def attn_backward_kernel(length, bits, based, prefix_ref, me_ref, mc_ref, n1_ref, wo_ref, w_ref, q_ref, k_ref, v_ref, ctx_ref, lse_ref, *refs):
    base_ref = refs[0] if based else None
    ng_ref, grad_ref, NG, DC, DK, DV, DQ = refs[based:]
    mid = length // 2
    prefix = prefix_ref[0]
    me = me_ref[0]
    pair = pl.program_id(0)
    mc = mc_ref[...]
    DC[...] = dot(mc, wo_ref[...], 1, 1).astype(BF)
    k2, v2 = k_ref[...], v_ref[...]
    kt = k2.T
    scale = jnp.asarray(HD ** -0.5, BF)
    for half in range(2):
        rows = pl.ds(half * mid, mid)
        q2 = q_ref[rows, :] * scale
        dc2 = DC[rows, :]
        keys = mid * (half + 1)
        dv = jnp.zeros((keys, LANES), F32)
        dk = jnp.zeros((keys, LANES), F32)
        dq = []
        for h in range(2):
            qm, dcm = head_part(q2, h), head_part(dc2, h)
            st = score_block(k2, qm, half, length, prefix)
            p = jnp.exp(st - lse_ref[0, h:h + 1, rows])
            dv = dv + dot(p.astype(BF), dcm, 1, 0)
            dp = dot(v2[0:keys], dcm, 1, 1)
            ds = (p * (dp - jnp.sum(p * dp, axis=0, keepdims=True))).astype(BF)
            dk = dk + dot(ds, qm, 1, 0)
            dq.append(dot(kt[h * HD:(h + 1) * HD, 0:keys], ds, 1, 0))
        DQ[rows, :] = (jnp.concatenate(dq, 0) * HD ** -0.5).T.astype(BF)
        if half == 0:
            DK[0:mid, :] = dk
            DV[0:mid, :] = dv
        else:
            DK[0:mid, :] += dk[0:mid]
            DV[0:mid, :] += dv[0:mid]
            DK[mid:length, :] = dk[mid:length]
            DV[mid:length, :] = dv[mid:length]
    dq, dk, dv = DQ[...], DK[...].astype(BF), DV[...].astype(BF)
    ng = dot(dq, w_ref[0], 1, 1) + dot(dk, w_ref[1], 1, 1) + dot(dv, w_ref[2], 1, 1)

    @pl.when(pair == 0)
    def _():
        NG[...] = ng

    @pl.when(pair > 0)
    def _():
        NG[...] += ng
    n1 = n1_ref[...]
    grads = [dot(n1, x, 0, 0) for x in (dq, dk, dv)] + [dot(mc, ctx_ref[...], 0, 0)]
    blk = n1.shape[1] >> bits
    for c in range(1 << bits):
        slot = slot_of(jnp.int32(c) ^ me, range(bits))
        for i in range(4):
            grad_ref[slot, i] = grads[i][c * blk:(c + 1) * blk].astype(BF)

    @pl.when(pair == pl.num_programs(0) - 1)
    def _():
        done = NG[...]
        if based:
            done = done + base_ref[...].astype(F32)
        ng_ref[...] = done.astype(BF)


def attn_backward(prefix, me, mc, n1, wo, w, saved, base, bits, deps=()):
    q, k, v, ctx, lse = saved
    length, d = n1.shape
    heads = w.shape[2]
    pairs = heads // LANES
    blk = d >> bits
    col = pl.BlockSpec((length, LANES), lambda p, *_: (0, p))
    full = pl.BlockSpec((length, d), lambda p, *_: (0, 0))
    extra = [] if base is None else [base]
    return pl.pallas_call(
        skip(partial(attn_backward_kernel, length, bits, len(extra)), 2, len(deps)),
        name="attn_backward",
        grid_spec=pltpu.PrefetchScalarGridSpec(
            num_scalar_prefetch=2, grid=(pairs,),
            in_specs=[ANY] * len(deps) + [full, full, pl.BlockSpec((LANES, d), lambda p, *_: (p, 0)), pl.BlockSpec((3, d, LANES), lambda p, *_: (0, 0, p)),
                      col, col, col, col, pl.BlockSpec((1, 8, length), lambda p, *_: (p, 0, 0))] + [full] * len(extra),
            out_specs=[full, pl.BlockSpec((1 << bits, 4, blk, LANES), lambda p, *_: (0, 0, 0, p))],
            scratch_shapes=[pltpu.VMEM((length, d), F32), pltpu.VMEM((length, LANES), BF),
                            pltpu.VMEM((length, LANES), F32), pltpu.VMEM((length, LANES), F32), pltpu.VMEM((length, LANES), BF)]),
        out_shape=[jax.ShapeDtypeStruct((length, d), BF), jax.ShapeDtypeStruct((1 << bits, 4, blk, heads), BF)],
        cost_estimate=SMALL,
        compiler_params=pltpu.CompilerParams(vmem_limit_bytes=VMEM),
    )(prefix, me, *deps, mc, n1, wo, w, q, k, v, ctx, lse, *extra)


EPS = 1e-5


def normalise(v):
    centered = v - jnp.mean(v, axis=1, keepdims=True)
    r = lax.rsqrt(jnp.mean(centered * centered, axis=1, keepdims=True) + EPS)
    return centered * r, r


def norm_backward(xhat, r, grad, gain):
    scaled = grad * gain
    return r * (scaled - jnp.mean(scaled, axis=1, keepdims=True) - xhat * jnp.mean(scaled * xhat, axis=1, keepdims=True))


def order_rows(pos, rows_to_slots):
    n = pos.shape[1] if rows_to_slots else pos.shape[0]
    slot = lax.broadcasted_iota(jnp.int32, (n, n), 0 if rows_to_slots else 1)
    return jnp.where(slot == pos, 1.0, 0.0).astype(BF)


def first_norm_kernel(members, j_ref, *refs):
    xs, (gain, shift, dy, pos, out, sorted_dy) = refs[:members], refs[members:]
    for k in range(members):
        @pl.when(pl.program_id(0) == k)
        def _(k=k):
            xhat, _ = normalise(xs[k][...].astype(F32))
            out[...] = (xhat * gain[...] + shift[...]).astype(BF)
            if k == 0:
                sorted_dy[...] = dot(order_rows(pos[...], True), dy[...], 1, 0).astype(BF)


def first_norm(j, xs, gain, shift, dy, pos):
    members = len(xs)
    rows, d = xs[0].shape
    fixed = lambda shape: pl.BlockSpec(shape, lambda p, *_: (0, 0))
    return pl.pallas_call(
        partial(first_norm_kernel, members),
        name="first_norm",
        grid_spec=pltpu.PrefetchScalarGridSpec(
            num_scalar_prefetch=1, grid=(members,),
            in_specs=[fixed((rows, d))] * members + [fixed((1, d))] * 2 + [fixed((rows, d)), fixed((1, rows))],
            out_specs=[pl.BlockSpec((rows, d), lambda p, j_ref: (lax.rem(j_ref[0] + p, members), 0)), fixed((rows, d))]),
        out_shape=[jax.ShapeDtypeStruct((members * rows, d), BF), jax.ShapeDtypeStruct((rows, d), BF)],
        cost_estimate=SMALL,
        compiler_params=pltpu.CompilerParams(vmem_limit_bytes=VMEM),
    )(j, *xs, gain, shift, dy, pos)


def project_kernel(parts, *refs):
    total = dot(refs[0][...], refs[parts][...], 1, 0)
    for i in range(1, parts):
        total = total + dot(refs[i][...], refs[parts + i][...], 1, 0)
    refs[-1][0] = total.astype(BF)


def project(contexts, weights, members):
    parts = len(contexts)
    length, heads = contexts[0].shape
    d = weights[0].shape[1]
    rows = length // members
    return pl.pallas_call(
        partial(project_kernel, parts),
        name="project",
        grid=(members,),
        in_specs=[pl.BlockSpec((rows, heads), lambda p: (p, 0))] * parts + [pl.BlockSpec((heads, d), lambda p: (0, 0))] * parts,
        out_specs=pl.BlockSpec((1, rows, d), lambda p: (p, 0, 0)),
        out_shape=jax.ShapeDtypeStruct((members, rows, d), BF),
        cost_estimate=SMALL,
        compiler_params=pltpu.CompilerParams(vmem_limit_bytes=VMEM),
    )(*contexts, *weights)


def second_norm_kernel(came, x, gain, shift, pos, middle, n2):
    mid = x[...].astype(F32)
    for k in range(came.shape[0]):
        mid = mid + came[k].astype(F32)
    middle[...] = mid
    xhat, _ = normalise(mid)
    normed = (xhat * gain[...] + shift[...]).astype(BF)
    n2[...] = dot(order_rows(pos[...], True), normed, 1, 0).astype(BF)


def second_norm(came, x, gain, shift, pos):
    rows, d = x.shape
    fixed = lambda shape: pl.BlockSpec(shape, lambda p: (0,) * len(shape))
    return pl.pallas_call(
        second_norm_kernel,
        name="second_norm",
        grid=(1,),
        in_specs=[fixed(came.shape), fixed((rows, d)), fixed((1, d)), fixed((1, d)), fixed((1, rows))],
        out_specs=[fixed((rows, d))] * 2,
        out_shape=[jax.ShapeDtypeStruct((rows, d), F32), jax.ShapeDtypeStruct((rows, d), BF)],
        cost_estimate=SMALL,
        compiler_params=pltpu.CompilerParams(vmem_limit_bytes=VMEM),
    )(came, x, gain, shift, pos)


def add_small(a, b, deps):
    def kernel(*refs):
        refs[-1][...] = refs[-3][...] + refs[-2][...]
    full = pl.BlockSpec(memory_space=pltpu.VMEM)
    return pl.pallas_call(kernel, name="add_small", in_specs=[ANY] * len(deps) + [full, full], out_specs=full,
                          out_shape=jax.ShapeDtypeStruct(a.shape, a.dtype), cost_estimate=SMALL)(*deps, a, b)


def hi_lo(v):
    hi = v.astype(BF)
    return hi, (v - hi.astype(F32)).astype(BF)


def middle_backward_kernel(single, bnd_ref, t_ref, *refs):
    it = iter(refs)
    parts = [next(it) for _ in range(single)]
    n2, rm, middle, dy, gain, pos, mg_ref, mc_ref, sums_ref = it
    t = t_ref[0]
    n2v, rmv = n2[...], rm[...]
    rows = n2v.shape[0]
    total = parts[0][0:rows, :].astype(F32)
    lines = parts[0][rows:rows + PIECE, 0:rows].astype(F32)
    for p in parts[1:]:
        total = total + p[0:rows, :].astype(F32)
        lines = lines + p[rows:rows + PIECE, 0:rows].astype(F32)
    dots = jnp.concatenate([lines, jnp.zeros((128 - PIECE, rows), F32)], axis=0).T
    experts = bnd_ref.shape[1] - 1
    logits = dot(n2v, rmv, 1, 0)
    route_prob = lane_softmax(logits, 0, experts)
    mixing = lane_softmax(logits, experts, experts + 2)
    row = lax.broadcasted_iota(jnp.int32, (rows, 1), 0)
    route = jnp.zeros((rows, 1), jnp.int32)
    for e in range(1, experts):
        route = route + (row >= bnd_ref[t, e]).astype(jnp.int32)
    gate = pick_lane(route_prob, route)
    m0, m1 = pick_lane(mixing, experts), pick_lane(mixing, experts + 1)
    dense_dot, expert_dot = dots[:, 0:1], dots[:, 1:2]
    d0, d1 = dense_dot, expert_dot * gate
    inner = m0 * d0 + m1 * d1
    lane = lax.broadcasted_iota(jnp.int32, logits.shape, 1)
    grad = expert_dot * (m1 * gate) * (jnp.where(lane == route, 1.0, 0.0) - route_prob)
    grad = jnp.where(lane < experts, grad, 0.0)
    grad = jnp.where(lane == experts, m0 * (d0 - inner), grad)
    grad = jnp.where(lane == experts + 1, m1 * (d1 - inner), grad)
    hi, lo = hi_lo(grad)
    total = total + dot(hi, rmv, 1, 1) + dot(lo, rmv, 1, 1)
    sums_ref[0:8, :] = (dot(hi.T, n2v, 1, 0) + dot(lo.T, n2v, 1, 0))[0:8]
    g = dot(order_rows(pos[...], False), total.astype(BF), 1, 0)
    xhat, r = normalise(middle[...])
    sums_ref[8:16, :] = jnp.zeros((8, g.shape[1]), F32)
    sums_ref[8:9, :] = jnp.sum(g * xhat, axis=0, keepdims=True)
    sums_ref[9:10, :] = jnp.sum(g, axis=0, keepdims=True)
    mg = dy[...].astype(F32) + norm_backward(xhat, r, g, gain[...])
    mg_ref[...] = mg
    for k in range(mc_ref.shape[0]):
        mc_ref[k] = mg.astype(BF)


def middle_backward(bounds, t, parts, n2, rm, middle, dy, gain, pos, members, deps=()):
    rows, d = n2.shape
    fixed = lambda shape: pl.BlockSpec(shape, lambda p, *_: (0, 0))
    big = fixed((rows, d))
    return pl.pallas_call(
        skip(partial(middle_backward_kernel, len(parts)), 2, len(deps)),
        name="middle_backward",
        grid_spec=pltpu.PrefetchScalarGridSpec(
            num_scalar_prefetch=2, grid=(1,),
            in_specs=[ANY] * len(deps) + [fixed((rows + PIECE, d))] * len(parts)
            + [big, fixed((d, 128)), big, big, fixed((1, d)), fixed((rows, 1))],
            out_specs=[big, pl.BlockSpec((members, rows, d), lambda p, *_: (0, 0, 0)), fixed((16, d))]),
        out_shape=[jax.ShapeDtypeStruct((rows, d), F32), jax.ShapeDtypeStruct((members, rows, d), BF), jax.ShapeDtypeStruct((16, d), F32)],
        cost_estimate=SMALL,
        compiler_params=pltpu.CompilerParams(vmem_limit_bytes=VMEM),
    )(bounds, t, *deps, *parts, n2, rm, middle, dy, gain, pos)


def layer_out_kernel(*refs):
    parts, (middle, pos, out) = refs[:-3], refs[-3:]
    total = parts[0][...].astype(F32)
    for p in parts[1:]:
        total = total + p[...].astype(F32)
    hi, lo = hi_lo(total)
    move = order_rows(pos[...], False)
    out[...] = (middle[...] + dot(move, hi, 1, 0) + dot(move, lo, 1, 0)).astype(BF)


def layer_out(parts, middle, pos, deps=()):
    rows, d = middle.shape
    big = pl.BlockSpec((rows, d), lambda p: (0, 0))
    return pl.pallas_call(
        skip(layer_out_kernel, 0, len(deps)),
        name="layer_out",
        grid=(1,),
        in_specs=[ANY] * len(deps) + [big] * (len(parts) + 1) + [pl.BlockSpec((rows, 1), lambda p: (0, 0))],
        out_specs=big,
        out_shape=jax.ShapeDtypeStruct((rows, d), BF),
        cost_estimate=SMALL,
        compiler_params=pltpu.CompilerParams(vmem_limit_bytes=VMEM),
    )(*deps, *parts, middle, pos)


def add_parts_kernel(*refs):
    total = refs[0][...].astype(F32)
    for p in refs[1:-1]:
        total = total + p[...].astype(F32)
    refs[-1][...] = total.astype(BF)


def add_parts(parts, deps=()):
    rows, d = parts[0].shape
    tile = pl.BlockSpec((rows, d), lambda p: (p, 0))
    return pl.pallas_call(
        skip(add_parts_kernel, 0, len(deps)),
        name="add_parts",
        grid=(1,),
        in_specs=[ANY] * len(deps) + [tile] * len(parts),
        out_specs=tile,
        out_shape=jax.ShapeDtypeStruct((rows, d), BF),
        cost_estimate=SMALL,
        compiler_params=pltpu.CompilerParams(vmem_limit_bytes=VMEM),
    )(*deps, *parts)


def input_backward_kernel(parts, x, mg, gain, out, sums):
    g = parts[0].astype(F32)
    for k in range(1, parts.shape[0]):
        g = g + parts[k].astype(F32)
    xhat, r = normalise(x[...].astype(F32))
    sums[...] = jnp.zeros_like(sums)
    sums[0:1, :] = jnp.sum(g * xhat, axis=0, keepdims=True)
    sums[1:2, :] = jnp.sum(g, axis=0, keepdims=True)
    out[...] = mg[...] + norm_backward(xhat, r, g, gain[...])


def input_backward(parts, x, mg, gain, deps=()):
    rows, d = x.shape
    fixed = lambda shape: pl.BlockSpec(shape, lambda p: (0, 0))
    big = fixed((rows, d))
    return pl.pallas_call(
        skip(input_backward_kernel, 0, len(deps)),
        name="input_backward",
        grid=(1,),
        in_specs=[ANY] * len(deps) + [pl.BlockSpec(parts.shape, lambda p: (0, 0, 0))] + [big] * 2 + [fixed((1, d))],
        out_specs=[big, fixed((8, d))],
        out_shape=[jax.ShapeDtypeStruct((rows, d), F32), jax.ShapeDtypeStruct((8, d), F32)],
        cost_estimate=SMALL,
        compiler_params=pltpu.CompilerParams(vmem_limit_bytes=VMEM),
    )(*deps, parts, x, mg, gain)


class Everywhere:
    def __init__(self, v):
        self.v = v
        bits = {axis: lax.axis_size(axis).bit_length() - 1 for axis in ("tensor", "dp")}
        self.hops = [("tensor", 1 << b) for b in range(bits["tensor"])] + [("dp", 1 << b) for b in range(bits["dp"])]
        self.launch()

    def launch(self):
        if self.hops:
            axis, bit = self.hops.pop(0)
            self.came = lax.ppermute(self.v, axis, [(i, i ^ bit) for i in range(lax.axis_size(axis))])
        else:
            self.came = None

    def add(self, mark):
        if self.came is None:
            return mark
        self.v = add_small(self.v, self.came, mark)
        self.launch()
        return (self.v,)


def over_dp(v, bit):
    return lax.ppermute(v, "dp", [(i, i ^ (1 << bit)) for i in range(lax.axis_size("dp"))])


def shards(inputs, cotangent, routes, prefixes, gain_one, shift_one, qkv_weight, out_weight, gain_two, shift_two,
           up_weight, down_weight, expert_up, expert_down, router_weight, mix_weight):
    rows, d = inputs.shape
    tensor = lax.axis_size("tensor")
    dp = lax.axis_size("dp")
    bits = dp.bit_length() - 1
    seqs = prefixes.shape[0]
    members = tensor // seqs
    experts = expert_up.shape[0]
    heads = qkv_weight.shape[2]
    pairs = heads // LANES
    t = lax.axis_index("tensor")
    s, j = t // members, t % members
    me = lax.axis_index("dp").astype(jnp.int32)
    me1, j1, t1 = me.reshape(1), j.astype(jnp.int32).reshape(1), t.astype(jnp.int32).reshape(1)
    place = lambda a, b: (a % seqs) * members + b % members
    everyone = [(a, b) for a in range(seqs) for b in range(members)]

    def from_member(v, k):
        return lax.ppermute(v, "tensor", [(place(a, b), place(a, b - k)) for a, b in everyone])

    def from_sequence(v, k):
        return lax.ppermute(v, "tensor", [(place(a, b), place(a - k, b)) for a, b in everyone])

    def to_member(v, k):
        return from_member(v, -k)

    def to_sequence(v, k):
        return from_sequence(v, -k)

    route_blocks = routes.reshape(tensor, rows)
    bounds = jnp.stack([jnp.sum((route_blocks < e).astype(jnp.int32), axis=1) for e in range(experts + 1)], axis=1)
    key_col = lax.dynamic_slice_in_dim(routes, t * rows, rows, 0) * rows + jnp.arange(rows, dtype=jnp.int32)[:, None]
    key_row = key_col.reshape(1, rows)
    pos_row = jnp.sum((key_col < key_row).astype(jnp.int32), axis=0, keepdims=True)
    pos_col = jnp.sum((key_row < key_col).astype(jnp.int32), axis=1, keepdims=True)
    chunk = [(dj, ds) for dj in range(members) for ds in range(seqs)]
    blocks = jnp.stack([((s + ds) % seqs) * members + (j + dj) % members for dj, ds in chunk]).astype(jnp.int32)
    near = [q for q, (dj, ds) in enumerate(chunk) if ds == 0]
    far = [q for q, (dj, ds) in enumerate(chunk) if ds > 0]

    xs = [inputs] + [from_member(inputs, k) for k in range(1, members)]
    flip = me & 1
    relay = pairs % 2 == 0 and dp > 1
    w_own = jnp.transpose(qkv_weight, (1, 0, 2))
    fetched = []
    for ds in range(1, seqs):
        if relay:
            half = lax.dynamic_slice_in_dim(qkv_weight, flip * (heads // 2), heads // 2, 2)
            fetched.append([from_sequence(jnp.transpose(half[:, a:b], (1, 0, 2)), ds) for a, b in ((0, 2), (2, 3))])
        else:
            fetched.append([from_sequence(w_own, ds)])
    wo_all = [out_weight] + [from_sequence(out_weight, ds) for ds in range(1, seqs)]
    gain_one, shift_one, gain_two, shift_two = [v.reshape(1, d) for v in (gain_one, shift_one, gain_two, shift_two)]
    prefix = lax.dynamic_slice_in_dim(prefixes, s, 1)
    rm = jnp.concatenate([router_weight, mix_weight, jnp.zeros((d, LANES - experts - 2), BF)], axis=1)
    n1, dys = first_norm(j1, xs, gain_one, shift_one, cotangent, pos_row)
    columns = jnp.arange(pairs, dtype=jnp.int32)
    pieces = [[] for _ in fetched]
    fence = (n1,)
    if relay:
        for k, got in enumerate(fetched):
            held = hold(got[0], (n1,))
            pieces[k] = [[held], [over_dp(held, 0)]]
            fence += (held,)
    saved = [attn_forward(prefix, columns, n1, [w_own], heads, deps=fence[1:] + (rm,))]
    if relay:
        for k, got in enumerate(fetched):
            held = hold(got[1], (saved[0][4],))
            pieces[k][0].append(held)
            pieces[k][1].append(over_dp(held, 0))
    else:
        pieces = [[got] for got in fetched]
    w_all = [w_own]
    for halves in pieces:
        part = ()
        for k, ws in enumerate(halves):
            at = (columns + (flip ^ k) * (pairs // 2))[:pairs // 2] if relay else columns
            part = attn_forward(prefix, at, n1, ws, heads, part, deps=() if part else (saved[-1][4],))
        saved.append(part)
        whole = [jnp.concatenate(ws, axis=0) for ws in halves]
        if relay:
            whole = [jnp.where(flip == 0, jnp.concatenate(whole, axis=2), jnp.concatenate(whole[::-1], axis=2))]
        w_all.append(whole[0])
    contexts = [v[3] for v in saved]

    def spread(mine):
        out = list(mine)
        for k in range(1, members):
            out += [from_member(m, k) for m in mine]
        return out

    dy_mine = [dys] + [from_sequence(dys, ds) for ds in range(1, seqs)]
    dy_near = [dys] + [from_member(dys, k) for k in range(1, members)]
    sent = project(contexts, wo_all, members)

    def exchange(v):
        return lax.all_to_all(v, "tensor", 0, 0, axis_index_groups=[[place(a, b) for b in range(members)] for a in range(seqs)], tiled=True)

    came = exchange(sent)
    middle, n2 = second_norm(came, inputs, gain_two, shift_two, pos_row)
    n2_mine = [n2] + [from_sequence(n2, ds) for ds in range(1, seqs)]
    n2_near = [n2] + [from_member(n2, k) for k in range(1, members)]

    straight = tuple(range(bits))
    pick = lambda v, which: [v[q] for q in which]
    out_a, rg_a, sums = ffn_dense(me1, n2_near, dy_near, rm, up_weight, down_weight, experts, straight, deps=tuple(dy_mine[1:]))
    n2_all, dy_all = [], []
    n2_far, dy_far = [[hold(v, (out_a[0],)) for v in mine[1:]] for mine in (n2_mine, dy_mine)]
    for k in range(members):
        n2_all += [n2_near[k]] + [from_member(v, k) if k else v for v in n2_far]
        dy_all += [dy_near[k]] + [from_member(v, k) if k else v for v in dy_far]
    base = [[None] * tensor, [None] * tensor]
    for k, q in enumerate(near):
        base[0][q], base[1][q] = out_a[k], rg_a[k]
    by_scatter = [e == 0 for e in range(experts)]
    out_e, rg_e, whole, keep_e, send_e = ffn_experts(me1, blocks, bounds, n2_all, dy_all, rm, expert_up, expert_down, 0, 1, (True,), base, straight)
    out_e, rg_e, whole = list(out_e), list(rg_e), list(whole)
    out_b, rg_b, ends = ffn_dense(me1, pick(n2_all, far), pick(dy_all, far), rm, up_weight, down_weight, experts, straight,
                                  (pick(out_e, far), pick(rg_e, far)), sums)
    for k, q in enumerate(far):
        out_e[q], rg_e[q] = out_b[k], rg_b[k]
    if experts > 1:
        out_e, rg_e, entire, keep_e, send_e = ffn_experts(me1, blocks, bounds, n2_all, dy_all, rm, expert_up, expert_down, 1, experts - 1, tuple(by_scatter[1:]), (out_e, rg_e), straight)
        whole += list(entire)

    index = {c: q for q, c in enumerate(chunk)}
    def to_owner(parts):
        mine = [[parts[index[0, ds]]] + [to_member(parts[index[k, ds]], k) for k in range(1, members)] for ds in range(seqs)]
        return mine[0], mine[1:]

    def onward(terms, deps):
        sums = [add_parts(v, deps) for v in terms]
        return [to_sequence(v, ds + 1) for ds, v in enumerate(sums)], sums

    class Halving:
        def __init__(self, keep, send, order):
            self.keep, self.send, self.order, self.at = keep, send, order, 0

        def launch(self, deps=()):
            if deps:
                self.send = hold(self.send, deps)
            self.came = over_dp(self.send, self.order[self.at])
            self.at += 1

        def add(self, mark):
            self.keep, self.send = split_add(self.keep, self.came, mark)
            self.launch()
            return (self.send,)

        def rest(self, mark):
            while self.at < bits:
                mark = self.add(mark)
            return mark

    scattered = []
    for v in whole:
        flat = lax.psum_scatter(v.reshape(-1, v.shape[-1]), "dp", scatter_dimension=0, tiled=True)
        scattered.append(flat.reshape((1,) + v.shape[1:]))

    halvings = [Halving(keep, send, straight) for keep, send in zip(keep_e, send_e)]
    dense_sum = Halving(ends[0], ends[1], straight)
    sum_of = dict(enumerate(scattered + halvings))
    rg_near, rg_far = to_owner(rg_e)
    for v in [dense_sum] + halvings[:2]:
        v.launch()
    mark = dense_sum.add((out_e[0],))
    came_far, terms = onward(rg_far, mark)
    mark = tuple(terms[:1]) + tuple(w_all[1:])
    mg, mc, sums_two = middle_backward(bounds, t1, rg_near + came_far, n2, rm, middle, cotangent, gain_two, pos_col, members, mark)
    mcs = exchange(mc).reshape(members * rows, d)
    mark = dense_sum.add((mc,))
    ngs = None
    grads = [None] * seqs
    for ds in list(range(1, seqs)) + [0]:
        ngs, grads[ds] = attn_backward(prefix, me1, mcs, n1, wo_all[ds], w_all[ds], saved[ds], ngs, bits, mark)
        mark = (grads[ds],)
        if ds == 1 or seqs == 1:
            for v in halvings[2:]:
                v.launch()
            for v in halvings[:1]:
                mark = v.add(mark)
    moved = [to_sequence(grads[ds], ds) for ds in range(1, seqs)]
    ng_parts = exchange(ngs.reshape(members, rows, d))
    mark = dense_sum.rest(mark)
    up_out, down_out = last_add([dense_sum.keep, dense_sum.came], (False, True), deps=mark)
    mark = (up_out,)
    for v in halvings[1:2]:
        mark = v.add(mark)
    for v in halvings[:1]:
        mark = v.add(mark)
    input_grad, sums_one = input_backward(ng_parts, inputs, mg, gain_one, mark)
    mark = (sums_one,)
    sums = Everywhere(jnp.concatenate([sums_two, sums_one], axis=0))
    stacks = None

    def finish(e, mark):
        if by_scatter[e]:
            terms = [sum_of[e]]
        else:
            mark = sum_of[e].rest(mark)
            terms = [sum_of[e].keep, sum_of[e].came]
        done = last_add(terms, (False, True), (experts, e), stacks, mark)
        return done, (done[1],)

    keep = grads[0]
    for v in moved[:-1]:
        keep = (keep.astype(F32) + v.astype(F32)).astype(BF)
    if moved:
        keep, send = split_add(keep, moved[-1], mark)
        mark = (send,)
    else:
        keep, send = keep[:dp // 2], keep[dp // 2:]
    attn_sum = Halving(keep, send, straight)
    attn_sum.launch()
    mark = sums.add(mark)
    stacks, mark = finish(0, mark)
    mark = sums.add(mark)
    for v in halvings[1:2]:
        mark = v.add(mark)
    for v in halvings[2:]:
        mark = v.add(mark)
    for e in range(1, min(3, experts)):
        stacks, mark = finish(e, mark)
    mark = sums.add(mark)
    mark = attn_sum.add(mark)
    for v in halvings[2:]:
        mark = v.add(mark)
    out_near, out_far = to_owner([hold(v, mark) for v in out_e])
    out_came, terms = onward(out_far, mark)
    mark = tuple(terms[:1]) or mark
    mark = attn_sum.add(mark)
    mark = sums.add(mark)
    for e in range(3, experts):
        stacks, mark = finish(e, mark)
    expert_up_out, expert_down_out = stacks
    mark = sums.add(mark)
    layer_output = layer_out(out_near + out_came, middle, pos_col, mark)
    mark = (layer_output,)
    while sums.came is not None:
        mark = sums.add(mark)
    mark = attn_sum.rest(mark)
    *qkv_parts, out_out = last_add([attn_sum.keep, attn_sum.came], (False, False, False, True), deps=mark)
    lanes = d // (dp * tensor)
    begin = (me * tensor + t) * lanes
    small = lax.dynamic_slice_in_dim(sums.v, begin, lanes, 1)
    return (layer_output, input_grad, small[16], small[17], jnp.stack(qkv_parts, axis=1), out_out, small[8], small[9], up_out, down_out,
            expert_up_out, expert_down_out, small[0:experts].T, small[experts:experts + 2].T)


def solution(mesh):
    both = ("dp", "tensor")
    in_specs = (P(both, None), P(both, None), P("dp", None), P("dp"), P(), P(), P(None, None, "tensor"), P("tensor", None), P(), P(),
                P(None, "tensor"), P("tensor", None), P(None, None, "tensor"), P(None, "tensor", None), P(), P())
    out_specs = (P(both, None), P(both, None), P(both), P(both), P("dp", None, "tensor"), P("tensor", "dp"), P(both), P(both),
                 P("dp", "tensor"), P("tensor", "dp"), P(None, "dp", "tensor"), P(None, "tensor", "dp"), P(both, None), P(both, None))
    return jax.shard_map(shards, mesh=mesh, in_specs=in_specs, out_specs=out_specs, check_vma=False)
```

```python
from functools import partial
import jax, jax.numpy as jnp
from jax import lax
from jax.experimental import pallas as pl
from jax.experimental.pallas import tpu as pltpu
from jax.sharding import PartitionSpec as P

BF = jnp.bfloat16
F32 = jnp.float32
TILE_DENSE = 512
TILE_EXPERT = 304
PIECE = 16
SMALL = pl.CostEstimate(flops=0, bytes_accessed=0, transcendentals=0)
VMEM = 60 * 1024 * 1024
ANY = pl.BlockSpec(memory_space=pltpu.HBM)
SMEM = pl.BlockSpec(memory_space=pltpu.SMEM)


def dot(a, b, ca, cb):
    return lax.dot_general(a, b, (((ca,), (cb,)), ((), ())), preferred_element_type=F32)


def slot_of(value, order):
    out = jnp.int32(0)
    for k, bit in enumerate(order):
        out = out | (((value >> bit) & 1) << (len(order) - 1 - k))
    return out


def skip(kernel, scalars, deps):
    return lambda *refs: kernel(*refs[:scalars], *refs[scalars + deps:])


def lane_softmax(logits, first, last):
    lane = lax.broadcasted_iota(jnp.int32, logits.shape, 1)
    inside = (lane >= first) & (lane < last)
    masked = jnp.where(inside, logits, -1e30)
    top = jnp.max(masked, axis=1, keepdims=True)
    e = jnp.where(inside, jnp.exp(masked - top), 0.0)
    return e / jnp.sum(e, axis=1, keepdims=True)


def pick_lane(v, index):
    lane = lax.broadcasted_iota(jnp.int32, v.shape, 1)
    return jnp.sum(jnp.where(lane == index, v, 0.0), axis=1, keepdims=True)


def gelu_parts(pre):
    phi = 0.5 * (1.0 + lax.erf(pre * 0.7071067811865476))
    pdf = jnp.exp(pre * pre * -0.5) * 0.3989422804014327
    return pre * phi, phi + pre * pdf


def ffn_tile(lanes, rm, xt, dyt, coef_of, up_w, dn_w, UA, DA, ready):
    logits = dot(xt, rm[...], 1, 0)
    mixing = lane_softmax(logits, lanes, lanes + 2)
    coef = coef_of(logits, mixing)
    pre = dot(xt, up_w[...], 1, 0)
    g = dot(dyt, dn_w[...], 1, 1)
    hid, dg = gelu_parts(pre)
    hid = hid.astype(BF)
    dots = jnp.sum(hid.astype(F32) * g, axis=1, keepdims=True)
    pg = (g * dg * coef).astype(BF)
    cot = (dyt.astype(F32) * coef).astype(BF)
    out = dot(hid, dn_w[...], 1, 0) * coef
    rg = dot(pg, up_w[...], 1, 1)
    ready()
    UA[...] += dot(xt, pg, 0, 0)
    DA[...] += dot(cot, hid, 0, 0)
    return dots, out, rg


def stage_grads(ST, UA, DA, me, order, whole):
    bits = len(order)
    blk = UA.shape[0] >> bits

    def body(c, _):
        r = pl.ds(pl.multiple_of(c * blk, blk), blk)
        slot = jnp.where(whole, c, slot_of(c ^ me, order))
        ST[slot, 0] = UA[r, :].astype(BF)
        ST[slot, 1] = DA[r, :].astype(BF)
        return 0
    lax.fori_loop(0, 1 << bits, body, 0)


def dots_rows(dots):
    return jnp.broadcast_to(dots, (dots.shape[0], 128)).T[0:PIECE, :]


def dense_kernel(cfg, me_ref, *refs):
    chunks, rows, tm, lanes, order, first, deps = cfg
    it = iter(refs[deps:])
    take = lambda k: [next(it) for _ in range(k)]
    x_hbm, dy_hbm = take(chunks), take(chunks)
    rm, up_hbm, dn_hbm = take(3)
    base_o, base_r, sums_in = ([], [], []) if first else (take(chunks), take(chunks), take(2))
    out_refs, rg_refs = take(chunks), take(chunks)
    ends = take(2)
    X, DY, UP, DN, UA, DA, OB, RB, DT, OD, xsem, wsem, gsem, osem, dsem = take(15)
    ST, BO, BR, BD, bsem = (None,) * 5 if first else take(5)
    per = rows // tm
    weights = [pltpu.make_async_copy(up_hbm, UP, wsem.at[0]), pltpu.make_async_copy(dn_hbm, DN, wsem.at[1])]
    loads, bases = [], []
    for q in range(chunks):
        sl = pl.ds(q * rows, rows)
        loads.append([pltpu.make_async_copy(x_hbm[q], X.at[sl], xsem.at[q]), pltpu.make_async_copy(dy_hbm[q], DY.at[sl], xsem.at[chunks + q])])
        if not first:
            bases.append([pltpu.make_async_copy(base_o[q], BO.at[sl], bsem.at[q]), pltpu.make_async_copy(base_r[q].at[pl.ds(0, rows)], BR.at[sl], bsem.at[chunks + q]),
                          pltpu.make_async_copy(base_r[q].at[pl.ds(rows, PIECE)], BD.at[q], bsem.at[2 * chunks + q])])
    sums = [] if first else [pltpu.make_async_copy(sums_in[0], UA, gsem.at[0]), pltpu.make_async_copy(sums_in[1], DA, gsem.at[1])]
    for c in loads[0] + weights + sums + [c for q in loads[1:] for c in q] + [c for q in bases for c in q]:
        c.start()
    DT[...] = jnp.zeros_like(DT)
    if first:
        UA[...] = jnp.zeros_like(UA)
        DA[...] = jnp.zeros_like(DA)
    for c in weights:
        c.wait()

    def outs(q, part, slot):
        sl = pl.ds(part * tm, tm)
        return [pltpu.make_async_copy(OB.at[slot], out_refs[q].at[sl], osem.at[0, slot]),
                pltpu.make_async_copy(RB.at[slot], rg_refs[q].at[sl], osem.at[1, slot])]

    def one(i, _):
        slot = i % 2
        sl = pl.ds(pl.multiple_of(i * tm, tm), tm)
        for q in range(chunks):
            @pl.when(i == q * per)
            def _(q=q):
                for c in loads[q]:
                    c.wait()

        def ready():
            if not first:
                @pl.when(i == 0)
                def _():
                    for c in sums:
                        c.wait()
        dots, out, rg = ffn_tile(lanes, rm, X[sl, :], DY[sl, :], lambda l, m: pick_lane(m, lanes), UP, DN, UA, DA, ready)
        lines = dots_rows(dots)
        line = lax.broadcasted_iota(jnp.int32, lines.shape, 0)
        for q in range(chunks):
            for part in range(per):
                @pl.when(i == q * per + part)
                def _(q=q, part=part):
                    DT[q, :, part * tm:(part + 1) * tm] = jnp.where(line == 0, lines, 0.0)
        if not first:
            for q in range(chunks):
                @pl.when(i == q * per)
                def _(q=q):
                    for c in bases[q]:
                        c.wait()
            out = out + BO[sl, :].astype(F32)
            rg = rg + BR[sl, :].astype(F32)

        @pl.when(i >= 2)
        def _():
            for c in outs(0, 0, slot):
                c.wait()
        OB[slot] = out.astype(BF)
        RB[slot] = rg.astype(BF)
        for q in range(chunks):
            for part in range(per):
                @pl.when(i == q * per + part)
                def _(q=q, part=part):
                    for c in outs(q, part, slot):
                        c.start()
        return 0
    lax.fori_loop(0, chunks * per, one, 0)
    lines = []
    for q in range(chunks):
        total = DT[q] if first else DT[q] + BD[q].astype(F32)
        OD[q] = total.astype(BF)
        lines.append(pltpu.make_async_copy(OD.at[q], rg_refs[q].at[pl.ds(rows, PIECE)], dsem.at[q]))
    if first:
        last = lines + [pltpu.make_async_copy(UA, ends[0], gsem.at[0]), pltpu.make_async_copy(DA, ends[1], gsem.at[1])]
    else:
        stage_grads(ST, UA, DA, me_ref[0], order, False)
        half = ST.shape[0] // 2
        last = lines + [pltpu.make_async_copy(ST.at[pl.ds(h * half, half)], ends[h], gsem.at[h]) for h in range(2)]
    for c in last:
        c.start()
    for slot in range(min(2, chunks * per)):
        for c in outs(0, 0, slot):
            c.wait()
    for c in last:
        c.wait()


def ffn_dense(me, xs, dys, rm, up, down, lanes, order, base=None, sums=None, deps=()):
    chunks = len(xs)
    rows, d = xs[0].shape
    f = up.shape[1]
    n = chunks * rows
    tm = min(TILE_DENSE, rows)
    first = base is None
    bits = len(order)
    half = 1 << (bits - 1)
    vm = pl.BlockSpec(memory_space=pltpu.VMEM)
    part, lined = jax.ShapeDtypeStruct((rows, d), BF), jax.ShapeDtypeStruct((rows + PIECE, d), BF)
    total = jax.ShapeDtypeStruct((d, f), F32)
    grad = jax.ShapeDtypeStruct((half, 2, d >> bits, f), BF)
    ends = [total] * 2 if first else [grad] * 2
    more = [] if first else list(base[0]) + list(base[1]) + list(sums)
    scratch = [pltpu.VMEM((n, d), BF), pltpu.VMEM((n, d), BF), pltpu.VMEM((d, f), BF), pltpu.VMEM((f, d), BF), pltpu.VMEM((d, f), F32), pltpu.VMEM((d, f), F32),
               pltpu.VMEM((2, tm, d), BF), pltpu.VMEM((2, tm, d), BF), pltpu.VMEM((chunks, PIECE, d), F32), pltpu.VMEM((chunks, PIECE, d), BF),
               pltpu.SemaphoreType.DMA((2 * chunks,)), pltpu.SemaphoreType.DMA((2,)), pltpu.SemaphoreType.DMA((2,)), pltpu.SemaphoreType.DMA((2, 2)), pltpu.SemaphoreType.DMA((chunks,))]
    if not first:
        scratch += [pltpu.VMEM((2 * half, 2, d >> bits, f), BF), pltpu.VMEM((n, d), BF), pltpu.VMEM((n, d), BF), pltpu.VMEM((chunks, PIECE, d), BF), pltpu.SemaphoreType.DMA((3 * chunks,))]
    res = pl.pallas_call(
        partial(dense_kernel, (chunks, rows, tm, lanes, order, first, len(deps))),
        name="ffn_dense",
        out_shape=[part] * chunks + [lined] * chunks + ends,
        in_specs=[SMEM] + [ANY] * (len(deps) + 2 * chunks) + [vm] + [ANY] * (2 + len(more)),
        out_specs=[ANY] * (2 * chunks + len(ends)),
        scratch_shapes=scratch,
        cost_estimate=SMALL,
        compiler_params=pltpu.CompilerParams(vmem_limit_bytes=VMEM),
    )(me, *deps, *xs, *dys, rm, up, down, *more)
    return res[:chunks], res[chunks:2 * chunks], res[2 * chunks:]


def expert_kernel(cfg, me_ref, blk_ref, bnd_ref, *refs):
    first, count, whole, chunks, rows, d, tm, lanes, order, has, deps = cfg
    n = chunks * rows
    it = iter(refs[deps:])
    take = lambda k: [next(it) for _ in range(k)]
    x_hbm, dy_hbm = take(chunks), take(chunks)
    rm, up_hbm, dn_hbm = take(3)
    based = [q for q in range(chunks) if has[q]]
    base_o, base_r = take(len(based)), take(len(based))
    out_refs, rg_refs = take(chunks), take(chunks)
    entire = [g for g in range(count) if whole[g]]
    halved = [g for g in range(count) if not whole[g]]
    whole_refs, keep_refs, send_refs = take(len(entire)), take(len(halved)), take(len(halved))
    X, DY, UP, DN, UA, DA, ST, XG, DG, VAL, OA, RA, DOT, BD, TR, TL, TH, xsem, wsem, gsem, osem, dsem = it
    half = ST.shape[0] // 2
    pieces = tm // PIECE
    rows_of = [pl.ds(q * rows, rows) for q in range(chunks)]
    copies = []
    for q in range(chunks):
        copies.append(pltpu.make_async_copy(x_hbm[q], X.at[rows_of[q]], xsem.at[q]))
        copies.append(pltpu.make_async_copy(dy_hbm[q], DY.at[rows_of[q]], xsem.at[chunks + q]))
    earlier = []
    for k, q in enumerate(based):
        earlier.append(pltpu.make_async_copy(base_o[k], X.at[rows_of[q]], xsem.at[q]))
        earlier.append(pltpu.make_async_copy(base_r[k].at[pl.ds(0, rows)], DY.at[rows_of[q]], xsem.at[chunks + q]))
        earlier.append(pltpu.make_async_copy(base_r[k].at[pl.ds(rows, PIECE)], BD.at[q], dsem.at[q]))

    def weights(e, slot):
        return [pltpu.make_async_copy(up_hbm.at[first + e], UP.at[slot], wsem.at[slot, 0]),
                pltpu.make_async_copy(dn_hbm.at[first + e], DN.at[slot], wsem.at[slot, 1])]

    def flush(g):
        if whole[g]:
            return [pltpu.make_async_copy(ST, whole_refs[entire.index(g)], gsem.at[0])]
        g = halved.index(g)
        return [pltpu.make_async_copy(ST.at[pl.ds(0, half)], keep_refs[g], gsem.at[0]),
                pltpu.make_async_copy(ST.at[pl.ds(half, half)], send_refs[g], gsem.at[1])]

    for c in copies + weights(0, 0):
        c.start()
    OA[...] = jnp.zeros_like(OA)
    RA[...] = jnp.zeros_like(RA)
    DOT[...] = jnp.zeros_like(DOT)
    iota16 = lax.broadcasted_iota(jnp.int32, (PIECE, 128), 0)

    def one_expert(e, _):
        slot = e % 2
        total = jnp.int32(0)
        for q in range(chunks):
            lo, hi = bnd_ref[blk_ref[q], first + e], bnd_ref[blk_ref[q], first + e + 1]
            p0 = lo // PIECE
            p1 = jnp.where(hi > lo, (hi + PIECE - 1) // PIECE, p0)

            def add(p, _, lo=lo, hi=hi, p0=p0, total=total, q=q):
                k = total + p - p0
                TR[k] = q * rows + p * PIECE
                TL[k] = lo - p * PIECE
                TH[k] = hi - p * PIECE
                return 0
            lax.fori_loop(p0, p1, add, 0)
            total = total + p1 - p0
        tiles = (total + pieces - 1) // pieces

        def pad(k, _):
            TR[k] = 0
            TL[k] = 0
            TH[k] = 0
            return 0
        lax.fori_loop(total, tiles * pieces, pad, 0)
        UA[...] = jnp.zeros_like(UA)
        DA[...] = jnp.zeros_like(DA)

        @pl.when(e == 0)
        def _():
            for c in copies:
                c.wait()
        for c in weights(e, slot):
            c.wait()

        @pl.when(e + 1 < count)
        def _():
            for c in weights(e + 1, 1 - slot):
                c.start()

        def one_tile(i, _):
            base = i * pieces
            for p in range(pieces):
                r = pl.ds(pl.multiple_of(TR[base + p], PIECE), PIECE)
                XG[pl.ds(p * PIECE, PIECE), :] = X[r, :]
                DG[pl.ds(p * PIECE, PIECE), :] = DY[r, :]
                ok = (iota16 >= TL[base + p]) & (iota16 < TH[base + p])
                VAL[pl.ds(p * PIECE, PIECE), :] = jnp.where(ok, 1.0, 0.0)
            valid = VAL[:, 0:1]

            def coef_of(logits, mixing):
                return pick_lane(mixing, lanes + 1) * pick_lane(lane_softmax(logits, 0, lanes), first + e) * valid
            dots, out, rg = ffn_tile(lanes, rm, XG[...], DG[...], coef_of, UP.at[slot], DN.at[slot], UA, DA, lambda: None)
            dots = jnp.broadcast_to(dots * valid, (tm, 128))
            for p in range(pieces):
                r = pl.ds(pl.multiple_of(TR[base + p], PIECE), PIECE)
                s = slice(p * PIECE, (p + 1) * PIECE)
                OA[r, :] += out[s]
                RA[r, :] += rg[s]
                DOT[r, :] += dots[s]
            return 0
        lax.fori_loop(0, tiles, one_tile, 0)

        @pl.when(e == count - 1)
        def _():
            for c in earlier:
                c.start()

        for g in range(count - 1):
            @pl.when(e == g + 1)
            def _(g=g):
                for c in flush(g):
                    c.wait()
        kind = False
        for g in entire:
            kind = kind | (e == g)
        stage_grads(ST, UA, DA, me_ref[0], order, kind)
        for g in range(count):
            @pl.when(e == g)
            def _(g=g):
                for c in flush(g):
                    c.start()
        return 0
    lax.fori_loop(0, count, one_expert, 0)
    for c in earlier:
        c.wait()
    last = []
    step = min(256, rows)
    line = lax.broadcasted_iota(jnp.int32, (PIECE, step), 0)
    for q in range(chunks):
        r = rows_of[q]
        o, g = OA[r, :], RA[r, :]
        if has[q]:
            o, g = o + X[r, :].astype(F32), g + DY[r, :].astype(F32)
        X[r, :] = o.astype(BF)
        DY[r, :] = g.astype(BF)
        if not has[q]:
            BD[q] = jnp.zeros(BD.shape[1:], BF)
        for i in range(rows // step):
            sl = slice(i * step, (i + 1) * step)
            dots = jnp.where(line == 1, DOT[pl.ds(q * rows + i * step, step), :].T[0:PIECE, :], 0.0)
            BD[q, :, sl] = (BD[q, :, sl].astype(F32) + dots).astype(BF)
        last += [pltpu.make_async_copy(X.at[r], out_refs[q], osem.at[0, q]), pltpu.make_async_copy(DY.at[r], rg_refs[q].at[pl.ds(0, rows)], osem.at[1, q]),
                 pltpu.make_async_copy(BD.at[q], rg_refs[q].at[pl.ds(rows, PIECE)], dsem.at[q])]
        for c in last[-3:]:
            c.start()
    for c in last + flush(count - 1):
        c.wait()


def ffn_experts(me, blocks, bounds, xs, dys, rm, up, down, first, count, whole, base, order, deps=()):
    chunks = len(xs)
    rows, d = xs[0].shape
    lanes, _, f = up.shape
    n = chunks * rows
    tm = TILE_EXPERT
    bits = len(order)
    half = 1 << (bits - 1)
    grad, entire = [jax.ShapeDtypeStruct((k * half, 2, d >> bits, f), BF) for k in (1, 2)]
    part, lined = jax.ShapeDtypeStruct((rows, d), BF), jax.ShapeDtypeStruct((rows + PIECE, d), BF)
    table = n // PIECE + chunks * lanes + 2 * tm // PIECE
    vm = pl.BlockSpec(memory_space=pltpu.VMEM)
    has = tuple(b is not None for b in base[0])
    more = [b for k in range(2) for b in base[k] if b is not None]
    res = pl.pallas_call(
        partial(expert_kernel, (first, count, whole, chunks, rows, d, tm, lanes, order, has, len(deps))),
        name="ffn_experts",
        out_shape=[part] * chunks + [lined] * chunks + [entire] * sum(whole) + [grad] * (2 * (count - sum(whole))),
        in_specs=[SMEM] * 3 + [ANY] * (len(deps) + 2 * chunks) + [vm] + [ANY] * (2 + len(more)),
        out_specs=[ANY] * (2 * chunks + 2 * count - sum(whole)),
        scratch_shapes=[
            pltpu.VMEM((n, d), BF), pltpu.VMEM((n, d), BF), pltpu.VMEM((2, d, f), BF), pltpu.VMEM((2, f, d), BF),
            pltpu.VMEM((d, f), F32), pltpu.VMEM((d, f), F32), pltpu.VMEM((2 * half, 2, d >> bits, f), BF),
            pltpu.VMEM((tm, d), BF), pltpu.VMEM((tm, d), BF), pltpu.VMEM((tm, 128), F32),
            pltpu.VMEM((n, d), F32), pltpu.VMEM((n, d), F32), pltpu.VMEM((n, 128), F32), pltpu.VMEM((chunks, PIECE, d), BF),
            pltpu.SMEM((table,), jnp.int32), pltpu.SMEM((table,), jnp.int32), pltpu.SMEM((table,), jnp.int32),
            pltpu.SemaphoreType.DMA((2 * chunks,)), pltpu.SemaphoreType.DMA((2, 2)), pltpu.SemaphoreType.DMA((2,)), pltpu.SemaphoreType.DMA((2, chunks)), pltpu.SemaphoreType.DMA((chunks,)),
        ],
        cost_estimate=SMALL,
        compiler_params=pltpu.CompilerParams(vmem_limit_bytes=VMEM),
    )(me, blocks, bounds, *deps, *xs, *dys, rm, up, down, *more)
    at = 2 * chunks + sum(whole)
    rest = iter(res[at:])
    keep = [next(rest) for g in range(count) if not whole[g]]
    return res[:chunks], res[chunks:2 * chunks], res[2 * chunks:at], keep, list(rest)


def split_add_kernel(deps, *refs):
    ka, kb, ca, cb, keep, send = refs[deps:]
    keep[...] = (ka[...].astype(F32) + ca[...].astype(F32)).astype(BF)
    send[...] = (kb[...].astype(F32) + cb[...].astype(F32)).astype(BF)


def split_add(kept, came, deps=()):
    h, m, blk, f = kept.shape
    near = pl.BlockSpec((1, m, blk, f), lambda i: (i, 0, 0, 0))
    far = pl.BlockSpec((1, m, blk, f), lambda i: (i + h // 2, 0, 0, 0))
    out = jax.ShapeDtypeStruct((h // 2, m, blk, f), BF)
    return pl.pallas_call(
        partial(split_add_kernel, len(deps)),
        name="split_add",
        grid=(h // 2,),
        in_specs=[ANY] * len(deps) + [near, far, near, far],
        out_specs=[near, near],
        out_shape=[out, out],
        cost_estimate=SMALL,
        compiler_params=pltpu.CompilerParams(vmem_limit_bytes=VMEM),
    )(*deps, kept, kept, came, came)


def last_add_kernel(deps, turns, *refs):
    terms = refs[deps:-len(turns)]
    outs = refs[-len(turns):]
    for k, turned in enumerate(turns):
        total = terms[0][0, k].astype(F32)
        for v in terms[1:]:
            total = total + v[0, k].astype(F32)
        outs[k][...] = (total.T if turned else total).reshape(outs[k].shape)


def last_add(terms, turns, place=None, stacks=None, deps=()):
    _, m, blk, f = terms[0].shape
    shapes = [(f, blk) if turned else (blk, f) for turned in turns]
    aliases = {}
    if place is None:
        out_shape = [jax.ShapeDtypeStruct(s, F32) for s in shapes]
        out_specs = [pl.BlockSpec(s, lambda i: (0, 0)) for s in shapes]
    else:
        count, at = place
        out_shape = [jax.ShapeDtypeStruct((count,) + s, F32) for s in shapes]
        out_specs = [pl.BlockSpec((1,) + s, lambda i: (at, 0, 0)) for s in shapes]
        if stacks is not None:
            aliases = {k: k for k in range(m)}
            deps = tuple(stacks) + tuple(deps)
    full = pl.BlockSpec((1, m, blk, f), lambda i: (0, 0, 0, 0))
    return pl.pallas_call(
        partial(last_add_kernel, len(deps), turns),
        name="last_add",
        grid=(1,),
        in_specs=[ANY] * len(deps) + [full] * len(terms),
        out_specs=out_specs,
        out_shape=out_shape,
        input_output_aliases=aliases,
        cost_estimate=SMALL,
        compiler_params=pltpu.CompilerParams(vmem_limit_bytes=VMEM),
    )(*deps, *terms)


def hold(v, deps):
    return pl.pallas_call(
        lambda *refs: None,
        name="hold",
        in_specs=[ANY] * (1 + len(deps)),
        out_specs=ANY,
        out_shape=jax.ShapeDtypeStruct(v.shape, v.dtype),
        input_output_aliases={0: 0},
        cost_estimate=SMALL,
    )(v, *deps)


HD = 64
LANES = 128


def head_part(v, h):
    lane = lax.broadcasted_iota(jnp.int32, v.shape, 1)
    return jnp.where((lane // HD) == h, v, jnp.zeros((), v.dtype))


def masked_scores(st, key_first, query_first, prefix):
    key_pos = key_first + lax.broadcasted_iota(jnp.int32, st.shape, 0)
    query_pos = query_first + lax.broadcasted_iota(jnp.int32, st.shape, 1)
    seen = key_pos <= query_pos
    if prefix is not None:
        seen = seen | (key_pos < prefix)
    return jnp.where(seen, st, -1e30)


def score_block(k2, qm, half, length, prefix):
    mid = length // 2
    if half == 0:
        return masked_scores(dot(k2[0:mid], qm, 1, 1), 0, 0, prefix)
    low = dot(k2[0:mid], qm, 1, 1)
    high = masked_scores(dot(k2[mid:length], qm, 1, 1), mid, mid, None)
    return jnp.concatenate([low, high], 0)


def attn_forward_kernel(length, pieces, aliased, prefix_ref, at_ref, *refs):
    n1_ref = refs[0]
    w_refs = [(r, i) for r, n in zip(refs[1:], pieces) for i in range(n)]
    q_ref, k_ref, v_ref, ctx_ref, lse_ref = refs[1 + len(pieces) + aliased:]
    mid = length // 2
    prefix = prefix_ref[0]
    n1 = n1_ref[...]
    for out, (w, i) in zip((q_ref, k_ref, v_ref), w_refs):
        out[...] = dot(n1, w[i], 1, 0).astype(BF)
    vt = v_ref[...].T
    k2 = k_ref[...]
    for half in range(2):
        rows = pl.ds(half * mid, mid)
        q2 = q_ref[rows, :] * jnp.asarray(HD ** -0.5, BF)
        keys = mid * (half + 1)
        parts = []
        for h in range(2):
            st = score_block(k2, head_part(q2, h), half, length, prefix)
            top = jnp.max(st, axis=0, keepdims=True)
            p = jnp.exp(st - top)
            total = jnp.sum(p, axis=0, keepdims=True)
            c = dot(vt[h * HD:(h + 1) * HD, 0:keys], p.astype(BF), 1, 0)
            parts.append(c / total)
            lse_ref[0, h:h + 1, rows] = top + jnp.log(total)
        ctx_ref[rows, :] = jnp.concatenate(parts, 0).T.astype(BF)


def attn_forward(prefix, at, n1, ws, heads, earlier=(), deps=()):
    length, d = n1.shape
    pairs = ws[0].shape[2] // LANES
    col = pl.BlockSpec((length, LANES), lambda p, _, at_ref: (0, at_ref[p]))
    out = jax.ShapeDtypeStruct((length, heads), BF)
    done = len(earlier)
    skipped = len(deps)
    return pl.pallas_call(
        skip(partial(attn_forward_kernel, length, tuple(w.shape[0] for w in ws), done), 2, skipped),
        name="attn_forward",
        grid_spec=pltpu.PrefetchScalarGridSpec(
            num_scalar_prefetch=2, grid=(pairs,),
            in_specs=[ANY] * skipped + [pl.BlockSpec((length, d), lambda p, *_: (0, 0))]
            + [pl.BlockSpec((w.shape[0], d, LANES), lambda p, *_: (0, 0, p)) for w in ws] + [ANY] * done,
            out_specs=[col] * 4 + [pl.BlockSpec((1, 8, length), lambda p, _, at_ref: (at_ref[p], 0, 0))]),
        out_shape=[out] * 4 + [jax.ShapeDtypeStruct((heads // LANES, 8, length), F32)],
        input_output_aliases={3 + skipped + len(ws) + k: k for k in range(done)},
        cost_estimate=SMALL,
        compiler_params=pltpu.CompilerParams(vmem_limit_bytes=VMEM),
    )(prefix, at, *deps, n1, *ws, *earlier)


def attn_backward_kernel(length, bits, based, prefix_ref, me_ref, mc_ref, n1_ref, wo_ref, w_ref, q_ref, k_ref, v_ref, ctx_ref, lse_ref, *refs):
    base_ref = refs[0] if based else None
    ng_ref, grad_ref, NG, DC, DK, DV, DQ = refs[based:]
    mid = length // 2
    prefix = prefix_ref[0]
    me = me_ref[0]
    pair = pl.program_id(0)
    mc = mc_ref[...]
    DC[...] = dot(mc, wo_ref[...], 1, 1).astype(BF)
    k2, v2 = k_ref[...], v_ref[...]
    kt = k2.T
    scale = jnp.asarray(HD ** -0.5, BF)
    for half in range(2):
        rows = pl.ds(half * mid, mid)
        q2 = q_ref[rows, :] * scale
        dc2 = DC[rows, :]
        keys = mid * (half + 1)
        dv = jnp.zeros((keys, LANES), F32)
        dk = jnp.zeros((keys, LANES), F32)
        dq = []
        for h in range(2):
            qm, dcm = head_part(q2, h), head_part(dc2, h)
            st = score_block(k2, qm, half, length, prefix)
            p = jnp.exp(st - lse_ref[0, h:h + 1, rows])
            dv = dv + dot(p.astype(BF), dcm, 1, 0)
            dp = dot(v2[0:keys], dcm, 1, 1)
            ds = (p * (dp - jnp.sum(p * dp, axis=0, keepdims=True))).astype(BF)
            dk = dk + dot(ds, qm, 1, 0)
            dq.append(dot(kt[h * HD:(h + 1) * HD, 0:keys], ds, 1, 0))
        DQ[rows, :] = (jnp.concatenate(dq, 0) * HD ** -0.5).T.astype(BF)
        if half == 0:
            DK[0:mid, :] = dk
            DV[0:mid, :] = dv
        else:
            DK[0:mid, :] += dk[0:mid]
            DV[0:mid, :] += dv[0:mid]
            DK[mid:length, :] = dk[mid:length]
            DV[mid:length, :] = dv[mid:length]
    dq, dk, dv = DQ[...], DK[...].astype(BF), DV[...].astype(BF)
    ng = dot(dq, w_ref[0], 1, 1) + dot(dk, w_ref[1], 1, 1) + dot(dv, w_ref[2], 1, 1)

    @pl.when(pair == 0)
    def _():
        NG[...] = ng

    @pl.when(pair > 0)
    def _():
        NG[...] += ng
    n1 = n1_ref[...]
    grads = [dot(n1, x, 0, 0) for x in (dq, dk, dv)] + [dot(mc, ctx_ref[...], 0, 0)]
    blk = n1.shape[1] >> bits
    for c in range(1 << bits):
        slot = slot_of(jnp.int32(c) ^ me, range(bits))
        for i in range(4):
            grad_ref[slot, i] = grads[i][c * blk:(c + 1) * blk].astype(BF)

    @pl.when(pair == pl.num_programs(0) - 1)
    def _():
        done = NG[...]
        if based:
            done = done + base_ref[...].astype(F32)
        ng_ref[...] = done.astype(BF)


def attn_backward(prefix, me, mc, n1, wo, w, saved, base, bits, deps=()):
    q, k, v, ctx, lse = saved
    length, d = n1.shape
    heads = w.shape[2]
    pairs = heads // LANES
    blk = d >> bits
    col = pl.BlockSpec((length, LANES), lambda p, *_: (0, p))
    full = pl.BlockSpec((length, d), lambda p, *_: (0, 0))
    extra = [] if base is None else [base]
    return pl.pallas_call(
        skip(partial(attn_backward_kernel, length, bits, len(extra)), 2, len(deps)),
        name="attn_backward",
        grid_spec=pltpu.PrefetchScalarGridSpec(
            num_scalar_prefetch=2, grid=(pairs,),
            in_specs=[ANY] * len(deps) + [full, full, pl.BlockSpec((LANES, d), lambda p, *_: (p, 0)), pl.BlockSpec((3, d, LANES), lambda p, *_: (0, 0, p)),
                      col, col, col, col, pl.BlockSpec((1, 8, length), lambda p, *_: (p, 0, 0))] + [full] * len(extra),
            out_specs=[full, pl.BlockSpec((1 << bits, 4, blk, LANES), lambda p, *_: (0, 0, 0, p))],
            scratch_shapes=[pltpu.VMEM((length, d), F32), pltpu.VMEM((length, LANES), BF),
                            pltpu.VMEM((length, LANES), F32), pltpu.VMEM((length, LANES), F32), pltpu.VMEM((length, LANES), BF)]),
        out_shape=[jax.ShapeDtypeStruct((length, d), BF), jax.ShapeDtypeStruct((1 << bits, 4, blk, heads), BF)],
        cost_estimate=SMALL,
        compiler_params=pltpu.CompilerParams(vmem_limit_bytes=VMEM),
    )(prefix, me, *deps, mc, n1, wo, w, q, k, v, ctx, lse, *extra)


EPS = 1e-5


def normalise(v):
    centered = v - jnp.mean(v, axis=1, keepdims=True)
    r = lax.rsqrt(jnp.mean(centered * centered, axis=1, keepdims=True) + EPS)
    return centered * r, r


def norm_backward(xhat, r, grad, gain):
    scaled = grad * gain
    return r * (scaled - jnp.mean(scaled, axis=1, keepdims=True) - xhat * jnp.mean(scaled * xhat, axis=1, keepdims=True))


def order_rows(pos, rows_to_slots):
    n = pos.shape[1] if rows_to_slots else pos.shape[0]
    slot = lax.broadcasted_iota(jnp.int32, (n, n), 0 if rows_to_slots else 1)
    return jnp.where(slot == pos, 1.0, 0.0).astype(BF)


def first_norm_kernel(members, j_ref, *refs):
    xs, (gain, shift, dy, pos, out, sorted_dy) = refs[:members], refs[members:]
    for k in range(members):
        @pl.when(pl.program_id(0) == k)
        def _(k=k):
            xhat, _ = normalise(xs[k][...].astype(F32))
            out[...] = (xhat * gain[...] + shift[...]).astype(BF)
            if k == 0:
                sorted_dy[...] = dot(order_rows(pos[...], True), dy[...], 1, 0).astype(BF)


def first_norm(j, xs, gain, shift, dy, pos):
    members = len(xs)
    rows, d = xs[0].shape
    fixed = lambda shape: pl.BlockSpec(shape, lambda p, *_: (0, 0))
    return pl.pallas_call(
        partial(first_norm_kernel, members),
        name="first_norm",
        grid_spec=pltpu.PrefetchScalarGridSpec(
            num_scalar_prefetch=1, grid=(members,),
            in_specs=[fixed((rows, d))] * members + [fixed((1, d))] * 2 + [fixed((rows, d)), fixed((1, rows))],
            out_specs=[pl.BlockSpec((rows, d), lambda p, j_ref: (lax.rem(j_ref[0] + p, members), 0)), fixed((rows, d))]),
        out_shape=[jax.ShapeDtypeStruct((members * rows, d), BF), jax.ShapeDtypeStruct((rows, d), BF)],
        cost_estimate=SMALL,
        compiler_params=pltpu.CompilerParams(vmem_limit_bytes=VMEM),
    )(j, *xs, gain, shift, dy, pos)


def project_kernel(parts, *refs):
    total = dot(refs[0][...], refs[parts][...], 1, 0)
    for i in range(1, parts):
        total = total + dot(refs[i][...], refs[parts + i][...], 1, 0)
    refs[-1][0] = total.astype(BF)


def project(contexts, weights, members):
    parts = len(contexts)
    length, heads = contexts[0].shape
    d = weights[0].shape[1]
    rows = length // members
    return pl.pallas_call(
        partial(project_kernel, parts),
        name="project",
        grid=(members,),
        in_specs=[pl.BlockSpec((rows, heads), lambda p: (p, 0))] * parts + [pl.BlockSpec((heads, d), lambda p: (0, 0))] * parts,
        out_specs=pl.BlockSpec((1, rows, d), lambda p: (p, 0, 0)),
        out_shape=jax.ShapeDtypeStruct((members, rows, d), BF),
        cost_estimate=SMALL,
        compiler_params=pltpu.CompilerParams(vmem_limit_bytes=VMEM),
    )(*contexts, *weights)


def second_norm_kernel(came, x, gain, shift, pos, middle, n2):
    mid = x[...].astype(F32)
    for k in range(came.shape[0]):
        mid = mid + came[k].astype(F32)
    middle[...] = mid
    xhat, _ = normalise(mid)
    normed = (xhat * gain[...] + shift[...]).astype(BF)
    n2[...] = dot(order_rows(pos[...], True), normed, 1, 0).astype(BF)


def second_norm(came, x, gain, shift, pos):
    rows, d = x.shape
    fixed = lambda shape: pl.BlockSpec(shape, lambda p: (0,) * len(shape))
    return pl.pallas_call(
        second_norm_kernel,
        name="second_norm",
        grid=(1,),
        in_specs=[fixed(came.shape), fixed((rows, d)), fixed((1, d)), fixed((1, d)), fixed((1, rows))],
        out_specs=[fixed((rows, d))] * 2,
        out_shape=[jax.ShapeDtypeStruct((rows, d), F32), jax.ShapeDtypeStruct((rows, d), BF)],
        cost_estimate=SMALL,
        compiler_params=pltpu.CompilerParams(vmem_limit_bytes=VMEM),
    )(came, x, gain, shift, pos)


def add_small(a, b, deps):
    def kernel(*refs):
        refs[-1][...] = refs[-3][...] + refs[-2][...]
    full = pl.BlockSpec(memory_space=pltpu.VMEM)
    return pl.pallas_call(kernel, name="add_small", in_specs=[ANY] * len(deps) + [full, full], out_specs=full,
                          out_shape=jax.ShapeDtypeStruct(a.shape, a.dtype), cost_estimate=SMALL)(*deps, a, b)


def hi_lo(v):
    hi = v.astype(BF)
    return hi, (v - hi.astype(F32)).astype(BF)


def middle_backward_kernel(single, bnd_ref, t_ref, *refs):
    it = iter(refs)
    parts = [next(it) for _ in range(single)]
    n2, rm, middle, dy, gain, pos, mg_ref, mc_ref, sums_ref = it
    t = t_ref[0]
    n2v, rmv = n2[...], rm[...]
    rows = n2v.shape[0]
    total = parts[0][0:rows, :].astype(F32)
    lines = parts[0][rows:rows + PIECE, 0:rows].astype(F32)
    for p in parts[1:]:
        total = total + p[0:rows, :].astype(F32)
        lines = lines + p[rows:rows + PIECE, 0:rows].astype(F32)
    dots = jnp.concatenate([lines, jnp.zeros((128 - PIECE, rows), F32)], axis=0).T
    experts = bnd_ref.shape[1] - 1
    logits = dot(n2v, rmv, 1, 0)
    route_prob = lane_softmax(logits, 0, experts)
    mixing = lane_softmax(logits, experts, experts + 2)
    row = lax.broadcasted_iota(jnp.int32, (rows, 1), 0)
    route = jnp.zeros((rows, 1), jnp.int32)
    for e in range(1, experts):
        route = route + (row >= bnd_ref[t, e]).astype(jnp.int32)
    gate = pick_lane(route_prob, route)
    m0, m1 = pick_lane(mixing, experts), pick_lane(mixing, experts + 1)
    dense_dot, expert_dot = dots[:, 0:1], dots[:, 1:2]
    d0, d1 = dense_dot, expert_dot * gate
    inner = m0 * d0 + m1 * d1
    lane = lax.broadcasted_iota(jnp.int32, logits.shape, 1)
    grad = expert_dot * (m1 * gate) * (jnp.where(lane == route, 1.0, 0.0) - route_prob)
    grad = jnp.where(lane < experts, grad, 0.0)
    grad = jnp.where(lane == experts, m0 * (d0 - inner), grad)
    grad = jnp.where(lane == experts + 1, m1 * (d1 - inner), grad)
    hi, lo = hi_lo(grad)
    total = total + dot(hi, rmv, 1, 1) + dot(lo, rmv, 1, 1)
    sums_ref[0:8, :] = (dot(hi.T, n2v, 1, 0) + dot(lo.T, n2v, 1, 0))[0:8]
    g = dot(order_rows(pos[...], False), total.astype(BF), 1, 0)
    xhat, r = normalise(middle[...])
    sums_ref[8:16, :] = jnp.zeros((8, g.shape[1]), F32)
    sums_ref[8:9, :] = jnp.sum(g * xhat, axis=0, keepdims=True)
    sums_ref[9:10, :] = jnp.sum(g, axis=0, keepdims=True)
    mg = dy[...].astype(F32) + norm_backward(xhat, r, g, gain[...])
    mg_ref[...] = mg
    for k in range(mc_ref.shape[0]):
        mc_ref[k] = mg.astype(BF)


def middle_backward(bounds, t, parts, n2, rm, middle, dy, gain, pos, members, deps=()):
    rows, d = n2.shape
    fixed = lambda shape: pl.BlockSpec(shape, lambda p, *_: (0, 0))
    big = fixed((rows, d))
    return pl.pallas_call(
        skip(partial(middle_backward_kernel, len(parts)), 2, len(deps)),
        name="middle_backward",
        grid_spec=pltpu.PrefetchScalarGridSpec(
            num_scalar_prefetch=2, grid=(1,),
            in_specs=[ANY] * len(deps) + [fixed((rows + PIECE, d))] * len(parts)
            + [big, fixed((d, 128)), big, big, fixed((1, d)), fixed((rows, 1))],
            out_specs=[big, pl.BlockSpec((members, rows, d), lambda p, *_: (0, 0, 0)), fixed((16, d))]),
        out_shape=[jax.ShapeDtypeStruct((rows, d), F32), jax.ShapeDtypeStruct((members, rows, d), BF), jax.ShapeDtypeStruct((16, d), F32)],
        cost_estimate=SMALL,
        compiler_params=pltpu.CompilerParams(vmem_limit_bytes=VMEM),
    )(bounds, t, *deps, *parts, n2, rm, middle, dy, gain, pos)


def layer_out_kernel(*refs):
    parts, (middle, pos, out) = refs[:-3], refs[-3:]
    total = parts[0][...].astype(F32)
    for p in parts[1:]:
        total = total + p[...].astype(F32)
    hi, lo = hi_lo(total)
    move = order_rows(pos[...], False)
    out[...] = (middle[...] + dot(move, hi, 1, 0) + dot(move, lo, 1, 0)).astype(BF)


def layer_out(parts, middle, pos, deps=()):
    rows, d = middle.shape
    big = pl.BlockSpec((rows, d), lambda p: (0, 0))
    return pl.pallas_call(
        skip(layer_out_kernel, 0, len(deps)),
        name="layer_out",
        grid=(1,),
        in_specs=[ANY] * len(deps) + [big] * (len(parts) + 1) + [pl.BlockSpec((rows, 1), lambda p: (0, 0))],
        out_specs=big,
        out_shape=jax.ShapeDtypeStruct((rows, d), BF),
        cost_estimate=SMALL,
        compiler_params=pltpu.CompilerParams(vmem_limit_bytes=VMEM),
    )(*deps, *parts, middle, pos)


def add_parts_kernel(*refs):
    total = refs[0][...].astype(F32)
    for p in refs[1:-1]:
        total = total + p[...].astype(F32)
    refs[-1][...] = total.astype(BF)


def add_parts(parts, deps=()):
    rows, d = parts[0].shape
    tile = pl.BlockSpec((rows, d), lambda p: (p, 0))
    return pl.pallas_call(
        skip(add_parts_kernel, 0, len(deps)),
        name="add_parts",
        grid=(1,),
        in_specs=[ANY] * len(deps) + [tile] * len(parts),
        out_specs=tile,
        out_shape=jax.ShapeDtypeStruct((rows, d), BF),
        cost_estimate=SMALL,
        compiler_params=pltpu.CompilerParams(vmem_limit_bytes=VMEM),
    )(*deps, *parts)


def input_backward_kernel(parts, x, mg, gain, out, sums):
    g = parts[0].astype(F32)
    for k in range(1, parts.shape[0]):
        g = g + parts[k].astype(F32)
    xhat, r = normalise(x[...].astype(F32))
    sums[...] = jnp.zeros_like(sums)
    sums[0:1, :] = jnp.sum(g * xhat, axis=0, keepdims=True)
    sums[1:2, :] = jnp.sum(g, axis=0, keepdims=True)
    out[...] = mg[...] + norm_backward(xhat, r, g, gain[...])


def input_backward(parts, x, mg, gain, deps=()):
    rows, d = x.shape
    fixed = lambda shape: pl.BlockSpec(shape, lambda p: (0, 0))
    big = fixed((rows, d))
    return pl.pallas_call(
        skip(input_backward_kernel, 0, len(deps)),
        name="input_backward",
        grid=(1,),
        in_specs=[ANY] * len(deps) + [pl.BlockSpec(parts.shape, lambda p: (0, 0, 0))] + [big] * 2 + [fixed((1, d))],
        out_specs=[big, fixed((8, d))],
        out_shape=[jax.ShapeDtypeStruct((rows, d), F32), jax.ShapeDtypeStruct((8, d), F32)],
        cost_estimate=SMALL,
        compiler_params=pltpu.CompilerParams(vmem_limit_bytes=VMEM),
    )(*deps, parts, x, mg, gain)


class Everywhere:
    def __init__(self, v):
        self.v = v
        bits = {axis: lax.axis_size(axis).bit_length() - 1 for axis in ("tensor", "dp")}
        self.hops = [("tensor", 1 << b) for b in range(bits["tensor"])] + [("dp", 1 << b) for b in range(bits["dp"])]
        self.launch()

    def launch(self):
        if self.hops:
            axis, bit = self.hops.pop(0)
            self.came = lax.ppermute(self.v, axis, [(i, i ^ bit) for i in range(lax.axis_size(axis))])
        else:
            self.came = None

    def add(self, mark):
        if self.came is None:
            return mark
        self.v = add_small(self.v, self.came, mark)
        self.launch()
        return (self.v,)


def over_dp(v, bit):
    return lax.ppermute(v, "dp", [(i, i ^ (1 << bit)) for i in range(lax.axis_size("dp"))])


def shards(inputs, cotangent, routes, prefixes, gain_one, shift_one, qkv_weight, out_weight, gain_two, shift_two,
           up_weight, down_weight, expert_up, expert_down, router_weight, mix_weight):
    rows, d = inputs.shape
    tensor = lax.axis_size("tensor")
    dp = lax.axis_size("dp")
    bits = dp.bit_length() - 1
    seqs = prefixes.shape[0]
    members = tensor // seqs
    experts = expert_up.shape[0]
    heads = qkv_weight.shape[2]
    pairs = heads // LANES
    t = lax.axis_index("tensor")
    s, j = t // members, t % members
    me = lax.axis_index("dp").astype(jnp.int32)
    me1, j1, t1 = me.reshape(1), j.astype(jnp.int32).reshape(1), t.astype(jnp.int32).reshape(1)
    place = lambda a, b: (a % seqs) * members + b % members
    everyone = [(a, b) for a in range(seqs) for b in range(members)]

    def from_member(v, k):
        return lax.ppermute(v, "tensor", [(place(a, b), place(a, b - k)) for a, b in everyone])

    def from_sequence(v, k):
        return lax.ppermute(v, "tensor", [(place(a, b), place(a - k, b)) for a, b in everyone])

    def to_member(v, k):
        return from_member(v, -k)

    def to_sequence(v, k):
        return from_sequence(v, -k)

    route_blocks = routes.reshape(tensor, rows)
    bounds = jnp.stack([jnp.sum((route_blocks < e).astype(jnp.int32), axis=1) for e in range(experts + 1)], axis=1)
    key_col = lax.dynamic_slice_in_dim(routes, t * rows, rows, 0) * rows + jnp.arange(rows, dtype=jnp.int32)[:, None]
    key_row = key_col.reshape(1, rows)
    pos_row = jnp.sum((key_col < key_row).astype(jnp.int32), axis=0, keepdims=True)
    pos_col = jnp.sum((key_row < key_col).astype(jnp.int32), axis=1, keepdims=True)
    chunk = [(dj, ds) for dj in range(members) for ds in range(seqs)]
    blocks = jnp.stack([((s + ds) % seqs) * members + (j + dj) % members for dj, ds in chunk]).astype(jnp.int32)
    near = [q for q, (dj, ds) in enumerate(chunk) if ds == 0]
    far = [q for q, (dj, ds) in enumerate(chunk) if ds > 0]

    xs = [inputs] + [from_member(inputs, k) for k in range(1, members)]
    flip = me & 1
    relay = pairs % 2 == 0 and dp > 1
    w_own = jnp.transpose(qkv_weight, (1, 0, 2))
    fetched = []
    for ds in range(1, seqs):
        if relay:
            half = lax.dynamic_slice_in_dim(qkv_weight, flip * (heads // 2), heads // 2, 2)
            fetched.append([from_sequence(jnp.transpose(half[:, a:b], (1, 0, 2)), ds) for a, b in ((0, 2), (2, 3))])
        else:
            fetched.append([from_sequence(w_own, ds)])
    wo_all = [out_weight] + [from_sequence(out_weight, ds) for ds in range(1, seqs)]
    gain_one, shift_one, gain_two, shift_two = [v.reshape(1, d) for v in (gain_one, shift_one, gain_two, shift_two)]
    prefix = lax.dynamic_slice_in_dim(prefixes, s, 1)
    rm = jnp.concatenate([router_weight, mix_weight, jnp.zeros((d, LANES - experts - 2), BF)], axis=1)
    n1, dys = first_norm(j1, xs, gain_one, shift_one, cotangent, pos_row)
    columns = jnp.arange(pairs, dtype=jnp.int32)
    pieces = [[] for _ in fetched]
    fence = (n1,)
    if relay:
        for k, got in enumerate(fetched):
            held = hold(got[0], (n1,))
            pieces[k] = [[held], [over_dp(held, 0)]]
            fence += (held,)
    saved = [attn_forward(prefix, columns, n1, [w_own], heads, deps=fence[1:] + (rm,))]
    if relay:
        for k, got in enumerate(fetched):
            held = hold(got[1], (saved[0][4],))
            pieces[k][0].append(held)
            pieces[k][1].append(over_dp(held, 0))
    else:
        pieces = [[got] for got in fetched]
    w_all = [w_own]
    for halves in pieces:
        part = ()
        for k, ws in enumerate(halves):
            at = (columns + (flip ^ k) * (pairs // 2))[:pairs // 2] if relay else columns
            part = attn_forward(prefix, at, n1, ws, heads, part, deps=() if part else (saved[-1][4],))
        saved.append(part)
        whole = [jnp.concatenate(ws, axis=0) for ws in halves]
        if relay:
            whole = [jnp.where(flip == 0, jnp.concatenate(whole, axis=2), jnp.concatenate(whole[::-1], axis=2))]
        w_all.append(whole[0])
    contexts = [v[3] for v in saved]

    def spread(mine):
        out = list(mine)
        for k in range(1, members):
            out += [from_member(m, k) for m in mine]
        return out

    dy_mine = [dys] + [from_sequence(dys, ds) for ds in range(1, seqs)]
    dy_near = [dys] + [from_member(dys, k) for k in range(1, members)]
    sent = project(contexts, wo_all, members)

    def exchange(v):
        return lax.all_to_all(v, "tensor", 0, 0, axis_index_groups=[[place(a, b) for b in range(members)] for a in range(seqs)], tiled=True)

    came = exchange(sent)
    middle, n2 = second_norm(came, inputs, gain_two, shift_two, pos_row)
    n2_mine = [n2] + [from_sequence(n2, ds) for ds in range(1, seqs)]
    n2_near = [n2] + [from_member(n2, k) for k in range(1, members)]

    straight = tuple(range(bits))
    pick = lambda v, which: [v[q] for q in which]
    out_a, rg_a, sums = ffn_dense(me1, n2_near, dy_near, rm, up_weight, down_weight, experts, straight, deps=tuple(dy_mine[1:]))
    n2_all, dy_all = [], []
    n2_far, dy_far = [[hold(v, (out_a[0],)) for v in mine[1:]] for mine in (n2_mine, dy_mine)]
    for k in range(members):
        n2_all += [n2_near[k]] + [from_member(v, k) if k else v for v in n2_far]
        dy_all += [dy_near[k]] + [from_member(v, k) if k else v for v in dy_far]
    base = [[None] * tensor, [None] * tensor]
    for k, q in enumerate(near):
        base[0][q], base[1][q] = out_a[k], rg_a[k]
    by_scatter = [e == 0 for e in range(experts)]
    out_e, rg_e, whole, keep_e, send_e = ffn_experts(me1, blocks, bounds, n2_all, dy_all, rm, expert_up, expert_down, 0, 1, (True,), base, straight)
    out_e, rg_e, whole = list(out_e), list(rg_e), list(whole)
    out_b, rg_b, ends = ffn_dense(me1, pick(n2_all, far), pick(dy_all, far), rm, up_weight, down_weight, experts, straight,
                                  (pick(out_e, far), pick(rg_e, far)), sums)
    for k, q in enumerate(far):
        out_e[q], rg_e[q] = out_b[k], rg_b[k]
    if experts > 1:
        out_e, rg_e, entire, keep_e, send_e = ffn_experts(me1, blocks, bounds, n2_all, dy_all, rm, expert_up, expert_down, 1, experts - 1, tuple(by_scatter[1:]), (out_e, rg_e), straight)
        whole += list(entire)

    index = {c: q for q, c in enumerate(chunk)}
    def to_owner(parts):
        mine = [[parts[index[0, ds]]] + [to_member(parts[index[k, ds]], k) for k in range(1, members)] for ds in range(seqs)]
        return mine[0], mine[1:]

    def onward(terms, deps):
        sums = [add_parts(v, deps) for v in terms]
        return [to_sequence(v, ds + 1) for ds, v in enumerate(sums)], sums

    class Halving:
        def __init__(self, keep, send, order):
            self.keep, self.send, self.order, self.at = keep, send, order, 0

        def launch(self, deps=()):
            if deps:
                self.send = hold(self.send, deps)
            self.came = over_dp(self.send, self.order[self.at])
            self.at += 1

        def add(self, mark):
            self.keep, self.send = split_add(self.keep, self.came, mark)
            self.launch()
            return (self.send,)

        def rest(self, mark):
            while self.at < bits:
                mark = self.add(mark)
            return mark

    scattered = []
    for v in whole:
        flat = lax.psum_scatter(v.reshape(-1, v.shape[-1]), "dp", scatter_dimension=0, tiled=True)
        scattered.append(flat.reshape((1,) + v.shape[1:]))

    halvings = [Halving(keep, send, straight) for keep, send in zip(keep_e, send_e)]
    dense_sum = Halving(ends[0], ends[1], straight)
    sum_of = dict(enumerate(scattered + halvings))
    rg_near, rg_far = to_owner(rg_e)
    for v in [dense_sum] + halvings[:2]:
        v.launch()
    mark = dense_sum.add((out_e[0],))
    came_far, terms = onward(rg_far, mark)
    mark = tuple(terms[:1]) + tuple(w_all[1:])
    mg, mc, sums_two = middle_backward(bounds, t1, rg_near + came_far, n2, rm, middle, cotangent, gain_two, pos_col, members, mark)
    mcs = exchange(mc).reshape(members * rows, d)
    mark = dense_sum.add((mc,))
    ngs = None
    grads = [None] * seqs
    for ds in list(range(1, seqs)) + [0]:
        ngs, grads[ds] = attn_backward(prefix, me1, mcs, n1, wo_all[ds], w_all[ds], saved[ds], ngs, bits, mark)
        mark = (grads[ds],)
        if ds == 1 or seqs == 1:
            for v in halvings[2:]:
                v.launch()
            mark = dense_sum.rest(mark)
            up_out, down_out = last_add([dense_sum.keep, dense_sum.came], (False, True), deps=mark)
            mark = (up_out,)
            if seqs > 1:
                grads[1] = hold(grads[1], mark)
            for v in halvings[:1]:
                mark = v.add(mark)
    moved = [to_sequence(grads[ds], ds) for ds in range(1, seqs)]
    ng_parts = exchange(ngs.reshape(members, rows, d))
    for v in halvings[1:2]:
        mark = v.add(mark)
    for v in halvings[:1]:
        mark = v.add(mark)
    input_grad, sums_one = input_backward(ng_parts, inputs, mg, gain_one, mark)
    mark = (sums_one,)
    sums = Everywhere(jnp.concatenate([sums_two, sums_one], axis=0))
    stacks = None

    def finish(e, mark):
        if by_scatter[e]:
            terms = [sum_of[e]]
        else:
            mark = sum_of[e].rest(mark)
            terms = [sum_of[e].keep, sum_of[e].came]
        done = last_add(terms, (False, True), (experts, e), stacks, mark)
        return done, (done[1],)

    keep = grads[0]
    for v in moved[:-1]:
        keep = (keep.astype(F32) + v.astype(F32)).astype(BF)
    if moved:
        keep, send = split_add(keep, moved[-1], mark)
        mark = (send,)
    else:
        keep, send = keep[:dp // 2], keep[dp // 2:]
    attn_sum = Halving(keep, send, straight)
    attn_sum.launch()
    for v in halvings[1:2]:
        mark = v.add(mark)
    for v in halvings[2:]:
        mark = v.add(mark)
    for e in range(min(3, experts)):
        stacks, mark = finish(e, mark)
    mark = attn_sum.add(mark)
    mark = sums.add(mark)
    for v in halvings[2:]:
        mark = v.add(mark)
    mark = sums.add(mark)
    out_near, out_far = to_owner([hold(v, mark) for v in out_e])
    out_came, terms = onward(out_far, mark)
    mark = tuple(terms[:1]) or mark
    mark = attn_sum.add(mark)
    mark = sums.add(mark)
    for e in range(3, experts):
        stacks, mark = finish(e, mark)
    expert_up_out, expert_down_out = stacks
    mark = sums.add(mark)
    layer_output = layer_out(out_near + out_came, middle, pos_col, mark)
    mark = (layer_output,)
    while sums.came is not None:
        mark = sums.add(mark)
    mark = attn_sum.rest(mark)
    *qkv_parts, out_out = last_add([attn_sum.keep, attn_sum.came], (False, False, False, True), deps=mark)
    lanes = d // (dp * tensor)
    begin = (me * tensor + t) * lanes
    small = lax.dynamic_slice_in_dim(sums.v, begin, lanes, 1)
    return (layer_output, input_grad, small[16], small[17], jnp.stack(qkv_parts, axis=1), out_out, small[8], small[9], up_out, down_out,
            expert_up_out, expert_down_out, small[0:experts].T, small[experts:experts + 2].T)


def solution(mesh):
    both = ("dp", "tensor")
    in_specs = (P(both, None), P(both, None), P("dp", None), P("dp"), P(), P(), P(None, None, "tensor"), P("tensor", None), P(), P(),
                P(None, "tensor"), P("tensor", None), P(None, None, "tensor"), P(None, "tensor", None), P(), P())
    out_specs = (P(both, None), P(both, None), P(both), P(both), P("dp", None, "tensor"), P("tensor", "dp"), P(both), P(both),
                 P("dp", "tensor"), P("tensor", "dp"), P(None, "dp", "tensor"), P(None, "tensor", "dp"), P(both, None), P(both, None))
    return jax.shard_map(shards, mesh=mesh, in_specs=in_specs, out_specs=out_specs, check_vma=False)
```
